32 devices in a mesh: dp: 2 (over core), expert: 4 (over z), tensor: 4 (over y, x).
Axes of the slice: x: 2, y: 2, z: 4, core: 2. Of those that a mesh axis runs over, the one named last changes fastest.
Arguments:
- tokens: bfloat16 [2048, 1024], P(('dp', 'expert')), may hold values from -6 to 6
- routes: int32 [2048, 8], P(('dp', 'expert')), may hold values from 0 to 31, all different within a row; in each aligned block of 256 rows (0 to 255, 256 to 511, ...) at most 80 rows name the same one
- gain_first: float32 [1024], replicated, may hold values from 0.5 to 1.5
- w_query: bfloat16 [1024, 1024], P(None, 'tensor'), may hold values from -0.25 to 0.25
- w_key: bfloat16 [1024, 512], P(None, 'tensor'), may hold values from -0.25 to 0.25
- w_value: bfloat16 [1024, 512], P(None, 'tensor'), may hold values from -0.1875 to 0.1875
- w_output: bfloat16 [1024, 1024], P('tensor'), may hold values from -1 to 1
- gain_second: float32 [1024], replicated, may hold values from 0.5 to 1.5
- w_router: bfloat16 [1024, 32], replicated, may hold values from -0.09375 to 0.09375
- w_gate: bfloat16 [32, 1024, 512], P('expert', None, 'tensor'), may hold values from -0.1875 to 0.1875
- w_up: bfloat16 [32, 1024, 512], P('expert', None, 'tensor'), may hold values from -0.1875 to 0.1875
- w_down: bfloat16 [32, 512, 1024], P('expert', 'tensor'), may hold values from -0.75 to 0.75
- cotangent: bfloat16 [2048, 1024], P(('dp', 'expert')), may hold values from -6 to 6
Outputs:
- output: bfloat16 [2048, 1024], P(('dp', 'expert'))
- loss_value: float32 [32], replicated
- input_grad: float32 [2048, 1024], P(('dp', 'expert'))
- grad_gain_first: float32 [1024], P(('dp', 'expert'))
- grad_w_query: float32 [1024, 1024], P(('dp', 'expert'), 'tensor')
- grad_w_key: float32 [1024, 512], P(('dp', 'expert'), 'tensor')
- grad_w_value: float32 [1024, 512], P(('dp', 'expert'), 'tensor')
- grad_w_output: float32 [1024, 1024], P('tensor', ('dp', 'expert'))
- grad_gain_second: float32 [1024], P(('dp', 'expert'))
- grad_router: float32 [1024, 32], P(('dp', 'expert'))
- grad_w_gate: float32 [32, 1024, 512], P('expert', None, 'tensor')
- grad_w_up: float32 [32, 1024, 512], P('expert', None, 'tensor')
- grad_w_down: float32 [32, 512, 1024], P('expert', 'tensor')
The draws below stay inside these ranges and needn't reach their ends.
Inputs may be any that keep to these rules, and one draw needn't show every extreme that they name: `routes`: each token names 8 different experts. Among the 256 tokens of one sequence no expert is named more than 80 times, and in some sequence some expert is named exactly 80 times.
All inputs are finite; a program needn't handle non-finite values.
Results may differ from the reference program's by a relative error of at most 0.017.
The reference program's roundings to bfloat16 on the way count: a program that leaves them out, or rounds other values in their place, can miss the bound.
Values may be sent and summed in bfloat16 or wider, within the bound.
No kernel may reach another device: no remote copies, remote signals or barrier semaphores. Data moves between devices by JAX's collectives and lax.ppermute only.
A program may use at most 192 MiB of HBM per device.

```python
import math
import jax
import jax.numpy as jnp
import numpy as np
from jax import lax

D = 1024
HEADS = 16
KV_HEADS = 8
HD = 64
FF = 512
EXPERTS = 32
TOP = 8
SEQ = 256
TOKENS = 2048
CAP = 80
SLICES = 4


def shard_levels(rng, extent, pieces, low, largest):
    factor_of, own = 1.0, jax.random.fold_in(rng, 6)
    for axis_at, blocks in pieces:
        steps = jnp.exp(jax.random.uniform(jax.random.fold_in(own, axis_at), (blocks,), jnp.float32, low / len(pieces), largest / len(pieces)))
        factor_of = factor_of * jnp.repeat(steps, extent[axis_at] // blocks).reshape([-1 if axis == axis_at else 1 for axis in range(len(extent))])
    return factor_of


def assign_block(rng, own, number, rows, amount, top, bound, lean):
    ranking = jax.random.permutation(rng, amount)
    heavy_load, usual = shares(amount, rows * top, bound, lean, True), shares(amount, rows * top, bound, lean, False)
    places = jnp.arange(amount)

    def named(sizes, rotation):
        used = int((sizes > 0).sum())
        fixed = max(1, used // 4)
        passed = fixed + (places - fixed + rotation * (used - fixed)) % max(1, amount - fixed)
        return jnp.zeros((amount,), jnp.int32).at[ranking[jnp.where(places < fixed, places, passed)]].set(jnp.asarray(sizes, jnp.int32))

    sizes = jnp.where(number % 4 == 0, named(heavy_load, number // 4), named(usual, number - number // 4 - 1))
    mixed = jax.random.permutation(jax.random.fold_in(own, 3), amount)
    source_of, receiver = mixed[0:amount // 2 * 2:2], mixed[1:amount // 2 * 2:2]
    room = jnp.minimum(sizes[source_of] - 1, bound - sizes[receiver]) // 2
    room = jnp.where((source_of == ranking[0]) | (receiver == ranking[0]) | (sizes[receiver] == 0), 0, jnp.maximum(room, 0))
    passed = jax.random.randint(jax.random.fold_in(own, 4), (amount // 2,), 0, 1 << 20) % (room + 1)
    sizes = sizes.at[source_of].add(-passed).at[receiver].add(passed)
    items = jnp.searchsorted(jnp.cumsum(sizes), jnp.arange(rows * top), side="right").astype(jnp.int32)
    grid = items.reshape(top, rows).T
    grid = grid[jax.random.permutation(jax.random.fold_in(own, 1), rows)]
    rotation = jax.random.randint(jax.random.fold_in(own, 2), (rows, 1), 0, top)
    return jnp.take_along_axis(grid, (jnp.arange(top)[None, :] + rotation) % top, axis=1)


def shares(count, total, bound, lean, full):
    portions = [(1 << 20) // math.isqrt(standing ** lean) + 1 for standing in range(1, count + 1)]
    largest = bound if full else min(bound, max(-(-total // count), total * portions[0] // sum(portions)))
    least = 1 if total - largest >= count - 1 else 0
    given, spare = [largest] + [least] * (count - 1), total - largest - least * (count - 1)
    while spare > 0:
        candidates = [i for i in range(1, count) if given[i] < largest] or [i for i in range(1, count) if given[i] < bound]
        mass, remaining = sum([portions[i] for i in candidates]), spare
        for i in candidates:
            extra = min(bound - given[i], max(1, remaining * portions[i] // mass), spare)
            given[i] = given[i] + extra
            spare = spare - extra
    return np.array(given)


def normal_values(stream_key, dims, scale, bound, pieces=(), kind=jnp.bfloat16):
    gain = shard_levels(stream_key, dims, pieces, -0.22, 0.18) if pieces else 1.0
    array = jax.random.normal(stream_key, dims, jnp.float32) * scale * gain
    return jnp.minimum(jnp.maximum(array, -bound), bound).astype(kind)


def setup_inputs(seed: int = 0) -> dict:
    splits = jax.random.split(jax.random.key(seed), 14)
    tokens = normal_values(splits[0], (TOKENS, D), 1.0, 6.0, ((0, 8),))
    routes_keys = jax.random.split(jax.random.fold_in(splits[1], 1), TOKENS // SEQ)
    routes_turns = jax.random.permutation(jax.random.fold_in(splits[1], 3), TOKENS // SEQ)
    routes = jax.vmap(lambda own, number: assign_block(jax.random.fold_in(splits[1], 2), own, number, SEQ, EXPERTS, TOP, CAP, 1))(routes_keys, routes_turns).reshape((TOKENS, TOP))
    gain_first = jnp.clip(1.0 + 0.1 * jax.random.normal(splits[2], (D,), jnp.float32), 0.5, 1.5)
    w_query = normal_values(splits[3], (D, HEADS * HD), (D // 2) ** -0.5, 0.25, ((1, 4),))
    w_key = normal_values(splits[4], (D, KV_HEADS * HD), (D // 2) ** -0.5, 0.25, ((1, 4),))
    w_value = normal_values(splits[5], (D, KV_HEADS * HD), D ** -0.5, 0.1875, ((1, 4),))
    w_output = normal_values(splits[6], (HEADS * HD, D), (HEADS * HD // 32) ** -0.5, 1.0, ((0, 4),))
    gain_second = jnp.clip(1.0 + 0.1 * jax.random.normal(splits[7], (D,), jnp.float32), 0.5, 1.5)
    w_router = normal_values(splits[8], (D, EXPERTS), (4 * D) ** -0.5, 0.09375)
    w_gate = normal_values(splits[9], (EXPERTS, D, FF), D ** -0.5, 0.1875, ((0, 4), (2, 4)))
    w_up = normal_values(splits[10], (EXPERTS, D, FF), D ** -0.5, 0.1875, ((0, 4), (2, 4)))
    w_down = normal_values(splits[11], (EXPERTS, FF, D), (FF // 8) ** -0.5, 0.75, ((0, 4), (1, 4)))
    cotangent = normal_values(splits[12], (TOKENS, D), 1.0, 6.0, ((0, 8),))
    return dict(tokens=tokens, routes=routes, gain_first=gain_first, w_query=w_query, w_key=w_key, w_value=w_value, w_output=w_output, gain_second=gain_second, w_router=w_router, w_gate=w_gate, w_up=w_up, w_down=w_down, cotangent=cotangent)


@jax.custom_vjp
def low(v):
    return lax.optimization_barrier(v.astype(jnp.bfloat16)).astype(jnp.float32)

@jax.custom_vjp
def low_back(v):
    return v

def low_keep(v):
    return (low(v), None)

def low_pass(kept, grad):
    return (grad,)

def back_keep(v):
    return (v, None)

def back_low(kept, grad):
    return (low(grad),)
low.defvjp(low_keep, low_pass)
low_back.defvjp(back_keep, back_low)
EPS = 1e-06
ROPE_BASE = 10000.0
MASKED = -1e+30
HIGH = lax.Precision.HIGHEST

def rope_tables(seq_len, head_dim):
    half_dim = head_dim // 2
    frequency = ROPE_BASE ** (-(jnp.arange(half_dim, dtype=jnp.float32) * 2.0) / head_dim)
    angles = jnp.arange(seq_len, dtype=jnp.float32)[:, None] * frequency[None, :]
    return (jnp.cos(angles)[:, None, :], jnp.sin(angles)[:, None, :])

def rotate(vectors, cosine_table, sine_table):
    half_dim = vectors.shape[-1] // 2
    first_half = vectors[..., :half_dim]
    second_half = vectors[..., half_dim:]
    return jnp.concatenate([first_half * cosine_table - second_half * sine_table, second_half * cosine_table + first_half * sine_table], axis=-1)

def normalize(values, gain_value):
    inverse = lax.rsqrt(lax.optimization_barrier(jnp.mean(values * values, axis=-1, keepdims=True)) + EPS)
    return values * inverse * gain_value

def softmax_rows(scores):
    row_peak = lax.optimization_barrier(jnp.max(scores, axis=-1, keepdims=True))
    exponent = jnp.exp(scores - row_peak)
    return exponent / lax.optimization_barrier(jnp.sum(exponent, axis=-1, keepdims=True))

def route_slots(route_seq):
    chosen = (route_seq[:, :, None] == jnp.arange(EXPERTS, dtype=jnp.int32)[None, None, :]).astype(jnp.int32)
    onehot = lax.optimization_barrier(jnp.sum(chosen, axis=1))
    before = jnp.cumsum(onehot, axis=0) - onehot
    return jnp.take_along_axis(before, route_seq, axis=1).astype(jnp.int32)

def layer(hidden_in, route_seq, params, balance_coef):
    gain_first, w_query, w_key, w_value, w_output, gain_second, w_router, w_gate, w_up, w_down = params
    seq_len = hidden_in.shape[0]
    groups = HEADS // KV_HEADS
    cosine_table, sine_table = rope_tables(seq_len, HD)
    normed_one = low(normalize(hidden_in, gain_first))
    query_proj = low_back(jnp.dot(normed_one, w_query, precision=HIGH)).reshape(seq_len, HEADS, HD)
    queries = low(rotate(query_proj, cosine_table, sine_table)).reshape(seq_len, KV_HEADS, groups, HD)
    key_proj = low_back(jnp.dot(normed_one, w_key, precision=HIGH)).reshape(seq_len, KV_HEADS, HD)
    key_rows = low(rotate(key_proj, cosine_table, sine_table))
    value_rows = low(low_back(jnp.dot(normed_one, w_value, precision=HIGH))).reshape(seq_len, KV_HEADS, HD)
    scores = low_back(jnp.einsum('skgd,tkd->kgst', queries, key_rows, precision=HIGH) * HD ** (-0.5))
    allowed = jnp.arange(seq_len)[None, :] <= jnp.arange(seq_len)[:, None]
    scores = jnp.where(allowed, scores, MASKED)
    soft_weights = softmax_rows(scores)
    mixed_heads = jnp.einsum('kgst,tkd->skgd', low(soft_weights), value_rows, precision=HIGH)
    mixed_heads = low(low_back(mixed_heads.reshape(seq_len, HEADS * HD)))
    branch = low_back(jnp.dot(mixed_heads, w_output, precision=HIGH))
    residual = hidden_in + branch
    normed_two = low(normalize(residual, gain_second))
    logits = low_back(jnp.dot(normed_two, w_router, precision=HIGH))
    probs_all = softmax_rows(logits)
    gate_weights = softmax_rows(jnp.take_along_axis(logits, route_seq, axis=1))
    loss_part = jnp.sum(probs_all * balance_coef[None, :])
    prob_part = lax.optimization_barrier(jnp.sum(probs_all, axis=0))
    slot_index = route_slots(route_seq)
    buffer = jnp.zeros((EXPERTS, CAP, D), jnp.float32).at[route_seq, slot_index].set(jnp.broadcast_to(normed_two[:, None, :], (seq_len, TOP, D)))
    slice_width = FF // SLICES
    mixture = jnp.zeros((seq_len, D), jnp.float32)
    for slice_index in range(SLICES):
        slice_start = slice_index * slice_width
        inputs = low_back(buffer)
        gate_part = low_back(jnp.einsum('ecd,edf->ecf', inputs, w_gate[:, :, slice_start:slice_start + slice_width], precision=HIGH))
        up_part = low_back(jnp.einsum('ecd,edf->ecf', inputs, w_up[:, :, slice_start:slice_start + slice_width], precision=HIGH))
        hidden = low(gate_part * jax.nn.sigmoid(gate_part) * up_part)
        outputs = low_back(low(jnp.einsum('ecf,efd->ecd', hidden, w_down[:, slice_start:slice_start + slice_width, :], precision=HIGH)))
        picked = outputs[route_seq, slot_index]
        mixture = mixture + lax.optimization_barrier(jnp.sum(gate_weights[:, :, None] * picked, axis=1))
    return (residual + mixture, loss_part, prob_part)

def reference(tokens, routes, gain_first, w_query, w_key, w_value, w_output, gain_second, w_router, w_gate, w_up, w_down, cotangent):
    num_seqs = TOKENS // SEQ
    counts = lax.optimization_barrier(jnp.sum((routes[:, :, None] == jnp.arange(EXPERTS, dtype=jnp.int32)[None, None, :]).astype(jnp.float32), axis=(0, 1)))
    balance_coef = EXPERTS * (counts / (TOKENS * TOP)) / TOKENS
    params = tuple((weight.astype(jnp.float32) for weight in (gain_first, w_query, w_key, w_value, w_output, gain_second, w_router, w_gate, w_up, w_down)))

    def one_seq(running, seq_item):
        grad_sum, prob_sum = running
        token_seq, route_seq, cot_seq = seq_item

        def forward(hidden_in, weights):
            return layer(hidden_in, route_seq, weights, balance_coef)
        (result, loss_part, prob_part), pull = jax.vjp(forward, token_seq.astype(jnp.float32), params)
        grad_input, weight_grads = pull((cot_seq.astype(jnp.float32), jnp.ones((), jnp.float32), jnp.zeros((EXPERTS,), jnp.float32)))
        grad_sum = jax.tree.map(lambda left, right: left + right, grad_sum, weight_grads)
        return ((grad_sum, prob_sum + prob_part), (result.astype(jnp.bfloat16), grad_input))
    zero_grads = jax.tree.map(jnp.zeros_like, params)
    (grads, prob_total), (outputs, grad_inputs) = lax.scan(one_seq, (zero_grads, jnp.zeros((EXPERTS,), jnp.float32)), (tokens.reshape(num_seqs, SEQ, D), routes.reshape(num_seqs, SEQ, TOP), cotangent.reshape(num_seqs, SEQ, D)))
    loss_value = EXPERTS * balance_coef * prob_total
    return (outputs.reshape(TOKENS, D), loss_value, grad_inputs.reshape(TOKENS, D), grads[0], grads[1], grads[2], grads[3], grads[4], grads[5], grads[6], grads[7], grads[8], grads[9])
```

```python
import jax
import jax.numpy as jnp
from jax import lax
from jax.sharding import PartitionSpec as P

HD = 64
TOP = 8
EPS = 1e-06
ROPE_BASE = 10000.0
MASKED = -1e30
BF = jnp.bfloat16
F32 = jnp.float32
FEW = 8


def dot(a, b, dims):
    return lax.dot_general(a, b, (dims, ((), ())), preferred_element_type=F32)


def nn(a, b):
    return dot(a, b, ((1,), (0,)))


def nt(a, b):
    return dot(a, b, ((1,), (1,)))


def tn(a, b):
    return dot(a, b, ((0,), (0,)))


def swap(x, axis, distance):
    size = lax.axis_size(axis)
    return lax.ppermute(x, axis, [(i, i ^ distance) for i in range(size)])


def spread(x, axis):
    size = lax.axis_size(axis)
    if size <= FEW:
        return jnp.stack([swap(x, axis, r) for r in range(1, size)])
    whole = lax.all_gather(x, axis)
    return jnp.take(whole, jnp.arange(1, size) ^ lax.axis_index(axis), axis=0)


def deal(parts, axis):
    size = lax.axis_size(axis)
    if size <= FEW:
        return jnp.stack([swap(parts[r - 1], axis, r) for r in range(1, size)])
    order = jnp.arange(size) ^ lax.axis_index(axis)
    whole = jnp.concatenate([parts[:1], parts], axis=0)
    back = lax.all_to_all(jnp.take(whole, order, axis=0), axis, 0, 0, tiled=True)
    return jnp.take(back, order, axis=0)[1:]


def rope_tables(seq_len, head_dim):
    half_dim = head_dim // 2
    frequency = ROPE_BASE ** (-(jnp.arange(half_dim, dtype=F32) * 2.0) / head_dim)
    angles = jnp.arange(seq_len, dtype=F32)[:, None] * frequency[None, :]
    return (jnp.cos(angles)[:, None, :], jnp.sin(angles)[:, None, :])


def rotate(vectors, cosine, sine):
    half = vectors.shape[-1] // 2
    a, b = vectors[..., :half], vectors[..., half:]
    return jnp.concatenate([a * cosine - b * sine, b * cosine + a * sine], axis=-1)


def softmax_rows(scores):
    exponent = jnp.exp(scores - jnp.max(scores, axis=-1, keepdims=True))
    return exponent / jnp.sum(exponent, axis=-1, keepdims=True)


def on_device(
    tokens,
    routes,
    gain_first,
    w_query,
    w_key,
    w_value,
    w_output,
    gain_second,
    w_router,
    w_gate,
    w_up,
    w_down,
    cotangent,
):
    seq_len, width = tokens.shape
    experts = w_router.shape[1]
    local, _, hidden_dev = w_gate.shape
    heads_dev = w_query.shape[1] // HD
    kv_dev = w_key.shape[1] // HD
    groups = heads_dev // kv_dev
    scale = HD ** (-0.5)
    tensor_size = lax.axis_size("tensor")
    expert_size = lax.axis_size("expert")
    token_count = seq_len * lax.axis_size("dp") * expert_size
    quarter_len = seq_len // tensor_size
    last = tensor_size - 1
    t_me, e_me, d_me = lax.axis_index("tensor"), lax.axis_index("expert"), lax.axis_index("dp")

    def quarter(x, r):
        return lax.dynamic_slice_in_dim(x, (t_me ^ r) * quarter_len, quarter_len, 0)

    def natural(pieces):
        whole = jnp.zeros((seq_len, *pieces[0].shape[1:]), pieces[0].dtype)
        for r, piece in enumerate(pieces):
            whole = lax.dynamic_update_slice_in_dim(whole, piece, (t_me ^ r) * quarter_len, 0)
        return whole

    routes_own = jnp.concatenate([quarter(routes, r) for r in range(tensor_size)], axis=0)
    routes_all = jnp.concatenate([routes_own[None], spread(routes_own, "expert")], axis=0)
    cot_own = jnp.concatenate([quarter(cotangent, r) for r in range(tensor_size)], axis=0)
    cot_far = spread(quarter(cotangent, 0), "expert")
    cot_far = jnp.concatenate(
        [cot_far] + [swap(cot_far, "tensor", r) for r in range(1, tensor_size)], axis=1
    )
    cot_all = jnp.concatenate([cot_own[None], cot_far], axis=0).reshape(-1, width)
    down_flat = w_down.reshape(local * hidden_dev, width)
    cot_hidden = nt(cot_all, down_flat)

    cosine, sine = rope_tables(seq_len, HD)
    xf = tokens.astype(F32)
    inv_one = lax.rsqrt(jnp.mean(xf * xf, axis=-1, keepdims=True) + EPS)
    n_one = (xf * inv_one * gain_first).astype(BF)
    queries = rotate(nn(n_one, w_query).reshape(seq_len, heads_dev, HD), cosine, sine).astype(BF)
    queries = queries.reshape(seq_len, kv_dev, groups, HD)
    keys = rotate(nn(n_one, w_key).reshape(seq_len, kv_dev, HD), cosine, sine).astype(BF)
    values = nn(n_one, w_value).astype(BF).reshape(seq_len, kv_dev, HD)
    place = jnp.arange(seq_len)
    allowed = place[None, :] <= place[:, None]

    def scores_of():
        s = jnp.einsum("bkgd,tkd->kgbt", queries, keys, preferred_element_type=F32) * scale
        return jnp.where(allowed, s, MASKED)

    s = scores_of()
    peak = jnp.max(s, axis=-1, keepdims=True)
    e = jnp.exp(s - peak)
    total = jnp.sum(e, axis=-1, keepdims=True)
    lse = peak + jnp.log(total)
    o = jnp.einsum("kgbt,tkd->bkgd", (e / total).astype(BF), values, preferred_element_type=F32)
    o = o.reshape(seq_len, heads_dev * HD).astype(BF)
    attn_part = nn(o, w_output)
    attn = quarter(attn_part, 0)
    for r in range(1, tensor_size):
        attn = attn + swap(quarter(attn_part, r).astype(BF), "tensor", r).astype(F32)
    h = quarter(xf, 0) + attn
    inv_two = lax.rsqrt(jnp.mean(h * h, axis=-1, keepdims=True) + EPS)
    n_two = (h * inv_two * gain_second).astype(BF)

    own = [n_two] + [swap(n_two, "tensor", r) for r in range(1, tensor_size)]
    far_first = spread(own[0], "expert")
    far_last = spread(own[last], "expert")
    far = (
        [far_first]
        + [swap(far_first, "tensor", r) for r in range(1, last)]
        + [far_last]
    )
    n_all = jnp.concatenate(
        [jnp.concatenate(own, axis=0)[None], jnp.concatenate(far, axis=1)], axis=0
    ).reshape(-1, width)

    def route(rows, chosen_of):
        z = nn(rows, w_router)
        probs = softmax_rows(z)
        mask = jnp.any(
            chosen_of[:, :, None] == jnp.arange(experts, dtype=jnp.int32), axis=1
        )
        zc = jnp.where(mask, z, MASKED)
        ez = jnp.where(mask, jnp.exp(zc - jnp.max(zc, axis=-1, keepdims=True)), 0.0)
        return mask.astype(F32), probs, ez / jnp.sum(ez, axis=-1, keepdims=True)

    mask_all, _, gates_all = route(n_all, routes_all.reshape(-1, TOP))
    mask, probs, gates = route(n_two, quarter(routes, 0))
    counts = jnp.sum(mask_all, axis=0)
    counts = counts + swap(counts, "dp", 1)
    fraction = counts / (token_count * TOP)
    balance = experts * fraction / token_count
    prob_sums = lax.psum(jnp.sum(probs, axis=0), ("dp", "expert", "tensor"))
    loss_value = experts * balance * prob_sums

    local_gates = lax.dynamic_slice_in_dim(gates_all, e_me * local, local, 1)
    g = jnp.repeat(local_gates, hidden_dev, axis=1)
    gate_flat = jnp.moveaxis(w_gate, 1, 0).reshape(width, local * hidden_dev)
    up_flat = jnp.moveaxis(w_up, 1, 0).reshape(width, local * hidden_dev)
    gate_val = nn(n_all, gate_flat)
    up_val = nn(n_all, up_flat)
    sig = jax.nn.sigmoid(gate_val)
    act = gate_val * sig
    hid = act * up_val
    hid_g = (g * hid).astype(BF)
    dgates = jnp.sum((hid * cot_hidden).reshape(-1, local, hidden_dev), axis=-1)
    dgates_wide = lax.dynamic_update_slice_in_dim(
        jnp.zeros((dgates.shape[0], 128), F32), dgates, e_me * local, 1
    )
    dhid = g * cot_hidden
    d_gate = (dhid * up_val * sig * (1.0 + gate_val * (1.0 - sig))).astype(BF)
    d_up = (dhid * act).astype(BF)
    dn_part = nt(d_gate, gate_flat) + nt(d_up, up_flat)
    dn_part = jnp.concatenate([dn_part, dgates_wide], axis=1)
    dn_part = dn_part.reshape(expert_size, tensor_size, quarter_len, width + 128)
    moe_part = nn(hid_g, down_flat).reshape(expert_size, tensor_size, quarter_len, width)

    dn_sent = dn_part.astype(BF)
    near = dn_part[0, 0]
    from_last = deal(dn_sent[1:, last], "expert").astype(F32)
    first_sum = dn_part[1:, 0]
    for r in range(1, last):
        first_sum = first_sum + swap(dn_sent[1:, r], "tensor", r).astype(F32)
        near = near + swap(dn_sent[0, r], "tensor", r).astype(F32)
    through = dn_part[0, last] + jnp.sum(from_last, axis=0)
    near = near + swap(through.astype(BF), "tensor", last).astype(F32)
    near = near + jnp.sum(deal(first_sum.astype(BF), "expert").astype(F32), axis=0)
    dn_two, dgates_sum = near[:, :width], near[:, width : width + experts]

    moe_sent = moe_part.astype(BF)
    moe = moe_part[:, 0]
    for r in range(1, tensor_size):
        moe = moe + swap(moe_sent[:, r], "tensor", r).astype(F32)
    moe_sum = moe[0] + jnp.sum(deal(moe[1:].astype(BF), "expert").astype(F32), axis=0)
    out_piece = (h + moe_sum).astype(BF)
    output = natural([out_piece] + [swap(out_piece, "tensor", r) for r in range(1, tensor_size)])

    rows = (-1, local, hidden_dev)
    grad_gate = jnp.einsum("td,tef->edf", n_all, d_gate.reshape(rows), preferred_element_type=F32)
    grad_up = jnp.einsum("td,tef->edf", n_all, d_up.reshape(rows), preferred_element_type=F32)
    grad_down = jnp.einsum("tef,td->efd", hid_g.reshape(rows), cot_all, preferred_element_type=F32)
    expert_grads = []
    for grad in (grad_gate, grad_up, grad_down):
        sent = grad.astype(BF)
        expert_grads.append(sent.astype(F32) + swap(sent, "dp", 1).astype(F32))

    d_chosen = gates * (dgates_sum - jnp.sum(gates * dgates_sum, axis=1, keepdims=True))
    dz = probs * (balance - jnp.sum(probs * balance, axis=1, keepdims=True)) + d_chosen
    dz = dz.astype(BF)
    dn_two = dn_two + nt(dz, w_router)
    u_two = gain_second * dn_two
    gain_two_part = jnp.sum(dn_two * h * inv_two, axis=0)
    dh = (
        quarter(cotangent, 0).astype(F32)
        + inv_two * u_two
        - h * inv_two**3 * jnp.mean(u_two * h, axis=-1, keepdims=True)
    )
    da = dh.astype(BF)
    wide = jnp.concatenate([da, dz, jnp.zeros((quarter_len, 128 - experts), BF)], axis=1)
    wide = natural([wide] + [swap(wide, "tensor", r) for r in range(1, tensor_size)])
    da_all, dz_all = wide[:, :width], wide[:, width : width + experts]
    n_two_all = natural(own)
    grad_router = tn(n_two_all, dz_all)

    grad_wo = tn(da_all, o)
    do = nt(da_all, w_output).astype(BF).reshape(seq_len, kv_dev, groups, HD)
    p = jnp.exp(scores_of() - lse)
    dp = jnp.einsum("bkgd,tkd->kgbt", do, values, preferred_element_type=F32)
    ds = (p * (dp - jnp.sum(p * dp, axis=-1, keepdims=True))).astype(BF)
    dv = jnp.einsum("kgbt,bkgd->tkd", p.astype(BF), do, preferred_element_type=F32)
    dq = jnp.einsum("kgbt,tkd->bkgd", ds, keys, preferred_element_type=F32) * scale
    dk = jnp.einsum("kgbt,bkgd->tkd", ds, queries, preferred_element_type=F32) * scale
    dq = rotate(dq.reshape(seq_len, heads_dev, HD), cosine, -sine).reshape(seq_len, -1)
    dk = rotate(dk, cosine, -sine).reshape(seq_len, -1)
    dqkv = jnp.concatenate([dq, dk, dv.reshape(seq_len, -1)], axis=1).astype(BF)
    w_qkv = jnp.concatenate([w_query, w_key, w_value], axis=1)
    dn_one_part = nt(dqkv, w_qkv)
    gain_one_part = jnp.sum(dn_one_part * xf * inv_one, axis=0)
    dense = jnp.concatenate([tn(n_one, dqkv), grad_wo, grad_router], axis=1).astype(BF)
    dn_one = quarter(dn_one_part, 0)
    for r in range(1, tensor_size):
        dn_one = dn_one + swap(quarter(dn_one_part, r).astype(BF), "tensor", r).astype(F32)
    u_one = gain_first * dn_one
    xq, invq = quarter(xf, 0), quarter(inv_one, 0)
    ig = dh + invq * u_one - xq * invq**3 * jnp.mean(u_one * xq, axis=-1, keepdims=True)
    ig = ig.astype(BF)
    ig = natural([ig] + [swap(ig, "tensor", r) for r in range(1, tensor_size)])
    input_grad = ig.astype(F32)

    chunk = width // (lax.axis_size("dp") * expert_size)
    half = dense.shape[0] // 2
    kept = lax.dynamic_slice_in_dim(dense, d_me * half, half, 0)
    sent = lax.dynamic_slice_in_dim(dense, (1 - d_me) * half, half, 0)
    summed = kept.astype(F32) + swap(sent, "dp", 1).astype(F32)
    blocks = summed.reshape(expert_size, chunk, -1)
    blocks = jnp.take(blocks, jnp.arange(expert_size) ^ e_me, axis=0)
    dense_sum = blocks[0] + jnp.sum(deal(blocks[1:].astype(BF), "expert").astype(F32), axis=0)
    nq, nk = w_query.shape[1], w_key.shape[1]
    at = [nq, nq + nk, nq + 2 * nk, 2 * nq + 2 * nk]
    g_query, g_key, g_value, g_out, g_router = jnp.split(dense_sum, at, axis=1)

    gains = jnp.stack([gain_one_part, gain_two_part])
    gains = lax.psum_scatter(
        lax.psum(gains, "tensor"), ("dp", "expert"), scatter_dimension=1, tiled=True
    )
    return (
        output,
        loss_value,
        input_grad,
        gains[0],
        g_query,
        g_key,
        g_value,
        g_out.T,
        gains[1],
        g_router,
        expert_grads[0],
        expert_grads[1],
        expert_grads[2],
    )


def solution(mesh):
    rows = ("dp", "expert")
    placed = (
        P(rows, None),
        P(rows, None),
        P(),
        P(None, "tensor"),
        P(None, "tensor"),
        P(None, "tensor"),
        P("tensor", None),
        P(),
        P(),
        P("expert", None, "tensor"),
        P("expert", None, "tensor"),
        P("expert", "tensor", None),
        P(rows, None),
    )
    return jax.shard_map(
        on_device,
        mesh=mesh,
        in_specs=placed,
        out_specs=(
            P(rows, None),
            P(),
            P(rows, None),
            P(rows),
            P(rows, "tensor"),
            P(rows, "tensor"),
            P(rows, "tensor"),
            P("tensor", rows),
            P(rows),
            P(rows, None),
            P("expert", None, "tensor"),
            P("expert", None, "tensor"),
            P("expert", "tensor", None),
        ),
        check_vma=False,
    )
```

```python
import functools

import jax
import jax.numpy as jnp
import numpy as np
from jax import lax
from jax.experimental import pallas as pl
from jax.experimental.pallas import tpu as pltpu
from jax.sharding import PartitionSpec as P

HD = 64
TOP = 8
EPS = 1e-06
ROPE_BASE = 10000.0
MASKED = -1e30
BF = jnp.bfloat16
F32 = jnp.float32
FEW = 8
LANES = 128
MIB = 1 << 20


def dot(a, b, dims):
    return lax.dot_general(a, b, (dims, ((), ())), preferred_element_type=F32)


def nn(a, b):
    return dot(a, b, ((1,), (0,)))


def nt(a, b):
    return dot(a, b, ((1,), (1,)))


def tn(a, b):
    return dot(a, b, ((0,), (0,)))


def swap(x, axis, distance):
    size = lax.axis_size(axis)
    return lax.ppermute(x, axis, [(i, i ^ distance) for i in range(size)])


def spread(x, axis):
    size = lax.axis_size(axis)
    if size <= FEW:
        return jnp.stack([swap(x, axis, r) for r in range(1, size)])
    whole = lax.all_gather(x, axis)
    return jnp.take(whole, jnp.arange(1, size) ^ lax.axis_index(axis), axis=0)


def deal(parts, axis):
    size = lax.axis_size(axis)
    if size <= FEW:
        return jnp.stack([swap(parts[r - 1], axis, r) for r in range(1, size)])
    order = jnp.arange(size) ^ lax.axis_index(axis)
    whole = jnp.concatenate([parts[:1], parts], axis=0)
    back = lax.all_to_all(jnp.take(whole, order, axis=0), axis, 0, 0, tiled=True)
    return jnp.take(back, order, axis=0)[1:]


def rope_tables(seq_len):
    half = HD // 2
    frequency = ROPE_BASE ** (-(np.arange(half, dtype=np.float32) * 2.0) / HD)
    angles = np.arange(seq_len, dtype=np.float32)[:, None] * frequency[None, :].astype(np.float32)
    cosine, sine = np.cos(angles), np.sin(angles)
    heads = LANES // HD
    return (
        np.tile(cosine, (1, 2 * heads)).astype(np.float32),
        np.tile(np.concatenate([-sine, sine], axis=1), (1, heads)).astype(np.float32),
    )


def lane_of(shape):
    return lax.broadcasted_iota(jnp.int32, shape, 1)


def halves_swapped(x):
    first = lane_of(x.shape) % HD < HD // 2
    half = HD // 2
    return jnp.where(first, pltpu.roll(x, LANES - half, 1), pltpu.roll(x, half, 1))


def low_high(x, head):
    other = pltpu.roll(x.astype(F32), HD, 1).astype(x.dtype)
    low = lane_of(x.shape) < HD
    zero = jnp.zeros_like(x)
    at_low, at_high = (x, other) if head == 0 else (other, x)
    return jnp.where(low, at_low, zero), jnp.where(low, zero, at_high)


def causal(scores):
    rows = lax.broadcasted_iota(jnp.int32, scores.shape, 0)
    return lane_of(scores.shape) <= rows


def vmem():
    return pl.BlockSpec(memory_space=pltpu.VMEM)


def smem():
    return pl.BlockSpec(memory_space=pltpu.SMEM)


def shape(dims, kind):
    return jax.ShapeDtypeStruct(dims, kind)


def call(kernel, out_shape, operands, scalars=0, scratch=(), limit=40, flops=0, moved=0, name=None):
    return pl.pallas_call(
        kernel,
        out_shape=out_shape,
        in_specs=[smem()] * scalars + [vmem()] * (len(operands) - scalars),
        out_specs=jax.tree.map(lambda _: vmem(), out_shape),
        scratch_shapes=list(scratch),
        compiler_params=pltpu.CompilerParams(vmem_limit_bytes=limit * MIB),
        cost_estimate=pl.CostEstimate(flops=flops, bytes_accessed=moved, transcendentals=0),
        name=name,
    )(*operands)


def attend_kernel(me_ref, x_ref, gain_ref, wq_ref, wk_ref, wv_ref, wo_ref, cos_ref, sin_ref, *refs):
    n_ref, q_ref, k_ref, v_ref, o_ref, lse_ref = refs[:6]
    parts, whole = refs[6:-1], refs[-1]
    x = x_ref[...].astype(F32)
    inv = lax.rsqrt(jnp.mean(x * x, axis=-1, keepdims=True) + EPS)
    n = (x * inv * gain_ref[...]).astype(BF)
    n_ref[...] = n
    cosine, sine = cos_ref[...], sin_ref[...]
    q, k = nn(n, wq_ref[...]), nn(n, wk_ref[...])
    v_ref[...] = nn(n, wv_ref[...]).astype(BF)
    for at in range(0, q.shape[1], LANES):
        tile = q[:, at : at + LANES]
        q_ref[:, at : at + LANES] = (tile * cosine + halves_swapped(tile) * sine).astype(BF)
    for at in range(0, k.shape[1], LANES):
        tile = k[:, at : at + LANES]
        k_ref[:, at : at + LANES] = (tile * cosine + halves_swapped(tile) * sine).astype(BF)
    lse_all = jnp.zeros(lse_ref.shape, F32)
    for head in range(q.shape[1] // LANES):
        at = head // 2 * LANES
        keys = low_high(k_ref[:, at : at + LANES], head % 2)
        values = low_high(v_ref[:, at : at + LANES], head % 2)
        pair = q_ref[:, head * LANES : (head + 1) * LANES]
        mixed = 0.0
        for g in range(2):
            s = nt(pair, keys[g]) * HD ** (-0.5)
            s = jnp.where(causal(s), s, MASKED)
            peak = jnp.max(s, axis=-1, keepdims=True)
            e = jnp.exp(s - peak)
            total = jnp.sum(e, axis=-1, keepdims=True)
            mixed = mixed + nn((e / total).astype(BF), values[g])
            lse = peak + jnp.log(total)
            lse_all = jnp.where(lane_of(lse_all.shape) == 2 * head + g, lse, lse_all)
        o_ref[:, head * LANES : (head + 1) * LANES] = mixed.astype(BF)
    lse_ref[...] = lse_all
    whole[...] = nn(o_ref[...], wo_ref[...])
    for r, part in enumerate(parts):
        rows = part.shape[0]
        start = pl.multiple_of((me_ref[0] ^ r) * rows, rows)
        part[...] = whole[pl.ds(start, rows), :].astype(part.dtype)


def norm_two_kernel(me_ref, x_ref, gain_ref, own_ref, *refs):
    others, (h_ref, n_ref) = refs[:-2], refs[-2:]
    rows = h_ref.shape[0]
    start = pl.multiple_of(me_ref[0] * rows, rows)
    attn = own_ref[...]
    for other in others:
        attn = attn + other[...].astype(F32)
    h = x_ref[pl.ds(start, rows), :].astype(F32) + attn
    inv = lax.rsqrt(jnp.mean(h * h, axis=-1, keepdims=True) + EPS)
    h_ref[...] = h
    n_ref[...] = (h * inv * gain_ref[...]).astype(BF)


def router_of(rows, router_ref, routes, experts):
    z = nn(rows, router_ref[...])
    lane = lane_of(z.shape)
    z = jnp.where(lane < experts, z, MASKED)
    e = jnp.exp(z - jnp.max(z, axis=-1, keepdims=True))
    probs = e / jnp.sum(e, axis=-1, keepdims=True)
    chosen = lane == routes[:, 0:1]
    for k in range(1, routes.shape[1]):
        chosen = chosen | (lane == routes[:, k : k + 1])
    zc = jnp.where(chosen, z, MASKED)
    ec = jnp.where(chosen, jnp.exp(zc - jnp.max(zc, axis=-1, keepdims=True)), 0.0)
    return probs, ec / jnp.sum(ec, axis=-1, keepdims=True)


def hidden_cot_kernel(c0, c1, c2, c3, wd_ref, cot_ref, v_ref):
    rows = jnp.concatenate([c[0] for c in (c0, c1, c2, c3)], axis=0)
    cot_ref[0] = rows
    v_ref[0] = nt(rows, wd_ref[...])


def hidden_cot(pieces, down_flat):
    count, rows, width = pieces[0].shape
    out = down_flat.shape[0]
    piece = pl.BlockSpec((1, rows, width), lambda s: (s, 0, 0))
    return pl.pallas_call(
        hidden_cot_kernel,
        grid=(count,),
        in_specs=[piece] * 4 + [pl.BlockSpec((out, width), lambda s: (0, 0))],
        out_specs=[
            pl.BlockSpec((1, 4 * rows, width), lambda s: (s, 0, 0)),
            pl.BlockSpec((1, 4 * rows, out), lambda s: (s, 0, 0)),
        ],
        out_shape=[shape((count, 4 * rows, width), BF), shape((count, 4 * rows, out), F32)],
        compiler_params=pltpu.CompilerParams(vmem_limit_bytes=40 * MIB),
        cost_estimate=pl.CostEstimate(
            flops=2 * count * 4 * rows * width * out, bytes_accessed=0, transcendentals=0
        ),
        name="hidden_cot",
    )(*pieces, down_flat)


def experts_kernel(experts, base_ref, x0, x1, x2, x3, routes_ref, router_ref, wg_ref, wu_ref, v_ref, *refs):
    n_ref, dgu_ref, hg_ref, d0, d1, d2, d3, wcat = refs
    local, width, hidden = wg_ref.shape
    pair = 2 * hidden

    @pl.when(pl.program_id(0) == 0)
    def _():
        for e in range(local):
            wcat[:, e * pair : e * pair + hidden] = wg_ref[e]
            wcat[:, e * pair + hidden : (e + 1) * pair] = wu_ref[e]

    x = jnp.concatenate([piece[0] for piece in (x0, x1, x2, x3)], axis=0)
    n_ref[0] = x
    _, gates = router_of(x, router_ref, routes_ref[0], experts)
    lane = lane_of(gates.shape)
    dots = jnp.zeros(gates.shape, F32)
    for e in range(local):
        mine = lane == base_ref[0] + e
        g = jnp.sum(jnp.where(mine, gates, 0.0), axis=-1, keepdims=True)
        both = nn(x, wcat[:, e * pair : (e + 1) * pair])
        gate, up = both[:, :hidden], both[:, hidden:]
        v = v_ref[0, :, e * hidden : (e + 1) * hidden]
        sig = 1.0 / (1.0 + jnp.exp(-gate))
        act = gate * sig
        hid = act * up
        dots = jnp.where(mine, jnp.sum(hid * v, axis=-1, keepdims=True), dots)
        gv = g * v
        hg_ref[0, :, e * hidden : (e + 1) * hidden] = (g * hid).astype(BF)
        d_gate = gv * up * sig * (1.0 + gate * (1.0 - sig))
        dgu_ref[0, :, e * pair : e * pair + hidden] = d_gate.astype(BF)
        dgu_ref[0, :, e * pair + hidden : (e + 1) * pair] = (gv * act).astype(BF)
    rows = d0.shape[1]
    for r, d in enumerate((d0, d1, d2, d3)):
        d[0, :, width:] = dots[r * rows : (r + 1) * rows].astype(d.dtype)
    step = 256
    for at in range(0, width, step):
        dx = nt(dgu_ref[0], wcat[at : at + step, :])
        for r, d in enumerate((d0, d1, d2, d3)):
            d[0, :, at : at + step] = dx[r * rows : (r + 1) * rows].astype(d.dtype)


def run_experts(experts, base, pieces, routes, router, w_gate, w_up, v, kinds):
    count, rows, width = pieces[0].shape
    local, _, hidden = w_gate.shape
    per = lambda *dims: pl.BlockSpec((1, *dims), lambda s: (s, 0, 0))
    fixed = lambda dims: pl.BlockSpec(dims, lambda s: (0,) * len(dims))
    seq = 4 * rows
    return pl.pallas_call(
        functools.partial(experts_kernel, experts),
        grid=(count,),
        in_specs=[smem()]
        + [per(rows, width)] * 4
        + [per(seq, routes.shape[2]), fixed(router.shape), fixed(w_gate.shape), fixed(w_up.shape)]
        + [per(seq, local * hidden)],
        out_specs=[per(seq, width), per(seq, 2 * local * hidden), per(seq, local * hidden)]
        + [per(rows, width + LANES)] * 4,
        out_shape=[
            shape((count, seq, width), BF),
            shape((count, seq, 2 * local * hidden), BF),
            shape((count, seq, local * hidden), BF),
        ]
        + [shape((count, rows, width + LANES), kind) for kind in kinds],
        scratch_shapes=[pltpu.VMEM((width, 2 * local * hidden), BF)],
        compiler_params=pltpu.CompilerParams(vmem_limit_bytes=52 * MIB),
        cost_estimate=pl.CostEstimate(
            flops=8 * count * seq * width * local * hidden, bytes_accessed=0, transcendentals=0
        ),
        name="experts",
    )(base, *pieces, routes, router, w_gate, w_up, v)


def moe_kernel(h_ref, wd_ref, *parts):
    out = nn(h_ref[0], wd_ref[...])
    rows = parts[0].shape[1]
    for r, part in enumerate(parts):
        part[0] = out[r * rows : (r + 1) * rows].astype(part.dtype)


def run_moe(h, down_flat, kinds):
    count, seq, inner = h.shape
    width = down_flat.shape[1]
    rows = seq // 4
    return pl.pallas_call(
        moe_kernel,
        grid=(count,),
        in_specs=[
            pl.BlockSpec((1, seq, inner), lambda s: (s, 0, 0)),
            pl.BlockSpec((inner, width), lambda s: (0, 0)),
        ],
        out_specs=[pl.BlockSpec((1, rows, width), lambda s: (s, 0, 0))] * 4,
        out_shape=[shape((count, rows, width), kind) for kind in kinds],
        compiler_params=pltpu.CompilerParams(vmem_limit_bytes=40 * MIB),
        cost_estimate=pl.CostEstimate(
            flops=2 * count * seq * width * inner, bytes_accessed=0, transcendentals=0
        ),
        name="moe",
    )(h, down_flat)


def grads_kernel(n0, nf, dgu0, dguf, h0, hf, c0, cf, gate_ref, up_ref, down_ref):
    hidden = down_ref.shape[1]
    both = tn(n0[0], dgu0[0])
    down = tn(h0[0], c0[0])
    for s in range(nf.shape[0]):
        both = both + tn(nf[s], dguf[s])
        down = down + tn(hf[s], cf[s])
    gate_ref[0] = both[:, :hidden].astype(BF)
    up_ref[0] = both[:, hidden:].astype(BF)
    down_ref[0] = down.astype(BF)


def run_grads(n0, nf, dgu0, dguf, h0, hf, c0, cf, local, hidden):
    width = n0.shape[2]
    whole = lambda a: pl.BlockSpec(a.shape, lambda e: (0, 0, 0))
    cols = lambda a, w: pl.BlockSpec((*a.shape[:2], w), lambda e: (0, 0, e))
    flops = 6 * (n0.shape[0] + nf.shape[0]) * n0.shape[1] * width * hidden * local
    return pl.pallas_call(
        grads_kernel,
        grid=(local,),
        in_specs=[whole(n0), whole(nf), cols(dgu0, 2 * hidden), cols(dguf, 2 * hidden)]
        + [cols(h0, hidden), cols(hf, hidden), whole(c0), whole(cf)],
        out_specs=[
            pl.BlockSpec((1, width, hidden), lambda e: (e, 0, 0)),
            pl.BlockSpec((1, width, hidden), lambda e: (e, 0, 0)),
            pl.BlockSpec((1, hidden, width), lambda e: (e, 0, 0)),
        ],
        out_shape=[
            shape((local, width, hidden), BF),
            shape((local, width, hidden), BF),
            shape((local, hidden, width), BF),
        ],
        compiler_params=pltpu.CompilerParams(vmem_limit_bytes=56 * MIB),
        cost_estimate=pl.CostEstimate(flops=flops, bytes_accessed=0, transcendentals=0),
        name="expert_grads",
    )(n0, nf, dgu0, dguf, h0, hf, c0, cf)


def norm_back_kernel(experts, me_ref, count, h_ref, n_ref, gain_ref, router_ref, routes_ref, bal_ref, cot_ref, *refs):
    sums, (wide_ref, dh_ref, small_ref) = refs[:count], refs[count:]
    near = sums[0][...].astype(F32)
    for other in sums[1:]:
        near = near + other[...].astype(F32)
    rows, width = h_ref.shape
    dots = near[:, width:]
    probs, gates = router_of(n_ref[...], router_ref, routes_ref[...], experts)
    bal = bal_ref[...]
    d_chosen = gates * (dots - jnp.sum(gates * dots, axis=-1, keepdims=True))
    dz = probs * (bal - jnp.sum(probs * bal, axis=-1, keepdims=True)) + d_chosen
    dz = dz.astype(BF)
    wide_ref[:, width:] = dz
    dn = near[:, :width] + nt(dz, router_ref[...])
    h = h_ref[...]
    inv = lax.rsqrt(jnp.mean(h * h, axis=-1, keepdims=True) + EPS)
    u = gain_ref[...] * dn
    start = pl.multiple_of(me_ref[0] * rows, rows)
    dy = cot_ref[pl.ds(start, rows), :].astype(F32)
    dh = dy + inv * u - h * (inv * inv * inv * jnp.mean(u * h, axis=-1, keepdims=True))
    dh_ref[...] = dh
    wide_ref[:, :width] = dh.astype(BF)
    small_ref[...] = jnp.zeros(small_ref.shape, F32)
    small_ref[1:2, :] = jnp.sum(dn * h * inv, axis=0, keepdims=True)
    small_ref[2:3, : probs.shape[1]] = jnp.sum(probs, axis=0, keepdims=True)


def attend_back_kernel(
    me_ref, w0, w1, w2, w3, x_ref, q_ref, k_ref, v_ref, lse_ref, wq_ref, wk_ref, wv_ref, wo_ref, cos_ref, sin_ref,
    small_in, wide_ref, dq_ref, small_ref, p0, p1, p2, p3, do_ref, whole
):
    rows = w0.shape[0]
    width = x_ref.shape[1]
    for r, piece in enumerate((w0, w1, w2, w3)):
        start = pl.multiple_of((me_ref[0] ^ r) * rows, rows)
        wide_ref[pl.ds(start, rows), :] = piece[...]
    do_ref[...] = nt(wide_ref[:, :width], wo_ref[...]).astype(BF)
    cosine, sine = cos_ref[...], sin_ref[...]
    scale = HD ** (-0.5)
    heads, keys_wide = q_ref.shape[1], k_ref.shape[1]
    dk_tiles = [0.0] * (keys_wide // LANES)
    dv_tiles = [0.0] * (keys_wide // LANES)

    def back(tile):
        return (tile * cosine - halves_swapped(tile) * sine).astype(BF)

    for head in range(heads // LANES):
        at = head // 2 * LANES
        side = head % 2
        keys = low_high(k_ref[:, at : at + LANES], side)
        values = low_high(v_ref[:, at : at + LANES], side)
        pair = q_ref[:, head * LANES : (head + 1) * LANES]
        grad = do_ref[:, head * LANES : (head + 1) * LANES]
        dq = 0.0
        dk, dv = [], []
        for g in range(2):
            s = nt(pair, keys[g]) * scale
            lse = lse_ref[:, 2 * head + g : 2 * head + g + 1]
            p = jnp.where(causal(s), jnp.exp(s - lse), 0.0)
            dp = nt(grad, values[g])
            ds = (p * (dp - jnp.sum(p * dp, axis=-1, keepdims=True))).astype(BF)
            dq = dq + nn(ds, keys[g])
            dk.append(tn(ds, pair))
            dv.append(tn(p.astype(BF), grad))
        dq_ref[:, head * LANES : (head + 1) * LANES] = back(dq * scale)
        mine = lane_of(dk[0].shape) < HD
        if side == 0:
            dk_sum = jnp.where(mine, dk[0] + pltpu.roll(dk[1], HD, 1), 0.0)
            dv_sum = jnp.where(mine, dv[0] + pltpu.roll(dv[1], HD, 1), 0.0)
        else:
            dk_sum = jnp.where(mine, 0.0, pltpu.roll(dk[0], HD, 1) + dk[1])
            dv_sum = jnp.where(mine, 0.0, pltpu.roll(dv[0], HD, 1) + dv[1])
        dk_tiles[head // 2] = dk_tiles[head // 2] + dk_sum
        dv_tiles[head // 2] = dv_tiles[head // 2] + dv_sum
    for i, tile in enumerate(dk_tiles):
        at = heads + i * LANES
        dq_ref[:, at : at + LANES] = back(tile * scale)
    for i, tile in enumerate(dv_tiles):
        at = heads + keys_wide + i * LANES
        dq_ref[:, at : at + LANES] = tile.astype(BF)
    dn = nt(dq_ref[:, :heads], wq_ref[...])
    dn = dn + nt(dq_ref[:, heads : heads + keys_wide], wk_ref[...])
    whole[...] = dn + nt(dq_ref[:, heads + keys_wide :], wv_ref[...])
    for r, part in enumerate((p0, p1, p2, p3)):
        start = pl.multiple_of((me_ref[0] ^ r) * rows, rows)
        part[...] = whole[pl.ds(start, rows), :].astype(part.dtype)
    x = x_ref[...].astype(F32)
    inv = lax.rsqrt(jnp.mean(x * x, axis=-1, keepdims=True) + EPS)
    small_ref[...] = small_in[...]
    small_ref[0:1, :] = jnp.sum(whole[...] * x * inv, axis=0, keepdims=True)


def dense_early_kernel(me_ref, a0, a1, a2, a3, wide_ref, o_ref, kept_ref, sent_ref, n_ref, whole):
    rows = a0.shape[0]
    width = a0.shape[1]
    for r, piece in enumerate((a0, a1, a2, a3)):
        start = pl.multiple_of((me_ref[1] ^ r) * rows, rows)
        n_ref[pl.ds(start, rows), :] = piece[...]
    heads = o_ref.shape[1]
    whole[:, :heads] = tn(wide_ref[:, :width], o_ref[...])
    whole[:, heads:] = tn(n_ref[...], wide_ref[:, width:])
    half = kept_ref.shape[0]
    kept_ref[...] = whole[pl.ds(pl.multiple_of(me_ref[0] * half, half), half), :]
    sent_ref[...] = whole[pl.ds(pl.multiple_of((1 - me_ref[0]) * half, half), half), :].astype(BF)


def dense_late_kernel(me_ref, n_ref, dq_ref, kept_ref, sent_ref, whole):
    whole[...] = tn(n_ref[...], dq_ref[...])
    half = kept_ref.shape[0]
    kept_ref[...] = whole[pl.ds(pl.multiple_of(me_ref[0] * half, half), half), :]
    sent_ref[...] = whole[pl.ds(pl.multiple_of((1 - me_ref[0]) * half, half), half), :].astype(BF)


def input_grad_kernel(me_ref, x_ref, gain_ref, dh_ref, own_ref, *refs):
    others, ig_ref = refs[:-1], refs[-1]
    rows = dh_ref.shape[0]
    start = pl.multiple_of(me_ref[0] * rows, rows)
    x = x_ref[pl.ds(start, rows), :].astype(F32)
    inv = lax.rsqrt(jnp.mean(x * x, axis=-1, keepdims=True) + EPS)
    dn = own_ref[...]
    for other in others:
        dn = dn + other[...].astype(F32)
    u = gain_ref[...] * dn
    ig = dh_ref[...] + inv * u - x * (inv * inv * inv * jnp.mean(u * x, axis=-1, keepdims=True))
    ig_ref[...] = ig.astype(BF)


def natural_kernel(me_ref, *refs):
    pieces, out = refs[:-1], refs[-1]
    rows = pieces[0].shape[0]
    for r, piece in enumerate(pieces):
        start = pl.multiple_of((me_ref[0] ^ r) * rows, rows)
        out[pl.ds(start, rows), :] = piece[...].astype(out.dtype)


def ordered_sum_kernel(me_ref, *refs):
    pieces, out, held = refs[:-2], refs[-2], refs[-1]
    for r, piece in enumerate(pieces):
        held[me_ref[0] ^ r] = piece[...]
    total = held[0]
    for i in range(1, len(pieces)):
        total = total + held[i]
    out[...] = total


def ordered_sum(me, pieces):
    return call(
        ordered_sum_kernel,
        shape(pieces[0].shape, F32),
        (me, *pieces),
        scalars=1,
        scratch=[pltpu.VMEM((len(pieces), *pieces[0].shape), F32)],
        name="ordered_sum",
    )


def on_device(
    tokens,
    routes,
    gain_first,
    w_query,
    w_key,
    w_value,
    w_output,
    gain_second,
    w_router,
    w_gate,
    w_up,
    w_down,
    cotangent,
):
    seq_len, width = tokens.shape
    experts = w_router.shape[1]
    local, _, hidden = w_gate.shape
    tensor_size = lax.axis_size("tensor")
    expert_size = lax.axis_size("expert")
    dp_size = lax.axis_size("dp")
    token_count = seq_len * dp_size * expert_size
    rows = seq_len // tensor_size
    last = tensor_size - 1
    around = range(1, tensor_size)
    t_me, e_me, d_me = lax.axis_index("tensor"), lax.axis_index("expert"), lax.axis_index("dp")
    t_at = t_me.astype(jnp.int32).reshape(1)
    e_at = e_me.astype(jnp.int32).reshape(1)
    cosine, sine = rope_tables(seq_len)
    gain_one, gain_two = gain_first[None], gain_second[None]
    router = jnp.pad(w_router, ((0, 0), (0, LANES - experts)))
    down_flat = w_down.reshape(local * hidden, width)

    def quarter(x, r):
        return lax.dynamic_slice_in_dim(x, (t_me ^ r) * rows, rows, 0)

    cot_near = [quarter(cotangent, r) for r in range(tensor_size)]
    cot_first = spread(cot_near[0], "expert")
    routes_near = jnp.concatenate([quarter(routes, r) for r in range(tensor_size)], axis=0)
    routes_far = spread(routes_near, "expert")
    cot_far = [cot_first] + [swap(cot_first, "tensor", r) for r in around]
    cot0, v0 = hidden_cot([c[None] for c in cot_near], down_flat)
    cotf, vf = hidden_cot(cot_far, down_flat)
    everyone = jnp.concatenate([routes_near, routes_far.reshape(-1, TOP)], axis=0)
    named = everyone[:, :, None] == jnp.arange(LANES, dtype=jnp.int32)
    counts = jnp.sum(named.astype(F32), axis=(0, 1))[None]
    counts = counts + swap(counts, "dp", 1)
    balance = experts * (counts / (token_count * TOP)) / token_count

    heads, keys_wide = w_query.shape[1], w_key.shape[1]
    kinds = [F32] + [BF] * last
    n_one, q, k, v, o, lse, *parts = call(
        attend_kernel,
        [
            shape((seq_len, width), BF),
            shape((seq_len, heads), BF),
            shape((seq_len, keys_wide), BF),
            shape((seq_len, keys_wide), BF),
            shape((seq_len, heads), BF),
            shape((seq_len, LANES), F32),
        ]
        + [shape((rows, width), kind) for kind in kinds],
        (t_at, tokens, gain_one, w_query, w_key, w_value, w_output, cosine, sine),
        scalars=1,
        scratch=[pltpu.VMEM((seq_len, width), F32)],
        flops=2 * seq_len * width * 4 * heads,
        name="attend",
    )
    h, n_two = call(
        norm_two_kernel,
        [shape((rows, width), F32), shape((rows, width), BF)],
        (t_at, tokens, gain_two, parts[0], *[swap(parts[r], "tensor", r) for r in around]),
        scalars=1,
        name="norm_two",
    )

    own = [n_two] + [swap(n_two, "tensor", r) for r in around]
    far_first = spread(own[0], "expert")
    far_last = spread(own[last], "expert")
    far = [far_first] + [swap(far_first, "tensor", r) for r in range(1, last)] + [far_last]

    base = (e_me * local).astype(jnp.int32).reshape(1)
    n0, dgu0, h0, *near = run_experts(
        experts, base, [x[None] for x in own], routes_near[None], router, w_gate, w_up, v0,
        [F32, BF, BF, F32],
    )
    nf, dguf, hf, *away = run_experts(
        experts, base, far, routes_far, router, w_gate, w_up, vf, [F32, BF, BF, BF]
    )
    near = [x[0] for x in near]

    near_sums = [near[0]] + [swap(near[r], "tensor", r) for r in range(1, last)]
    first_sum = away[0]
    for r in range(1, last):
        first_sum = first_sum + swap(away[r], "tensor", r).astype(F32)
    from_last = deal(away[last], "expert")
    through = near[last] + jnp.sum(from_last.astype(F32), axis=0)
    near_sums.append(swap(through.astype(BF), "tensor", last))
    across = deal(first_sum.astype(BF), "expert")
    if expert_size <= FEW:
        near_sums.extend(across[r] for r in range(expert_size - 1))
    else:
        near_sums.append(jnp.sum(across.astype(F32), axis=0))

    m0 = run_moe(h0, down_flat, kinds)
    mf = run_moe(hf, down_flat, kinds)
    moe_near, moe_far = m0[0][0], mf[0]
    for r in around:
        moe_near = moe_near + swap(m0[r], "tensor", r)[0].astype(F32)
        moe_far = moe_far + swap(mf[r], "tensor", r).astype(F32)
    moe_sum = moe_near + jnp.sum(deal(moe_far.astype(BF), "expert").astype(F32), axis=0)
    out_piece = (h + moe_sum).astype(BF)
    output = call(
        natural_kernel,
        shape((seq_len, width), BF),
        (t_at, out_piece, *[swap(out_piece, "tensor", r) for r in around]),
        scalars=1,
        name="output",
    )

    grads = run_grads(n0, nf, dgu0, dguf, h0, hf, cot0, cotf, local, hidden)
    expert_grads = [x.astype(F32) + swap(x, "dp", 1).astype(F32) for x in grads]

    wide, dh, small = call(
        lambda me, *refs: norm_back_kernel(experts, me, len(near_sums), *refs),
        [shape((rows, width + LANES), BF), shape((rows, width), F32), shape((8, width), F32)],
        (t_at, h, n_two, gain_two, router, quarter(routes, 0), balance, cotangent, *near_sums),
        scalars=1,
        name="norm_back",
    )
    wides = [wide] + [swap(wide, "tensor", r) for r in around]

    wide_all, dqkv, small, *back_parts = call(
        attend_back_kernel,
        [
            shape((seq_len, width + LANES), BF),
            shape((seq_len, heads + 2 * keys_wide), BF),
            shape((8, width), F32),
        ]
        + [shape((rows, width), kind) for kind in kinds],
        (t_at, *wides, tokens, q, k, v, lse, w_query, w_key, w_value, w_output, cosine, sine, small),
        scalars=1,
        scratch=[pltpu.VMEM((seq_len, heads), BF), pltpu.VMEM((seq_len, width), F32)],
        flops=2 * seq_len * width * 4 * heads,
        name="attend_back",
    )
    ig = call(
        input_grad_kernel,
        shape((rows, width), BF),
        (t_at, tokens, gain_one, dh, back_parts[0])
        + tuple(swap(back_parts[r], "tensor", r) for r in around),
        scalars=1,
        name="input_grad",
    )
    input_grad = call(
        natural_kernel,
        shape((seq_len, width), F32),
        (t_at, ig, *[swap(ig, "tensor", r) for r in around]),
        scalars=1,
        name="input_grad_whole",
    )

    d_at = jnp.stack([d_me, t_me]).astype(jnp.int32)
    half = width // dp_size

    def summed(kept, sent):
        total = kept + swap(sent, "dp", 1).astype(F32)
        blocks = total.reshape(expert_size, half // expert_size, -1)
        first = lax.dynamic_index_in_dim(blocks, e_me, 0, keepdims=False)
        others = jnp.stack(
            [
                lax.dynamic_index_in_dim(blocks, e_me ^ r, 0, keepdims=False)
                for r in range(1, expert_size)
            ]
        )
        return first + jnp.sum(deal(others.astype(BF), "expert").astype(F32), axis=0)

    kept, sent, _ = call(
        dense_early_kernel,
        [
            shape((half, heads + LANES), F32),
            shape((half, heads + LANES), BF),
            shape((seq_len, width), BF),
        ],
        (d_at, *own, wide_all, o),
        scalars=1,
        scratch=[pltpu.VMEM((width, heads + LANES), F32)],
        flops=2 * seq_len * width * (heads + LANES),
        name="dense_early",
    )
    early = summed(kept, sent)
    kept, sent = call(
        dense_late_kernel,
        [shape((half, heads + 2 * keys_wide), F32), shape((half, heads + 2 * keys_wide), BF)],
        (d_at, n_one, dqkv),
        scalars=1,
        scratch=[pltpu.VMEM((width, heads + 2 * keys_wide), F32)],
        flops=2 * seq_len * width * (heads + 2 * keys_wide),
        name="dense_late",
    )
    late = summed(kept, sent)

    small = ordered_sum(t_at, [small] + [swap(small, "tensor", r) for r in around])
    small = small + swap(small, "dp", 1)
    if expert_size <= FEW:
        small = ordered_sum(e_at, [small] + [swap(small, "expert", r) for r in range(1, expert_size)])
    else:
        small = jnp.sum(lax.all_gather(small, "expert"), axis=0)
    chunk = width // (dp_size * expert_size)
    at = (d_me * expert_size + e_me) * chunk
    loss_value = (experts * balance * small[2:3, :LANES])[0, :experts]
    return (
        output,
        loss_value,
        input_grad,
        lax.dynamic_slice(small, (0, at), (1, chunk))[0],
        late[:, :heads],
        late[:, heads : heads + keys_wide],
        late[:, heads + keys_wide :],
        early[:, :heads].T,
        lax.dynamic_slice(small, (1, at), (1, chunk))[0],
        early[:, heads : heads + experts],
        expert_grads[0],
        expert_grads[1],
        expert_grads[2],
    )


def solution(mesh):
    rows = ("dp", "expert")
    placed = (
        P(rows, None),
        P(rows, None),
        P(),
        P(None, "tensor"),
        P(None, "tensor"),
        P(None, "tensor"),
        P("tensor", None),
        P(),
        P(),
        P("expert", None, "tensor"),
        P("expert", None, "tensor"),
        P("expert", "tensor", None),
        P(rows, None),
    )
    return jax.shard_map(
        on_device,
        mesh=mesh,
        in_specs=placed,
        out_specs=(
            P(rows, None),
            P(),
            P(rows, None),
            P(rows),
            P(rows, "tensor"),
            P(rows, "tensor"),
            P(rows, "tensor"),
            P("tensor", rows),
            P(rows),
            P(rows, None),
            P("expert", None, "tensor"),
            P("expert", None, "tensor"),
            P("expert", "tensor", None),
        ),
        check_vma=False,
    )
```

```python
import functools

import jax
import jax.numpy as jnp
import numpy as np
from jax import lax
from jax.experimental import pallas as pl
from jax.experimental.pallas import tpu as pltpu
from jax.sharding import PartitionSpec as P

HD = 64
TOP = 8
EPS = 1e-06
ROPE_BASE = 10000.0
MASKED = -1e30
BF = jnp.bfloat16
F32 = jnp.float32
FEW = 8
LANES = 128
MIB = 1 << 20


def dot(a, b, dims):
    return lax.dot_general(a, b, (dims, ((), ())), preferred_element_type=F32)


def nn(a, b):
    return dot(a, b, ((1,), (0,)))


def nt(a, b):
    return dot(a, b, ((1,), (1,)))


def tn(a, b):
    return dot(a, b, ((0,), (0,)))


def swap(x, axis, distance):
    size = lax.axis_size(axis)
    return lax.ppermute(x, axis, [(i, i ^ distance) for i in range(size)])


def spread(x, axis):
    size = lax.axis_size(axis)
    if size <= FEW:
        return [swap(x, axis, r) for r in range(1, size)]
    whole = lax.all_gather(x, axis)
    order = jnp.arange(1, size) ^ lax.axis_index(axis)
    return list(jnp.take(whole, order, axis=0))


def deal(parts, axis):
    size = lax.axis_size(axis)
    if size <= FEW:
        return [swap(part, axis, r + 1) for r, part in enumerate(parts)]
    order = jnp.arange(size) ^ lax.axis_index(axis)
    whole = jnp.take(jnp.stack([parts[0], *parts]), order, axis=0)
    back = lax.all_to_all(whole, axis, 0, 0, tiled=True)
    return list(jnp.take(back, order, axis=0)[1:])


def rope_tables(seq_len):
    half = HD // 2
    frequency = ROPE_BASE ** (-(np.arange(half, dtype=np.float32) * 2.0) / HD)
    angles = np.arange(seq_len, dtype=np.float32)[:, None] * frequency[None, :].astype(np.float32)
    cosine, sine = np.cos(angles), np.sin(angles)
    heads = LANES // HD
    return (
        np.tile(cosine, (1, 2 * heads)).astype(np.float32),
        np.tile(np.concatenate([-sine, sine], axis=1), (1, heads)).astype(np.float32),
    )


def lane_of(shape):
    return lax.broadcasted_iota(jnp.int32, shape, 1)


def halves_swapped(x):
    first = lane_of(x.shape) % HD < HD // 2
    half = HD // 2
    return jnp.where(first, pltpu.roll(x, LANES - half, 1), pltpu.roll(x, half, 1))


def low_high(x, head):
    other = pltpu.roll(x.astype(F32), HD, 1).astype(x.dtype)
    low = lane_of(x.shape) < HD
    zero = jnp.zeros_like(x)
    at_low, at_high = (x, other) if head == 0 else (other, x)
    return jnp.where(low, at_low, zero), jnp.where(low, zero, at_high)


def causal(scores):
    rows = lax.broadcasted_iota(jnp.int32, scores.shape, 0)
    return lane_of(scores.shape) <= rows


def shape(dims, kind):
    return jax.ShapeDtypeStruct(dims, kind)


def whole_block(dims):
    return pl.BlockSpec(dims, lambda i: (0,) * len(dims))


def call(kernel, outs, operands, name, places="", out_places="", scratch=(), limit=40, flops=0):
    kinds = {"s": pltpu.SMEM, "v": pltpu.VMEM}

    def spec(place, x):
        if not isinstance(place, str):
            return place
        if place == "b":
            return whole_block(x.shape)
        return pl.BlockSpec(memory_space=kinds[place])

    places = [*places] + ["v"] * (len(operands) - len(places))
    out_places = [*out_places] + ["v"] * (len(outs) - len(out_places))
    return pl.pallas_call(
        kernel,
        grid=(1,),
        out_shape=outs,
        in_specs=[spec(p, x) for p, x in zip(places, operands)],
        out_specs=[spec(p, x) for p, x in zip(out_places, outs)],
        scratch_shapes=list(scratch),
        compiler_params=pltpu.CompilerParams(vmem_limit_bytes=limit * MIB),
        cost_estimate=pl.CostEstimate(flops=int(100.0*(flops)), bytes_accessed=0, transcendentals=0),
        name=name,
    )(*operands)


def tied(first, then):
    return lax.optimization_barrier((first, then))


def pieces_kernel(me_ref, cot_ref, routes_ref, router_ref, both_ref, c1, c2, router_out, held):
    rows, width = c1.shape[0], cot_ref.shape[1]
    eye = lax.broadcasted_iota(jnp.int32, (TOP, LANES), 0) == lane_of((TOP, LANES))
    held[...] = tn(routes_ref[...].astype(F32).astype(BF), eye.astype(F32).astype(BF))
    for r, c in enumerate((both_ref.at[0], c1, c2, both_ref.at[1])):
        start = pl.multiple_of((me_ref[0] ^ r) * rows, rows)
        c[:, :width] = cot_ref[pl.ds(start, rows), :]
        c[:, width:] = held[pl.ds(start, rows), :].astype(BF)
    router_out[...] = jnp.zeros(router_out.shape, BF)
    router_out[: router_ref.shape[0], :] = router_ref[...]


def sorted_cots_kernel(own_ref, *refs):
    others, (far_ref, first_ref, last_ref) = refs[:-3], refs[-3:]
    for i, x in enumerate((own_ref, *others)):
        first_ref[i] = x[0]
        last_ref[i] = x[1]
        if i:
            far_ref[i - 1] = x[0]


def attend_kernel(
    me_ref, x_ref, gain_ref, wq_ref, wk_ref, wv_ref, wo_ref, cos_ref, sin_ref, *refs
):
    n_ref, q_ref, k_ref, v_ref, o_ref, lse_ref, xq_ref = refs[:7]
    parts, whole = refs[7:-1], refs[-1]
    rows, width = xq_ref.shape
    starts = [pl.multiple_of((me_ref[0] ^ r) * rows, rows) for r in range(4)]
    xq_ref[...] = x_ref[pl.ds(starts[0], rows), :]
    x = x_ref[...].astype(F32)
    inv = lax.rsqrt(jnp.mean(x * x, axis=-1, keepdims=True) + EPS)
    n = (x * inv * gain_ref[...]).astype(BF)
    n_ref[...] = n
    cosine, sine = cos_ref[...], sin_ref[...]
    q, k = nn(n, wq_ref[...]), nn(n, wk_ref[...])
    v_ref[...] = nn(n, wv_ref[...]).astype(BF)
    for at in range(0, q.shape[1], LANES):
        tile = q[:, at : at + LANES]
        q_ref[:, at : at + LANES] = (tile * cosine + halves_swapped(tile) * sine).astype(BF)
    for at in range(0, k.shape[1], LANES):
        tile = k[:, at : at + LANES]
        k_ref[:, at : at + LANES] = (tile * cosine + halves_swapped(tile) * sine).astype(BF)
    lse_all = jnp.zeros(lse_ref.shape, F32)
    for head in range(q.shape[1] // LANES):
        at = head // 2 * LANES
        keys = low_high(k_ref[:, at : at + LANES], head % 2)
        values = low_high(v_ref[:, at : at + LANES], head % 2)
        pair = q_ref[:, head * LANES : (head + 1) * LANES]
        mixed = 0.0
        for g in range(2):
            s = nt(pair, keys[g]) * HD ** (-0.5)
            s = jnp.where(causal(s), s, MASKED)
            peak = jnp.max(s, axis=-1, keepdims=True)
            e = jnp.exp(s - peak)
            total = jnp.sum(e, axis=-1, keepdims=True)
            mixed = mixed + nn((e / total).astype(BF), values[g])
            lse = peak + jnp.log(total)
            lse_all = jnp.where(lane_of(lse_all.shape) == 2 * head + g, lse, lse_all)
        o_ref[:, head * LANES : (head + 1) * LANES] = mixed.astype(BF)
    lse_ref[...] = lse_all
    whole[...] = nn(o_ref[...], wo_ref[...])
    for start, part in zip(starts, parts):
        part[...] = whole[pl.ds(start, rows), :].astype(part.dtype)


def norm_two_kernel(x_ref, gain_ref, own_ref, *refs):
    others, (h_ref, n_ref) = refs[:-2], refs[-2:]
    attn = own_ref[...]
    for other in others:
        attn = attn + other[...].astype(F32)
    h = x_ref[...].astype(F32) + attn
    inv = lax.rsqrt(jnp.mean(h * h, axis=-1, keepdims=True) + EPS)
    h_ref[...] = h
    n_ref[...] = (h * inv * gain_ref[...]).astype(BF)


def together_kernel(*refs):
    pieces, out = refs[:-1], refs[-1]
    at = 0
    for piece in pieces:
        if len(piece.shape) == 2:
            out[at] = piece[...]
            at += 1
        else:
            out[at : at + piece.shape[0]] = piece[...]
            at += piece.shape[0]


def together(pieces):
    count = sum(1 if x.ndim == 2 else x.shape[0] for x in pieces)
    return call(
        together_kernel, [shape((count, *pieces[0].shape[-2:]), pieces[0].dtype)], pieces, "together"
    )[0]


def router_of(rows, router_ref, routes, experts):
    z = nt(rows, router_ref[...])
    lane = lane_of(z.shape)
    z = jnp.where(lane < experts, z, MASKED)
    e = jnp.exp(z - jnp.max(z, axis=-1, keepdims=True))
    probs = e / jnp.sum(e, axis=-1, keepdims=True)
    chosen = chosen_of(lane, routes)
    zc = jnp.where(chosen, z, MASKED)
    ec = jnp.where(chosen, jnp.exp(zc - jnp.max(zc, axis=-1, keepdims=True)), 0.0)
    return probs, ec / jnp.sum(ec, axis=-1, keepdims=True)


def chosen_of(lane, routes):
    place, named = lane.astype(F32), routes.astype(F32)
    chosen = place == named[:, 0:1]
    for k in range(1, TOP):
        chosen = chosen | (place == named[:, k : k + 1])
    return chosen


def weights_kernel(wg_ref, wu_ref, out_ref):
    hidden = wg_ref.shape[2]
    out_ref[:, :hidden] = wg_ref[0]
    out_ref[:, hidden:] = wu_ref[0]


def gate_up_weights(w_gate, w_up):
    local, width, hidden = w_gate.shape
    block = pl.BlockSpec((1, width, hidden), lambda e: (e, 0, 0))
    return pl.pallas_call(
        weights_kernel,
        grid=(local,),
        in_specs=[block, block],
        out_specs=pl.BlockSpec((width, 2 * hidden), lambda e: (0, e)),
        out_shape=shape((width, 2 * hidden * local), BF),
        compiler_params=pltpu.CompilerParams(vmem_limit_bytes=30 * MIB),
        cost_estimate=pl.CostEstimate(flops=int(100.0*(0)), bytes_accessed=4 * w_gate.size * 2, transcendentals=0),
        name="gate_up_weights",
    )(w_gate, w_up)


def experts_kernel(experts, base_ref, x_ref, c_ref, router_ref, wcat, wd_ref, dgu_ref, hg_ref, d_ref, m_ref, count_ref):
    hidden = LANES
    pair = 2 * hidden
    width = x_ref.shape[1]
    x = x_ref[...]
    routes = c_ref[:, width:]
    named = chosen_of(lane_of(routes.shape), routes).astype(F32)
    count_ref[0] = jnp.broadcast_to(jnp.sum(named, axis=0, keepdims=True), count_ref.shape[1:])
    _, gates = router_of(x, router_ref, routes, experts)
    lane = lane_of(gates.shape)
    dots = jnp.zeros(gates.shape, F32)
    for e in range(hg_ref.shape[1] // hidden):
        mine = lane == base_ref[0] + e
        g = jnp.sum(jnp.where(mine, gates, 0.0), axis=-1, keepdims=True)
        both = nn(x, wcat[:, e * pair : (e + 1) * pair])
        v = nt(c_ref[:, :width], wd_ref[e * hidden : (e + 1) * hidden, :])
        gate, up = both[:, :hidden], both[:, hidden:]
        sig = 1.0 / (1.0 + jnp.exp(-gate))
        act = gate * sig
        hid = act * up
        dots = jnp.where(mine, jnp.sum(hid * v, axis=-1, keepdims=True), dots)
        gv = g * v
        hg_ref[:, e * hidden : (e + 1) * hidden] = (g * hid).astype(BF)
        d_gate = gv * up * sig * (1.0 + gate * (1.0 - sig))
        dgu_ref[:, e * pair : e * pair + hidden] = d_gate.astype(BF)
        dgu_ref[:, e * pair + hidden : (e + 1) * pair] = (gv * act).astype(BF)
    d_ref[:, width:] = dots.astype(d_ref.dtype)
    step = 256
    for at in range(0, width, step):
        d_ref[:, at : at + step] = nt(dgu_ref[...], wcat[at : at + step, :]).astype(d_ref.dtype)
    m_ref[...] = nn(hg_ref[...], wd_ref[...]).astype(m_ref.dtype)


def run_experts(experts, base, x, c, router, wcat, down_flat, kind):
    count, rows, width = x.shape
    inner = down_flat.shape[0]
    wide = width + LANES
    total = count * rows
    step = min(total, 256)
    per = lambda w: pl.BlockSpec((step, w), lambda i: (i, 0))
    resident = pl.BlockSpec(memory_space=pltpu.VMEM)
    dgu, hid, d, m, counts = pl.pallas_call(
        functools.partial(experts_kernel, experts),
        grid=(total // step,),
        in_specs=[pl.BlockSpec(memory_space=pltpu.SMEM), per(width), per(wide)] + [resident] * 3,
        out_specs=[per(2 * inner), per(inner), per(wide), per(width)]
        + [pl.BlockSpec((1, 8, LANES), lambda i: (i, 0, 0))],
        out_shape=[
            shape((total, 2 * inner), BF),
            shape((total, inner), BF),
            shape((total, wide), kind),
            shape((total, width), kind),
            shape((total // step, 8, LANES), F32),
        ],
        compiler_params=pltpu.CompilerParams(vmem_limit_bytes=30 * MIB),
        cost_estimate=pl.CostEstimate(flops=int(100.0*(12 * total * width * inner)), bytes_accessed=0, transcendentals=0),
        name="experts",
    )(base, x.reshape(total, width), c.reshape(total, wide), router, wcat, down_flat)
    return dgu, hid, d.reshape(count, rows, wide), m.reshape(count, rows, width), counts


def split_sum_kernel(count, near, *refs):
    ins, outs = refs[:count], refs[count:]
    for s in range(ins[0].shape[0]):
        total = ins[0][s].astype(F32)
        for x in ins[1:]:
            total = total + x[s].astype(F32)
        outs[s][...] = total.astype(outs[s].dtype)


def split_sum(arrays, name):
    count, *dims = arrays[0].shape
    outs = [shape(dims, F32)] + [shape(dims, BF)] * (count - 1)
    return call(functools.partial(split_sum_kernel, len(arrays), True), outs, arrays, name)


def add_kernel(*refs):
    pieces, out = refs[:-1], refs[-1]
    total = pieces[0][...].astype(F32)
    for piece in pieces[1:]:
        total = total + piece[...].astype(F32)
    out[...] = total.astype(out.dtype)


def added(pieces, kind, name):
    return call(add_kernel, [shape(pieces[0].shape, kind)], pieces, name)[0]


def grads_kernel(*refs):
    ns, dgus, hs, cs = (refs[4 * i : 4 * i + 4] for i in range(4))
    out_ref = refs[16]
    hidden, width = hs[0].shape[1], ns[0].shape[1]
    both, down = 0.0, 0.0
    for n, dgu, h, c in zip(ns, dgus, hs, cs):
        both = both + tn(n[...], dgu[...])
        down = down + tn(h[...], c[:, :width])
    out_ref[0, :width, :] = both[:, :hidden].astype(BF)
    out_ref[0, width : 2 * width, :] = both[:, hidden:].astype(BF)
    for at in range(0, width, hidden):
        out_ref[0, 2 * width + at : 2 * width + at + hidden, :] = down[:, at : at + hidden].astype(BF)


def run_grads(n, dgu, h, c, local, hidden):
    width = n[0].shape[-1]
    flat = lambda xs: [x.reshape(-1, x.shape[-1]) for x in xs]
    n, c = flat(n), flat(c)
    whole = lambda xs: [pl.BlockSpec(x.shape, lambda e: (0, 0)) for x in xs]
    cols = lambda xs, w: [pl.BlockSpec((x.shape[0], w), lambda e: (0, e)) for x in xs]
    few = n[0].shape[0] <= 512
    return pl.pallas_call(
        grads_kernel,
        grid=(local,),
        in_specs=whole(n) + cols(dgu, 2 * hidden) + cols(h, hidden) + whole(c),
        out_specs=pl.BlockSpec((1, 3 * width, hidden), lambda e: (e, 0, 0)),
        out_shape=shape((local, 3 * width, hidden), BF),
        compiler_params=pltpu.CompilerParams(vmem_limit_bytes=(32 if few else 58) * MIB),
        cost_estimate=pl.CostEstimate(flops=int(100.0*(24 * n[0].size * hidden * local)), bytes_accessed=0, transcendentals=0),
        name="expert_grads",
    )(*n, *dgu, *h, *c)


def both_copies_kernel(mine_ref, other_ref, gate_ref, up_ref, down_ref):
    width, hidden = gate_ref.shape[1:]

    def total(at, count):
        rows = pl.ds(at, count)
        return mine_ref[0, rows, :].astype(F32) + other_ref[0, rows, :].astype(F32)

    gate_ref[0] = total(0, width)
    up_ref[0] = total(width, width)
    for at in range(0, width, hidden):
        down_ref[0, :, at : at + hidden] = total(2 * width + at, hidden)


def both_copies(mine, other):
    local, rows, hidden = mine.shape
    width = rows // 3
    block = lambda *dims: pl.BlockSpec((1, *dims), lambda e: (e, 0, 0))
    return pl.pallas_call(
        both_copies_kernel,
        grid=(local,),
        in_specs=[block(rows, hidden)] * 2,
        out_specs=[block(width, hidden), block(width, hidden), block(hidden, width)],
        out_shape=[
            shape((local, width, hidden), F32),
            shape((local, width, hidden), F32),
            shape((local, hidden, width), F32),
        ],
        compiler_params=pltpu.CompilerParams(vmem_limit_bytes=58 * MIB),
        cost_estimate=pl.CostEstimate(flops=int(100.0*(0)), bytes_accessed=8 * mine.size, transcendentals=0),
        name="both_copies",
    )(mine, other)


def norm_back_kernel(experts, count, h_ref, n_ref, gain_ref, router_ref, bal_ref, cot_ref, *refs):
    sums, (wide_ref, dh_ref, small_ref) = refs[:count], refs[count:]
    near = sums[0][...].astype(F32)
    for other in sums[1:]:
        near = near + other[...].astype(F32)
    rows, width = h_ref.shape
    dots = near[:, width:]
    probs, gates = router_of(n_ref[...], router_ref, cot_ref[0, :, width:], experts)
    bal = bal_ref[...]
    d_chosen = gates * (dots - jnp.sum(gates * dots, axis=-1, keepdims=True))
    dz = probs * (bal - jnp.sum(probs * bal, axis=-1, keepdims=True)) + d_chosen
    dz = dz.astype(BF)
    wide_ref[:, width:] = dz
    dn = near[:, :width] + nn(dz, router_ref[...])
    h = h_ref[...]
    inv = lax.rsqrt(jnp.mean(h * h, axis=-1, keepdims=True) + EPS)
    u = gain_ref[...] * dn
    dy = cot_ref[0, :, :width].astype(F32)
    dh = dy + inv * u - h * (inv * inv * inv * jnp.mean(u * h, axis=-1, keepdims=True))
    dh_ref[...] = dh
    wide_ref[:, :width] = dh.astype(BF)
    small_ref[...] = jnp.zeros(small_ref.shape, F32)
    small_ref[1:2, :] = jnp.sum(dn * h * inv, axis=0, keepdims=True)
    small_ref[2:3, : probs.shape[1]] = jnp.sum(probs, axis=0, keepdims=True)


def attend_back_kernel(
    me_ref, w0, w1, w2, w3, x_ref, q_ref, k_ref, v_ref, lse_ref, wq_ref, wk_ref, wv_ref, wo_ref, cos_ref, sin_ref,
    small_in, wide_ref, dq_ref, p0, p1, p2, p3, do_ref, whole, small_ref
):
    rows = w0.shape[0]
    width = x_ref.shape[1]
    for r, piece in enumerate((w0, w1, w2, w3)):
        start = pl.multiple_of((me_ref[0] ^ r) * rows, rows)
        wide_ref[pl.ds(start, rows), :] = piece[...]
    do_ref[...] = nt(wide_ref[:, :width], wo_ref[...]).astype(BF)
    cosine, sine = cos_ref[...], sin_ref[...]
    scale = HD ** (-0.5)
    heads, keys_wide = q_ref.shape[1], k_ref.shape[1]
    dk_tiles = [0.0] * (keys_wide // LANES)
    dv_tiles = [0.0] * (keys_wide // LANES)

    def back(tile):
        return (tile * cosine - halves_swapped(tile) * sine).astype(BF)

    for head in range(heads // LANES):
        at = head // 2 * LANES
        side = head % 2
        keys = low_high(k_ref[:, at : at + LANES], side)
        values = low_high(v_ref[:, at : at + LANES], side)
        pair = q_ref[:, head * LANES : (head + 1) * LANES]
        grad = do_ref[:, head * LANES : (head + 1) * LANES]
        dq = 0.0
        dk, dv = [], []
        for g in range(2):
            s = nt(pair, keys[g]) * scale
            lse = lse_ref[:, 2 * head + g : 2 * head + g + 1]
            p = jnp.where(causal(s), jnp.exp(s - lse), 0.0)
            dp = nt(grad, values[g])
            ds = (p * (dp - jnp.sum(p * dp, axis=-1, keepdims=True))).astype(BF)
            dq = dq + nn(ds, keys[g])
            dk.append(tn(ds, pair))
            dv.append(tn(p.astype(BF), grad))
        dq_ref[:, head * LANES : (head + 1) * LANES] = back(dq * scale)
        mine = lane_of(dk[0].shape) < HD
        if side == 0:
            dk_sum = jnp.where(mine, dk[0] + pltpu.roll(dk[1], HD, 1), 0.0)
            dv_sum = jnp.where(mine, dv[0] + pltpu.roll(dv[1], HD, 1), 0.0)
        else:
            dk_sum = jnp.where(mine, 0.0, pltpu.roll(dk[0], HD, 1) + dk[1])
            dv_sum = jnp.where(mine, 0.0, pltpu.roll(dv[0], HD, 1) + dv[1])
        dk_tiles[head // 2] = dk_tiles[head // 2] + dk_sum
        dv_tiles[head // 2] = dv_tiles[head // 2] + dv_sum
    for i, tile in enumerate(dk_tiles):
        at = heads + i * LANES
        dq_ref[:, at : at + LANES] = back(tile * scale)
    for i, tile in enumerate(dv_tiles):
        at = heads + keys_wide + i * LANES
        dq_ref[:, at : at + LANES] = tile.astype(BF)
    dn = nt(dq_ref[:, :heads], wq_ref[...])
    dn = dn + nt(dq_ref[:, heads : heads + keys_wide], wk_ref[...])
    whole[...] = dn + nt(dq_ref[:, heads + keys_wide :], wv_ref[...])
    x = x_ref[...].astype(F32)
    inv = lax.rsqrt(jnp.mean(x * x, axis=-1, keepdims=True) + EPS)
    small_ref[...] = small_in[...]
    small_ref[0:1, :] = jnp.sum(whole[...] * x * inv, axis=0, keepdims=True)
    small = small_ref[...]
    high = small.astype(BF)
    both = jnp.concatenate([high.astype(F32), small - high.astype(F32)], axis=0).astype(BF)
    for r, part in enumerate((p0, p1, p2, p3)):
        start = pl.multiple_of((me_ref[0] ^ r) * rows, rows)
        part[:rows, :] = whole[pl.ds(start, rows), :].astype(part.dtype)
        part[rows:, :] = both.astype(part.dtype)


def dense_kernel(me_ref, a0, a1, a2, a3, wide_ref, o_ref, n_ref, dq_ref, kept_ref, sent_ref, two_ref, whole):
    rows, width = a0.shape[1:]
    for r, piece in enumerate((a0, a1, a2, a3)):
        start = pl.multiple_of((me_ref[1] ^ r) * rows, rows)
        two_ref[pl.ds(start, rows), :] = piece[0]
    columns, heads = dq_ref.shape[1], o_ref.shape[1]
    whole[:, :columns] = tn(n_ref[...], dq_ref[...])
    whole[:, columns : columns + heads] = tn(wide_ref[:, :width], o_ref[...])
    whole[:, columns + heads :] = tn(two_ref[...], wide_ref[:, width:])
    half = kept_ref.shape[0]
    kept_ref[...] = whole[pl.ds(pl.multiple_of(me_ref[0] * half, half), half), :]
    sent_ref[...] = whole[pl.ds(pl.multiple_of((1 - me_ref[0]) * half, half), half), :].astype(BF)


def input_grad_kernel(me_ref, x_ref, gain_ref, dh_ref, *refs):
    parts, (ig_ref, small_ref, held) = refs[:-3], refs[-3:]
    rows = dh_ref.shape[0]
    x = x_ref[...].astype(F32)
    inv = lax.rsqrt(jnp.mean(x * x, axis=-1, keepdims=True) + EPS)
    dn = parts[0][:rows, :].astype(F32)
    for part in parts[1:]:
        dn = dn + part[:rows, :].astype(F32)
    u = gain_ref[...] * dn
    ig = dh_ref[...] + inv * u - x * (inv * inv * inv * jnp.mean(u * x, axis=-1, keepdims=True))
    ig_ref[...] = ig.astype(BF)
    for r, part in enumerate(parts):
        both = part[rows:, :].astype(F32)
        held[me_ref[0] ^ r] = both[:8] + both[8:]
    total = held[0]
    for i in range(1, len(parts)):
        total = total + held[i]
    small_ref[...] = total


def natural_kernel(me_ref, *refs):
    pieces, out = refs[:-1], refs[-1]
    rows = pieces[0].shape[0]
    for r, piece in enumerate(pieces):
        start = pl.multiple_of((me_ref[0] ^ r) * rows, rows)
        out[pl.ds(start, rows), :] = piece[...].astype(out.dtype)


def ordered_sum_kernel(me_ref, *refs):
    pieces, out, held = refs[:-2], refs[-2], refs[-1]
    for r, piece in enumerate(pieces):
        held[me_ref[0] ^ r] = piece[...]
    total = held[0]
    for i in range(1, len(pieces)):
        total = total + held[i]
    out[...] = total


def ordered_sum(me, pieces):
    return call(
        ordered_sum_kernel,
        [shape(pieces[0].shape, F32)],
        (me, *pieces),
        "ordered_sum",
        "s",
        scratch=[pltpu.VMEM((len(pieces), *pieces[0].shape), F32)],
    )[0]


def kept_and_dealt_kernel(me_ref, kept_ref, got_ref, *outs):
    rows = outs[0].shape[0]
    for r, out in enumerate(outs):
        start = pl.multiple_of((me_ref[0] ^ r) * rows, rows)
        at = pl.ds(start, rows)
        out[...] = (kept_ref[at, :] + got_ref[at, :].astype(F32)).astype(out.dtype)


def dense_sum_kernel(mine_ref, *refs):
    others, (q_ref, k_ref, v_ref, o_ref, r_ref) = refs[:-5], refs[-5:]
    total = mine_ref[...]
    for other in others:
        total = total + other[...].astype(F32)
    at = 0
    for out in (q_ref, k_ref, v_ref):
        out[...] = total[:, at : at + out.shape[1]]
        at += out.shape[1]
    o_ref[...] = total[:, at : at + o_ref.shape[0]].T
    at += o_ref.shape[0]
    r_ref[...] = total[:, at : at + r_ref.shape[1]]


def on_device(
    tokens,
    routes,
    gain_first,
    w_query,
    w_key,
    w_value,
    w_output,
    gain_second,
    w_router,
    w_gate,
    w_up,
    w_down,
    cotangent,
):
    seq_len, width = tokens.shape
    experts = w_router.shape[1]
    local, _, hidden = w_gate.shape
    tensor_size = lax.axis_size("tensor")
    expert_size = lax.axis_size("expert")
    dp_size = lax.axis_size("dp")
    token_count = seq_len * dp_size * expert_size
    rows = seq_len // tensor_size
    wide_width = width + LANES
    last = tensor_size - 1
    around = range(1, tensor_size)
    t_me, e_me, d_me = lax.axis_index("tensor"), lax.axis_index("expert"), lax.axis_index("dp")
    t_at = t_me.astype(jnp.int32).reshape(1)
    e_at = e_me.astype(jnp.int32).reshape(1)
    base = (e_me * local).astype(jnp.int32).reshape(1)
    d_at = jnp.stack([d_me, t_me]).astype(jnp.int32)
    cosine, sine = rope_tables(seq_len)
    gain_one, gain_two = gain_first[None], gain_second[None]
    down_flat = w_down.reshape(local * hidden, width)

    cot_ends, cot_one, cot_two, router = call(
        pieces_kernel,
        [shape((2, rows, wide_width), BF)]
        + [shape((rows, wide_width), BF)] * 2
        + [shape((LANES, width), BF)],
        (t_at, cotangent, routes.T, w_router.T),
        "pieces",
        "sbbb",
        scratch=[pltpu.VMEM((seq_len, LANES), F32)],
        limit=58,
    )
    cot_got = spread(cot_ends, "expert")

    heads, keys_wide = w_query.shape[1], w_key.shape[1]
    n_one, q, k, v, o, lse, xq, *rest = call(
        attend_kernel,
        [
            shape((seq_len, width), BF),
            shape((seq_len, heads), BF),
            shape((seq_len, keys_wide), BF),
            shape((seq_len, keys_wide), BF),
            shape((seq_len, heads), BF),
            shape((seq_len, LANES), F32),
            shape((rows, width), BF),
        ]
        + [shape((rows, width), F32)]
        + [shape((rows, width), BF)] * last,
        (t_at, tokens, gain_one, w_query, w_key, w_value, w_output, cosine, sine),
        "attend",
        "s" + "b" * 8,
        "bbbbbbv",
        scratch=[pltpu.VMEM((seq_len, width), F32)],
        limit=58,
        flops=2 * seq_len * width * 4 * heads,
    )
    parts = rest
    got = [swap(parts[r], "tensor", r) for r in around]
    h, n_two = call(
        norm_two_kernel,
        [shape((rows, width), F32), shape((rows, width), BF)],
        (xq, gain_two, parts[0], *got),
        "norm_two",
        "vb",
        "vv",
    )

    wcat = gate_up_weights(w_gate, w_up)
    count = expert_size
    cot_far, cot_first, cot_last = call(
        sorted_cots_kernel,
        [shape((n, rows, wide_width), BF) for n in (count - 1, count, count)],
        (cot_ends, *cot_got),
        "sorted_cots",
    )
    cot_middle = [swap(cot_far, "tensor", r) for r in range(1, last)]
    cots = [
        cot_first,
        together([cot_one, cot_middle[0]]),
        together([cot_two, cot_middle[1]]),
        cot_last,
    ]

    two_got = []
    for r in range(1, expert_size):
        if expert_size <= FEW:
            cot_got[r - 1], two = tied(cot_got[r - 1], n_two)
            two_got.append(swap(two, "expert", r))
    if expert_size > FEW:
        two_got = spread(n_two, "expert")
    first = together([n_two, *two_got])
    twos = [first] + [swap(first, "tensor", r) for r in range(1, last)]
    _, late = tied(cot_middle, first)
    twos.append(swap(late, "tensor", last))

    run = functools.partial(
        run_experts, experts, base, router=router, wcat=wcat, down_flat=down_flat
    )
    made = [run(twos[0], cots[0], kind=F32)]
    got = []
    for r in around:
        held, (two, cot) = tied(made[-1], (twos[r], cots[r]))
        made[-1] = held
        made.append(run(two, cot, kind=BF))
        got.append(swap(made[-1][2], "tensor", r))
    dgus, hids, ds, moes, counts = zip(*made)
    grads = run_grads(twos, dgus, hids, cots, local, hidden)
    counts = sum(jnp.sum(x[:, :1], axis=0) for x in counts)
    counts = counts + swap(counts, "dp", 1)
    balance = experts * (counts / (token_count * TOP)) / token_count
    grads, got = tied(grads, got)
    got, moes = tied(got, moes)
    near, *across = split_sum([ds[0], *got], "dn_sum")
    near_sums = [near, *deal(across, "expert")]
    moe_got = [swap(moes[r], "tensor", r) for r in range(1, last)]
    moe_got, near_sums = tied(moe_got, near_sums)

    wide, dh, small = call(
        functools.partial(norm_back_kernel, experts, len(near_sums)),
        [shape((rows, wide_width), BF), shape((rows, width), F32), shape((8, width), F32)],
        (h, n_two, gain_two, router, balance, cot_ends, *near_sums),
        "norm_back",
        "v",
        "vvv",
    )
    wides = [wide] + [swap(wide, "tensor", r) for r in around]
    wides, grads = tied(wides, grads)
    moe_got.append(swap(moes[last], "tensor", last))
    moe_got, wides = tied(moe_got, wides)
    part_rows = rows + 16
    wide_all, dqkv, *back_parts = call(
        attend_back_kernel,
        [
            shape((seq_len, wide_width), BF),
            shape((seq_len, heads + 2 * keys_wide), BF),
            shape((part_rows, width), F32),
        ]
        + [shape((part_rows, width), BF)] * last,
        (t_at, *wides, tokens, q, k, v, lse, w_query, w_key, w_value, w_output, cosine, sine, small),
        "attend_back",
        "s" + "v" * tensor_size + "b" * 11,
        "bb",
        limit=58,
        scratch=[
            pltpu.VMEM((seq_len, heads), BF),
            pltpu.VMEM((seq_len, width), F32),
            pltpu.VMEM((8, width), F32),
        ],
        flops=2 * seq_len * width * 4 * heads,
    )
    part_sums = [back_parts[0]] + [swap(back_parts[r], "tensor", r) for r in around]
    part_sums, moe_got = tied(part_sums, moe_got)
    moe_near, *moe_across = split_sum([moes[0], *moe_got], "moe_sum")
    moe_sums = [moe_near, *deal(moe_across, "expert")]
    ig, small = call(
        input_grad_kernel,
        [shape((rows, width), BF), shape((8, width), F32)],
        (t_at, xq, gain_one, dh, *part_sums),
        "input_grad",
        "svbv",
        scratch=[pltpu.VMEM((tensor_size, 8, width), F32)],
    )
    igs = [ig] + [swap(ig, "tensor", r) for r in around]
    expert_grads = both_copies(grads, swap(grads, "dp", 1))
    expert_grads, igs = tied(expert_grads, igs)
    input_grad = call(
        natural_kernel, [shape((seq_len, width), F32)], (t_at, *igs), "input_grad_whole", "s", "b"
    )[0]
    out_piece = added([h, *moe_sums], BF, "out_piece")
    output = call(
        natural_kernel,
        [shape((seq_len, width), BF)],
        (t_at, out_piece, *[swap(out_piece, "tensor", r) for r in around]),
        "output",
        "s",
        "b",
    )[0]

    half = width // dp_size
    chunk = half // expert_size

    columns = heads + 2 * keys_wide
    all_columns = columns + heads + LANES
    own_block = pl.BlockSpec((1, rows, width), lambda i: (0, 0, 0))
    kept, sent = call(
        dense_kernel,
        [shape((half, all_columns), F32), shape((half, all_columns), BF)],
        (d_at, *twos, wide_all, o, n_one, dqkv),
        "dense",
        ["s"] + [own_block] * tensor_size + ["b"] * 4,
        "vv",
        limit=54,
        scratch=[
            pltpu.VMEM((seq_len, width), BF),
            pltpu.VMEM((width, all_columns), F32),
        ],
        flops=2 * seq_len * width * all_columns,
    )
    mine, *others = call(
        kept_and_dealt_kernel,
        [shape((chunk, all_columns), F32)] + [shape((chunk, all_columns), BF)] * (expert_size - 1),
        (e_at, kept, swap(sent, "dp", 1)),
        "dense_dealt",
        "s",
    )
    g_query, g_key, g_value, g_out, g_router = call(
        dense_sum_kernel,
        [
            shape((chunk, heads), F32),
            shape((chunk, keys_wide), F32),
            shape((chunk, keys_wide), F32),
            shape((heads, chunk), F32),
            shape((chunk, LANES), F32),
        ],
        (mine, *deal(others, "expert")),
        "dense_sum",
        "",
        "bbbbb",
    )

    small = small + swap(small, "dp", 1)
    small = ordered_sum(e_at, [small, *spread(small, "expert")])
    at = (d_me * expert_size + e_me) * chunk
    loss_value = (experts * balance * small[2:3, :LANES])[0, :experts]
    return (
        output,
        loss_value,
        input_grad,
        lax.dynamic_slice(small, (0, at), (1, chunk))[0],
        g_query,
        g_key,
        g_value,
        g_out,
        lax.dynamic_slice(small, (1, at), (1, chunk))[0],
        g_router[:, :experts],
        expert_grads[0],
        expert_grads[1],
        expert_grads[2],
    )


def solution(mesh):
    rows = ("dp", "expert")
    placed = (
        P(rows, None),
        P(rows, None),
        P(),
        P(None, "tensor"),
        P(None, "tensor"),
        P(None, "tensor"),
        P("tensor", None),
        P(),
        P(),
        P("expert", None, "tensor"),
        P("expert", None, "tensor"),
        P("expert", "tensor", None),
        P(rows, None),
    )
    return jax.shard_map(
        on_device,
        mesh=mesh,
        in_specs=placed,
        out_specs=(
            P(rows, None),
            P(),
            P(rows, None),
            P(rows),
            P(rows, "tensor"),
            P(rows, "tensor"),
            P(rows, "tensor"),
            P("tensor", rows),
            P(rows),
            P(rows, None),
            P("expert", None, "tensor"),
            P("expert", None, "tensor"),
            P("expert", "tensor", None),
        ),
        check_vma=False,
    )
```

```python
import functools

import jax
import jax.numpy as jnp
import numpy as np
from jax import lax
from jax.experimental import pallas as pl
from jax.experimental.pallas import tpu as pltpu
from jax.sharding import PartitionSpec as P

HD = 64
TOP = 8
EPS = 1e-06
ROPE_BASE = 10000.0
MASKED = -1e30
BF = jnp.bfloat16
F32 = jnp.float32
FEW = 8
LANES = 128
MIB = 1 << 20


def dot(a, b, dims):
    return lax.dot_general(a, b, (dims, ((), ())), preferred_element_type=F32)


def nn(a, b):
    return dot(a, b, ((1,), (0,)))


def nt(a, b):
    return dot(a, b, ((1,), (1,)))


def tn(a, b):
    return dot(a, b, ((0,), (0,)))


def swap(x, axis, distance):
    size = lax.axis_size(axis)
    return lax.ppermute(x, axis, [(i, i ^ distance) for i in range(size)])


def spread(x, axis):
    size = lax.axis_size(axis)
    if size <= FEW:
        return [swap(x, axis, r) for r in range(1, size)]
    whole = lax.all_gather(x, axis)
    order = jnp.arange(1, size) ^ lax.axis_index(axis)
    return list(jnp.take(whole, order, axis=0))


def deal(parts, axis):
    size = lax.axis_size(axis)
    if size <= FEW:
        return [swap(part, axis, r + 1) for r, part in enumerate(parts)]
    order = jnp.arange(size) ^ lax.axis_index(axis)
    whole = jnp.take(jnp.stack([parts[0], *parts]), order, axis=0)
    back = lax.all_to_all(whole, axis, 0, 0, tiled=True)
    return list(jnp.take(back, order, axis=0)[1:])


def rope_tables(seq_len):
    half = HD // 2
    frequency = ROPE_BASE ** (-(np.arange(half, dtype=np.float32) * 2.0) / HD)
    angles = np.arange(seq_len, dtype=np.float32)[:, None] * frequency[None, :].astype(np.float32)
    cosine, sine = np.cos(angles), np.sin(angles)
    heads = LANES // HD
    return (
        np.tile(cosine, (1, 2 * heads)).astype(np.float32),
        np.tile(np.concatenate([-sine, sine], axis=1), (1, heads)).astype(np.float32),
    )


def lane_of(shape):
    return lax.broadcasted_iota(jnp.int32, shape, 1)


def halves_swapped(x):
    first = lane_of(x.shape) % HD < HD // 2
    half = HD // 2
    return jnp.where(first, pltpu.roll(x, LANES - half, 1), pltpu.roll(x, half, 1))


def low_high(x, head):
    other = pltpu.roll(x.astype(F32), HD, 1).astype(x.dtype)
    low = lane_of(x.shape) < HD
    zero = jnp.zeros_like(x)
    at_low, at_high = (x, other) if head == 0 else (other, x)
    return jnp.where(low, at_low, zero), jnp.where(low, zero, at_high)


def causal(scores):
    rows = lax.broadcasted_iota(jnp.int32, scores.shape, 0)
    return lane_of(scores.shape) <= rows


def shape(dims, kind):
    return jax.ShapeDtypeStruct(dims, kind)


def whole_block(dims):
    return pl.BlockSpec(dims, lambda i: (0,) * len(dims))


def call(kernel, outs, operands, name, places="", out_places="", scratch=(), limit=40, flops=0):
    kinds = {"s": pltpu.SMEM, "v": pltpu.VMEM}

    def spec(place, x):
        if not isinstance(place, str):
            return place
        if place == "b":
            return whole_block(x.shape)
        return pl.BlockSpec(memory_space=kinds[place])

    places = [*places] + ["v"] * (len(operands) - len(places))
    out_places = [*out_places] + ["v"] * (len(outs) - len(out_places))
    return pl.pallas_call(
        kernel,
        grid=(1,),
        out_shape=outs,
        in_specs=[spec(p, x) for p, x in zip(places, operands)],
        out_specs=[spec(p, x) for p, x in zip(out_places, outs)],
        scratch_shapes=list(scratch),
        compiler_params=pltpu.CompilerParams(vmem_limit_bytes=limit * MIB),
        cost_estimate=pl.CostEstimate(flops=int(100.0*(flops)), bytes_accessed=0, transcendentals=0),
        name=name,
    )(*operands)


def tied(first, then):
    return lax.optimization_barrier((first, then))


def pieces_kernel(me_ref, cot_ref, routes_ref, router_ref, *refs):
    cots, (router_out, held) = refs[:-2], refs[-2:]
    rows, width = cots[0].shape[0], cot_ref.shape[1]
    eye = lax.broadcasted_iota(jnp.int32, (TOP, LANES), 0) == lane_of((TOP, LANES))
    held[...] = tn(routes_ref[...].astype(F32).astype(BF), eye.astype(F32).astype(BF))
    for r, c in enumerate(cots):
        start = pl.multiple_of((me_ref[0] ^ r) * rows, rows)
        c[:, :width] = cot_ref[pl.ds(start, rows), :]
        c[:, width:] = held[pl.ds(start, rows), :].astype(BF)
    router_out[...] = jnp.zeros(router_out.shape, BF)
    router_out[: router_ref.shape[0], :] = router_ref[...]


def attend_kernel(
    me_ref, x_ref, gain_ref, wq_ref, wk_ref, wv_ref, wo_ref, cos_ref, sin_ref, *refs
):
    n_ref, q_ref, k_ref, v_ref, o_ref, lse_ref, xq_ref = refs[:7]
    parts, whole = refs[7:-1], refs[-1]
    rows, width = xq_ref.shape
    starts = [pl.multiple_of((me_ref[0] ^ r) * rows, rows) for r in range(4)]
    xq_ref[...] = x_ref[pl.ds(starts[0], rows), :]
    x = x_ref[...].astype(F32)
    inv = lax.rsqrt(jnp.mean(x * x, axis=-1, keepdims=True) + EPS)
    n = (x * inv * gain_ref[...]).astype(BF)
    n_ref[...] = n
    cosine, sine = cos_ref[...], sin_ref[...]
    q, k = nn(n, wq_ref[...]), nn(n, wk_ref[...])
    v_ref[...] = nn(n, wv_ref[...]).astype(BF)
    for at in range(0, q.shape[1], LANES):
        tile = q[:, at : at + LANES]
        q_ref[:, at : at + LANES] = (tile * cosine + halves_swapped(tile) * sine).astype(BF)
    for at in range(0, k.shape[1], LANES):
        tile = k[:, at : at + LANES]
        k_ref[:, at : at + LANES] = (tile * cosine + halves_swapped(tile) * sine).astype(BF)
    lse_all = jnp.zeros(lse_ref.shape, F32)
    for head in range(q.shape[1] // LANES):
        at = head // 2 * LANES
        keys = low_high(k_ref[:, at : at + LANES], head % 2)
        values = low_high(v_ref[:, at : at + LANES], head % 2)
        pair = q_ref[:, head * LANES : (head + 1) * LANES]
        mixed = 0.0
        for g in range(2):
            s = nt(pair, keys[g]) * HD ** (-0.5)
            s = jnp.where(causal(s), s, MASKED)
            peak = jnp.max(s, axis=-1, keepdims=True)
            e = jnp.exp(s - peak)
            total = jnp.sum(e, axis=-1, keepdims=True)
            mixed = mixed + nn((e / total).astype(BF), values[g])
            lse = peak + jnp.log(total)
            lse_all = jnp.where(lane_of(lse_all.shape) == 2 * head + g, lse, lse_all)
        o_ref[:, head * LANES : (head + 1) * LANES] = mixed.astype(BF)
    lse_ref[...] = lse_all
    whole[...] = nn(o_ref[...], wo_ref[...])
    for start, part in zip(starts, parts):
        part[...] = whole[pl.ds(start, rows), :].astype(part.dtype)


def norm_two_kernel(x_ref, gain_ref, own_ref, *refs):
    others, (h_ref, n_ref) = refs[:-2], refs[-2:]
    attn = own_ref[...]
    for other in others:
        attn = attn + other[...].astype(F32)
    h = x_ref[...].astype(F32) + attn
    inv = lax.rsqrt(jnp.mean(h * h, axis=-1, keepdims=True) + EPS)
    h_ref[...] = h
    n_ref[...] = (h * inv * gain_ref[...]).astype(BF)


def together_kernel(*refs):
    pieces, out = refs[:-1], refs[-1]
    at = 0
    for piece in pieces:
        if len(piece.shape) == 2:
            out[at] = piece[...]
            at += 1
        else:
            out[at : at + piece.shape[0]] = piece[...]
            at += piece.shape[0]


def together(pieces):
    count = sum(1 if x.ndim == 2 else x.shape[0] for x in pieces)
    return call(
        together_kernel, [shape((count, *pieces[0].shape[-2:]), pieces[0].dtype)], pieces, "together"
    )[0]


def router_of(rows, router_ref, routes, experts):
    z = nt(rows, router_ref[...])
    lane = lane_of(z.shape)
    z = jnp.where(lane < experts, z, MASKED)
    e = jnp.exp(z - jnp.max(z, axis=-1, keepdims=True))
    probs = e / jnp.sum(e, axis=-1, keepdims=True)
    chosen = chosen_of(lane, routes)
    zc = jnp.where(chosen, z, MASKED)
    ec = jnp.where(chosen, jnp.exp(zc - jnp.max(zc, axis=-1, keepdims=True)), 0.0)
    return probs, ec / jnp.sum(ec, axis=-1, keepdims=True)


def chosen_of(lane, routes):
    place, named = lane.astype(F32), routes.astype(F32)
    chosen = place == named[:, 0:1]
    for k in range(1, TOP):
        chosen = chosen | (place == named[:, k : k + 1])
    return chosen


def counts_kernel(*refs):
    pieces, out = refs[:-1], refs[-1]
    total = 0.0
    for piece in pieces:
        width = piece.shape[-1] - LANES
        blocks = [piece[:, width:]] if len(piece.shape) == 2 else [
            piece[i, :, width:] for i in range(piece.shape[0])
        ]
        for routes in blocks:
            named = chosen_of(lane_of(routes.shape), routes).astype(F32)
            total = total + jnp.sum(named, axis=0, keepdims=True)
    out[...] = total


def weights_kernel(wg_ref, wu_ref, out_ref):
    hidden = wg_ref.shape[2]
    out_ref[:, :hidden] = wg_ref[0]
    out_ref[:, hidden:] = wu_ref[0]


def gate_up_weights(w_gate, w_up):
    local, width, hidden = w_gate.shape
    block = pl.BlockSpec((1, width, hidden), lambda e: (e, 0, 0))
    return pl.pallas_call(
        weights_kernel,
        grid=(local,),
        in_specs=[block, block],
        out_specs=pl.BlockSpec((width, 2 * hidden), lambda e: (0, e)),
        out_shape=shape((width, 2 * hidden * local), BF),
        compiler_params=pltpu.CompilerParams(vmem_limit_bytes=30 * MIB),
        cost_estimate=pl.CostEstimate(flops=int(100.0*(0)), bytes_accessed=4 * w_gate.size * 2, transcendentals=0),
        name="gate_up_weights",
    )(w_gate, w_up)


def experts_kernel(experts, base_ref, x_ref, own_ref, far_ref, router_ref, wcat, wd_ref, *refs):
    cot_ref, dgu_ref, hg_ref, *ds, m_ref = refs
    hidden = LANES
    pair = 2 * hidden
    rows, width = cot_ref.shape
    x = x_ref[...].reshape(rows, width)
    if far_ref is None:
        routes = own_ref[:, width:]
        cot_ref[...] = own_ref[:, :width]
    else:
        pieces = [own_ref[...]] + [far_ref[i] for i in range(far_ref.shape[0])]
        routes = jnp.concatenate([piece[:, width:] for piece in pieces], axis=0)
        cot_ref[...] = jnp.concatenate([piece[:, :width] for piece in pieces], axis=0)
    _, gates = router_of(x, router_ref, routes, experts)
    lane = lane_of(gates.shape)
    dots = jnp.zeros(gates.shape, F32)
    for e in range(hg_ref.shape[1] // hidden):
        mine = lane == base_ref[0] + e
        g = jnp.sum(jnp.where(mine, gates, 0.0), axis=-1, keepdims=True)
        both = nn(x, wcat[:, e * pair : (e + 1) * pair])
        v = nt(cot_ref[...], wd_ref[e * hidden : (e + 1) * hidden, :])
        gate, up = both[:, :hidden], both[:, hidden:]
        sig = 1.0 / (1.0 + jnp.exp(-gate))
        act = gate * sig
        hid = act * up
        dots = jnp.where(mine, jnp.sum(hid * v, axis=-1, keepdims=True), dots)
        gv = g * v
        hg_ref[:, e * hidden : (e + 1) * hidden] = (g * hid).astype(BF)
        d_gate = gv * up * sig * (1.0 + gate * (1.0 - sig))
        dgu_ref[:, e * pair : e * pair + hidden] = d_gate.astype(BF)
        dgu_ref[:, e * pair + hidden : (e + 1) * pair] = (gv * act).astype(BF)

    def put(outs, columns, value):
        at = 0
        for out in outs:
            part = value.astype(out.dtype)
            if len(out.shape) == 2:
                out[:, columns] = part[at : at + out.shape[0]]
                at += out.shape[0]
            else:
                step = out.shape[1]
                for i in range(out.shape[0]):
                    out[i, :, columns] = part[i * step : (i + 1) * step]

    put(ds, slice(width, width + LANES), dots)
    step = 256
    for at in range(0, width, step):
        put(ds, slice(at, at + step), nt(dgu_ref[...], wcat[at : at + step, :]))
    put([m_ref], slice(0, width), nn(hg_ref[...], wd_ref[...]))


def run_experts(experts, base, x, own, far, router, wcat, down_flat, kind, apart=False):
    count, rows, width = x.shape
    inner = down_flat.shape[0]
    wide = width + LANES
    total = count * rows
    few = count <= FEW
    step = total if few else 256
    resident = pl.BlockSpec(memory_space=pltpu.VMEM)
    per = lambda w: resident if few else pl.BlockSpec((step, w), lambda i: (i, 0))
    kernel = functools.partial(experts_kernel, experts)
    if few:
        data, dims = [x, own, far], lambda w: (count, rows, w)
    else:
        joined = jnp.concatenate([own[None], far], axis=0)
        data, dims = [x.reshape(total, width), joined.reshape(total, wide)], lambda w: (total, w)
        whole_kernel = kernel
        kernel = lambda b, x, c, *refs: whole_kernel(b, x, c, None, *refs)
    if few and apart:
        d_shapes = [shape((rows, wide), BF if i else F32) for i in range(count)]
    else:
        d_shapes = [shape(dims(wide), kind)]
    cot, dgu, hid, *d, m = pl.pallas_call(
        kernel,
        grid=(total // step,),
        in_specs=[pl.BlockSpec(memory_space=pltpu.SMEM)]
        + [per(z.shape[-1]) for z in data]
        + [resident] * 3,
        out_specs=[per(width), per(2 * inner), per(inner)]
        + [per(wide)] * len(d_shapes)
        + [per(width)],
        out_shape=[
            shape((total, width), BF),
            shape((total, 2 * inner), BF),
            shape((total, inner), BF),
            *d_shapes,
            shape(dims(width), BF),
        ],
        compiler_params=pltpu.CompilerParams(vmem_limit_bytes=30 * MIB),
        cost_estimate=pl.CostEstimate(flops=int(100.0*(total * width * inner // 8)), bytes_accessed=0, transcendentals=0),
        name="experts",
    )(base, *data, router, wcat, down_flat)
    if not few:
        d = list(d[0].reshape(count, rows, wide)) if apart else [d[0].reshape(count, rows, wide)]
    return cot, dgu, hid, d if apart else d[0], m.reshape(count, rows, width)


def ordered_rows_kernel(me_ref, *refs):
    pieces, out = refs[:-1], refs[-1]
    for r, piece in enumerate(pieces):
        for i in range(piece.shape[0]):
            out[me_ref[1] ^ r, me_ref[0] ^ i] = piece[i]


def ordered_rows(me, pieces):
    count, *dims = pieces[0].shape
    if count <= FEW:
        out = [shape((len(pieces), count, *dims), pieces[0].dtype)]
        return call(ordered_rows_kernel, out, (me, *pieces), "ordered_rows", "s")[0]
    rows = jnp.take(jnp.stack(pieces), jnp.arange(len(pieces)) ^ me[1], axis=0)
    return jnp.take(rows, jnp.arange(count) ^ me[0], axis=1)


def split_sum_kernel(count, near, *refs):
    ins, outs = refs[:count], refs[count:]
    for s in range(ins[0].shape[0]):
        total = ins[0][s].astype(F32)
        for x in ins[1:]:
            total = total + x[s].astype(F32)
        outs[s][...] = total.astype(outs[s].dtype)


def split_sum(arrays, name):
    count, *dims = arrays[0].shape
    outs = [shape(dims, F32)] + [shape(dims, BF)] * (count - 1)
    return call(functools.partial(split_sum_kernel, len(arrays), True), outs, arrays, name)


def add_kernel(*refs):
    pieces, out = refs[:-1], refs[-1]
    total = pieces[0][...].astype(F32)
    for piece in pieces[1:]:
        total = total + piece[...].astype(F32)
    out[...] = total.astype(out.dtype)


def added(pieces, kind, name):
    return call(add_kernel, [shape(pieces[0].shape, kind)], pieces, name)[0]


def grads_kernel(*refs):
    ns, dgus, hs, cs = (refs[4 * i : 4 * i + 4] for i in range(4))
    out_ref = refs[16]
    hidden, width = hs[0].shape[1], ns[0].shape[1]
    both, down = 0.0, 0.0
    for n, dgu, h, c in zip(ns, dgus, hs, cs):
        both = both + tn(n[...], dgu[...])
        down = down + tn(h[...], c[...])
    out_ref[0, :width, :] = both[:, :hidden].astype(BF)
    out_ref[0, width : 2 * width, :] = both[:, hidden:].astype(BF)
    for at in range(0, width, hidden):
        out_ref[0, 2 * width + at : 2 * width + at + hidden, :] = down[:, at : at + hidden].astype(BF)


def run_grads(n, dgu, h, c, local, hidden):
    width = n[0].shape[-1]
    flat = lambda xs: [x.reshape(-1, x.shape[-1]) for x in xs]
    n, c = flat(n), flat(c)
    whole = lambda xs: [pl.BlockSpec(x.shape, lambda e: (0, 0)) for x in xs]
    cols = lambda xs, w: [pl.BlockSpec((x.shape[0], w), lambda e: (0, e)) for x in xs]
    few = n[0].shape[0] <= 512
    return pl.pallas_call(
        grads_kernel,
        grid=(local,),
        in_specs=whole(n) + cols(dgu, 2 * hidden) + cols(h, hidden) + whole(c),
        out_specs=pl.BlockSpec((1, 3 * width, hidden), lambda e: (e, 0, 0)),
        out_shape=shape((local, 3 * width, hidden), BF),
        compiler_params=pltpu.CompilerParams(vmem_limit_bytes=(32 if few else 58) * MIB),
        cost_estimate=pl.CostEstimate(flops=int(100.0*(24 * n[0].size * hidden * local)), bytes_accessed=0, transcendentals=0),
        name="expert_grads",
    )(*n, *dgu, *h, *c)


def both_copies_kernel(mine_ref, other_ref, gate_ref, up_ref, down_ref):
    width, hidden = gate_ref.shape[1:]

    def total(at, count):
        rows = pl.ds(at, count)
        return mine_ref[0, rows, :].astype(F32) + other_ref[0, rows, :].astype(F32)

    gate_ref[0] = total(0, width)
    up_ref[0] = total(width, width)
    for at in range(0, width, hidden):
        down_ref[0, :, at : at + hidden] = total(2 * width + at, hidden)


def both_copies(mine, other):
    local, rows, hidden = mine.shape
    width = rows // 3
    block = lambda *dims: pl.BlockSpec((1, *dims), lambda e: (e, 0, 0))
    return pl.pallas_call(
        both_copies_kernel,
        grid=(local,),
        in_specs=[block(rows, hidden)] * 2,
        out_specs=[block(width, hidden), block(width, hidden), block(hidden, width)],
        out_shape=[
            shape((local, width, hidden), F32),
            shape((local, width, hidden), F32),
            shape((local, hidden, width), F32),
        ],
        compiler_params=pltpu.CompilerParams(vmem_limit_bytes=58 * MIB),
        cost_estimate=pl.CostEstimate(flops=int(100.0*(0)), bytes_accessed=8 * mine.size, transcendentals=0),
        name="both_copies",
    )(mine, other)


def norm_back_kernel(experts, count, h_ref, n_ref, gain_ref, router_ref, bal_ref, cot_ref, *refs):
    sums, (wide_ref, dh_ref, small_ref) = refs[:count], refs[count:]
    near = sums[0][...].astype(F32)
    for other in sums[1:]:
        near = near + other[...].astype(F32)
    rows, width = h_ref.shape
    dots = near[:, width:]
    probs, gates = router_of(n_ref[...], router_ref, cot_ref[:, width:], experts)
    bal = bal_ref[...]
    d_chosen = gates * (dots - jnp.sum(gates * dots, axis=-1, keepdims=True))
    dz = probs * (bal - jnp.sum(probs * bal, axis=-1, keepdims=True)) + d_chosen
    dz = dz.astype(BF)
    wide_ref[:, width:] = dz
    dn = near[:, :width] + nn(dz, router_ref[...])
    h = h_ref[...]
    inv = lax.rsqrt(jnp.mean(h * h, axis=-1, keepdims=True) + EPS)
    u = gain_ref[...] * dn
    dy = cot_ref[:, :width].astype(F32)
    dh = dy + inv * u - h * (inv * inv * inv * jnp.mean(u * h, axis=-1, keepdims=True))
    dh_ref[...] = dh
    wide_ref[:, :width] = dh.astype(BF)
    small_ref[...] = jnp.zeros(small_ref.shape, F32)
    small_ref[1:2, :] = jnp.sum(dn * h * inv, axis=0, keepdims=True)
    small_ref[2:3, : probs.shape[1]] = jnp.sum(probs, axis=0, keepdims=True)


def attend_back_kernel(
    me_ref, w0, w1, w2, w3, x_ref, q_ref, k_ref, v_ref, lse_ref, wq_ref, wk_ref, wv_ref, wo_ref, cos_ref, sin_ref,
    small_in, wide_ref, dq_ref, small_ref, p0, p1, p2, p3, do_ref, whole
):
    rows = w0.shape[0]
    width = x_ref.shape[1]
    for r, piece in enumerate((w0, w1, w2, w3)):
        start = pl.multiple_of((me_ref[0] ^ r) * rows, rows)
        wide_ref[pl.ds(start, rows), :] = piece[...]
    do_ref[...] = nt(wide_ref[:, :width], wo_ref[...]).astype(BF)
    cosine, sine = cos_ref[...], sin_ref[...]
    scale = HD ** (-0.5)
    heads, keys_wide = q_ref.shape[1], k_ref.shape[1]
    dk_tiles = [0.0] * (keys_wide // LANES)
    dv_tiles = [0.0] * (keys_wide // LANES)

    def back(tile):
        return (tile * cosine - halves_swapped(tile) * sine).astype(BF)

    for head in range(heads // LANES):
        at = head // 2 * LANES
        side = head % 2
        keys = low_high(k_ref[:, at : at + LANES], side)
        values = low_high(v_ref[:, at : at + LANES], side)
        pair = q_ref[:, head * LANES : (head + 1) * LANES]
        grad = do_ref[:, head * LANES : (head + 1) * LANES]
        dq = 0.0
        dk, dv = [], []
        for g in range(2):
            s = nt(pair, keys[g]) * scale
            lse = lse_ref[:, 2 * head + g : 2 * head + g + 1]
            p = jnp.where(causal(s), jnp.exp(s - lse), 0.0)
            dp = nt(grad, values[g])
            ds = (p * (dp - jnp.sum(p * dp, axis=-1, keepdims=True))).astype(BF)
            dq = dq + nn(ds, keys[g])
            dk.append(tn(ds, pair))
            dv.append(tn(p.astype(BF), grad))
        dq_ref[:, head * LANES : (head + 1) * LANES] = back(dq * scale)
        mine = lane_of(dk[0].shape) < HD
        if side == 0:
            dk_sum = jnp.where(mine, dk[0] + pltpu.roll(dk[1], HD, 1), 0.0)
            dv_sum = jnp.where(mine, dv[0] + pltpu.roll(dv[1], HD, 1), 0.0)
        else:
            dk_sum = jnp.where(mine, 0.0, pltpu.roll(dk[0], HD, 1) + dk[1])
            dv_sum = jnp.where(mine, 0.0, pltpu.roll(dv[0], HD, 1) + dv[1])
        dk_tiles[head // 2] = dk_tiles[head // 2] + dk_sum
        dv_tiles[head // 2] = dv_tiles[head // 2] + dv_sum
    for i, tile in enumerate(dk_tiles):
        at = heads + i * LANES
        dq_ref[:, at : at + LANES] = back(tile * scale)
    for i, tile in enumerate(dv_tiles):
        at = heads + keys_wide + i * LANES
        dq_ref[:, at : at + LANES] = tile.astype(BF)
    dn = nt(dq_ref[:, :heads], wq_ref[...])
    dn = dn + nt(dq_ref[:, heads : heads + keys_wide], wk_ref[...])
    whole[...] = dn + nt(dq_ref[:, heads + keys_wide :], wv_ref[...])
    x = x_ref[...].astype(F32)
    inv = lax.rsqrt(jnp.mean(x * x, axis=-1, keepdims=True) + EPS)
    small_ref[...] = small_in[...]
    small_ref[0:1, :] = jnp.sum(whole[...] * x * inv, axis=0, keepdims=True)
    for r, part in enumerate((p0, p1, p2, p3)):
        start = pl.multiple_of((me_ref[0] ^ r) * rows, rows)
        part[...] = whole[pl.ds(start, rows), :].astype(part.dtype)


def dense_kernel(me_ref, a0, a1, a2, a3, wide_ref, o_ref, n_ref, dq_ref, kept_ref, sent_ref, two_ref, whole):
    rows, width = a0.shape[1:]
    for r, piece in enumerate((a0, a1, a2, a3)):
        start = pl.multiple_of((me_ref[1] ^ r) * rows, rows)
        two_ref[pl.ds(start, rows), :] = piece[0]
    columns, heads = dq_ref.shape[1], o_ref.shape[1]
    whole[:, :columns] = tn(n_ref[...], dq_ref[...])
    whole[:, columns : columns + heads] = tn(wide_ref[:, :width], o_ref[...])
    whole[:, columns + heads :] = tn(two_ref[...], wide_ref[:, width:])
    half = kept_ref.shape[0]
    kept_ref[...] = whole[pl.ds(pl.multiple_of(me_ref[0] * half, half), half), :]
    sent_ref[...] = whole[pl.ds(pl.multiple_of((1 - me_ref[0]) * half, half), half), :].astype(BF)


def input_grad_kernel(x_ref, gain_ref, dh_ref, *refs):
    parts, ig_ref = refs[:-1], refs[-1]
    x = x_ref[...].astype(F32)
    inv = lax.rsqrt(jnp.mean(x * x, axis=-1, keepdims=True) + EPS)
    dn = parts[0][...].astype(F32)
    for part in parts[1:]:
        dn = dn + part[...].astype(F32)
    u = gain_ref[...] * dn
    ig = dh_ref[...] + inv * u - x * (inv * inv * inv * jnp.mean(u * x, axis=-1, keepdims=True))
    ig_ref[...] = ig.astype(BF)


def out_kernel(h_ref, moe_ref, small_ref, out_ref):
    rows = h_ref.shape[0]
    out_ref[:rows, :] = (h_ref[...] + moe_ref[...].astype(F32)).astype(BF)
    small = small_ref[...]
    high = small.astype(BF).astype(F32)
    out_ref[rows:, :] = jnp.concatenate([high, small - high], axis=0).astype(BF)


def natural_kernel(me_ref, *refs):
    pieces, out = refs[:-1], refs[-1]
    rows = pieces[0].shape[0]
    for r, piece in enumerate(pieces):
        start = pl.multiple_of((me_ref[0] ^ r) * rows, rows)
        out[pl.ds(start, rows), :] = piece[...].astype(out.dtype)


def out_whole_kernel(me_ref, *refs):
    pieces, (out_ref, small_ref, held) = refs[:-3], refs[-3:]
    rows = pieces[0].shape[0] - 16
    for r, piece in enumerate(pieces):
        start = pl.multiple_of((me_ref[0] ^ r) * rows, rows)
        out_ref[pl.ds(start, rows), :] = piece[:rows, :]
        both = piece[rows:, :].astype(F32)
        held[me_ref[0] ^ r] = both[:8] + both[8:]
    total = held[0]
    for i in range(1, len(pieces)):
        total = total + held[i]
    small_ref[...] = total


def ordered_sum_kernel(me_ref, *refs):
    pieces, out, held = refs[:-2], refs[-2], refs[-1]
    for r, piece in enumerate(pieces):
        held[me_ref[0] ^ r] = piece[...]
    total = held[0]
    for i in range(1, len(pieces)):
        total = total + held[i]
    out[...] = total


def ordered_sum(me, pieces):
    return call(
        ordered_sum_kernel,
        [shape(pieces[0].shape, F32)],
        (me, *pieces),
        "ordered_sum",
        "s",
        scratch=[pltpu.VMEM((len(pieces), *pieces[0].shape), F32)],
    )[0]


def kept_and_dealt_kernel(me_ref, kept_ref, got_ref, *outs):
    rows = outs[0].shape[0]
    for r, out in enumerate(outs):
        start = pl.multiple_of((me_ref[0] ^ r) * rows, rows)
        at = pl.ds(start, rows)
        out[...] = (kept_ref[at, :] + got_ref[at, :].astype(F32)).astype(out.dtype)


def dense_sum_kernel(mine_ref, *refs):
    others, (q_ref, k_ref, v_ref, o_ref, r_ref) = refs[:-5], refs[-5:]
    total = mine_ref[...]
    for other in others:
        total = total + other[...].astype(F32)
    at = 0
    for out in (q_ref, k_ref, v_ref):
        out[...] = total[:, at : at + out.shape[1]]
        at += out.shape[1]
    o_ref[...] = total[:, at : at + o_ref.shape[0]].T
    at += o_ref.shape[0]
    r_ref[...] = total[:, at : at + r_ref.shape[1]]


def on_device(
    tokens,
    routes,
    gain_first,
    w_query,
    w_key,
    w_value,
    w_output,
    gain_second,
    w_router,
    w_gate,
    w_up,
    w_down,
    cotangent,
):
    seq_len, width = tokens.shape
    experts = w_router.shape[1]
    local, _, hidden = w_gate.shape
    tensor_size = lax.axis_size("tensor")
    expert_size = lax.axis_size("expert")
    dp_size = lax.axis_size("dp")
    token_count = seq_len * dp_size * expert_size
    rows = seq_len // tensor_size
    wide_width = width + LANES
    last = tensor_size - 1
    around = range(1, tensor_size)
    t_me, e_me, d_me = lax.axis_index("tensor"), lax.axis_index("expert"), lax.axis_index("dp")
    t_at = t_me.astype(jnp.int32).reshape(1)
    e_at = e_me.astype(jnp.int32).reshape(1)
    base = (e_me * local).astype(jnp.int32).reshape(1)
    d_at = jnp.stack([d_me, t_me]).astype(jnp.int32)
    me = jnp.stack([e_me, t_me]).astype(jnp.int32)
    cosine, sine = rope_tables(seq_len)
    gain_one, gain_two = gain_first[None], gain_second[None]
    down_flat = w_down.reshape(local * hidden, width)

    *cot_near, router = call(
        pieces_kernel,
        [shape((rows, wide_width), BF)] * tensor_size + [shape((LANES, width), BF)],
        (t_at, cotangent, routes.T, w_router.T),
        "pieces",
        "sbbb",
        scratch=[pltpu.VMEM((seq_len, LANES), F32)],
        limit=58,
    )
    cot_got = spread(cot_near[0], "expert")
    cot_got[0], tokens = tied(cot_got[0], tokens)

    heads, keys_wide = w_query.shape[1], w_key.shape[1]
    n_one, q, k, v, o, lse, xq, *rest = call(
        attend_kernel,
        [
            shape((seq_len, width), BF),
            shape((seq_len, heads), BF),
            shape((seq_len, keys_wide), BF),
            shape((seq_len, keys_wide), BF),
            shape((seq_len, heads), BF),
            shape((seq_len, LANES), F32),
            shape((rows, width), BF),
        ]
        + [shape((rows, width), F32)]
        + [shape((rows, width), BF)] * last,
        (t_at, tokens, gain_one, w_query, w_key, w_value, w_output, cosine, sine),
        "attend",
        "s" + "b" * 8,
        "bbbbbbv",
        scratch=[pltpu.VMEM((seq_len, width), F32)],
        limit=30,
        flops=2 * seq_len * width * 4 * heads,
    )
    parts = rest
    got = [swap(parts[r], "tensor", r) for r in around]
    h, n_two = call(
        norm_two_kernel,
        [shape((rows, width), F32), shape((rows, width), BF)],
        (xq, gain_two, parts[0], *got),
        "norm_two",
        "vb",
        "vv",
    )

    n_two, cot_got = tied(n_two, cot_got)
    cot_far = together(cot_got)
    wcat = gate_up_weights(w_gate, w_up)
    two_got = spread(n_two, "expert")
    two_got[0], cot_late = tied(two_got[0], cot_far)
    cot_far = [cot_far] + [swap(cot_far, "tensor", r) for r in range(1, last)]
    cot_far.append(swap(cot_late, "tensor", last))

    first = together([n_two, *two_got])
    twos = [first] + [swap(first, "tensor", r) for r in range(1, last)]
    _, late = tied(cot_far[:last], first)
    twos.append(swap(late, "tensor", last))

    run = functools.partial(
        run_experts, experts, base, router=router, wcat=wcat, down_flat=down_flat
    )
    counts = call(counts_kernel, [shape((1, LANES), F32)], (*cot_near, *cot_far), "counts")[0]
    counts = counts + swap(counts, "dp", 1)
    balance = experts * (counts / (token_count * TOP)) / token_count
    made = [run(twos[0], cot_near[0], cot_far[0], kind=F32)]
    got = []
    for r in around:
        made[-1], (two, cot) = tied(made[-1], (twos[r], cot_far[r]))
        if r == last:
            balance, two = tied(balance, two)
        made.append(run(two, cot_near[r], cot, kind=BF, apart=r == last))
        if r < last:
            got.append(swap(made[-1][3], "tensor", r))
    cots, dgus, hids, ds, moes = zip(*made)
    near_last, *far_last = ds[last]
    from_last = deal(far_last, "expert")
    grads = run_grads(twos, dgus, hids, cots, local, hidden)
    grads, (got, from_last) = tied(grads, (got, from_last))
    near, *across = split_sum([ds[0], *got], "dn_sum")
    across, moes = tied(across, moes)
    moe = lax.psum_scatter(ordered_rows(me, moes), "tensor", scatter_dimension=0, tiled=False)
    through = added([near_last, *from_last], BF, "through")
    near_sums = [near, swap(through, "tensor", last), *deal(across, "expert")]

    wide, dh, small = call(
        functools.partial(norm_back_kernel, experts, len(near_sums)),
        [shape((rows, wide_width), BF), shape((rows, width), F32), shape((8, width), F32)],
        (h, n_two, gain_two, router, balance, cot_near[0], *near_sums),
        "norm_back",
        "v",
        "vvv",
    )
    wides = [wide] + [swap(wide, "tensor", r) for r in around]
    grads_got = swap(grads, "dp", 1)
    (moe, grads_got), wides = tied((moe, grads_got), wides)
    moe = lax.psum_scatter(moe, "expert", scatter_dimension=0, tiled=False)

    wide_all, dqkv, small, *back_parts = call(
        attend_back_kernel,
        [
            shape((seq_len, wide_width), BF),
            shape((seq_len, heads + 2 * keys_wide), BF),
            shape((8, width), F32),
            shape((rows, width), F32),
        ]
        + [shape((rows, width), BF)] * last,
        (t_at, *wides, tokens, q, k, v, lse, w_query, w_key, w_value, w_output, cosine, sine, small),
        "attend_back",
        "s" + "v" * tensor_size + "b" * 11,
        "bb",
        limit=58,
        scratch=[
            pltpu.VMEM((seq_len, heads), BF),
            pltpu.VMEM((seq_len, width), F32),
        ],
        flops=2 * seq_len * width * 4 * heads,
    )
    part_sums = [back_parts[0]] + [swap(back_parts[r], "tensor", r) for r in around]
    half = width // dp_size
    chunk = half // expert_size

    columns = heads + 2 * keys_wide
    all_columns = columns + heads + LANES
    own_block = pl.BlockSpec((1, rows, width), lambda i: (0, 0, 0))
    kept, sent = call(
        dense_kernel,
        [shape((half, all_columns), F32), shape((half, all_columns), BF)],
        (d_at, *twos, wide_all, o, n_one, dqkv),
        "dense",
        ["s"] + [own_block] * tensor_size + ["b"] * 4,
        "vv",
        limit=54,
        scratch=[
            pltpu.VMEM((seq_len, width), BF),
            pltpu.VMEM((width, all_columns), F32),
        ],
        flops=1,
    )
    mine, *others = call(
        kept_and_dealt_kernel,
        [shape((chunk, all_columns), F32)] + [shape((chunk, all_columns), BF)] * (expert_size - 1),
        (e_at, kept, swap(sent, "dp", 1)),
        "dense_dealt",
        "s",
    )
    (mine, others), part_sums = tied((mine, others), part_sums)
    ig = call(
        input_grad_kernel, [shape((rows, width), BF)], (xq, gain_one, dh, *part_sums), "input_grad", "vb"
    )[0]
    igs = [ig] + [swap(ig, "tensor", r) for r in around]
    expert_grads = both_copies(grads, grads_got)
    expert_grads, igs = tied(expert_grads, igs)
    input_grad = call(
        natural_kernel, [shape((seq_len, width), F32)], (t_at, *igs), "input_grad_whole", "s", "b"
    )[0]
    small = small + swap(small, "dp", 1)
    small = ordered_sum(e_at, [small, *spread(small, "expert")])
    out_piece = call(out_kernel, [shape((rows + 16, width), BF)], (h, moe, small), "out_piece")[0]
    output, small = call(
        out_whole_kernel,
        [shape((seq_len, width), BF), shape((8, width), F32)],
        (t_at, out_piece, *[swap(out_piece, "tensor", r) for r in around]),
        "output",
        "s",
        "bv",
        scratch=[pltpu.VMEM((tensor_size, 8, width), F32)],
    )
    g_query, g_key, g_value, g_out, g_router = call(
        dense_sum_kernel,
        [
            shape((chunk, heads), F32),
            shape((chunk, keys_wide), F32),
            shape((chunk, keys_wide), F32),
            shape((heads, chunk), F32),
            shape((chunk, LANES), F32),
        ],
        (mine, *deal(others, "expert")),
        "dense_sum",
        "",
        "bbbbb",
    )

    at = (d_me * expert_size + e_me) * chunk
    loss_value = (experts * balance * small[2:3, :LANES])[0, :experts]
    return (
        output,
        loss_value,
        input_grad,
        lax.dynamic_slice(small, (0, at), (1, chunk))[0],
        g_query,
        g_key,
        g_value,
        g_out,
        lax.dynamic_slice(small, (1, at), (1, chunk))[0],
        g_router[:, :experts],
        *expert_grads,
    )


def solution(mesh):
    rows = ("dp", "expert")
    placed = (
        P(rows, None),
        P(rows, None),
        P(),
        P(None, "tensor"),
        P(None, "tensor"),
        P(None, "tensor"),
        P("tensor", None),
        P(),
        P(),
        P("expert", None, "tensor"),
        P("expert", None, "tensor"),
        P("expert", "tensor", None),
        P(rows, None),
    )
    return jax.shard_map(
        on_device,
        mesh=mesh,
        in_specs=placed,
        out_specs=(
            P(rows, None),
            P(),
            P(rows, None),
            P(rows),
            P(rows, "tensor"),
            P(rows, "tensor"),
            P(rows, "tensor"),
            P("tensor", rows),
            P(rows),
            P(rows, None),
            P("expert", None, "tensor"),
            P("expert", None, "tensor"),
            P("expert", "tensor", None),
        ),
        check_vma=False,
    )
```

```python
import functools

import jax
import jax.numpy as jnp
import numpy as np
from jax import lax
from jax.experimental import pallas as pl
from jax.experimental.pallas import tpu as pltpu
from jax.sharding import PartitionSpec as P

HD = 64
TOP = 8
EPS = 1e-06
ROPE_BASE = 10000.0
MASKED = -1e30
BF = jnp.bfloat16
F32 = jnp.float32
FEW = 8
LANES = 128
MIB = 1 << 20


def dot(a, b, dims):
    return lax.dot_general(a, b, (dims, ((), ())), preferred_element_type=F32)


def nn(a, b):
    return dot(a, b, ((1,), (0,)))


def nt(a, b):
    return dot(a, b, ((1,), (1,)))


def tn(a, b):
    return dot(a, b, ((0,), (0,)))


def swap(x, axis, distance):
    size = lax.axis_size(axis)
    return lax.ppermute(x, axis, [(i, i ^ distance) for i in range(size)])


def spread(x, axis):
    size = lax.axis_size(axis)
    if size <= FEW:
        return [swap(x, axis, r) for r in range(1, size)]
    whole = lax.all_gather(x, axis)
    order = jnp.arange(1, size) ^ lax.axis_index(axis)
    return list(jnp.take(whole, order, axis=0))


def deal(parts, axis):
    size = lax.axis_size(axis)
    if size <= FEW:
        return [swap(part, axis, r + 1) for r, part in enumerate(parts)]
    order = jnp.arange(size) ^ lax.axis_index(axis)
    whole = jnp.take(jnp.stack([parts[0], *parts]), order, axis=0)
    back = lax.all_to_all(whole, axis, 0, 0, tiled=True)
    return list(jnp.take(back, order, axis=0)[1:])


def rope_tables(seq_len):
    half = HD // 2
    frequency = ROPE_BASE ** (-(np.arange(half, dtype=np.float32) * 2.0) / HD)
    angles = np.arange(seq_len, dtype=np.float32)[:, None] * frequency[None, :].astype(np.float32)
    cosine, sine = np.cos(angles), np.sin(angles)
    heads = LANES // HD
    return (
        np.tile(cosine, (1, 2 * heads)).astype(np.float32),
        np.tile(np.concatenate([-sine, sine], axis=1), (1, heads)).astype(np.float32),
    )


def lane_of(shape):
    return lax.broadcasted_iota(jnp.int32, shape, 1)


def halves_swapped(x):
    first = lane_of(x.shape) % HD < HD // 2
    half = HD // 2
    return jnp.where(first, pltpu.roll(x, LANES - half, 1), pltpu.roll(x, half, 1))


def low_high(x, head):
    other = pltpu.roll(x.astype(F32), HD, 1).astype(x.dtype)
    low = lane_of(x.shape) < HD
    zero = jnp.zeros_like(x)
    at_low, at_high = (x, other) if head == 0 else (other, x)
    return jnp.where(low, at_low, zero), jnp.where(low, zero, at_high)


def causal(scores):
    rows = lax.broadcasted_iota(jnp.int32, scores.shape, 0)
    return lane_of(scores.shape) <= rows


def shape(dims, kind):
    return jax.ShapeDtypeStruct(dims, kind)


def whole_block(dims):
    return pl.BlockSpec(dims, lambda i: (0,) * len(dims))


def call(kernel, outs, operands, name, places="", out_places="", scratch=(), limit=40, flops=0):
    kinds = {"s": pltpu.SMEM, "v": pltpu.VMEM}

    def spec(place, x):
        if not isinstance(place, str):
            return place
        if place == "b":
            return whole_block(x.shape)
        return pl.BlockSpec(memory_space=kinds[place])

    places = [*places] + ["v"] * (len(operands) - len(places))
    out_places = [*out_places] + ["v"] * (len(outs) - len(out_places))
    return pl.pallas_call(
        kernel,
        grid=(1,),
        out_shape=outs,
        in_specs=[spec(p, x) for p, x in zip(places, operands)],
        out_specs=[spec(p, x) for p, x in zip(out_places, outs)],
        scratch_shapes=list(scratch),
        compiler_params=pltpu.CompilerParams(vmem_limit_bytes=limit * MIB),
        cost_estimate=pl.CostEstimate(flops=int(100.0*(flops)), bytes_accessed=0, transcendentals=0),
        name=name,
    )(*operands)


def tied(first, then):
    return lax.optimization_barrier((first, then))


def pieces_kernel(me_ref, cot_ref, routes_ref, router_ref, *refs):
    cots, (router_out, held) = refs[:-2], refs[-2:]
    rows, width = cots[0].shape[0], cot_ref.shape[1]
    eye = lax.broadcasted_iota(jnp.int32, (TOP, LANES), 0) == lane_of((TOP, LANES))
    held[...] = tn(routes_ref[...].astype(F32).astype(BF), eye.astype(F32).astype(BF))
    for r, c in enumerate(cots):
        start = pl.multiple_of((me_ref[0] ^ r) * rows, rows)
        c[:, :width] = cot_ref[pl.ds(start, rows), :]
        c[:, width:] = held[pl.ds(start, rows), :].astype(BF)
    router_out[...] = jnp.zeros(router_out.shape, BF)
    router_out[: router_ref.shape[0], :] = router_ref[...]


def attend_kernel(
    me_ref, x_ref, gain_ref, wq_ref, wk_ref, wv_ref, wo_ref, cos_ref, sin_ref, *refs
):
    n_ref, q_ref, k_ref, v_ref, o_ref, lse_ref, xq_ref = refs[:7]
    parts, whole = refs[7:-1], refs[-1]
    rows, width = xq_ref.shape
    starts = [pl.multiple_of((me_ref[0] ^ r) * rows, rows) for r in range(4)]
    xq_ref[...] = x_ref[pl.ds(starts[0], rows), :]
    x = x_ref[...].astype(F32)
    inv = lax.rsqrt(jnp.mean(x * x, axis=-1, keepdims=True) + EPS)
    n = (x * inv * gain_ref[...]).astype(BF)
    n_ref[...] = n
    cosine, sine = cos_ref[...], sin_ref[...]
    q, k = nn(n, wq_ref[...]), nn(n, wk_ref[...])
    v_ref[...] = nn(n, wv_ref[...]).astype(BF)
    for at in range(0, q.shape[1], LANES):
        tile = q[:, at : at + LANES]
        q_ref[:, at : at + LANES] = (tile * cosine + halves_swapped(tile) * sine).astype(BF)
    for at in range(0, k.shape[1], LANES):
        tile = k[:, at : at + LANES]
        k_ref[:, at : at + LANES] = (tile * cosine + halves_swapped(tile) * sine).astype(BF)
    lse_all = jnp.zeros(lse_ref.shape, F32)
    for head in range(q.shape[1] // LANES):
        at = head // 2 * LANES
        keys = low_high(k_ref[:, at : at + LANES], head % 2)
        values = low_high(v_ref[:, at : at + LANES], head % 2)
        pair = q_ref[:, head * LANES : (head + 1) * LANES]
        mixed = 0.0
        for g in range(2):
            s = nt(pair, keys[g]) * HD ** (-0.5)
            s = jnp.where(causal(s), s, MASKED)
            peak = jnp.max(s, axis=-1, keepdims=True)
            e = jnp.exp(s - peak)
            total = jnp.sum(e, axis=-1, keepdims=True)
            mixed = mixed + nn((e / total).astype(BF), values[g])
            lse = peak + jnp.log(total)
            lse_all = jnp.where(lane_of(lse_all.shape) == 2 * head + g, lse, lse_all)
        o_ref[:, head * LANES : (head + 1) * LANES] = mixed.astype(BF)
    lse_ref[...] = lse_all
    whole[...] = nn(o_ref[...], wo_ref[...])
    for start, part in zip(starts, parts):
        part[...] = whole[pl.ds(start, rows), :].astype(part.dtype)


def norm_two_kernel(x_ref, gain_ref, own_ref, *refs):
    others, (h_ref, n_ref) = refs[:-2], refs[-2:]
    attn = own_ref[...]
    for other in others:
        attn = attn + other[...].astype(F32)
    h = x_ref[...].astype(F32) + attn
    inv = lax.rsqrt(jnp.mean(h * h, axis=-1, keepdims=True) + EPS)
    h_ref[...] = h
    n_ref[...] = (h * inv * gain_ref[...]).astype(BF)


def together_kernel(*refs):
    pieces, out = refs[:-1], refs[-1]
    at = 0
    for piece in pieces:
        if len(piece.shape) == 2:
            out[at] = piece[...]
            at += 1
        else:
            out[at : at + piece.shape[0]] = piece[...]
            at += piece.shape[0]


def together(pieces):
    count = sum(1 if x.ndim == 2 else x.shape[0] for x in pieces)
    return call(
        together_kernel, [shape((count, *pieces[0].shape[-2:]), pieces[0].dtype)], pieces, "together"
    )[0]


def router_of(rows, router_ref, routes, experts):
    z = nt(rows, router_ref[...])
    lane = lane_of(z.shape)
    z = jnp.where(lane < experts, z, MASKED)
    e = jnp.exp(z - jnp.max(z, axis=-1, keepdims=True))
    probs = e / jnp.sum(e, axis=-1, keepdims=True)
    chosen = chosen_of(lane, routes)
    zc = jnp.where(chosen, z, MASKED)
    ec = jnp.where(chosen, jnp.exp(zc - jnp.max(zc, axis=-1, keepdims=True)), 0.0)
    return probs, ec / jnp.sum(ec, axis=-1, keepdims=True)


def chosen_of(lane, routes):
    place, named = lane.astype(F32), routes.astype(F32)
    chosen = place == named[:, 0:1]
    for k in range(1, TOP):
        chosen = chosen | (place == named[:, k : k + 1])
    return chosen


def counts_kernel(*refs):
    pieces, out = refs[:-1], refs[-1]
    total = 0.0
    for piece in pieces:
        width = piece.shape[-1] - LANES
        blocks = [piece[:, width:]] if len(piece.shape) == 2 else [
            piece[i, :, width:] for i in range(piece.shape[0])
        ]
        for routes in blocks:
            named = chosen_of(lane_of(routes.shape), routes).astype(F32)
            total = total + jnp.sum(named, axis=0, keepdims=True)
    out[...] = total


def weights_kernel(wg_ref, wu_ref, out_ref):
    hidden = wg_ref.shape[2]
    out_ref[:, :hidden] = wg_ref[0]
    out_ref[:, hidden:] = wu_ref[0]


def gate_up_weights(w_gate, w_up):
    local, width, hidden = w_gate.shape
    block = pl.BlockSpec((1, width, hidden), lambda e: (e, 0, 0))
    return pl.pallas_call(
        weights_kernel,
        grid=(local,),
        in_specs=[block, block],
        out_specs=pl.BlockSpec((width, 2 * hidden), lambda e: (0, e)),
        out_shape=shape((width, 2 * hidden * local), BF),
        compiler_params=pltpu.CompilerParams(vmem_limit_bytes=30 * MIB),
        cost_estimate=pl.CostEstimate(flops=int(100.0*(0)), bytes_accessed=4 * w_gate.size * 2, transcendentals=0),
        name="gate_up_weights",
    )(w_gate, w_up)


def experts_kernel(experts, base_ref, x_ref, own_ref, far_ref, router_ref, wcat, wd_ref, *refs):
    cot_ref, dgu_ref, hg_ref, *ds, m_ref = refs
    hidden = LANES
    pair = 2 * hidden
    rows, width = cot_ref.shape
    x = x_ref[...].reshape(rows, width)
    if far_ref is None:
        routes = own_ref[:, width:]
        cot_ref[...] = own_ref[:, :width]
    else:
        pieces = [own_ref[...]] + [far_ref[i] for i in range(far_ref.shape[0])]
        routes = jnp.concatenate([piece[:, width:] for piece in pieces], axis=0)
        cot_ref[...] = jnp.concatenate([piece[:, :width] for piece in pieces], axis=0)
    _, gates = router_of(x, router_ref, routes, experts)
    lane = lane_of(gates.shape)
    dots = jnp.zeros(gates.shape, F32)
    for e in range(hg_ref.shape[1] // hidden):
        mine = lane == base_ref[0] + e
        g = jnp.sum(jnp.where(mine, gates, 0.0), axis=-1, keepdims=True)
        both = nn(x, wcat[:, e * pair : (e + 1) * pair])
        v = nt(cot_ref[...], wd_ref[e * hidden : (e + 1) * hidden, :])
        gate, up = both[:, :hidden], both[:, hidden:]
        sig = 1.0 / (1.0 + jnp.exp(-gate))
        act = gate * sig
        hid = act * up
        dots = jnp.where(mine, jnp.sum(hid * v, axis=-1, keepdims=True), dots)
        gv = g * v
        hg_ref[:, e * hidden : (e + 1) * hidden] = (g * hid).astype(BF)
        d_gate = gv * up * sig * (1.0 + gate * (1.0 - sig))
        dgu_ref[:, e * pair : e * pair + hidden] = d_gate.astype(BF)
        dgu_ref[:, e * pair + hidden : (e + 1) * pair] = (gv * act).astype(BF)

    def put(outs, columns, value):
        at = 0
        for out in outs:
            part = value.astype(out.dtype)
            if len(out.shape) == 2:
                out[:, columns] = part[at : at + out.shape[0]]
                at += out.shape[0]
            else:
                step = out.shape[1]
                for i in range(out.shape[0]):
                    out[i, :, columns] = part[i * step : (i + 1) * step]

    put(ds, slice(width, width + LANES), dots)
    step = 256
    for at in range(0, width, step):
        put(ds, slice(at, at + step), nt(dgu_ref[...], wcat[at : at + step, :]))
    put([m_ref], slice(0, width), nn(hg_ref[...], wd_ref[...]))


def run_experts(experts, base, x, own, far, router, wcat, down_flat, kind, apart=False):
    count, rows, width = x.shape
    inner = down_flat.shape[0]
    wide = width + LANES
    total = count * rows
    few = count <= FEW
    step = total if few else 256
    resident = pl.BlockSpec(memory_space=pltpu.VMEM)
    per = lambda w: resident if few else pl.BlockSpec((step, w), lambda i: (i, 0))
    kernel = functools.partial(experts_kernel, experts)
    if few:
        data, dims = [x, own, far], lambda w: (count, rows, w)
    else:
        joined = jnp.concatenate([own[None], far], axis=0)
        data, dims = [x.reshape(total, width), joined.reshape(total, wide)], lambda w: (total, w)
        whole_kernel = kernel
        kernel = lambda b, x, c, *refs: whole_kernel(b, x, c, None, *refs)
    if few and apart:
        d_shapes = [shape((rows, wide), BF if i else F32) for i in range(count)]
    else:
        d_shapes = [shape(dims(wide), kind)]
    cot, dgu, hid, *d, m = pl.pallas_call(
        kernel,
        grid=(total // step,),
        in_specs=[pl.BlockSpec(memory_space=pltpu.SMEM)]
        + [per(z.shape[-1]) for z in data]
        + [resident] * 3,
        out_specs=[per(width), per(2 * inner), per(inner)]
        + [per(wide)] * len(d_shapes)
        + [per(width)],
        out_shape=[
            shape((total, width), BF),
            shape((total, 2 * inner), BF),
            shape((total, inner), BF),
            *d_shapes,
            shape(dims(width), kind),
        ],
        compiler_params=pltpu.CompilerParams(vmem_limit_bytes=30 * MIB),
        cost_estimate=pl.CostEstimate(flops=int(100.0*(total * width * inner // 8)), bytes_accessed=0, transcendentals=0),
        name="experts",
    )(base, *data, router, wcat, down_flat)
    if not few:
        d = list(d[0].reshape(count, rows, wide)) if apart else [d[0].reshape(count, rows, wide)]
    return cot, dgu, hid, d if apart else d[0], m.reshape(count, rows, width)


def split_sum_kernel(count, near, *refs):
    ins, outs = refs[:count], refs[count:]
    for s in range(ins[0].shape[0]):
        total = ins[0][s].astype(F32)
        for x in ins[1:]:
            total = total + x[s].astype(F32)
        outs[s][...] = total.astype(outs[s].dtype)


def split_sum(arrays, name):
    count, *dims = arrays[0].shape
    outs = [shape(dims, F32)] + [shape(dims, BF)] * (count - 1)
    return call(functools.partial(split_sum_kernel, len(arrays), True), outs, arrays, name)


def moe_sum_kernel(me_ref, *refs):
    pieces, out = refs[:-1], refs[-1]
    for s in range(out.shape[0]):
        total = pieces[0][s].astype(F32)
        for x in pieces[1:]:
            total = total + x[s].astype(F32)
        out[me_ref[0] ^ s] = total.astype(out.dtype)


def add_kernel(*refs):
    pieces, out = refs[:-1], refs[-1]
    total = pieces[0][...].astype(F32)
    for piece in pieces[1:]:
        total = total + piece[...].astype(F32)
    out[...] = total.astype(out.dtype)


def added(pieces, kind, name):
    return call(add_kernel, [shape(pieces[0].shape, kind)], pieces, name)[0]


def grads_kernel(*refs):
    ns, dgus, hs, cs = (refs[4 * i : 4 * i + 4] for i in range(4))
    out_ref = refs[16]
    hidden, width = hs[0].shape[1], ns[0].shape[1]
    both, down = 0.0, 0.0
    for n, dgu, h, c in zip(ns, dgus, hs, cs):
        both = both + tn(n[...], dgu[...])
        down = down + tn(h[...], c[...])
    out_ref[0, :width, :] = both[:, :hidden].astype(BF)
    out_ref[0, width : 2 * width, :] = both[:, hidden:].astype(BF)
    for at in range(0, width, hidden):
        out_ref[0, 2 * width + at : 2 * width + at + hidden, :] = down[:, at : at + hidden].astype(BF)


def run_grads(n, dgu, h, c, local, hidden):
    width = n[0].shape[-1]
    flat = lambda xs: [x.reshape(-1, x.shape[-1]) for x in xs]
    n, c = flat(n), flat(c)
    whole = lambda xs: [pl.BlockSpec(x.shape, lambda e: (0, 0)) for x in xs]
    cols = lambda xs, w: [pl.BlockSpec((x.shape[0], w), lambda e: (0, e)) for x in xs]
    few = n[0].shape[0] <= 512
    return pl.pallas_call(
        grads_kernel,
        grid=(local,),
        in_specs=whole(n) + cols(dgu, 2 * hidden) + cols(h, hidden) + whole(c),
        out_specs=pl.BlockSpec((1, 3 * width, hidden), lambda e: (e, 0, 0)),
        out_shape=shape((local, 3 * width, hidden), BF),
        compiler_params=pltpu.CompilerParams(vmem_limit_bytes=(32 if few else 58) * MIB),
        cost_estimate=pl.CostEstimate(flops=int(100.0*(24 * n[0].size * hidden * local)), bytes_accessed=0, transcendentals=0),
        name="expert_grads",
    )(*n, *dgu, *h, *c)


def both_copies_kernel(mine_ref, other_ref, gate_ref, up_ref, down_ref):
    width, hidden = gate_ref.shape[1:]

    def total(at, count):
        rows = pl.ds(at, count)
        return mine_ref[0, rows, :].astype(F32) + other_ref[0, rows, :].astype(F32)

    gate_ref[0] = total(0, width)
    up_ref[0] = total(width, width)
    for at in range(0, width, hidden):
        down_ref[0, :, at : at + hidden] = total(2 * width + at, hidden)


def both_copies(mine, other):
    local, rows, hidden = mine.shape
    width = rows // 3
    block = lambda *dims: pl.BlockSpec((1, *dims), lambda e: (e, 0, 0))
    return pl.pallas_call(
        both_copies_kernel,
        grid=(local,),
        in_specs=[block(rows, hidden)] * 2,
        out_specs=[block(width, hidden), block(width, hidden), block(hidden, width)],
        out_shape=[
            shape((local, width, hidden), F32),
            shape((local, width, hidden), F32),
            shape((local, hidden, width), F32),
        ],
        compiler_params=pltpu.CompilerParams(vmem_limit_bytes=58 * MIB),
        cost_estimate=pl.CostEstimate(flops=int(100.0*(0)), bytes_accessed=8 * mine.size, transcendentals=0),
        name="both_copies",
    )(mine, other)


def norm_back_kernel(experts, count, h_ref, n_ref, gain_ref, router_ref, bal_ref, cot_ref, *refs):
    sums, (wide_ref, dh_ref, small_ref) = refs[:count], refs[count:]
    near = sums[0][...].astype(F32)
    for other in sums[1:]:
        near = near + other[...].astype(F32)
    rows, width = h_ref.shape
    dots = near[:, width:]
    probs, gates = router_of(n_ref[...], router_ref, cot_ref[:, width:], experts)
    bal = bal_ref[...]
    d_chosen = gates * (dots - jnp.sum(gates * dots, axis=-1, keepdims=True))
    dz = probs * (bal - jnp.sum(probs * bal, axis=-1, keepdims=True)) + d_chosen
    dz = dz.astype(BF)
    wide_ref[:, width:] = dz
    dn = near[:, :width] + nn(dz, router_ref[...])
    h = h_ref[...]
    inv = lax.rsqrt(jnp.mean(h * h, axis=-1, keepdims=True) + EPS)
    u = gain_ref[...] * dn
    dy = cot_ref[:, :width].astype(F32)
    dh = dy + inv * u - h * (inv * inv * inv * jnp.mean(u * h, axis=-1, keepdims=True))
    dh_ref[...] = dh
    wide_ref[:, :width] = dh.astype(BF)
    small_ref[...] = jnp.zeros(small_ref.shape, F32)
    small_ref[1:2, :] = jnp.sum(dn * h * inv, axis=0, keepdims=True)
    small_ref[2:3, : probs.shape[1]] = jnp.sum(probs, axis=0, keepdims=True)


def attend_back_kernel(
    me_ref, w0, w1, w2, w3, x_ref, q_ref, k_ref, v_ref, lse_ref, wq_ref, wk_ref, wv_ref, wo_ref, cos_ref, sin_ref,
    small_in, wide_ref, dq_ref, small_ref, p0, p1, p2, p3, do_ref, whole
):
    rows = w0.shape[0]
    width = x_ref.shape[1]
    for r, piece in enumerate((w0, w1, w2, w3)):
        start = pl.multiple_of((me_ref[0] ^ r) * rows, rows)
        wide_ref[pl.ds(start, rows), :] = piece[...]
    do_ref[...] = nt(wide_ref[:, :width], wo_ref[...]).astype(BF)
    cosine, sine = cos_ref[...], sin_ref[...]
    scale = HD ** (-0.5)
    heads, keys_wide = q_ref.shape[1], k_ref.shape[1]
    dk_tiles = [0.0] * (keys_wide // LANES)
    dv_tiles = [0.0] * (keys_wide // LANES)

    def back(tile):
        return (tile * cosine - halves_swapped(tile) * sine).astype(BF)

    for head in range(heads // LANES):
        at = head // 2 * LANES
        side = head % 2
        keys = low_high(k_ref[:, at : at + LANES], side)
        values = low_high(v_ref[:, at : at + LANES], side)
        pair = q_ref[:, head * LANES : (head + 1) * LANES]
        grad = do_ref[:, head * LANES : (head + 1) * LANES]
        dq = 0.0
        dk, dv = [], []
        for g in range(2):
            s = nt(pair, keys[g]) * scale
            lse = lse_ref[:, 2 * head + g : 2 * head + g + 1]
            p = jnp.where(causal(s), jnp.exp(s - lse), 0.0)
            dp = nt(grad, values[g])
            ds = (p * (dp - jnp.sum(p * dp, axis=-1, keepdims=True))).astype(BF)
            dq = dq + nn(ds, keys[g])
            dk.append(tn(ds, pair))
            dv.append(tn(p.astype(BF), grad))
        dq_ref[:, head * LANES : (head + 1) * LANES] = back(dq * scale)
        mine = lane_of(dk[0].shape) < HD
        if side == 0:
            dk_sum = jnp.where(mine, dk[0] + pltpu.roll(dk[1], HD, 1), 0.0)
            dv_sum = jnp.where(mine, dv[0] + pltpu.roll(dv[1], HD, 1), 0.0)
        else:
            dk_sum = jnp.where(mine, 0.0, pltpu.roll(dk[0], HD, 1) + dk[1])
            dv_sum = jnp.where(mine, 0.0, pltpu.roll(dv[0], HD, 1) + dv[1])
        dk_tiles[head // 2] = dk_tiles[head // 2] + dk_sum
        dv_tiles[head // 2] = dv_tiles[head // 2] + dv_sum
    for i, tile in enumerate(dk_tiles):
        at = heads + i * LANES
        dq_ref[:, at : at + LANES] = back(tile * scale)
    for i, tile in enumerate(dv_tiles):
        at = heads + keys_wide + i * LANES
        dq_ref[:, at : at + LANES] = tile.astype(BF)
    dn = nt(dq_ref[:, :heads], wq_ref[...])
    dn = dn + nt(dq_ref[:, heads : heads + keys_wide], wk_ref[...])
    whole[...] = dn + nt(dq_ref[:, heads + keys_wide :], wv_ref[...])
    x = x_ref[...].astype(F32)
    inv = lax.rsqrt(jnp.mean(x * x, axis=-1, keepdims=True) + EPS)
    small_ref[...] = small_in[...]
    small_ref[0:1, :] = jnp.sum(whole[...] * x * inv, axis=0, keepdims=True)
    for r, part in enumerate((p0, p1, p2, p3)):
        start = pl.multiple_of((me_ref[0] ^ r) * rows, rows)
        part[...] = whole[pl.ds(start, rows), :].astype(part.dtype)


def dense_kernel(me_ref, a0, a1, a2, a3, wide_ref, o_ref, n_ref, dq_ref, kept_ref, sent_ref, two_ref, whole):
    rows, width = a0.shape[1:]
    for r, piece in enumerate((a0, a1, a2, a3)):
        start = pl.multiple_of((me_ref[1] ^ r) * rows, rows)
        two_ref[pl.ds(start, rows), :] = piece[0]
    columns, heads = dq_ref.shape[1], o_ref.shape[1]
    whole[:, :columns] = tn(n_ref[...], dq_ref[...])
    whole[:, columns : columns + heads] = tn(wide_ref[:, :width], o_ref[...])
    whole[:, columns + heads :] = tn(two_ref[...], wide_ref[:, width:])
    half = kept_ref.shape[0]
    kept_ref[...] = whole[pl.ds(pl.multiple_of(me_ref[0] * half, half), half), :]
    sent_ref[...] = whole[pl.ds(pl.multiple_of((1 - me_ref[0]) * half, half), half), :].astype(BF)


def input_grad_kernel(x_ref, gain_ref, dh_ref, *refs):
    parts, ig_ref = refs[:-1], refs[-1]
    x = x_ref[...].astype(F32)
    inv = lax.rsqrt(jnp.mean(x * x, axis=-1, keepdims=True) + EPS)
    dn = parts[0][...].astype(F32)
    for part in parts[1:]:
        dn = dn + part[...].astype(F32)
    u = gain_ref[...] * dn
    ig = dh_ref[...] + inv * u - x * (inv * inv * inv * jnp.mean(u * x, axis=-1, keepdims=True))
    ig_ref[...] = ig.astype(BF)


def out_kernel(h_ref, small_ref, *refs):
    moes, out_ref = refs[:-1], refs[-1]
    rows = h_ref.shape[0]
    out = h_ref[...]
    for moe in moes:
        out = out + moe[...].astype(F32)
    out_ref[:rows, :] = out.astype(BF)
    small = small_ref[...]
    high = small.astype(BF).astype(F32)
    out_ref[rows:, :] = jnp.concatenate([high, small - high], axis=0).astype(BF)


def natural_kernel(me_ref, *refs):
    pieces, out = refs[:-1], refs[-1]
    rows = pieces[0].shape[0]
    for r, piece in enumerate(pieces):
        start = pl.multiple_of((me_ref[0] ^ r) * rows, rows)
        out[pl.ds(start, rows), :] = piece[...].astype(out.dtype)


def out_whole_kernel(me_ref, *refs):
    pieces, (out_ref, small_ref, held) = refs[:-3], refs[-3:]
    rows = pieces[0].shape[0] - 16
    for r, piece in enumerate(pieces):
        start = pl.multiple_of((me_ref[0] ^ r) * rows, rows)
        out_ref[pl.ds(start, rows), :] = piece[:rows, :]
        both = piece[rows:, :].astype(F32)
        held[me_ref[0] ^ r] = both[:8] + both[8:]
    total = held[0]
    for i in range(1, len(pieces)):
        total = total + held[i]
    small_ref[...] = total


def kept_and_dealt_kernel(me_ref, kept_ref, got_ref, small_ref, small_got_ref, *outs):
    small_out, outs = outs[-1], outs[:-1]
    small = small_ref[...] + small_got_ref[...]
    high = small[:4].astype(BF).astype(F32)
    both = jnp.concatenate([high, small[:4] - high], axis=0).astype(BF).astype(F32)
    small_out[...] = both
    rows, columns = outs[0].shape
    upper = lane_of((8, LANES)) >= HD
    parts = []
    for at in range(0, both.shape[1], LANES):
        tile = both[:, at : at + LANES]
        parts += [jnp.where(upper, pltpu.roll(tile, HD, 1), 0.0), jnp.where(upper, tile, 0.0)]
    if len(parts) * 8 == rows:
        extra = jnp.concatenate(parts, axis=0)
    else:
        extra = jnp.zeros((rows, LANES), F32)
    for r, out in enumerate(outs):
        start = pl.multiple_of((me_ref[0] ^ r) * rows, rows)
        at = pl.ds(start, rows)
        total = kept_ref[at, :] + got_ref[at, :].astype(F32)
        out[:, : columns - LANES] = total[:, : columns - LANES].astype(out.dtype)
        out[:, columns - LANES :] = (total[:, columns - LANES :] + extra).astype(out.dtype)


def dense_sum_kernel(me_ref, small_ref, mine_ref, *refs):
    others, outs, held = refs[:-7], refs[-7:-1], refs[-1]
    q_ref, k_ref, v_ref, o_ref, r_ref, small_out = outs
    total = mine_ref[...]
    for other in others:
        total = total + other[...].astype(F32)
    at = 0
    for out in (q_ref, k_ref, v_ref):
        out[...] = total[:, at : at + out.shape[1]]
        at += out.shape[1]
    o_ref[...] = total[:, at : at + o_ref.shape[0]].T
    at += o_ref.shape[0]
    r_ref[...] = total[:, at : at + r_ref.shape[1]]
    held[me_ref[0]] = small_ref[...]
    if total.shape[0] * HD != 8 * small_ref.shape[1]:
        others = []
    lower = lane_of((8, LANES)) < HD
    for i, other in enumerate(others):
        for j in range(small_ref.shape[1] // LANES):
            first = other[16 * j : 16 * j + 16, at : at + LANES].astype(F32)
            tile = jnp.where(lower, pltpu.roll(first[:8], HD, 1), first[8:])
            held[me_ref[0] ^ (i + 1), :, j * LANES : (j + 1) * LANES] = tile
    small = held[0] if others else small_ref[...]
    for i in range(1, len(others) + 1):
        small = small + held[i]
    small_out[...] = jnp.concatenate([small[:4] + small[4:], jnp.zeros_like(small[:4])], axis=0)


def on_device(
    tokens,
    routes,
    gain_first,
    w_query,
    w_key,
    w_value,
    w_output,
    gain_second,
    w_router,
    w_gate,
    w_up,
    w_down,
    cotangent,
):
    seq_len, width = tokens.shape
    experts = w_router.shape[1]
    local, _, hidden = w_gate.shape
    tensor_size = lax.axis_size("tensor")
    expert_size = lax.axis_size("expert")
    dp_size = lax.axis_size("dp")
    token_count = seq_len * dp_size * expert_size
    rows = seq_len // tensor_size
    wide_width = width + LANES
    last = tensor_size - 1
    around = range(1, tensor_size)
    t_me, e_me, d_me = lax.axis_index("tensor"), lax.axis_index("expert"), lax.axis_index("dp")
    t_at = t_me.astype(jnp.int32).reshape(1)
    e_at = e_me.astype(jnp.int32).reshape(1)
    base = (e_me * local).astype(jnp.int32).reshape(1)
    d_at = jnp.stack([d_me, t_me]).astype(jnp.int32)
    cosine, sine = rope_tables(seq_len)
    gain_one, gain_two = gain_first[None], gain_second[None]
    down_flat = w_down.reshape(local * hidden, width)

    *cot_near, router = call(
        pieces_kernel,
        [shape((rows, wide_width), BF)] * tensor_size + [shape((LANES, width), BF)],
        (t_at, cotangent, routes.T, w_router.T),
        "pieces",
        "sbbb",
        scratch=[pltpu.VMEM((seq_len, LANES), F32)],
        limit=58,
    )
    cot_got = spread(cot_near[0], "expert")
    cot_got[0], tokens = tied(cot_got[0], tokens)

    heads, keys_wide = w_query.shape[1], w_key.shape[1]
    n_one, q, k, v, o, lse, xq, *rest = call(
        attend_kernel,
        [
            shape((seq_len, width), BF),
            shape((seq_len, heads), BF),
            shape((seq_len, keys_wide), BF),
            shape((seq_len, keys_wide), BF),
            shape((seq_len, heads), BF),
            shape((seq_len, LANES), F32),
            shape((rows, width), BF),
        ]
        + [shape((rows, width), F32)]
        + [shape((rows, width), BF)] * last,
        (t_at, tokens, gain_one, w_query, w_key, w_value, w_output, cosine, sine),
        "attend",
        "s" + "b" * 8,
        "bbbbbbv",
        scratch=[pltpu.VMEM((seq_len, width), F32)],
        limit=58,
        flops=2 * seq_len * width * 4 * heads,
    )
    parts = rest
    got = [swap(parts[r], "tensor", r) for r in around]
    h, n_two = call(
        norm_two_kernel,
        [shape((rows, width), F32), shape((rows, width), BF)],
        (xq, gain_two, parts[0], *got),
        "norm_two",
        "vb",
        "vv",
    )

    n_two, cot_got = tied(n_two, cot_got)
    cot_far = together(cot_got)
    wcat = gate_up_weights(w_gate, w_up)
    two_got = spread(n_two, "expert")
    two_got[0], cot_late = tied(two_got[0], cot_far)
    cot_far = [cot_far] + [swap(cot_far, "tensor", r) for r in range(1, last)]
    cot_far.append(swap(cot_late, "tensor", last))

    first = together([n_two, *two_got])
    twos = [first] + [swap(first, "tensor", r) for r in range(1, last)]
    _, late = tied(cot_far[:last], first)
    twos.append(swap(late, "tensor", last))

    run = functools.partial(
        run_experts, experts, base, router=router, wcat=wcat, down_flat=down_flat
    )
    counts = call(counts_kernel, [shape((1, LANES), F32)], (*cot_near, *cot_far), "counts")[0]
    counts = counts + swap(counts, "dp", 1)
    balance = experts * (counts / (token_count * TOP)) / token_count
    made = [run(twos[0], cot_near[0], cot_far[0], kind=F32)]
    got = []
    for r in around:
        made[-1], (two, cot) = tied(made[-1], (twos[r], cot_far[r]))
        if r == last:
            balance, two = tied(balance, two)
        made.append(run(two, cot_near[r], cot, kind=BF, apart=r == last))
        if r < last:
            got.append(swap(made[-1][3], "tensor", r))
    cots, dgus, hids, ds, moes = zip(*made)
    near_last, *far_last = ds[last]
    from_last = deal(far_last, "expert")
    grads = run_grads(twos, dgus, hids, cots, local, hidden)
    grads, (got, from_last) = tied(grads, (got, from_last))
    near, *across = split_sum([ds[0], *got], "dn_sum")
    through = added([near_last, *from_last], BF, "through")
    across[0], middle = tied(across[0], moes[1:last])
    across = deal(across, "expert")
    near_sums = [near, swap(through, "tensor", last), *across]
    moe_got = [swap(middle[r - 1], "tensor", r) for r in range(1, last)]
    moe_got, near_sums = tied(moe_got, near_sums)
    near_sums[2], moe_last = tied(near_sums[2], moes[last])
    moe_got.append(swap(moe_last, "tensor", last))

    wide, dh, small = call(
        functools.partial(norm_back_kernel, experts, len(near_sums)),
        [shape((rows, wide_width), BF), shape((rows, width), F32), shape((8, width), F32)],
        (h, n_two, gain_two, router, balance, cot_near[0], *near_sums),
        "norm_back",
        "v",
        "vvv",
    )
    wides = [wide] + [swap(wide, "tensor", r) for r in around]
    _, late_grads = tied(wide, grads)
    grads_got = swap(late_grads, "dp", 1)
    grads_got, wides = tied(grads_got, wides)
    moe = call(
        moe_sum_kernel,
        [shape((expert_size, rows, width), BF)],
        (e_at, moes[0], *moe_got),
        "moe_sum",
        "s",
    )[0]
    moe = lax.psum_scatter(moe, "expert", scatter_dimension=0, tiled=False)

    wide_all, dqkv, small, *back_parts = call(
        attend_back_kernel,
        [
            shape((seq_len, wide_width), BF),
            shape((seq_len, heads + 2 * keys_wide), BF),
            shape((8, width), F32),
            shape((rows, width), F32),
        ]
        + [shape((rows, width), BF)] * last,
        (t_at, *wides, tokens, q, k, v, lse, w_query, w_key, w_value, w_output, cosine, sine, small),
        "attend_back",
        "s" + "v" * tensor_size + "b" * 11,
        "bb",
        limit=58,
        scratch=[
            pltpu.VMEM((seq_len, heads), BF),
            pltpu.VMEM((seq_len, width), F32),
        ],
        flops=2 * seq_len * width * 4 * heads,
    )
    part_sums = [back_parts[0]] + [swap(back_parts[r], "tensor", r) for r in around]
    half = width // dp_size
    chunk = half // expert_size

    columns = heads + 2 * keys_wide
    all_columns = columns + heads + LANES
    own_block = pl.BlockSpec((1, rows, width), lambda i: (0, 0, 0))
    kept, sent = call(
        dense_kernel,
        [shape((half, all_columns), F32), shape((half, all_columns), BF)],
        (d_at, *twos, wide_all, o, n_one, dqkv),
        "dense",
        ["s"] + [own_block] * tensor_size + ["b"] * 4,
        "vv",
        limit=54,
        scratch=[
            pltpu.VMEM((seq_len, width), BF),
            pltpu.VMEM((width, all_columns), F32),
        ],
        flops=1,
    )
    mine, *others, small = call(
        kept_and_dealt_kernel,
        [shape((chunk, all_columns), F32)]
        + [shape((chunk, all_columns), BF)] * (expert_size - 1)
        + [shape((8, width), F32)],
        (e_at, kept, swap(sent, "dp", 1), small, swap(small, "dp", 1)),
        "dense_dealt",
        "s",
    )
    others = deal(others, "expert")
    others[0], part_sums = tied(others[0], part_sums)
    ig = call(
        input_grad_kernel, [shape((rows, width), BF)], (xq, gain_one, dh, *part_sums), "input_grad", "vb"
    )[0]
    igs = [ig] + [swap(ig, "tensor", r) for r in around]
    g_query, g_key, g_value, g_out, g_router, small = call(
        dense_sum_kernel,
        [
            shape((chunk, heads), F32),
            shape((chunk, keys_wide), F32),
            shape((chunk, keys_wide), F32),
            shape((heads, chunk), F32),
            shape((chunk, LANES), F32),
            shape((8, width), F32),
        ],
        (e_at, small, mine, *others),
        "dense_sum",
        "s",
        "bbbbbv",
        scratch=[pltpu.VMEM((expert_size, 8, width), F32)],
    )
    if chunk * HD != 8 * width:
        small = jnp.sum(lax.all_gather(small, "expert"), axis=0)
    igs, small = tied(igs, small)
    input_grad = call(
        natural_kernel, [shape((seq_len, width), F32)], (t_at, *igs), "input_grad_whole", "s", "b"
    )[0]
    out_piece = call(out_kernel, [shape((rows + 16, width), BF)], (h, small, moe), "out_piece")[0]
    outs = [out_piece] + [swap(out_piece, "tensor", r) for r in around]
    expert_grads = both_copies(grads, grads_got)
    expert_grads, outs = tied(expert_grads, outs)
    output, small = call(
        out_whole_kernel,
        [shape((seq_len, width), BF), shape((8, width), F32)],
        (t_at, *outs),
        "output",
        "s",
        "bv",
        scratch=[pltpu.VMEM((tensor_size, 8, width), F32)],
    )
    at = (d_me * expert_size + e_me) * chunk
    loss_value = (experts * balance * small[2:3, :LANES])[0, :experts]
    return (
        output,
        loss_value,
        input_grad,
        lax.dynamic_slice(small, (0, at), (1, chunk))[0],
        g_query,
        g_key,
        g_value,
        g_out,
        lax.dynamic_slice(small, (1, at), (1, chunk))[0],
        g_router[:, :experts],
        *expert_grads,
    )


def solution(mesh):
    rows = ("dp", "expert")
    placed = (
        P(rows, None),
        P(rows, None),
        P(),
        P(None, "tensor"),
        P(None, "tensor"),
        P(None, "tensor"),
        P("tensor", None),
        P(),
        P(),
        P("expert", None, "tensor"),
        P("expert", None, "tensor"),
        P("expert", "tensor", None),
        P(rows, None),
    )
    return jax.shard_map(
        on_device,
        mesh=mesh,
        in_specs=placed,
        out_specs=(
            P(rows, None),
            P(),
            P(rows, None),
            P(rows),
            P(rows, "tensor"),
            P(rows, "tensor"),
            P(rows, "tensor"),
            P("tensor", rows),
            P(rows),
            P(rows, None),
            P("expert", None, "tensor"),
            P("expert", None, "tensor"),
            P("expert", "tensor", None),
        ),
        check_vma=False,
    )
```

```python
import functools

import jax
import jax.numpy as jnp
import numpy as np
from jax import lax
from jax.experimental import pallas as pl
from jax.experimental.pallas import tpu as pltpu
from jax.sharding import PartitionSpec as P

HD = 64
TOP = 8
EPS = 1e-06
ROPE_BASE = 10000.0
MASKED = -1e30
BF = jnp.bfloat16
F32 = jnp.float32
FEW = 8
LANES = 128
MIB = 1 << 20


def dot(a, b, dims):
    return lax.dot_general(a, b, (dims, ((), ())), preferred_element_type=F32)


def nn(a, b):
    return dot(a, b, ((1,), (0,)))


def nt(a, b):
    return dot(a, b, ((1,), (1,)))


def tn(a, b):
    return dot(a, b, ((0,), (0,)))


def swap(x, axis, distance):
    size = lax.axis_size(axis)
    return lax.ppermute(x, axis, [(i, i ^ distance) for i in range(size)])


def spread(x, axis):
    size = lax.axis_size(axis)
    if size <= FEW:
        return [swap(x, axis, r) for r in range(1, size)]
    whole = lax.all_gather(x, axis)
    order = jnp.arange(1, size) ^ lax.axis_index(axis)
    return list(jnp.take(whole, order, axis=0))


def deal(parts, axis):
    size = lax.axis_size(axis)
    if size <= FEW:
        return [swap(part, axis, r + 1) for r, part in enumerate(parts)]
    order = jnp.arange(size) ^ lax.axis_index(axis)
    whole = jnp.take(jnp.stack([parts[0], *parts]), order, axis=0)
    back = lax.all_to_all(whole, axis, 0, 0, tiled=True)
    return list(jnp.take(back, order, axis=0)[1:])


def rope_tables(seq_len):
    half = HD // 2
    frequency = ROPE_BASE ** (-(np.arange(half, dtype=np.float32) * 2.0) / HD)
    angles = np.arange(seq_len, dtype=np.float32)[:, None] * frequency[None, :].astype(np.float32)
    cosine, sine = np.cos(angles), np.sin(angles)
    heads = LANES // HD
    return (
        np.tile(cosine, (1, 2 * heads)).astype(np.float32),
        np.tile(np.concatenate([-sine, sine], axis=1), (1, heads)).astype(np.float32),
    )


def lane_of(shape):
    return lax.broadcasted_iota(jnp.int32, shape, 1)


def halves_swapped(x):
    first = lane_of(x.shape) % HD < HD // 2
    half = HD // 2
    return jnp.where(first, pltpu.roll(x, LANES - half, 1), pltpu.roll(x, half, 1))


def low_high(x, head):
    other = pltpu.roll(x.astype(F32), HD, 1).astype(x.dtype)
    low = lane_of(x.shape) < HD
    zero = jnp.zeros_like(x)
    at_low, at_high = (x, other) if head == 0 else (other, x)
    return jnp.where(low, at_low, zero), jnp.where(low, zero, at_high)


def causal(scores):
    rows = lax.broadcasted_iota(jnp.int32, scores.shape, 0)
    return lane_of(scores.shape) <= rows


def shape(dims, kind):
    return jax.ShapeDtypeStruct(dims, kind)


def whole_block(dims):
    return pl.BlockSpec(dims, lambda i: (0,) * len(dims))


def call(kernel, outs, operands, name, places="", out_places="", scratch=(), limit=40, flops=0):
    kinds = {"s": pltpu.SMEM, "v": pltpu.VMEM}

    def spec(place, x):
        if not isinstance(place, str):
            return place
        if place == "b":
            return whole_block(x.shape)
        return pl.BlockSpec(memory_space=kinds[place])

    places = [*places] + ["v"] * (len(operands) - len(places))
    out_places = [*out_places] + ["v"] * (len(outs) - len(out_places))
    return pl.pallas_call(
        kernel,
        grid=(1,),
        out_shape=outs,
        in_specs=[spec(p, x) for p, x in zip(places, operands)],
        out_specs=[spec(p, x) for p, x in zip(out_places, outs)],
        scratch_shapes=list(scratch),
        compiler_params=pltpu.CompilerParams(vmem_limit_bytes=limit * MIB),
        cost_estimate=pl.CostEstimate(flops=int(100.0*(flops)), bytes_accessed=0, transcendentals=0),
        name=name,
    )(*operands)


def tied(first, then):
    return lax.optimization_barrier((first, then))


def pieces_kernel(me_ref, cot_ref, routes_ref, router_ref, *refs):
    cots, (router_out, held) = refs[:-2], refs[-2:]
    rows, width = cots[0].shape[0], cot_ref.shape[1]
    eye = lax.broadcasted_iota(jnp.int32, (TOP, LANES), 0) == lane_of((TOP, LANES))
    held[...] = tn(routes_ref[...].astype(F32).astype(BF), eye.astype(F32).astype(BF))
    for r, c in enumerate(cots):
        start = pl.multiple_of((me_ref[0] ^ r) * rows, rows)
        c[:, :width] = cot_ref[pl.ds(start, rows), :]
        c[:, width:] = held[pl.ds(start, rows), :].astype(BF)
    router_out[...] = jnp.zeros(router_out.shape, BF)
    router_out[: router_ref.shape[0], :] = router_ref[...]


def attend_kernel(
    me_ref, x_ref, gain_ref, wq_ref, wk_ref, wv_ref, wo_ref, cos_ref, sin_ref, *refs
):
    n_ref, q_ref, k_ref, v_ref, o_ref, lse_ref, xq_ref = refs[:7]
    parts, whole = refs[7:-1], refs[-1]
    rows, width = xq_ref.shape
    starts = [pl.multiple_of((me_ref[0] ^ r) * rows, rows) for r in range(4)]
    xq_ref[...] = x_ref[pl.ds(starts[0], rows), :]
    x = x_ref[...].astype(F32)
    inv = lax.rsqrt(jnp.mean(x * x, axis=-1, keepdims=True) + EPS)
    n = (x * inv * gain_ref[...]).astype(BF)
    n_ref[...] = n
    cosine, sine = cos_ref[...], sin_ref[...]
    q, k = nn(n, wq_ref[...]), nn(n, wk_ref[...])
    v_ref[...] = nn(n, wv_ref[...]).astype(BF)
    for at in range(0, q.shape[1], LANES):
        tile = q[:, at : at + LANES]
        q_ref[:, at : at + LANES] = (tile * cosine + halves_swapped(tile) * sine).astype(BF)
    for at in range(0, k.shape[1], LANES):
        tile = k[:, at : at + LANES]
        k_ref[:, at : at + LANES] = (tile * cosine + halves_swapped(tile) * sine).astype(BF)
    lse_all = jnp.zeros(lse_ref.shape, F32)
    for head in range(q.shape[1] // LANES):
        at = head // 2 * LANES
        keys = low_high(k_ref[:, at : at + LANES], head % 2)
        values = low_high(v_ref[:, at : at + LANES], head % 2)
        pair = q_ref[:, head * LANES : (head + 1) * LANES]
        mixed = 0.0
        for g in range(2):
            s = nt(pair, keys[g]) * HD ** (-0.5)
            s = jnp.where(causal(s), s, MASKED)
            peak = jnp.max(s, axis=-1, keepdims=True)
            e = jnp.exp(s - peak)
            total = jnp.sum(e, axis=-1, keepdims=True)
            mixed = mixed + nn((e / total).astype(BF), values[g])
            lse = peak + jnp.log(total)
            lse_all = jnp.where(lane_of(lse_all.shape) == 2 * head + g, lse, lse_all)
        o_ref[:, head * LANES : (head + 1) * LANES] = mixed.astype(BF)
    lse_ref[...] = lse_all
    whole[...] = nn(o_ref[...], wo_ref[...])
    for start, part in zip(starts, parts):
        part[...] = whole[pl.ds(start, rows), :].astype(part.dtype)


def norm_two_kernel(x_ref, gain_ref, own_ref, *refs):
    others, (h_ref, n_ref) = refs[:-2], refs[-2:]
    attn = own_ref[...]
    for other in others:
        attn = attn + other[...].astype(F32)
    h = x_ref[...].astype(F32) + attn
    inv = lax.rsqrt(jnp.mean(h * h, axis=-1, keepdims=True) + EPS)
    h_ref[...] = h
    n_ref[...] = (h * inv * gain_ref[...]).astype(BF)


def together_kernel(*refs):
    pieces, out = refs[:-1], refs[-1]
    at = 0
    for piece in pieces:
        if len(piece.shape) == 2:
            out[at] = piece[...]
            at += 1
        else:
            out[at : at + piece.shape[0]] = piece[...]
            at += piece.shape[0]


def together(pieces):
    count = sum(1 if x.ndim == 2 else x.shape[0] for x in pieces)
    return call(
        together_kernel, [shape((count, *pieces[0].shape[-2:]), pieces[0].dtype)], pieces, "together"
    )[0]


def router_of(rows, router_ref, routes, experts):
    z = nt(rows, router_ref[...])
    lane = lane_of(z.shape)
    z = jnp.where(lane < experts, z, MASKED)
    e = jnp.exp(z - jnp.max(z, axis=-1, keepdims=True))
    probs = e / jnp.sum(e, axis=-1, keepdims=True)
    chosen = chosen_of(lane, routes)
    zc = jnp.where(chosen, z, MASKED)
    ec = jnp.where(chosen, jnp.exp(zc - jnp.max(zc, axis=-1, keepdims=True)), 0.0)
    return probs, ec / jnp.sum(ec, axis=-1, keepdims=True)


def chosen_of(lane, routes):
    place, named = lane.astype(F32), routes.astype(F32)
    chosen = place == named[:, 0:1]
    for k in range(1, TOP):
        chosen = chosen | (place == named[:, k : k + 1])
    return chosen


def counts_kernel(*refs):
    pieces, out = refs[:-1], refs[-1]
    total = 0.0
    for piece in pieces:
        width = piece.shape[-1] - LANES
        blocks = [piece[:, width:]] if len(piece.shape) == 2 else [
            piece[i, :, width:] for i in range(piece.shape[0])
        ]
        for routes in blocks:
            named = chosen_of(lane_of(routes.shape), routes).astype(F32)
            total = total + jnp.sum(named, axis=0, keepdims=True)
    out[...] = total


def weights_kernel(wg_ref, wu_ref, out_ref):
    hidden = wg_ref.shape[2]
    out_ref[:, :hidden] = wg_ref[0]
    out_ref[:, hidden:] = wu_ref[0]


def gate_up_weights(w_gate, w_up):
    local, width, hidden = w_gate.shape
    block = pl.BlockSpec((1, width, hidden), lambda e: (e, 0, 0))
    return pl.pallas_call(
        weights_kernel,
        grid=(local,),
        in_specs=[block, block],
        out_specs=pl.BlockSpec((width, 2 * hidden), lambda e: (0, e)),
        out_shape=shape((width, 2 * hidden * local), BF),
        compiler_params=pltpu.CompilerParams(vmem_limit_bytes=30 * MIB),
        cost_estimate=pl.CostEstimate(flops=int(100.0*(0)), bytes_accessed=4 * w_gate.size * 2, transcendentals=0),
        name="gate_up_weights",
    )(w_gate, w_up)


def experts_kernel(experts, base_ref, x_ref, own_ref, far_ref, router_ref, wcat, wd_ref, *refs):
    cot_ref, dgu_ref, hg_ref, *ds, m_ref = refs
    hidden = LANES
    pair = 2 * hidden
    rows, width = cot_ref.shape
    x = x_ref[...].reshape(rows, width)
    if far_ref is None:
        routes = own_ref[:, width:]
        cot_ref[...] = own_ref[:, :width]
    else:
        pieces = [own_ref[...]] + [far_ref[i] for i in range(far_ref.shape[0])]
        routes = jnp.concatenate([piece[:, width:] for piece in pieces], axis=0)
        cot_ref[...] = jnp.concatenate([piece[:, :width] for piece in pieces], axis=0)
    _, gates = router_of(x, router_ref, routes, experts)
    lane = lane_of(gates.shape)
    dots = jnp.zeros(gates.shape, F32)
    for e in range(hg_ref.shape[1] // hidden):
        mine = lane == base_ref[0] + e
        g = jnp.sum(jnp.where(mine, gates, 0.0), axis=-1, keepdims=True)
        both = nn(x, wcat[:, e * pair : (e + 1) * pair])
        v = nt(cot_ref[...], wd_ref[e * hidden : (e + 1) * hidden, :])
        gate, up = both[:, :hidden], both[:, hidden:]
        sig = 1.0 / (1.0 + jnp.exp(-gate))
        act = gate * sig
        hid = act * up
        dots = jnp.where(mine, jnp.sum(hid * v, axis=-1, keepdims=True), dots)
        gv = g * v
        hg_ref[:, e * hidden : (e + 1) * hidden] = (g * hid).astype(BF)
        d_gate = gv * up * sig * (1.0 + gate * (1.0 - sig))
        dgu_ref[:, e * pair : e * pair + hidden] = d_gate.astype(BF)
        dgu_ref[:, e * pair + hidden : (e + 1) * pair] = (gv * act).astype(BF)

    def put(outs, columns, value):
        at = 0
        for out in outs:
            part = value.astype(out.dtype)
            if len(out.shape) == 2:
                out[:, columns] = part[at : at + out.shape[0]]
                at += out.shape[0]
            else:
                step = out.shape[1]
                for i in range(out.shape[0]):
                    out[i, :, columns] = part[i * step : (i + 1) * step]

    put(ds, slice(width, width + LANES), dots)
    step = 256
    for at in range(0, width, step):
        put(ds, slice(at, at + step), nt(dgu_ref[...], wcat[at : at + step, :]))
    put([m_ref], slice(0, width), nn(hg_ref[...], wd_ref[...]))


def run_experts(experts, base, x, own, far, router, wcat, down_flat, kind, apart=False):
    count, rows, width = x.shape
    inner = down_flat.shape[0]
    wide = width + LANES
    total = count * rows
    few = count <= FEW
    step = total if few else 256
    resident = pl.BlockSpec(memory_space=pltpu.VMEM)
    per = lambda w: resident if few else pl.BlockSpec((step, w), lambda i: (i, 0))
    kernel = functools.partial(experts_kernel, experts)
    if few:
        data, dims = [x, own, far], lambda w: (count, rows, w)
    else:
        joined = jnp.concatenate([own[None], far], axis=0)
        data, dims = [x.reshape(total, width), joined.reshape(total, wide)], lambda w: (total, w)
        whole_kernel = kernel
        kernel = lambda b, x, c, *refs: whole_kernel(b, x, c, None, *refs)
    if few and apart:
        d_shapes = [shape((rows, wide), BF if i else F32) for i in range(count)]
    else:
        d_shapes = [shape(dims(wide), kind)]
    cot, dgu, hid, *d, m = pl.pallas_call(
        kernel,
        grid=(total // step,),
        in_specs=[pl.BlockSpec(memory_space=pltpu.SMEM)]
        + [per(z.shape[-1]) for z in data]
        + [resident] * 3,
        out_specs=[per(width), per(2 * inner), per(inner)]
        + [per(wide)] * len(d_shapes)
        + [per(width)],
        out_shape=[
            shape((total, width), BF),
            shape((total, 2 * inner), BF),
            shape((total, inner), BF),
            *d_shapes,
            shape(dims(width), kind),
        ],
        compiler_params=pltpu.CompilerParams(vmem_limit_bytes=30 * MIB),
        cost_estimate=pl.CostEstimate(flops=int(100.0*(total * width * inner // 8)), bytes_accessed=0, transcendentals=0),
        name="experts",
    )(base, *data, router, wcat, down_flat)
    if not few:
        d = list(d[0].reshape(count, rows, wide)) if apart else [d[0].reshape(count, rows, wide)]
    return cot, dgu, hid, d if apart else d[0], m.reshape(count, rows, width)


def split_sum_kernel(count, near, *refs):
    ins, outs = refs[:count], refs[count:]
    for s in range(ins[0].shape[0]):
        total = ins[0][s].astype(F32)
        for x in ins[1:]:
            total = total + x[s].astype(F32)
        outs[s][...] = total.astype(outs[s].dtype)


def split_sum(arrays, name):
    count, *dims = arrays[0].shape
    outs = [shape(dims, F32)] + [shape(dims, BF)] * (count - 1)
    return call(functools.partial(split_sum_kernel, len(arrays), True), outs, arrays, name)


def add_kernel(*refs):
    pieces, out = refs[:-1], refs[-1]
    total = pieces[0][...].astype(F32)
    for piece in pieces[1:]:
        total = total + piece[...].astype(F32)
    out[...] = total.astype(out.dtype)


def added(pieces, kind, name):
    return call(add_kernel, [shape(pieces[0].shape, kind)], pieces, name)[0]


def grads_kernel(*refs):
    ns, dgus, hs, cs = (refs[4 * i : 4 * i + 4] for i in range(4))
    out_ref = refs[16]
    hidden, width = hs[0].shape[1], ns[0].shape[1]
    both, down = 0.0, 0.0
    for n, dgu, h, c in zip(ns, dgus, hs, cs):
        both = both + tn(n[...], dgu[...])
        down = down + tn(h[...], c[...])
    out_ref[0, :width, :] = both[:, :hidden].astype(BF)
    out_ref[0, width : 2 * width, :] = both[:, hidden:].astype(BF)
    for at in range(0, width, hidden):
        out_ref[0, 2 * width + at : 2 * width + at + hidden, :] = down[:, at : at + hidden].astype(BF)


def run_grads(n, dgu, h, c, local, hidden):
    width = n[0].shape[-1]
    flat = lambda xs: [x.reshape(-1, x.shape[-1]) for x in xs]
    n, c = flat(n), flat(c)
    whole = lambda xs: [pl.BlockSpec(x.shape, lambda e: (0, 0)) for x in xs]
    cols = lambda xs, w: [pl.BlockSpec((x.shape[0], w), lambda e: (0, e)) for x in xs]
    few = n[0].shape[0] <= 512
    return pl.pallas_call(
        grads_kernel,
        grid=(local,),
        in_specs=whole(n) + cols(dgu, 2 * hidden) + cols(h, hidden) + whole(c),
        out_specs=pl.BlockSpec((1, 3 * width, hidden), lambda e: (e, 0, 0)),
        out_shape=shape((local, 3 * width, hidden), BF),
        compiler_params=pltpu.CompilerParams(vmem_limit_bytes=(32 if few else 58) * MIB),
        cost_estimate=pl.CostEstimate(flops=int(100.0*(24 * n[0].size * hidden * local)), bytes_accessed=0, transcendentals=0),
        name="expert_grads",
    )(*n, *dgu, *h, *c)


def both_copies_kernel(mine_ref, other_ref, gate_ref, up_ref, down_ref):
    width, hidden = gate_ref.shape[1:]

    def total(at, count):
        rows = pl.ds(at, count)
        return mine_ref[0, rows, :].astype(F32) + other_ref[0, rows, :].astype(F32)

    gate_ref[0] = total(0, width)
    up_ref[0] = total(width, width)
    for at in range(0, width, hidden):
        down_ref[0, :, at : at + hidden] = total(2 * width + at, hidden)


def both_copies(mine, other):
    local, rows, hidden = mine.shape
    width = rows // 3
    block = lambda *dims: pl.BlockSpec((1, *dims), lambda e: (e, 0, 0))
    return pl.pallas_call(
        both_copies_kernel,
        grid=(local,),
        in_specs=[block(rows, hidden)] * 2,
        out_specs=[block(width, hidden), block(width, hidden), block(hidden, width)],
        out_shape=[
            shape((local, width, hidden), F32),
            shape((local, width, hidden), F32),
            shape((local, hidden, width), F32),
        ],
        compiler_params=pltpu.CompilerParams(vmem_limit_bytes=58 * MIB),
        cost_estimate=pl.CostEstimate(flops=int(100.0*(0)), bytes_accessed=8 * mine.size, transcendentals=0),
        name="both_copies",
    )(mine, other)


def norm_back_kernel(experts, count, h_ref, n_ref, gain_ref, router_ref, bal_ref, cot_ref, *refs):
    sums, (wide_ref, dh_ref, small_ref) = refs[:count], refs[count:]
    near = sums[0][...].astype(F32)
    for other in sums[1:]:
        near = near + other[...].astype(F32)
    rows, width = h_ref.shape
    dots = near[:, width:]
    probs, gates = router_of(n_ref[...], router_ref, cot_ref[:, width:], experts)
    bal = bal_ref[...]
    d_chosen = gates * (dots - jnp.sum(gates * dots, axis=-1, keepdims=True))
    dz = probs * (bal - jnp.sum(probs * bal, axis=-1, keepdims=True)) + d_chosen
    dz = dz.astype(BF)
    wide_ref[:, width:] = dz
    dn = near[:, :width] + nn(dz, router_ref[...])
    h = h_ref[...]
    inv = lax.rsqrt(jnp.mean(h * h, axis=-1, keepdims=True) + EPS)
    u = gain_ref[...] * dn
    dy = cot_ref[:, :width].astype(F32)
    dh = dy + inv * u - h * (inv * inv * inv * jnp.mean(u * h, axis=-1, keepdims=True))
    dh_ref[...] = dh
    wide_ref[:, :width] = dh.astype(BF)
    small_ref[...] = jnp.zeros(small_ref.shape, F32)
    small_ref[1:2, :] = jnp.sum(dn * h * inv, axis=0, keepdims=True)
    small_ref[2:3, : probs.shape[1]] = jnp.sum(probs, axis=0, keepdims=True)


def attend_back_kernel(
    me_ref, w0, w1, w2, w3, x_ref, q_ref, k_ref, v_ref, lse_ref, wq_ref, wk_ref, wv_ref, wo_ref, cos_ref, sin_ref,
    small_in, wide_ref, dq_ref, small_ref, p0, p1, p2, p3, do_ref, whole
):
    rows = w0.shape[0]
    width = x_ref.shape[1]
    for r, piece in enumerate((w0, w1, w2, w3)):
        start = pl.multiple_of((me_ref[0] ^ r) * rows, rows)
        wide_ref[pl.ds(start, rows), :] = piece[...]
    do_ref[...] = nt(wide_ref[:, :width], wo_ref[...]).astype(BF)
    cosine, sine = cos_ref[...], sin_ref[...]
    scale = HD ** (-0.5)
    heads, keys_wide = q_ref.shape[1], k_ref.shape[1]
    dk_tiles = [0.0] * (keys_wide // LANES)
    dv_tiles = [0.0] * (keys_wide // LANES)

    def back(tile):
        return (tile * cosine - halves_swapped(tile) * sine).astype(BF)

    for head in range(heads // LANES):
        at = head // 2 * LANES
        side = head % 2
        keys = low_high(k_ref[:, at : at + LANES], side)
        values = low_high(v_ref[:, at : at + LANES], side)
        pair = q_ref[:, head * LANES : (head + 1) * LANES]
        grad = do_ref[:, head * LANES : (head + 1) * LANES]
        dq = 0.0
        dk, dv = [], []
        for g in range(2):
            s = nt(pair, keys[g]) * scale
            lse = lse_ref[:, 2 * head + g : 2 * head + g + 1]
            p = jnp.where(causal(s), jnp.exp(s - lse), 0.0)
            dp = nt(grad, values[g])
            ds = (p * (dp - jnp.sum(p * dp, axis=-1, keepdims=True))).astype(BF)
            dq = dq + nn(ds, keys[g])
            dk.append(tn(ds, pair))
            dv.append(tn(p.astype(BF), grad))
        dq_ref[:, head * LANES : (head + 1) * LANES] = back(dq * scale)
        mine = lane_of(dk[0].shape) < HD
        if side == 0:
            dk_sum = jnp.where(mine, dk[0] + pltpu.roll(dk[1], HD, 1), 0.0)
            dv_sum = jnp.where(mine, dv[0] + pltpu.roll(dv[1], HD, 1), 0.0)
        else:
            dk_sum = jnp.where(mine, 0.0, pltpu.roll(dk[0], HD, 1) + dk[1])
            dv_sum = jnp.where(mine, 0.0, pltpu.roll(dv[0], HD, 1) + dv[1])
        dk_tiles[head // 2] = dk_tiles[head // 2] + dk_sum
        dv_tiles[head // 2] = dv_tiles[head // 2] + dv_sum
    for i, tile in enumerate(dk_tiles):
        at = heads + i * LANES
        dq_ref[:, at : at + LANES] = back(tile * scale)
    for i, tile in enumerate(dv_tiles):
        at = heads + keys_wide + i * LANES
        dq_ref[:, at : at + LANES] = tile.astype(BF)
    dn = nt(dq_ref[:, :heads], wq_ref[...])
    dn = dn + nt(dq_ref[:, heads : heads + keys_wide], wk_ref[...])
    whole[...] = dn + nt(dq_ref[:, heads + keys_wide :], wv_ref[...])
    x = x_ref[...].astype(F32)
    inv = lax.rsqrt(jnp.mean(x * x, axis=-1, keepdims=True) + EPS)
    small_ref[...] = small_in[...]
    small_ref[0:1, :] = jnp.sum(whole[...] * x * inv, axis=0, keepdims=True)
    for r, part in enumerate((p0, p1, p2, p3)):
        start = pl.multiple_of((me_ref[0] ^ r) * rows, rows)
        part[...] = whole[pl.ds(start, rows), :].astype(part.dtype)


def dense_kernel(me_ref, a0, a1, a2, a3, wide_ref, o_ref, n_ref, dq_ref, kept_ref, sent_ref, two_ref, whole):
    rows, width = a0.shape[1:]
    for r, piece in enumerate((a0, a1, a2, a3)):
        start = pl.multiple_of((me_ref[1] ^ r) * rows, rows)
        two_ref[pl.ds(start, rows), :] = piece[0]
    columns, heads = dq_ref.shape[1], o_ref.shape[1]
    whole[:, :columns] = tn(n_ref[...], dq_ref[...])
    whole[:, columns : columns + heads] = tn(wide_ref[:, :width], o_ref[...])
    whole[:, columns + heads :] = tn(two_ref[...], wide_ref[:, width:])
    half = kept_ref.shape[0]
    kept_ref[...] = whole[pl.ds(pl.multiple_of(me_ref[0] * half, half), half), :]
    sent_ref[...] = whole[pl.ds(pl.multiple_of((1 - me_ref[0]) * half, half), half), :].astype(BF)


def input_grad_kernel(x_ref, gain_ref, dh_ref, *refs):
    parts, ig_ref = refs[:-1], refs[-1]
    x = x_ref[...].astype(F32)
    inv = lax.rsqrt(jnp.mean(x * x, axis=-1, keepdims=True) + EPS)
    dn = parts[0][...].astype(F32)
    for part in parts[1:]:
        dn = dn + part[...].astype(F32)
    u = gain_ref[...] * dn
    ig = dh_ref[...] + inv * u - x * (inv * inv * inv * jnp.mean(u * x, axis=-1, keepdims=True))
    ig_ref[...] = ig.astype(BF)


def out_kernel(h_ref, small_ref, *refs):
    moes, out_ref = refs[:-1], refs[-1]
    rows = h_ref.shape[0]
    out = h_ref[...]
    for moe in moes:
        out = out + moe[...].astype(F32)
    out_ref[:rows, :] = out.astype(BF)
    small = small_ref[...]
    high = small.astype(BF).astype(F32)
    out_ref[rows:, :] = jnp.concatenate([high, small - high], axis=0).astype(BF)


def natural_kernel(me_ref, *refs):
    pieces, out = refs[:-1], refs[-1]
    rows = pieces[0].shape[0]
    for r, piece in enumerate(pieces):
        start = pl.multiple_of((me_ref[0] ^ r) * rows, rows)
        out[pl.ds(start, rows), :] = piece[...].astype(out.dtype)


def out_whole_kernel(me_ref, *refs):
    pieces, (out_ref, small_ref, held) = refs[:-3], refs[-3:]
    rows = pieces[0].shape[0] - 16
    for r, piece in enumerate(pieces):
        start = pl.multiple_of((me_ref[0] ^ r) * rows, rows)
        out_ref[pl.ds(start, rows), :] = piece[:rows, :]
        both = piece[rows:, :].astype(F32)
        held[me_ref[0] ^ r] = both[:8] + both[8:]
    total = held[0]
    for i in range(1, len(pieces)):
        total = total + held[i]
    small_ref[...] = total


def kept_and_dealt_kernel(me_ref, kept_ref, got_ref, small_ref, small_got_ref, *outs):
    small_out, outs = outs[-1], outs[:-1]
    small = small_ref[...] + small_got_ref[...]
    high = small[:4].astype(BF).astype(F32)
    both = jnp.concatenate([high, small[:4] - high], axis=0).astype(BF).astype(F32)
    small_out[...] = both
    rows, columns = outs[0].shape
    upper = lane_of((8, LANES)) >= HD
    parts = []
    for at in range(0, both.shape[1], LANES):
        tile = both[:, at : at + LANES]
        parts += [jnp.where(upper, pltpu.roll(tile, HD, 1), 0.0), jnp.where(upper, tile, 0.0)]
    if len(parts) * 8 == rows:
        extra = jnp.concatenate(parts, axis=0)
    else:
        extra = jnp.zeros((rows, LANES), F32)
    for r, out in enumerate(outs):
        start = pl.multiple_of((me_ref[0] ^ r) * rows, rows)
        at = pl.ds(start, rows)
        total = kept_ref[at, :] + got_ref[at, :].astype(F32)
        out[:, : columns - LANES] = total[:, : columns - LANES].astype(out.dtype)
        out[:, columns - LANES :] = (total[:, columns - LANES :] + extra).astype(out.dtype)


def dense_sum_kernel(me_ref, small_ref, mine_ref, *refs):
    others, outs, held = refs[:-7], refs[-7:-1], refs[-1]
    q_ref, k_ref, v_ref, o_ref, r_ref, small_out = outs
    total = mine_ref[...]
    for other in others:
        total = total + other[...].astype(F32)
    at = 0
    for out in (q_ref, k_ref, v_ref):
        out[...] = total[:, at : at + out.shape[1]]
        at += out.shape[1]
    o_ref[...] = total[:, at : at + o_ref.shape[0]].T
    at += o_ref.shape[0]
    r_ref[...] = total[:, at : at + r_ref.shape[1]]
    held[me_ref[0]] = small_ref[...]
    if total.shape[0] * HD != 8 * small_ref.shape[1]:
        others = []
    lower = lane_of((8, LANES)) < HD
    for i, other in enumerate(others):
        for j in range(small_ref.shape[1] // LANES):
            first = other[16 * j : 16 * j + 16, at : at + LANES].astype(F32)
            tile = jnp.where(lower, pltpu.roll(first[:8], HD, 1), first[8:])
            held[me_ref[0] ^ (i + 1), :, j * LANES : (j + 1) * LANES] = tile
    small = held[0] if others else small_ref[...]
    for i in range(1, len(others) + 1):
        small = small + held[i]
    small_out[...] = jnp.concatenate([small[:4] + small[4:], jnp.zeros_like(small[:4])], axis=0)


def on_device(
    tokens,
    routes,
    gain_first,
    w_query,
    w_key,
    w_value,
    w_output,
    gain_second,
    w_router,
    w_gate,
    w_up,
    w_down,
    cotangent,
):
    seq_len, width = tokens.shape
    experts = w_router.shape[1]
    local, _, hidden = w_gate.shape
    tensor_size = lax.axis_size("tensor")
    expert_size = lax.axis_size("expert")
    dp_size = lax.axis_size("dp")
    token_count = seq_len * dp_size * expert_size
    rows = seq_len // tensor_size
    wide_width = width + LANES
    last = tensor_size - 1
    around = range(1, tensor_size)
    t_me, e_me, d_me = lax.axis_index("tensor"), lax.axis_index("expert"), lax.axis_index("dp")
    t_at = t_me.astype(jnp.int32).reshape(1)
    e_at = e_me.astype(jnp.int32).reshape(1)
    base = (e_me * local).astype(jnp.int32).reshape(1)
    d_at = jnp.stack([d_me, t_me]).astype(jnp.int32)
    cosine, sine = rope_tables(seq_len)
    gain_one, gain_two = gain_first[None], gain_second[None]
    down_flat = w_down.reshape(local * hidden, width)

    *cot_near, router = call(
        pieces_kernel,
        [shape((rows, wide_width), BF)] * tensor_size + [shape((LANES, width), BF)],
        (t_at, cotangent, routes.T, w_router.T),
        "pieces",
        "sbbb",
        scratch=[pltpu.VMEM((seq_len, LANES), F32)],
        limit=58,
    )
    cot_got = spread(cot_near[0], "expert")
    cot_got[0], tokens = tied(cot_got[0], tokens)

    heads, keys_wide = w_query.shape[1], w_key.shape[1]
    n_one, q, k, v, o, lse, xq, *rest = call(
        attend_kernel,
        [
            shape((seq_len, width), BF),
            shape((seq_len, heads), BF),
            shape((seq_len, keys_wide), BF),
            shape((seq_len, keys_wide), BF),
            shape((seq_len, heads), BF),
            shape((seq_len, LANES), F32),
            shape((rows, width), BF),
        ]
        + [shape((rows, width), F32)]
        + [shape((rows, width), BF)] * last,
        (t_at, tokens, gain_one, w_query, w_key, w_value, w_output, cosine, sine),
        "attend",
        "s" + "b" * 8,
        "bbbbbbv",
        scratch=[pltpu.VMEM((seq_len, width), F32)],
        limit=58,
        flops=2 * seq_len * width * 4 * heads,
    )
    parts = rest
    got = [swap(parts[r], "tensor", r) for r in around]
    h, n_two = call(
        norm_two_kernel,
        [shape((rows, width), F32), shape((rows, width), BF)],
        (xq, gain_two, parts[0], *got),
        "norm_two",
        "bbb",
        "vv",
    )

    n_two, cot_got = tied(n_two, cot_got)
    cot_far = together(cot_got)
    wcat = gate_up_weights(w_gate, w_up)
    two_got = spread(n_two, "expert")
    two_got[0], cot_late = tied(two_got[0], cot_far)
    cot_far = [cot_far] + [swap(cot_far, "tensor", r) for r in range(1, last)]
    cot_far.append(swap(cot_late, "tensor", last))

    first = together([n_two, *two_got])
    twos = [first] + [swap(first, "tensor", r) for r in range(1, last)]
    _, late = tied(cot_far[:last], first)
    twos.append(swap(late, "tensor", last))

    run = functools.partial(
        run_experts, experts, base, router=router, wcat=wcat, down_flat=down_flat
    )
    counts = call(counts_kernel, [shape((1, LANES), F32)], (*cot_near, *cot_far), "counts")[0]
    counts = counts + swap(counts, "dp", 1)
    balance = experts * (counts / (token_count * TOP)) / token_count
    made = [run(twos[0], cot_near[0], cot_far[0], kind=F32)]
    got = []
    for r in around:
        made[-1], (two, cot) = tied(made[-1], (twos[r], cot_far[r]))
        if r == last:
            balance, two = tied(balance, two)
        made.append(run(two, cot_near[r], cot, kind=BF, apart=r == last))
        if r < last:
            got.append(swap(made[-1][3], "tensor", r))
    cots, dgus, hids, ds, moes = zip(*made)
    near_last, *far_last = ds[last]
    from_last = deal(far_last, "expert")
    grads = run_grads(twos, dgus, hids, cots, local, hidden)
    grads, (got, from_last) = tied(grads, (got, from_last))
    near, *across = split_sum([ds[0], *got], "dn_sum")
    through = added([near_last, *from_last], BF, "through")
    across[0], (middle, moe_last) = tied(across[0], (moes[1:last], moes[last]))
    across = deal(across, "expert")
    near_sums = [near, swap(through, "tensor", last), *across]
    moe_got = [swap(middle[r - 1], "tensor", r) for r in range(1, last)]
    moe_got.append(swap(moe_last, "tensor", last))
    moe_got, near_sums = tied(moe_got, near_sums)

    wide, dh, small = call(
        functools.partial(norm_back_kernel, experts, len(near_sums)),
        [shape((rows, wide_width), BF), shape((rows, width), F32), shape((8, width), F32)],
        (h, n_two, gain_two, router, balance, cot_near[0], *near_sums),
        "norm_back",
        "v",
        "vvv",
    )
    wides = [wide] + [swap(wide, "tensor", r) for r in around]
    _, late_grads = tied(wide, grads)
    grads_got = swap(late_grads, "dp", 1)
    grads_got, wides = tied(grads_got, wides)
    moe_near, *moe_across = split_sum([moes[0], *moe_got], "moe_sum")
    moe_across, wides = tied(moe_across, wides)
    moe_sums = [moe_near, *deal(moe_across, "expert")]

    wide_all, dqkv, small, *back_parts = call(
        attend_back_kernel,
        [
            shape((seq_len, wide_width), BF),
            shape((seq_len, heads + 2 * keys_wide), BF),
            shape((8, width), F32),
            shape((rows, width), F32),
        ]
        + [shape((rows, width), BF)] * last,
        (t_at, *wides, tokens, q, k, v, lse, w_query, w_key, w_value, w_output, cosine, sine, small),
        "attend_back",
        "s" + "v" * tensor_size + "b" * 11,
        "bb",
        limit=58,
        scratch=[
            pltpu.VMEM((seq_len, heads), BF),
            pltpu.VMEM((seq_len, width), F32),
        ],
        flops=2 * seq_len * width * 4 * heads,
    )
    part_sums = [back_parts[0]] + [swap(back_parts[r], "tensor", r) for r in around]
    half = width // dp_size
    chunk = half // expert_size

    columns = heads + 2 * keys_wide
    all_columns = columns + heads + LANES
    own_block = pl.BlockSpec((1, rows, width), lambda i: (0, 0, 0))
    kept, sent = call(
        dense_kernel,
        [shape((half, all_columns), F32), shape((half, all_columns), BF)],
        (d_at, *twos, wide_all, o, n_one, dqkv),
        "dense",
        ["s"] + [own_block] * tensor_size + ["b"] * 4,
        "vv",
        limit=54,
        scratch=[
            pltpu.VMEM((seq_len, width), BF),
            pltpu.VMEM((width, all_columns), F32),
        ],
        flops=1,
    )
    mine, *others, small = call(
        kept_and_dealt_kernel,
        [shape((chunk, all_columns), F32)]
        + [shape((chunk, all_columns), BF)] * (expert_size - 1)
        + [shape((8, width), F32)],
        (e_at, kept, swap(sent, "dp", 1), small, swap(small, "dp", 1)),
        "dense_dealt",
        "s",
    )
    others = deal(others, "expert")
    others[0], part_sums = tied(others[0], part_sums)
    ig = call(
        input_grad_kernel, [shape((rows, width), BF)], (xq, gain_one, dh, *part_sums), "input_grad", "bbbb"
    )[0]
    igs = [ig] + [swap(ig, "tensor", r) for r in around]
    g_query, g_key, g_value, g_out, g_router, small = call(
        dense_sum_kernel,
        [
            shape((chunk, heads), F32),
            shape((chunk, keys_wide), F32),
            shape((chunk, keys_wide), F32),
            shape((heads, chunk), F32),
            shape((chunk, LANES), F32),
            shape((8, width), F32),
        ],
        (e_at, small, mine, *others),
        "dense_sum",
        "s",
        "bbbbbv",
        scratch=[pltpu.VMEM((expert_size, 8, width), F32)],
    )
    if chunk * HD != 8 * width:
        small = jnp.sum(lax.all_gather(small, "expert"), axis=0)
    igs, small = tied(igs, small)
    input_grad = call(
        natural_kernel, [shape((seq_len, width), F32)], (t_at, *igs), "input_grad_whole", "s", "b"
    )[0]
    out_piece = call(out_kernel, [shape((rows + 16, width), BF)], (h, small, *moe_sums), "out_piece")[0]
    outs = [out_piece] + [swap(out_piece, "tensor", r) for r in around]
    expert_grads = both_copies(grads, grads_got)
    expert_grads, outs = tied(expert_grads, outs)
    output, small = call(
        out_whole_kernel,
        [shape((seq_len, width), BF), shape((8, width), F32)],
        (t_at, *outs),
        "output",
        "s",
        "bv",
        scratch=[pltpu.VMEM((tensor_size, 8, width), F32)],
    )
    at = (d_me * expert_size + e_me) * chunk
    loss_value = (experts * balance * small[2:3, :LANES])[0, :experts]
    return (
        output,
        loss_value,
        input_grad,
        lax.dynamic_slice(small, (0, at), (1, chunk))[0],
        g_query,
        g_key,
        g_value,
        g_out,
        lax.dynamic_slice(small, (1, at), (1, chunk))[0],
        g_router[:, :experts],
        *expert_grads,
    )


def solution(mesh):
    rows = ("dp", "expert")
    placed = (
        P(rows, None),
        P(rows, None),
        P(),
        P(None, "tensor"),
        P(None, "tensor"),
        P(None, "tensor"),
        P("tensor", None),
        P(),
        P(),
        P("expert", None, "tensor"),
        P("expert", None, "tensor"),
        P("expert", "tensor", None),
        P(rows, None),
    )
    return jax.shard_map(
        on_device,
        mesh=mesh,
        in_specs=placed,
        out_specs=(
            P(rows, None),
            P(),
            P(rows, None),
            P(rows),
            P(rows, "tensor"),
            P(rows, "tensor"),
            P(rows, "tensor"),
            P("tensor", rows),
            P(rows),
            P(rows, None),
            P("expert", None, "tensor"),
            P("expert", None, "tensor"),
            P("expert", "tensor", None),
        ),
        check_vma=False,
    )
```

```python
import functools

import jax
import jax.numpy as jnp
import numpy as np
from jax import lax
from jax.experimental import pallas as pl
from jax.experimental.pallas import tpu as pltpu
from jax.sharding import PartitionSpec as P

HD = 64
TOP = 8
EPS = 1e-06
ROPE_BASE = 10000.0
MASKED = -1e30
BF = jnp.bfloat16
F32 = jnp.float32
FEW = 8
LANES = 128
MIB = 1 << 20


def dot(a, b, dims):
    return lax.dot_general(a, b, (dims, ((), ())), preferred_element_type=F32)


def nn(a, b):
    return dot(a, b, ((1,), (0,)))


def nt(a, b):
    return dot(a, b, ((1,), (1,)))


def tn(a, b):
    return dot(a, b, ((0,), (0,)))


def swap(x, axis, distance):
    size = lax.axis_size(axis)
    return lax.ppermute(x, axis, [(i, i ^ distance) for i in range(size)])


def spread(x, axis):
    size = lax.axis_size(axis)
    if size <= FEW:
        return [swap(x, axis, r) for r in range(1, size)]
    whole = lax.all_gather(x, axis)
    order = jnp.arange(1, size) ^ lax.axis_index(axis)
    return list(jnp.take(whole, order, axis=0))


def deal(parts, axis):
    size = lax.axis_size(axis)
    if size <= FEW:
        return [swap(part, axis, r + 1) for r, part in enumerate(parts)]
    order = jnp.arange(size) ^ lax.axis_index(axis)
    whole = jnp.take(jnp.stack([parts[0], *parts]), order, axis=0)
    back = lax.all_to_all(whole, axis, 0, 0, tiled=True)
    return list(jnp.take(back, order, axis=0)[1:])


def rope_tables(seq_len):
    half = HD // 2
    frequency = ROPE_BASE ** (-(np.arange(half, dtype=np.float32) * 2.0) / HD)
    angles = np.arange(seq_len, dtype=np.float32)[:, None] * frequency[None, :].astype(np.float32)
    cosine, sine = np.cos(angles), np.sin(angles)
    heads = LANES // HD
    return (
        np.tile(cosine, (1, 2 * heads)).astype(np.float32),
        np.tile(np.concatenate([-sine, sine], axis=1), (1, heads)).astype(np.float32),
    )


def lane_of(shape):
    return lax.broadcasted_iota(jnp.int32, shape, 1)


def halves_swapped(x):
    first = lane_of(x.shape) % HD < HD // 2
    half = HD // 2
    return jnp.where(first, pltpu.roll(x, LANES - half, 1), pltpu.roll(x, half, 1))


def low_high(x, head):
    other = pltpu.roll(x.astype(F32), HD, 1).astype(x.dtype)
    low = lane_of(x.shape) < HD
    zero = jnp.zeros_like(x)
    at_low, at_high = (x, other) if head == 0 else (other, x)
    return jnp.where(low, at_low, zero), jnp.where(low, zero, at_high)


def causal(scores):
    rows = lax.broadcasted_iota(jnp.int32, scores.shape, 0)
    return lane_of(scores.shape) <= rows


def shape(dims, kind):
    return jax.ShapeDtypeStruct(dims, kind)


def whole_block(dims):
    return pl.BlockSpec(dims, lambda i: (0,) * len(dims))


def call(kernel, outs, operands, name, places="", out_places="", scratch=(), limit=40, flops=0):
    kinds = {"s": pltpu.SMEM, "v": pltpu.VMEM}

    def spec(place, x):
        if not isinstance(place, str):
            return place
        if place == "b":
            return whole_block(x.shape)
        return pl.BlockSpec(memory_space=kinds[place])

    places = [*places] + ["v"] * (len(operands) - len(places))
    out_places = [*out_places] + ["v"] * (len(outs) - len(out_places))
    return pl.pallas_call(
        kernel,
        grid=(1,),
        out_shape=outs,
        in_specs=[spec(p, x) for p, x in zip(places, operands)],
        out_specs=[spec(p, x) for p, x in zip(out_places, outs)],
        scratch_shapes=list(scratch),
        compiler_params=pltpu.CompilerParams(vmem_limit_bytes=limit * MIB),
        cost_estimate=pl.CostEstimate(flops=int(100.0*(flops)), bytes_accessed=0, transcendentals=0),
        name=name,
    )(*operands)


def tied(first, then):
    return lax.optimization_barrier((first, then))


def pieces_kernel(me_ref, cot_ref, routes_ref, router_ref, *refs):
    cots, (router_out, held) = refs[:-2], refs[-2:]
    rows, width = cots[0].shape[0], cot_ref.shape[1]
    eye = lax.broadcasted_iota(jnp.int32, (TOP, LANES), 0) == lane_of((TOP, LANES))
    held[...] = tn(routes_ref[...].astype(F32).astype(BF), eye.astype(F32).astype(BF))
    for r, c in enumerate(cots):
        start = pl.multiple_of((me_ref[0] ^ r) * rows, rows)
        c[:, :width] = cot_ref[pl.ds(start, rows), :]
        c[:, width:] = held[pl.ds(start, rows), :].astype(BF)
    router_out[...] = jnp.zeros(router_out.shape, BF)
    router_out[: router_ref.shape[0], :] = router_ref[...]


def attend_kernel(
    me_ref, x_ref, gain_ref, wq_ref, wk_ref, wv_ref, wo_ref, cos_ref, sin_ref, *refs
):
    n_ref, q_ref, k_ref, v_ref, o_ref, lse_ref, xq_ref = refs[:7]
    parts, whole = refs[7:-1], refs[-1]
    rows, width = xq_ref.shape
    starts = [pl.multiple_of((me_ref[0] ^ r) * rows, rows) for r in range(4)]
    xq_ref[...] = x_ref[pl.ds(starts[0], rows), :]
    x = x_ref[...].astype(F32)
    inv = lax.rsqrt(jnp.mean(x * x, axis=-1, keepdims=True) + EPS)
    n = (x * inv * gain_ref[...]).astype(BF)
    n_ref[...] = n
    cosine, sine = cos_ref[...], sin_ref[...]
    q, k = nn(n, wq_ref[...]), nn(n, wk_ref[...])
    v_ref[...] = nn(n, wv_ref[...]).astype(BF)
    for at in range(0, q.shape[1], LANES):
        tile = q[:, at : at + LANES]
        q_ref[:, at : at + LANES] = (tile * cosine + halves_swapped(tile) * sine).astype(BF)
    for at in range(0, k.shape[1], LANES):
        tile = k[:, at : at + LANES]
        k_ref[:, at : at + LANES] = (tile * cosine + halves_swapped(tile) * sine).astype(BF)
    lse_all = jnp.zeros(lse_ref.shape, F32)
    for head in range(q.shape[1] // LANES):
        at = head // 2 * LANES
        keys = low_high(k_ref[:, at : at + LANES], head % 2)
        values = low_high(v_ref[:, at : at + LANES], head % 2)
        pair = q_ref[:, head * LANES : (head + 1) * LANES]
        mixed = 0.0
        for g in range(2):
            s = nt(pair, keys[g]) * HD ** (-0.5)
            s = jnp.where(causal(s), s, MASKED)
            peak = jnp.max(s, axis=-1, keepdims=True)
            e = jnp.exp(s - peak)
            total = jnp.sum(e, axis=-1, keepdims=True)
            mixed = mixed + nn((e / total).astype(BF), values[g])
            lse = peak + jnp.log(total)
            lse_all = jnp.where(lane_of(lse_all.shape) == 2 * head + g, lse, lse_all)
        o_ref[:, head * LANES : (head + 1) * LANES] = mixed.astype(BF)
    lse_ref[...] = lse_all
    whole[...] = nn(o_ref[...], wo_ref[...])
    for start, part in zip(starts, parts):
        part[...] = whole[pl.ds(start, rows), :].astype(part.dtype)


def norm_two_kernel(x_ref, gain_ref, own_ref, *refs):
    others, (h_ref, n_ref) = refs[:-2], refs[-2:]
    attn = own_ref[...]
    for other in others:
        attn = attn + other[...].astype(F32)
    h = x_ref[...].astype(F32) + attn
    inv = lax.rsqrt(jnp.mean(h * h, axis=-1, keepdims=True) + EPS)
    h_ref[...] = h
    n_ref[...] = (h * inv * gain_ref[...]).astype(BF)


def together_kernel(*refs):
    pieces, out = refs[:-1], refs[-1]
    at = 0
    for piece in pieces:
        if len(piece.shape) == 2:
            out[at] = piece[...]
            at += 1
        else:
            out[at : at + piece.shape[0]] = piece[...]
            at += piece.shape[0]


def together(pieces):
    count = sum(1 if x.ndim == 2 else x.shape[0] for x in pieces)
    return call(
        together_kernel, [shape((count, *pieces[0].shape[-2:]), pieces[0].dtype)], pieces, "together"
    )[0]


def router_of(rows, router_ref, routes, experts):
    z = nt(rows, router_ref[...])
    lane = lane_of(z.shape)
    z = jnp.where(lane < experts, z, MASKED)
    e = jnp.exp(z - jnp.max(z, axis=-1, keepdims=True))
    probs = e / jnp.sum(e, axis=-1, keepdims=True)
    chosen = chosen_of(lane, routes)
    zc = jnp.where(chosen, z, MASKED)
    ec = jnp.where(chosen, jnp.exp(zc - jnp.max(zc, axis=-1, keepdims=True)), 0.0)
    return probs, ec / jnp.sum(ec, axis=-1, keepdims=True)


def chosen_of(lane, routes):
    place, named = lane.astype(F32), routes.astype(F32)
    chosen = place == named[:, 0:1]
    for k in range(1, TOP):
        chosen = chosen | (place == named[:, k : k + 1])
    return chosen


def counts_kernel(*refs):
    pieces, out = refs[:-1], refs[-1]
    total = 0.0
    for piece in pieces:
        width = piece.shape[-1] - LANES
        blocks = [piece[:, width:]] if len(piece.shape) == 2 else [
            piece[i, :, width:] for i in range(piece.shape[0])
        ]
        for routes in blocks:
            named = chosen_of(lane_of(routes.shape), routes).astype(F32)
            total = total + jnp.sum(named, axis=0, keepdims=True)
    out[...] = total


def weights_kernel(wg_ref, wu_ref, out_ref):
    hidden = wg_ref.shape[2]
    out_ref[:, :hidden] = wg_ref[0]
    out_ref[:, hidden:] = wu_ref[0]


def gate_up_weights(w_gate, w_up):
    local, width, hidden = w_gate.shape
    block = pl.BlockSpec((1, width, hidden), lambda e: (e, 0, 0))
    return pl.pallas_call(
        weights_kernel,
        grid=(local,),
        in_specs=[block, block],
        out_specs=pl.BlockSpec((width, 2 * hidden), lambda e: (0, e)),
        out_shape=shape((width, 2 * hidden * local), BF),
        compiler_params=pltpu.CompilerParams(vmem_limit_bytes=30 * MIB),
        cost_estimate=pl.CostEstimate(flops=int(100.0*(0)), bytes_accessed=4 * w_gate.size * 2, transcendentals=0),
        name="gate_up_weights",
    )(w_gate, w_up)


def experts_kernel(experts, base_ref, x_ref, own_ref, far_ref, router_ref, wcat, wd_ref, *refs):
    cot_ref, dgu_ref, hg_ref, *ds, m_ref = refs
    hidden = LANES
    pair = 2 * hidden
    rows, width = cot_ref.shape
    x = x_ref[...].reshape(rows, width)
    if far_ref is None:
        routes = own_ref[:, width:]
        cot_ref[...] = own_ref[:, :width]
    else:
        pieces = [own_ref[...]] + [far_ref[i] for i in range(far_ref.shape[0])]
        routes = jnp.concatenate([piece[:, width:] for piece in pieces], axis=0)
        cot_ref[...] = jnp.concatenate([piece[:, :width] for piece in pieces], axis=0)
    _, gates = router_of(x, router_ref, routes, experts)
    lane = lane_of(gates.shape)
    dots = jnp.zeros(gates.shape, F32)
    for e in range(hg_ref.shape[1] // hidden):
        mine = lane == base_ref[0] + e
        g = jnp.sum(jnp.where(mine, gates, 0.0), axis=-1, keepdims=True)
        both = nn(x, wcat[:, e * pair : (e + 1) * pair])
        v = nt(cot_ref[...], wd_ref[e * hidden : (e + 1) * hidden, :])
        gate, up = both[:, :hidden], both[:, hidden:]
        sig = 1.0 / (1.0 + jnp.exp(-gate))
        act = gate * sig
        hid = act * up
        dots = jnp.where(mine, jnp.sum(hid * v, axis=-1, keepdims=True), dots)
        gv = g * v
        hg_ref[:, e * hidden : (e + 1) * hidden] = (g * hid).astype(BF)
        d_gate = gv * up * sig * (1.0 + gate * (1.0 - sig))
        dgu_ref[:, e * pair : e * pair + hidden] = d_gate.astype(BF)
        dgu_ref[:, e * pair + hidden : (e + 1) * pair] = (gv * act).astype(BF)

    def put(outs, columns, value):
        at = 0
        for out in outs:
            part = value.astype(out.dtype)
            if len(out.shape) == 2:
                out[:, columns] = part[at : at + out.shape[0]]
                at += out.shape[0]
            else:
                step = out.shape[1]
                for i in range(out.shape[0]):
                    out[i, :, columns] = part[i * step : (i + 1) * step]

    put(ds, slice(width, width + LANES), dots)
    step = 256
    for at in range(0, width, step):
        put(ds, slice(at, at + step), nt(dgu_ref[...], wcat[at : at + step, :]))
    put([m_ref], slice(0, width), nn(hg_ref[...], wd_ref[...]))


def run_experts(experts, base, x, own, far, router, wcat, down_flat, kind, apart=False):
    count, rows, width = x.shape
    inner = down_flat.shape[0]
    wide = width + LANES
    total = count * rows
    few = count <= FEW
    step = total if few else 256
    resident = pl.BlockSpec(memory_space=pltpu.VMEM)
    per = lambda w: resident if few else pl.BlockSpec((step, w), lambda i: (i, 0))
    kernel = functools.partial(experts_kernel, experts)
    if few:
        data, dims = [x, own, far], lambda w: (count, rows, w)
    else:
        joined = jnp.concatenate([own[None], far], axis=0)
        data, dims = [x.reshape(total, width), joined.reshape(total, wide)], lambda w: (total, w)
        whole_kernel = kernel
        kernel = lambda b, x, c, *refs: whole_kernel(b, x, c, None, *refs)
    if few and apart:
        d_shapes = [shape((rows, wide), BF if i else F32) for i in range(count)]
    else:
        d_shapes = [shape(dims(wide), kind)]
    cot, dgu, hid, *d, m = pl.pallas_call(
        kernel,
        grid=(total // step,),
        in_specs=[pl.BlockSpec(memory_space=pltpu.SMEM)]
        + [per(z.shape[-1]) for z in data]
        + [resident] * 3,
        out_specs=[per(width), per(2 * inner), per(inner)]
        + [per(wide)] * len(d_shapes)
        + [per(width)],
        out_shape=[
            shape((total, width), BF),
            shape((total, 2 * inner), BF),
            shape((total, inner), BF),
            *d_shapes,
            shape(dims(width), kind),
        ],
        compiler_params=pltpu.CompilerParams(vmem_limit_bytes=(14 if few else 30) * MIB),
        cost_estimate=pl.CostEstimate(flops=int(100.0*(total * width * inner // 8)), bytes_accessed=0, transcendentals=0),
        name="experts",
    )(base, *data, router, wcat, down_flat)
    if not few:
        d = list(d[0].reshape(count, rows, wide)) if apart else [d[0].reshape(count, rows, wide)]
    return cot, dgu, hid, d if apart else d[0], m.reshape(count, rows, width)


def split_sum_kernel(count, near, *refs):
    ins, outs = refs[:count], refs[count:]
    for s in range(ins[0].shape[0]):
        total = ins[0][s].astype(F32)
        for x in ins[1:]:
            total = total + x[s].astype(F32)
        outs[s][...] = total.astype(outs[s].dtype)


def split_sum(arrays, name):
    count, *dims = arrays[0].shape
    outs = [shape(dims, F32)] + [shape(dims, BF)] * (count - 1)
    return call(functools.partial(split_sum_kernel, len(arrays), True), outs, arrays, name)


def add_kernel(*refs):
    pieces, out = refs[:-1], refs[-1]
    total = pieces[0][...].astype(F32)
    for piece in pieces[1:]:
        total = total + piece[...].astype(F32)
    out[...] = total.astype(out.dtype)


def added(pieces, kind, name):
    return call(add_kernel, [shape(pieces[0].shape, kind)], pieces, name)[0]


def grads_kernel(*refs):
    ns, dgus, hs, cs = (refs[4 * i : 4 * i + 4] for i in range(4))
    out_ref = refs[16]
    hidden, width = hs[0].shape[1], ns[0].shape[1]
    both, down = 0.0, 0.0
    for n, dgu, h, c in zip(ns, dgus, hs, cs):
        both = both + tn(n[...], dgu[...])
        down = down + tn(h[...], c[...])
    out_ref[0, :width, :] = both[:, :hidden].astype(BF)
    out_ref[0, width : 2 * width, :] = both[:, hidden:].astype(BF)
    for at in range(0, width, hidden):
        out_ref[0, 2 * width + at : 2 * width + at + hidden, :] = down[:, at : at + hidden].astype(BF)


def run_grads(n, dgu, h, c, local, hidden):
    width = n[0].shape[-1]
    flat = lambda xs: [x.reshape(-1, x.shape[-1]) for x in xs]
    n, c = flat(n), flat(c)
    whole = lambda xs: [pl.BlockSpec(x.shape, lambda e: (0, 0)) for x in xs]
    cols = lambda xs, w: [pl.BlockSpec((x.shape[0], w), lambda e: (0, e)) for x in xs]
    few = n[0].shape[0] <= 512
    return pl.pallas_call(
        grads_kernel,
        grid=(local,),
        in_specs=whole(n) + cols(dgu, 2 * hidden) + cols(h, hidden) + whole(c),
        out_specs=pl.BlockSpec((1, 3 * width, hidden), lambda e: (e, 0, 0)),
        out_shape=shape((local, 3 * width, hidden), BF),
        compiler_params=pltpu.CompilerParams(vmem_limit_bytes=(20 if few else 58) * MIB),
        cost_estimate=pl.CostEstimate(flops=int(100.0*(24 * n[0].size * hidden * local)), bytes_accessed=0, transcendentals=0),
        name="expert_grads",
    )(*n, *dgu, *h, *c)


def both_copies_kernel(mine_ref, other_ref, gate_ref, up_ref, down_ref):
    width, hidden = gate_ref.shape[1:]

    def total(at, count):
        rows = pl.ds(at, count)
        return mine_ref[0, rows, :].astype(F32) + other_ref[0, rows, :].astype(F32)

    gate_ref[0] = total(0, width)
    up_ref[0] = total(width, width)
    for at in range(0, width, hidden):
        down_ref[0, :, at : at + hidden] = total(2 * width + at, hidden)


def both_copies(mine, other):
    local, rows, hidden = mine.shape
    width = rows // 3
    block = lambda *dims: pl.BlockSpec((1, *dims), lambda e: (e, 0, 0))
    return pl.pallas_call(
        both_copies_kernel,
        grid=(local,),
        in_specs=[block(rows, hidden)] * 2,
        out_specs=[block(width, hidden), block(width, hidden), block(hidden, width)],
        out_shape=[
            shape((local, width, hidden), F32),
            shape((local, width, hidden), F32),
            shape((local, hidden, width), F32),
        ],
        compiler_params=pltpu.CompilerParams(vmem_limit_bytes=58 * MIB),
        cost_estimate=pl.CostEstimate(flops=int(100.0*(0)), bytes_accessed=8 * mine.size, transcendentals=0),
        name="both_copies",
    )(mine, other)


def norm_back_kernel(experts, count, h_ref, n_ref, gain_ref, router_ref, bal_ref, cot_ref, *refs):
    sums, (wide_ref, dh_ref, small_ref) = refs[:count], refs[count:]
    near = sums[0][...].astype(F32)
    for other in sums[1:]:
        near = near + other[...].astype(F32)
    rows, width = h_ref.shape
    dots = near[:, width:]
    probs, gates = router_of(n_ref[...], router_ref, cot_ref[:, width:], experts)
    bal = bal_ref[...]
    d_chosen = gates * (dots - jnp.sum(gates * dots, axis=-1, keepdims=True))
    dz = probs * (bal - jnp.sum(probs * bal, axis=-1, keepdims=True)) + d_chosen
    dz = dz.astype(BF)
    wide_ref[:, width:] = dz
    dn = near[:, :width] + nn(dz, router_ref[...])
    h = h_ref[...]
    inv = lax.rsqrt(jnp.mean(h * h, axis=-1, keepdims=True) + EPS)
    u = gain_ref[...] * dn
    dy = cot_ref[:, :width].astype(F32)
    dh = dy + inv * u - h * (inv * inv * inv * jnp.mean(u * h, axis=-1, keepdims=True))
    dh_ref[...] = dh
    wide_ref[:, :width] = dh.astype(BF)
    small_ref[...] = jnp.zeros(small_ref.shape, F32)
    small_ref[1:2, :] = jnp.sum(dn * h * inv, axis=0, keepdims=True)
    small_ref[2:3, : probs.shape[1]] = jnp.sum(probs, axis=0, keepdims=True)


def attend_back_kernel(
    me_ref, w0, w1, w2, w3, x_ref, q_ref, k_ref, v_ref, lse_ref, wq_ref, wk_ref, wv_ref, wo_ref, cos_ref, sin_ref,
    small_in, wide_ref, dq_ref, small_ref, p0, p1, p2, p3, do_ref, whole
):
    rows = w0.shape[0]
    width = x_ref.shape[1]
    for r, piece in enumerate((w0, w1, w2, w3)):
        start = pl.multiple_of((me_ref[0] ^ r) * rows, rows)
        wide_ref[pl.ds(start, rows), :] = piece[...]
    do_ref[...] = nt(wide_ref[:, :width], wo_ref[...]).astype(BF)
    cosine, sine = cos_ref[...], sin_ref[...]
    scale = HD ** (-0.5)
    heads, keys_wide = q_ref.shape[1], k_ref.shape[1]
    dk_tiles = [0.0] * (keys_wide // LANES)
    dv_tiles = [0.0] * (keys_wide // LANES)

    def back(tile):
        return (tile * cosine - halves_swapped(tile) * sine).astype(BF)

    for head in range(heads // LANES):
        at = head // 2 * LANES
        side = head % 2
        keys = low_high(k_ref[:, at : at + LANES], side)
        values = low_high(v_ref[:, at : at + LANES], side)
        pair = q_ref[:, head * LANES : (head + 1) * LANES]
        grad = do_ref[:, head * LANES : (head + 1) * LANES]
        dq = 0.0
        dk, dv = [], []
        for g in range(2):
            s = nt(pair, keys[g]) * scale
            lse = lse_ref[:, 2 * head + g : 2 * head + g + 1]
            p = jnp.where(causal(s), jnp.exp(s - lse), 0.0)
            dp = nt(grad, values[g])
            ds = (p * (dp - jnp.sum(p * dp, axis=-1, keepdims=True))).astype(BF)
            dq = dq + nn(ds, keys[g])
            dk.append(tn(ds, pair))
            dv.append(tn(p.astype(BF), grad))
        dq_ref[:, head * LANES : (head + 1) * LANES] = back(dq * scale)
        mine = lane_of(dk[0].shape) < HD
        if side == 0:
            dk_sum = jnp.where(mine, dk[0] + pltpu.roll(dk[1], HD, 1), 0.0)
            dv_sum = jnp.where(mine, dv[0] + pltpu.roll(dv[1], HD, 1), 0.0)
        else:
            dk_sum = jnp.where(mine, 0.0, pltpu.roll(dk[0], HD, 1) + dk[1])
            dv_sum = jnp.where(mine, 0.0, pltpu.roll(dv[0], HD, 1) + dv[1])
        dk_tiles[head // 2] = dk_tiles[head // 2] + dk_sum
        dv_tiles[head // 2] = dv_tiles[head // 2] + dv_sum
    for i, tile in enumerate(dk_tiles):
        at = heads + i * LANES
        dq_ref[:, at : at + LANES] = back(tile * scale)
    for i, tile in enumerate(dv_tiles):
        at = heads + keys_wide + i * LANES
        dq_ref[:, at : at + LANES] = tile.astype(BF)
    dn = nt(dq_ref[:, :heads], wq_ref[...])
    dn = dn + nt(dq_ref[:, heads : heads + keys_wide], wk_ref[...])
    whole[...] = dn + nt(dq_ref[:, heads + keys_wide :], wv_ref[...])
    x = x_ref[...].astype(F32)
    inv = lax.rsqrt(jnp.mean(x * x, axis=-1, keepdims=True) + EPS)
    small_ref[...] = small_in[...]
    small_ref[0:1, :] = jnp.sum(whole[...] * x * inv, axis=0, keepdims=True)
    for r, part in enumerate((p0, p1, p2, p3)):
        start = pl.multiple_of((me_ref[0] ^ r) * rows, rows)
        part[...] = whole[pl.ds(start, rows), :].astype(part.dtype)


def dense_kernel(me_ref, a0, a1, a2, a3, wide_ref, o_ref, n_ref, dq_ref, kept_ref, sent_ref, two_ref, whole):
    rows, width = a0.shape[1:]
    for r, piece in enumerate((a0, a1, a2, a3)):
        start = pl.multiple_of((me_ref[1] ^ r) * rows, rows)
        two_ref[pl.ds(start, rows), :] = piece[0]
    columns, heads = dq_ref.shape[1], o_ref.shape[1]
    whole[:, :columns] = tn(n_ref[...], dq_ref[...])
    whole[:, columns : columns + heads] = tn(wide_ref[:, :width], o_ref[...])
    whole[:, columns + heads :] = tn(two_ref[...], wide_ref[:, width:])
    half = kept_ref.shape[0]
    kept_ref[...] = whole[pl.ds(pl.multiple_of(me_ref[0] * half, half), half), :]
    sent_ref[...] = whole[pl.ds(pl.multiple_of((1 - me_ref[0]) * half, half), half), :].astype(BF)


def input_grad_kernel(x_ref, gain_ref, dh_ref, *refs):
    parts, ig_ref = refs[:-1], refs[-1]
    x = x_ref[...].astype(F32)
    inv = lax.rsqrt(jnp.mean(x * x, axis=-1, keepdims=True) + EPS)
    dn = parts[0][...].astype(F32)
    for part in parts[1:]:
        dn = dn + part[...].astype(F32)
    u = gain_ref[...] * dn
    ig = dh_ref[...] + inv * u - x * (inv * inv * inv * jnp.mean(u * x, axis=-1, keepdims=True))
    ig_ref[...] = ig.astype(BF)


def out_kernel(h_ref, small_ref, *refs):
    moes, out_ref = refs[:-1], refs[-1]
    rows = h_ref.shape[0]
    out = h_ref[...]
    for moe in moes:
        out = out + moe[...].astype(F32)
    out_ref[:rows, :] = out.astype(BF)
    small = small_ref[...]
    high = small.astype(BF).astype(F32)
    out_ref[rows:, :] = jnp.concatenate([high, small - high], axis=0).astype(BF)


def natural_kernel(me_ref, *refs):
    pieces, out = refs[:-1], refs[-1]
    rows = pieces[0].shape[0]
    for r, piece in enumerate(pieces):
        start = pl.multiple_of((me_ref[0] ^ r) * rows, rows)
        out[pl.ds(start, rows), :] = piece[...].astype(out.dtype)


def out_whole_kernel(me_ref, *refs):
    pieces, (out_ref, small_ref, held) = refs[:-3], refs[-3:]
    rows = pieces[0].shape[0] - 16
    for r, piece in enumerate(pieces):
        start = pl.multiple_of((me_ref[0] ^ r) * rows, rows)
        out_ref[pl.ds(start, rows), :] = piece[:rows, :]
        both = piece[rows:, :].astype(F32)
        held[me_ref[0] ^ r] = both[:8] + both[8:]
    total = held[0]
    for i in range(1, len(pieces)):
        total = total + held[i]
    small_ref[...] = total


def kept_and_dealt_kernel(me_ref, kept_ref, got_ref, small_ref, small_got_ref, *outs):
    small_out, outs = outs[-1], outs[:-1]
    small = small_ref[...] + small_got_ref[...]
    high = small[:4].astype(BF).astype(F32)
    both = jnp.concatenate([high, small[:4] - high], axis=0).astype(BF).astype(F32)
    small_out[...] = both
    rows, columns = outs[0].shape
    upper = lane_of((8, LANES)) >= HD
    parts = []
    for at in range(0, both.shape[1], LANES):
        tile = both[:, at : at + LANES]
        parts += [jnp.where(upper, pltpu.roll(tile, HD, 1), 0.0), jnp.where(upper, tile, 0.0)]
    if len(parts) * 8 == rows:
        extra = jnp.concatenate(parts, axis=0)
    else:
        extra = jnp.zeros((rows, LANES), F32)
    for r, out in enumerate(outs):
        start = pl.multiple_of((me_ref[0] ^ r) * rows, rows)
        at = pl.ds(start, rows)
        total = kept_ref[at, :] + got_ref[at, :].astype(F32)
        out[:, : columns - LANES] = total[:, : columns - LANES].astype(out.dtype)
        out[:, columns - LANES :] = (total[:, columns - LANES :] + extra).astype(out.dtype)


def dense_sum_kernel(me_ref, small_ref, mine_ref, *refs):
    others, outs, held = refs[:-7], refs[-7:-1], refs[-1]
    q_ref, k_ref, v_ref, o_ref, r_ref, small_out = outs
    total = mine_ref[...]
    for other in others:
        total = total + other[...].astype(F32)
    at = 0
    for out in (q_ref, k_ref, v_ref):
        out[...] = total[:, at : at + out.shape[1]]
        at += out.shape[1]
    o_ref[...] = total[:, at : at + o_ref.shape[0]].T
    at += o_ref.shape[0]
    r_ref[...] = total[:, at : at + r_ref.shape[1]]
    held[me_ref[0]] = small_ref[...]
    if total.shape[0] * HD != 8 * small_ref.shape[1]:
        others = []
    lower = lane_of((8, LANES)) < HD
    for i, other in enumerate(others):
        for j in range(small_ref.shape[1] // LANES):
            first = other[16 * j : 16 * j + 16, at : at + LANES].astype(F32)
            tile = jnp.where(lower, pltpu.roll(first[:8], HD, 1), first[8:])
            held[me_ref[0] ^ (i + 1), :, j * LANES : (j + 1) * LANES] = tile
    small = held[0] if others else small_ref[...]
    for i in range(1, len(others) + 1):
        small = small + held[i]
    small_out[...] = jnp.concatenate([small[:4] + small[4:], jnp.zeros_like(small[:4])], axis=0)


def on_device(
    tokens,
    routes,
    gain_first,
    w_query,
    w_key,
    w_value,
    w_output,
    gain_second,
    w_router,
    w_gate,
    w_up,
    w_down,
    cotangent,
):
    seq_len, width = tokens.shape
    experts = w_router.shape[1]
    local, _, hidden = w_gate.shape
    tensor_size = lax.axis_size("tensor")
    expert_size = lax.axis_size("expert")
    dp_size = lax.axis_size("dp")
    token_count = seq_len * dp_size * expert_size
    rows = seq_len // tensor_size
    wide_width = width + LANES
    last = tensor_size - 1
    around = range(1, tensor_size)
    t_me, e_me, d_me = lax.axis_index("tensor"), lax.axis_index("expert"), lax.axis_index("dp")
    t_at = t_me.astype(jnp.int32).reshape(1)
    e_at = e_me.astype(jnp.int32).reshape(1)
    base = (e_me * local).astype(jnp.int32).reshape(1)
    d_at = jnp.stack([d_me, t_me]).astype(jnp.int32)
    cosine, sine = rope_tables(seq_len)
    gain_one, gain_two = gain_first[None], gain_second[None]
    down_flat = w_down.reshape(local * hidden, width)

    *cot_near, router = call(
        pieces_kernel,
        [shape((rows, wide_width), BF)] * tensor_size + [shape((LANES, width), BF)],
        (t_at, cotangent, routes.T, w_router.T),
        "pieces",
        "sbbb",
        scratch=[pltpu.VMEM((seq_len, LANES), F32)],
        limit=58,
    )
    cot_got = spread(cot_near[0], "expert")
    cot_got[0], tokens = tied(cot_got[0], tokens)

    heads, keys_wide = w_query.shape[1], w_key.shape[1]
    n_one, q, k, v, o, lse, xq, *rest = call(
        attend_kernel,
        [
            shape((seq_len, width), BF),
            shape((seq_len, heads), BF),
            shape((seq_len, keys_wide), BF),
            shape((seq_len, keys_wide), BF),
            shape((seq_len, heads), BF),
            shape((seq_len, LANES), F32),
            shape((rows, width), BF),
        ]
        + [shape((rows, width), F32)]
        + [shape((rows, width), BF)] * last,
        (t_at, tokens, gain_one, w_query, w_key, w_value, w_output, cosine, sine),
        "attend",
        "s" + "b" * 8,
        "bbbbbbv",
        scratch=[pltpu.VMEM((seq_len, width), F32)],
        limit=58,
        flops=2 * seq_len * width * 4 * heads,
    )
    parts = rest
    got = [swap(parts[r], "tensor", r) for r in around]
    h, n_two = call(
        norm_two_kernel,
        [shape((rows, width), F32), shape((rows, width), BF)],
        (xq, gain_two, parts[0], *got),
        "norm_two",
        "bbb",
        "vv",
        limit=58,
    )

    n_two, cot_got = tied(n_two, cot_got)
    cot_far = together(cot_got)
    wcat = gate_up_weights(w_gate, w_up)
    two_got = spread(n_two, "expert")
    two_got[0], cot_late = tied(two_got[0], cot_far)
    cot_far = [cot_far] + [swap(cot_far, "tensor", r) for r in range(1, last)]
    cot_far.append(swap(cot_late, "tensor", last))

    first = together([n_two, *two_got])
    twos = [first] + [swap(first, "tensor", r) for r in range(1, last)]
    _, late = tied(cot_far[:last], first)
    twos.append(swap(late, "tensor", last))

    run = functools.partial(
        run_experts, experts, base, router=router, wcat=wcat, down_flat=down_flat
    )
    counts = call(counts_kernel, [shape((1, LANES), F32)], (*cot_near, *cot_far), "counts")[0]
    counts = counts + swap(counts, "dp", 1)
    balance = experts * (counts / (token_count * TOP)) / token_count
    made = [run(twos[0], cot_near[0], cot_far[0], kind=F32)]
    got = []
    for r in around:
        made[-1], (two, cot) = tied(made[-1], (twos[r], cot_far[r]))
        if r == last:
            balance, two = tied(balance, two)
        made.append(run(two, cot_near[r], cot, kind=BF, apart=r == last))
        if r < last:
            got.append(swap(made[-1][3], "tensor", r))
    cots, dgus, hids, ds, moes = zip(*made)
    near_last, *far_last = ds[last]
    from_last = deal(far_last, "expert")
    grads = run_grads(twos, dgus, hids, cots, local, hidden)
    grads, (got, from_last) = tied(grads, (got, from_last))
    near, *across = split_sum([ds[0], *got], "dn_sum")
    through = added([near_last, *from_last], BF, "through")
    across[0], middle = tied(across[0], moes[1:last])
    across = deal(across, "expert")
    near_sums = [near, swap(through, "tensor", last), *across]
    moe_got = [swap(middle[r - 1], "tensor", r) for r in range(1, last)]
    moe_got, near_sums = tied(moe_got, near_sums)

    wide, dh, small = call(
        functools.partial(norm_back_kernel, experts, len(near_sums)),
        [shape((rows, wide_width), BF), shape((rows, width), F32), shape((8, width), F32)],
        (h, n_two, gain_two, router, balance, cot_near[0], *near_sums),
        "norm_back",
        "v",
        "vvv",
    )
    wides = [wide] + [swap(wide, "tensor", r) for r in around]
    _, late_grads = tied(wide, grads)
    grads_got = swap(late_grads, "dp", 1)
    grads_got, wides = tied(grads_got, wides)
    wides, moe_last = tied(wides, moes[last])
    moe_got.append(swap(moe_last, "tensor", last))

    wide_all, dqkv, small, *back_parts = call(
        attend_back_kernel,
        [
            shape((seq_len, wide_width), BF),
            shape((seq_len, heads + 2 * keys_wide), BF),
            shape((8, width), F32),
            shape((rows, width), F32),
        ]
        + [shape((rows, width), BF)] * last,
        (t_at, *wides, tokens, q, k, v, lse, w_query, w_key, w_value, w_output, cosine, sine, small),
        "attend_back",
        "s" + "v" * tensor_size + "b" * 11,
        "bb",
        limit=58,
        scratch=[
            pltpu.VMEM((seq_len, heads), BF),
            pltpu.VMEM((seq_len, width), F32),
        ],
        flops=2 * seq_len * width * 4 * heads,
    )
    part_sums = [back_parts[0]] + [swap(back_parts[r], "tensor", r) for r in around]
    half = width // dp_size
    chunk = half // expert_size

    columns = heads + 2 * keys_wide
    all_columns = columns + heads + LANES
    own_block = pl.BlockSpec((1, rows, width), lambda i: (0, 0, 0))
    kept, sent = call(
        dense_kernel,
        [shape((half, all_columns), F32), shape((half, all_columns), BF)],
        (d_at, *twos, wide_all, o, n_one, dqkv),
        "dense",
        ["s"] + [own_block] * tensor_size + ["b"] * 4,
        "vv",
        limit=54,
        scratch=[
            pltpu.VMEM((seq_len, width), BF),
            pltpu.VMEM((width, all_columns), F32),
        ],
        flops=1,
    )
    mine, *others, small = call(
        kept_and_dealt_kernel,
        [shape((chunk, all_columns), F32)]
        + [shape((chunk, all_columns), BF)] * (expert_size - 1)
        + [shape((8, width), F32)],
        (e_at, kept, swap(sent, "dp", 1), small, swap(small, "dp", 1)),
        "dense_dealt",
        "s",
    )
    others = deal(others, "expert")
    others[0], part_sums = tied(others[0], part_sums)
    moe_near, *moe_across = split_sum([moes[0], *moe_got], "moe_sum")
    moe_sums = [moe_near, *deal(moe_across, "expert")]
    ig = call(
        input_grad_kernel, [shape((rows, width), BF)], (xq, gain_one, dh, *part_sums), "input_grad", "bbbb", limit=58
    )[0]
    igs = [ig] + [swap(ig, "tensor", r) for r in around]
    expert_grads = both_copies(grads, grads_got)
    expert_grads, others = tied(expert_grads, others)
    g_query, g_key, g_value, g_out, g_router, small = call(
        dense_sum_kernel,
        [
            shape((chunk, heads), F32),
            shape((chunk, keys_wide), F32),
            shape((chunk, keys_wide), F32),
            shape((heads, chunk), F32),
            shape((chunk, LANES), F32),
            shape((8, width), F32),
        ],
        (e_at, small, mine, *others),
        "dense_sum",
        "s",
        "bbbbbv",
        scratch=[pltpu.VMEM((expert_size, 8, width), F32)],
    )
    if chunk * HD != 8 * width:
        small = jnp.sum(lax.all_gather(small, "expert"), axis=0)
    igs, small = tied(igs, small)
    input_grad = call(
        natural_kernel, [shape((seq_len, width), F32)], (t_at, *igs), "input_grad_whole", "s", "b"
    )[0]
    out_piece = call(out_kernel, [shape((rows + 16, width), BF)], (h, small, *moe_sums), "out_piece")[0]
    outs = [out_piece] + [swap(out_piece, "tensor", r) for r in around]
    output, small = call(
        out_whole_kernel,
        [shape((seq_len, width), BF), shape((8, width), F32)],
        (t_at, *outs),
        "output",
        "s",
        "bv",
        scratch=[pltpu.VMEM((tensor_size, 8, width), F32)],
    )
    at = (d_me * expert_size + e_me) * chunk
    loss_value = (experts * balance * small[2:3, :LANES])[0, :experts]
    return (
        output,
        loss_value,
        input_grad,
        lax.dynamic_slice(small, (0, at), (1, chunk))[0],
        g_query,
        g_key,
        g_value,
        g_out,
        lax.dynamic_slice(small, (1, at), (1, chunk))[0],
        g_router[:, :experts],
        *expert_grads,
    )


def solution(mesh):
    rows = ("dp", "expert")
    placed = (
        P(rows, None),
        P(rows, None),
        P(),
        P(None, "tensor"),
        P(None, "tensor"),
        P(None, "tensor"),
        P("tensor", None),
        P(),
        P(),
        P("expert", None, "tensor"),
        P("expert", None, "tensor"),
        P("expert", "tensor", None),
        P(rows, None),
    )
    return jax.shard_map(
        on_device,
        mesh=mesh,
        in_specs=placed,
        out_specs=(
            P(rows, None),
            P(),
            P(rows, None),
            P(rows),
            P(rows, "tensor"),
            P(rows, "tensor"),
            P(rows, "tensor"),
            P("tensor", rows),
            P(rows),
            P(rows, None),
            P("expert", None, "tensor"),
            P("expert", None, "tensor"),
            P("expert", "tensor", None),
        ),
        check_vma=False,
    )
```

```python
import functools

import jax
import jax.numpy as jnp
import numpy as np
from jax import lax
from jax.experimental import pallas as pl
from jax.experimental.pallas import tpu as pltpu
from jax.sharding import PartitionSpec as P

HD = 64
TOP = 8
EPS = 1e-06
ROPE_BASE = 10000.0
MASKED = -1e30
BF = jnp.bfloat16
F32 = jnp.float32
FEW = 8
LANES = 128
MIB = 1 << 20


def dot(a, b, dims):
    return lax.dot_general(a, b, (dims, ((), ())), preferred_element_type=F32)


def nn(a, b):
    return dot(a, b, ((1,), (0,)))


def nt(a, b):
    return dot(a, b, ((1,), (1,)))


def tn(a, b):
    return dot(a, b, ((0,), (0,)))


def swap(x, axis, distance):
    size = lax.axis_size(axis)
    return lax.ppermute(x, axis, [(i, i ^ distance) for i in range(size)])


def spread(x, axis):
    size = lax.axis_size(axis)
    if size <= FEW:
        return [swap(x, axis, r) for r in range(1, size)]
    whole = lax.all_gather(x, axis)
    order = jnp.arange(1, size) ^ lax.axis_index(axis)
    return list(jnp.take(whole, order, axis=0))


def deal(parts, axis):
    size = lax.axis_size(axis)
    if size <= FEW:
        return [swap(part, axis, r + 1) for r, part in enumerate(parts)]
    order = jnp.arange(size) ^ lax.axis_index(axis)
    whole = jnp.take(jnp.stack([parts[0], *parts]), order, axis=0)
    back = lax.all_to_all(whole, axis, 0, 0, tiled=True)
    return list(jnp.take(back, order, axis=0)[1:])


def rope_tables(seq_len):
    half = HD // 2
    frequency = ROPE_BASE ** (-(np.arange(half, dtype=np.float32) * 2.0) / HD)
    angles = np.arange(seq_len, dtype=np.float32)[:, None] * frequency[None, :].astype(np.float32)
    cosine, sine = np.cos(angles), np.sin(angles)
    heads = LANES // HD
    return (
        np.tile(cosine, (1, 2 * heads)).astype(np.float32),
        np.tile(np.concatenate([-sine, sine], axis=1), (1, heads)).astype(np.float32),
    )


def lane_of(shape):
    return lax.broadcasted_iota(jnp.int32, shape, 1)


def halves_swapped(x):
    first = lane_of(x.shape) % HD < HD // 2
    half = HD // 2
    return jnp.where(first, pltpu.roll(x, LANES - half, 1), pltpu.roll(x, half, 1))


def low_high(x, head):
    other = pltpu.roll(x.astype(F32), HD, 1).astype(x.dtype)
    low = lane_of(x.shape) < HD
    zero = jnp.zeros_like(x)
    at_low, at_high = (x, other) if head == 0 else (other, x)
    return jnp.where(low, at_low, zero), jnp.where(low, zero, at_high)


def causal(scores):
    rows = lax.broadcasted_iota(jnp.int32, scores.shape, 0)
    return lane_of(scores.shape) <= rows


def shape(dims, kind):
    return jax.ShapeDtypeStruct(dims, kind)


def whole_block(dims):
    return pl.BlockSpec(dims, lambda i: (0,) * len(dims))


def call(kernel, outs, operands, name, places="", out_places="", scratch=(), limit=40, flops=0):
    kinds = {"s": pltpu.SMEM, "v": pltpu.VMEM}

    def spec(place, x):
        if not isinstance(place, str):
            return place
        if place == "b":
            return whole_block(x.shape)
        return pl.BlockSpec(memory_space=kinds[place])

    places = [*places] + ["v"] * (len(operands) - len(places))
    out_places = [*out_places] + ["v"] * (len(outs) - len(out_places))
    return pl.pallas_call(
        kernel,
        grid=(1,),
        out_shape=outs,
        in_specs=[spec(p, x) for p, x in zip(places, operands)],
        out_specs=[spec(p, x) for p, x in zip(out_places, outs)],
        scratch_shapes=list(scratch),
        compiler_params=pltpu.CompilerParams(vmem_limit_bytes=limit * MIB),
        cost_estimate=pl.CostEstimate(flops=int(100.0*(flops)), bytes_accessed=0, transcendentals=0),
        name=name,
    )(*operands)


def tied(first, then):
    return lax.optimization_barrier((first, then))


def pieces_kernel(me_ref, cot_ref, routes_ref, router_ref, *refs):
    cots, (router_out, held) = refs[:-2], refs[-2:]
    rows, width = cots[0].shape[0], cot_ref.shape[1]
    eye = lax.broadcasted_iota(jnp.int32, (TOP, LANES), 0) == lane_of((TOP, LANES))
    held[...] = tn(routes_ref[...].astype(F32).astype(BF), eye.astype(F32).astype(BF))
    for r, c in enumerate(cots):
        start = pl.multiple_of((me_ref[0] ^ r) * rows, rows)
        c[:, :width] = cot_ref[pl.ds(start, rows), :]
        c[:, width:] = held[pl.ds(start, rows), :].astype(BF)
    router_out[...] = jnp.zeros(router_out.shape, BF)
    router_out[: router_ref.shape[0], :] = router_ref[...]


def attend_kernel(
    me_ref, x_ref, gain_ref, wq_ref, wk_ref, wv_ref, wo_ref, cos_ref, sin_ref, *refs
):
    n_ref, q_ref, k_ref, v_ref, o_ref, lse_ref, xq_ref = refs[:7]
    parts, whole = refs[7:-1], refs[-1]
    rows, width = xq_ref.shape
    starts = [pl.multiple_of((me_ref[0] ^ r) * rows, rows) for r in range(4)]
    xq_ref[...] = x_ref[pl.ds(starts[0], rows), :]
    x = x_ref[...].astype(F32)
    inv = lax.rsqrt(jnp.mean(x * x, axis=-1, keepdims=True) + EPS)
    n = (x * inv * gain_ref[...]).astype(BF)
    n_ref[...] = n
    cosine, sine = cos_ref[...], sin_ref[...]
    q, k = nn(n, wq_ref[...]), nn(n, wk_ref[...])
    v_ref[...] = nn(n, wv_ref[...]).astype(BF)
    for at in range(0, q.shape[1], LANES):
        tile = q[:, at : at + LANES]
        q_ref[:, at : at + LANES] = (tile * cosine + halves_swapped(tile) * sine).astype(BF)
    for at in range(0, k.shape[1], LANES):
        tile = k[:, at : at + LANES]
        k_ref[:, at : at + LANES] = (tile * cosine + halves_swapped(tile) * sine).astype(BF)
    lse_all = jnp.zeros(lse_ref.shape, F32)
    for head in range(q.shape[1] // LANES):
        at = head // 2 * LANES
        keys = low_high(k_ref[:, at : at + LANES], head % 2)
        values = low_high(v_ref[:, at : at + LANES], head % 2)
        pair = q_ref[:, head * LANES : (head + 1) * LANES]
        mixed = 0.0
        for g in range(2):
            s = nt(pair, keys[g]) * HD ** (-0.5)
            s = jnp.where(causal(s), s, MASKED)
            peak = jnp.max(s, axis=-1, keepdims=True)
            e = jnp.exp(s - peak)
            total = jnp.sum(e, axis=-1, keepdims=True)
            mixed = mixed + nn((e / total).astype(BF), values[g])
            lse = peak + jnp.log(total)
            lse_all = jnp.where(lane_of(lse_all.shape) == 2 * head + g, lse, lse_all)
        o_ref[:, head * LANES : (head + 1) * LANES] = mixed.astype(BF)
    lse_ref[...] = lse_all
    whole[...] = nn(o_ref[...], wo_ref[...])
    for start, part in zip(starts, parts):
        part[...] = whole[pl.ds(start, rows), :].astype(part.dtype)


def norm_two_kernel(x_ref, gain_ref, own_ref, *refs):
    others, (h_ref, n_ref) = refs[:-2], refs[-2:]
    attn = own_ref[...]
    for other in others:
        attn = attn + other[...].astype(F32)
    h = x_ref[...].astype(F32) + attn
    inv = lax.rsqrt(jnp.mean(h * h, axis=-1, keepdims=True) + EPS)
    h_ref[...] = h
    n_ref[...] = (h * inv * gain_ref[...]).astype(BF)


def together_kernel(*refs):
    pieces, out = refs[:-1], refs[-1]
    at = 0
    for piece in pieces:
        if len(piece.shape) == 2:
            out[at] = piece[...]
            at += 1
        else:
            out[at : at + piece.shape[0]] = piece[...]
            at += piece.shape[0]


def together(pieces):
    count = sum(1 if x.ndim == 2 else x.shape[0] for x in pieces)
    return call(
        together_kernel, [shape((count, *pieces[0].shape[-2:]), pieces[0].dtype)], pieces, "together"
    )[0]


def router_of(rows, router_ref, routes, experts):
    z = nt(rows, router_ref[...])
    lane = lane_of(z.shape)
    z = jnp.where(lane < experts, z, MASKED)
    e = jnp.exp(z - jnp.max(z, axis=-1, keepdims=True))
    probs = e / jnp.sum(e, axis=-1, keepdims=True)
    chosen = chosen_of(lane, routes)
    zc = jnp.where(chosen, z, MASKED)
    ec = jnp.where(chosen, jnp.exp(zc - jnp.max(zc, axis=-1, keepdims=True)), 0.0)
    return probs, ec / jnp.sum(ec, axis=-1, keepdims=True)


def chosen_of(lane, routes):
    place, named = lane.astype(F32), routes.astype(F32)
    chosen = place == named[:, 0:1]
    for k in range(1, TOP):
        chosen = chosen | (place == named[:, k : k + 1])
    return chosen


def counts_kernel(*refs):
    pieces, out = refs[:-1], refs[-1]
    total = 0.0
    for piece in pieces:
        width = piece.shape[-1] - LANES
        blocks = [piece[:, width:]] if len(piece.shape) == 2 else [
            piece[i, :, width:] for i in range(piece.shape[0])
        ]
        for routes in blocks:
            named = chosen_of(lane_of(routes.shape), routes).astype(F32)
            total = total + jnp.sum(named, axis=0, keepdims=True)
    out[...] = total


def weights_kernel(wg_ref, wu_ref, out_ref):
    hidden = wg_ref.shape[2]
    out_ref[:, :hidden] = wg_ref[0]
    out_ref[:, hidden:] = wu_ref[0]


def gate_up_weights(w_gate, w_up):
    local, width, hidden = w_gate.shape
    block = pl.BlockSpec((1, width, hidden), lambda e: (e, 0, 0))
    return pl.pallas_call(
        weights_kernel,
        grid=(local,),
        in_specs=[block, block],
        out_specs=pl.BlockSpec((width, 2 * hidden), lambda e: (0, e)),
        out_shape=shape((width, 2 * hidden * local), BF),
        compiler_params=pltpu.CompilerParams(vmem_limit_bytes=30 * MIB),
        cost_estimate=pl.CostEstimate(flops=int(100.0*(0)), bytes_accessed=4 * w_gate.size * 2, transcendentals=0),
        name="gate_up_weights",
    )(w_gate, w_up)


def experts_kernel(experts, base_ref, x_ref, own_ref, far_ref, router_ref, wcat, wd_ref, *refs):
    cot_ref, dgu_ref, hg_ref, *ds, m_ref = refs
    hidden = LANES
    pair = 2 * hidden
    rows, width = cot_ref.shape
    x = x_ref[...].reshape(rows, width)
    if far_ref is None:
        routes = own_ref[:, width:]
        cot_ref[...] = own_ref[:, :width]
    else:
        pieces = [own_ref[...]] + [far_ref[i] for i in range(far_ref.shape[0])]
        routes = jnp.concatenate([piece[:, width:] for piece in pieces], axis=0)
        cot_ref[...] = jnp.concatenate([piece[:, :width] for piece in pieces], axis=0)
    _, gates = router_of(x, router_ref, routes, experts)
    lane = lane_of(gates.shape)
    dots = jnp.zeros(gates.shape, F32)
    for e in range(hg_ref.shape[1] // hidden):
        mine = lane == base_ref[0] + e
        g = jnp.sum(jnp.where(mine, gates, 0.0), axis=-1, keepdims=True)
        both = nn(x, wcat[:, e * pair : (e + 1) * pair])
        v = nt(cot_ref[...], wd_ref[e * hidden : (e + 1) * hidden, :])
        gate, up = both[:, :hidden], both[:, hidden:]
        sig = 1.0 / (1.0 + jnp.exp(-gate))
        act = gate * sig
        hid = act * up
        dots = jnp.where(mine, jnp.sum(hid * v, axis=-1, keepdims=True), dots)
        gv = g * v
        hg_ref[:, e * hidden : (e + 1) * hidden] = (g * hid).astype(BF)
        d_gate = gv * up * sig * (1.0 + gate * (1.0 - sig))
        dgu_ref[:, e * pair : e * pair + hidden] = d_gate.astype(BF)
        dgu_ref[:, e * pair + hidden : (e + 1) * pair] = (gv * act).astype(BF)

    def put(outs, columns, value):
        at = 0
        for out in outs:
            part = value.astype(out.dtype)
            if len(out.shape) == 2:
                out[:, columns] = part[at : at + out.shape[0]]
                at += out.shape[0]
            else:
                step = out.shape[1]
                for i in range(out.shape[0]):
                    out[i, :, columns] = part[i * step : (i + 1) * step]

    put(ds, slice(width, width + LANES), dots)
    step = 256
    for at in range(0, width, step):
        put(ds, slice(at, at + step), nt(dgu_ref[...], wcat[at : at + step, :]))
    put([m_ref], slice(0, width), nn(hg_ref[...], wd_ref[...]))


def run_experts(experts, base, x, own, far, router, wcat, down_flat, kind, apart=False):
    count, rows, width = x.shape
    inner = down_flat.shape[0]
    wide = width + LANES
    total = count * rows
    few = count <= FEW
    step = total if few else 256
    resident = pl.BlockSpec(memory_space=pltpu.VMEM)
    per = lambda w: resident if few else pl.BlockSpec((step, w), lambda i: (i, 0))
    kernel = functools.partial(experts_kernel, experts)
    if few:
        data, dims = [x, own, far], lambda w: (count, rows, w)
    else:
        joined = jnp.concatenate([own[None], far], axis=0)
        data, dims = [x.reshape(total, width), joined.reshape(total, wide)], lambda w: (total, w)
        whole_kernel = kernel
        kernel = lambda b, x, c, *refs: whole_kernel(b, x, c, None, *refs)
    if few and apart:
        d_shapes = [shape((rows, wide), BF if i else F32) for i in range(count)]
    else:
        d_shapes = [shape(dims(wide), kind)]
    cot, dgu, hid, *d, m = pl.pallas_call(
        kernel,
        grid=(total // step,),
        in_specs=[pl.BlockSpec(memory_space=pltpu.SMEM)]
        + [per(z.shape[-1]) for z in data]
        + [resident] * 3,
        out_specs=[per(width), per(2 * inner), per(inner)]
        + [per(wide)] * len(d_shapes)
        + [per(width)],
        out_shape=[
            shape((total, width), BF),
            shape((total, 2 * inner), BF),
            shape((total, inner), BF),
            *d_shapes,
            shape(dims(width), kind),
        ],
        compiler_params=pltpu.CompilerParams(vmem_limit_bytes=(14 if few else 30) * MIB),
        cost_estimate=pl.CostEstimate(flops=int(100.0*(total * width * inner // 8)), bytes_accessed=0, transcendentals=0),
        name="experts",
    )(base, *data, router, wcat, down_flat)
    if not few:
        d = list(d[0].reshape(count, rows, wide)) if apart else [d[0].reshape(count, rows, wide)]
    return cot, dgu, hid, d if apart else d[0], m.reshape(count, rows, width)


def split_sum_kernel(count, near, *refs):
    ins, outs = refs[:count], refs[count:]
    for s in range(ins[0].shape[0]):
        total = ins[0][s].astype(F32)
        for x in ins[1:]:
            total = total + x[s].astype(F32)
        outs[s][...] = total.astype(outs[s].dtype)


def split_sum(arrays, name):
    count, *dims = arrays[0].shape
    outs = [shape(dims, F32)] + [shape(dims, BF)] * (count - 1)
    return call(functools.partial(split_sum_kernel, len(arrays), True), outs, arrays, name)


def add_kernel(*refs):
    pieces, out = refs[:-1], refs[-1]
    total = pieces[0][...].astype(F32)
    for piece in pieces[1:]:
        total = total + piece[...].astype(F32)
    out[...] = total.astype(out.dtype)


def added(pieces, kind, name):
    return call(add_kernel, [shape(pieces[0].shape, kind)], pieces, name)[0]


def grads_kernel(*refs):
    ns, dgus, hs, cs = (refs[4 * i : 4 * i + 4] for i in range(4))
    out_ref = refs[16]
    hidden, width = hs[0].shape[1], ns[0].shape[1]
    both, down = 0.0, 0.0
    for n, dgu, h, c in zip(ns, dgus, hs, cs):
        both = both + tn(n[...], dgu[...])
        down = down + tn(h[...], c[...])
    out_ref[0, :width, :] = both[:, :hidden].astype(BF)
    out_ref[0, width : 2 * width, :] = both[:, hidden:].astype(BF)
    for at in range(0, width, hidden):
        out_ref[0, 2 * width + at : 2 * width + at + hidden, :] = down[:, at : at + hidden].astype(BF)


def run_grads(n, dgu, h, c, local, hidden):
    width = n[0].shape[-1]
    flat = lambda xs: [x.reshape(-1, x.shape[-1]) for x in xs]
    n, c = flat(n), flat(c)
    whole = lambda xs: [pl.BlockSpec(x.shape, lambda e: (0, 0)) for x in xs]
    cols = lambda xs, w: [pl.BlockSpec((x.shape[0], w), lambda e: (0, e)) for x in xs]
    few = n[0].shape[0] <= 512
    return pl.pallas_call(
        grads_kernel,
        grid=(local,),
        in_specs=whole(n) + cols(dgu, 2 * hidden) + cols(h, hidden) + whole(c),
        out_specs=pl.BlockSpec((1, 3 * width, hidden), lambda e: (e, 0, 0)),
        out_shape=shape((local, 3 * width, hidden), BF),
        compiler_params=pltpu.CompilerParams(vmem_limit_bytes=(20 if few else 58) * MIB),
        cost_estimate=pl.CostEstimate(flops=int(100.0*(24 * n[0].size * hidden * local)), bytes_accessed=0, transcendentals=0),
        name="expert_grads",
    )(*n, *dgu, *h, *c)


def both_copies_kernel(mine_ref, other_ref, gate_ref, up_ref, down_ref):
    width, hidden = gate_ref.shape[1:]

    def total(at, count):
        rows = pl.ds(at, count)
        return mine_ref[0, rows, :].astype(F32) + other_ref[0, rows, :].astype(F32)

    gate_ref[0] = total(0, width)
    up_ref[0] = total(width, width)
    for at in range(0, width, hidden):
        down_ref[0, :, at : at + hidden] = total(2 * width + at, hidden)


def both_copies(mine, other):
    local, rows, hidden = mine.shape
    width = rows // 3
    block = lambda *dims: pl.BlockSpec((1, *dims), lambda e: (e, 0, 0))
    return pl.pallas_call(
        both_copies_kernel,
        grid=(local,),
        in_specs=[block(rows, hidden)] * 2,
        out_specs=[block(width, hidden), block(width, hidden), block(hidden, width)],
        out_shape=[
            shape((local, width, hidden), F32),
            shape((local, width, hidden), F32),
            shape((local, hidden, width), F32),
        ],
        compiler_params=pltpu.CompilerParams(vmem_limit_bytes=58 * MIB),
        cost_estimate=pl.CostEstimate(flops=int(100.0*(0)), bytes_accessed=8 * mine.size, transcendentals=0),
        name="both_copies",
    )(mine, other)


def norm_back_kernel(experts, count, h_ref, n_ref, gain_ref, router_ref, bal_ref, cot_ref, *refs):
    sums, (wide_ref, dh_ref, small_ref) = refs[:count], refs[count:]
    near = sums[0][...].astype(F32)
    for other in sums[1:]:
        near = near + other[...].astype(F32)
    rows, width = h_ref.shape
    dots = near[:, width:]
    probs, gates = router_of(n_ref[...], router_ref, cot_ref[:, width:], experts)
    bal = bal_ref[...]
    d_chosen = gates * (dots - jnp.sum(gates * dots, axis=-1, keepdims=True))
    dz = probs * (bal - jnp.sum(probs * bal, axis=-1, keepdims=True)) + d_chosen
    dz = dz.astype(BF)
    wide_ref[:, width:] = dz
    dn = near[:, :width] + nn(dz, router_ref[...])
    h = h_ref[...]
    inv = lax.rsqrt(jnp.mean(h * h, axis=-1, keepdims=True) + EPS)
    u = gain_ref[...] * dn
    dy = cot_ref[:, :width].astype(F32)
    dh = dy + inv * u - h * (inv * inv * inv * jnp.mean(u * h, axis=-1, keepdims=True))
    dh_ref[...] = dh
    wide_ref[:, :width] = dh.astype(BF)
    small_ref[...] = jnp.zeros(small_ref.shape, F32)
    small_ref[1:2, :] = jnp.sum(dn * h * inv, axis=0, keepdims=True)
    small_ref[2:3, : probs.shape[1]] = jnp.sum(probs, axis=0, keepdims=True)


def attend_back_kernel(
    me_ref, w0, w1, w2, w3, x_ref, q_ref, k_ref, v_ref, lse_ref, wq_ref, wk_ref, wv_ref, wo_ref, cos_ref, sin_ref,
    small_in, a0, a1, a2, a3, o_ref, n_ref, small_ref, p0, p1, p2, p3, kept_ref, sent_ref,
    do_ref, whole, wide_ref, dq_ref, two_ref, dense
):
    rows = w0.shape[0]
    width = x_ref.shape[1]
    for r, piece in enumerate((w0, w1, w2, w3)):
        start = pl.multiple_of((me_ref[1] ^ r) * rows, rows)
        wide_ref[pl.ds(start, rows), :] = piece[...]
    do_ref[...] = nt(wide_ref[:, :width], wo_ref[...]).astype(BF)
    cosine, sine = cos_ref[...], sin_ref[...]
    scale = HD ** (-0.5)
    heads, keys_wide = q_ref.shape[1], k_ref.shape[1]
    dk_tiles = [0.0] * (keys_wide // LANES)
    dv_tiles = [0.0] * (keys_wide // LANES)

    def back(tile):
        return (tile * cosine - halves_swapped(tile) * sine).astype(BF)

    for head in range(heads // LANES):
        at = head // 2 * LANES
        side = head % 2
        keys = low_high(k_ref[:, at : at + LANES], side)
        values = low_high(v_ref[:, at : at + LANES], side)
        pair = q_ref[:, head * LANES : (head + 1) * LANES]
        grad = do_ref[:, head * LANES : (head + 1) * LANES]
        dq = 0.0
        dk, dv = [], []
        for g in range(2):
            s = nt(pair, keys[g]) * scale
            lse = lse_ref[:, 2 * head + g : 2 * head + g + 1]
            p = jnp.where(causal(s), jnp.exp(s - lse), 0.0)
            dp = nt(grad, values[g])
            ds = (p * (dp - jnp.sum(p * dp, axis=-1, keepdims=True))).astype(BF)
            dq = dq + nn(ds, keys[g])
            dk.append(tn(ds, pair))
            dv.append(tn(p.astype(BF), grad))
        dq_ref[:, head * LANES : (head + 1) * LANES] = back(dq * scale)
        mine = lane_of(dk[0].shape) < HD
        if side == 0:
            dk_sum = jnp.where(mine, dk[0] + pltpu.roll(dk[1], HD, 1), 0.0)
            dv_sum = jnp.where(mine, dv[0] + pltpu.roll(dv[1], HD, 1), 0.0)
        else:
            dk_sum = jnp.where(mine, 0.0, pltpu.roll(dk[0], HD, 1) + dk[1])
            dv_sum = jnp.where(mine, 0.0, pltpu.roll(dv[0], HD, 1) + dv[1])
        dk_tiles[head // 2] = dk_tiles[head // 2] + dk_sum
        dv_tiles[head // 2] = dv_tiles[head // 2] + dv_sum
    for i, tile in enumerate(dk_tiles):
        at = heads + i * LANES
        dq_ref[:, at : at + LANES] = back(tile * scale)
    for i, tile in enumerate(dv_tiles):
        at = heads + keys_wide + i * LANES
        dq_ref[:, at : at + LANES] = tile.astype(BF)
    dn = nt(dq_ref[:, :heads], wq_ref[...])
    dn = dn + nt(dq_ref[:, heads : heads + keys_wide], wk_ref[...])
    whole[...] = dn + nt(dq_ref[:, heads + keys_wide :], wv_ref[...])
    x = x_ref[...].astype(F32)
    inv = lax.rsqrt(jnp.mean(x * x, axis=-1, keepdims=True) + EPS)
    small_ref[...] = small_in[...]
    small_ref[0:1, :] = jnp.sum(whole[...] * x * inv, axis=0, keepdims=True)
    for r, part in enumerate((p0, p1, p2, p3)):
        start = pl.multiple_of((me_ref[1] ^ r) * rows, rows)
        part[...] = whole[pl.ds(start, rows), :].astype(part.dtype)
    for r, piece in enumerate((a0, a1, a2, a3)):
        start = pl.multiple_of((me_ref[1] ^ r) * rows, rows)
        two_ref[pl.ds(start, rows), :] = piece[0]
    columns = dq_ref.shape[1]
    dense[:, :columns] = tn(n_ref[...], dq_ref[...])
    dense[:, columns : columns + heads] = tn(wide_ref[:, :width], o_ref[...])
    dense[:, columns + heads :] = tn(two_ref[...], wide_ref[:, width:])
    half = kept_ref.shape[0]
    kept_ref[...] = dense[pl.ds(pl.multiple_of(me_ref[0] * half, half), half), :]
    sent_ref[...] = dense[pl.ds(pl.multiple_of((1 - me_ref[0]) * half, half), half), :].astype(BF)


def input_grad_kernel(x_ref, gain_ref, dh_ref, *refs):
    parts, ig_ref = refs[:-1], refs[-1]
    x = x_ref[...].astype(F32)
    inv = lax.rsqrt(jnp.mean(x * x, axis=-1, keepdims=True) + EPS)
    dn = parts[0][...].astype(F32)
    for part in parts[1:]:
        dn = dn + part[...].astype(F32)
    u = gain_ref[...] * dn
    ig = dh_ref[...] + inv * u - x * (inv * inv * inv * jnp.mean(u * x, axis=-1, keepdims=True))
    ig_ref[...] = ig.astype(BF)


def out_kernel(h_ref, small_ref, *refs):
    moes, out_ref = refs[:-1], refs[-1]
    rows = h_ref.shape[0]
    out = h_ref[...]
    for moe in moes:
        out = out + moe[...].astype(F32)
    out_ref[:rows, :] = out.astype(BF)
    small = small_ref[...]
    high = small.astype(BF).astype(F32)
    out_ref[rows:, :] = jnp.concatenate([high, small - high], axis=0).astype(BF)


def natural_kernel(me_ref, *refs):
    pieces, out = refs[:-1], refs[-1]
    rows = pieces[0].shape[0]
    for r, piece in enumerate(pieces):
        start = pl.multiple_of((me_ref[0] ^ r) * rows, rows)
        out[pl.ds(start, rows), :] = piece[...].astype(out.dtype)


def out_whole_kernel(me_ref, *refs):
    pieces, (out_ref, small_ref, held) = refs[:-3], refs[-3:]
    rows = pieces[0].shape[0] - 16
    for r, piece in enumerate(pieces):
        start = pl.multiple_of((me_ref[0] ^ r) * rows, rows)
        out_ref[pl.ds(start, rows), :] = piece[:rows, :]
        both = piece[rows:, :].astype(F32)
        held[me_ref[0] ^ r] = both[:8] + both[8:]
    total = held[0]
    for i in range(1, len(pieces)):
        total = total + held[i]
    small_ref[...] = total


def kept_and_dealt_kernel(me_ref, kept_ref, got_ref, small_ref, small_got_ref, *outs):
    small_out, outs = outs[-1], outs[:-1]
    small = small_ref[...] + small_got_ref[...]
    high = small[:4].astype(BF).astype(F32)
    both = jnp.concatenate([high, small[:4] - high], axis=0).astype(BF).astype(F32)
    small_out[...] = both
    rows, columns = outs[0].shape
    upper = lane_of((8, LANES)) >= HD
    parts = []
    for at in range(0, both.shape[1], LANES):
        tile = both[:, at : at + LANES]
        parts += [jnp.where(upper, pltpu.roll(tile, HD, 1), 0.0), jnp.where(upper, tile, 0.0)]
    if len(parts) * 8 == rows:
        extra = jnp.concatenate(parts, axis=0)
    else:
        extra = jnp.zeros((rows, LANES), F32)
    for r, out in enumerate(outs):
        start = pl.multiple_of((me_ref[0] ^ r) * rows, rows)
        at = pl.ds(start, rows)
        total = kept_ref[at, :] + got_ref[at, :].astype(F32)
        out[:, : columns - LANES] = total[:, : columns - LANES].astype(out.dtype)
        out[:, columns - LANES :] = (total[:, columns - LANES :] + extra).astype(out.dtype)


def dense_sum_kernel(me_ref, small_ref, mine_ref, *refs):
    others, outs, held = refs[:-7], refs[-7:-1], refs[-1]
    q_ref, k_ref, v_ref, o_ref, r_ref, small_out = outs
    total = mine_ref[...]
    for other in others:
        total = total + other[...].astype(F32)
    at = 0
    for out in (q_ref, k_ref, v_ref):
        out[...] = total[:, at : at + out.shape[1]]
        at += out.shape[1]
    o_ref[...] = total[:, at : at + o_ref.shape[0]].T
    at += o_ref.shape[0]
    r_ref[...] = total[:, at : at + r_ref.shape[1]]
    held[me_ref[0]] = small_ref[...]
    if total.shape[0] * HD != 8 * small_ref.shape[1]:
        others = []
    lower = lane_of((8, LANES)) < HD
    for i, other in enumerate(others):
        for j in range(small_ref.shape[1] // LANES):
            first = other[16 * j : 16 * j + 16, at : at + LANES].astype(F32)
            tile = jnp.where(lower, pltpu.roll(first[:8], HD, 1), first[8:])
            held[me_ref[0] ^ (i + 1), :, j * LANES : (j + 1) * LANES] = tile
    small = held[0] if others else small_ref[...]
    for i in range(1, len(others) + 1):
        small = small + held[i]
    small_out[...] = jnp.concatenate([small[:4] + small[4:], jnp.zeros_like(small[:4])], axis=0)


def on_device(
    tokens,
    routes,
    gain_first,
    w_query,
    w_key,
    w_value,
    w_output,
    gain_second,
    w_router,
    w_gate,
    w_up,
    w_down,
    cotangent,
):
    seq_len, width = tokens.shape
    experts = w_router.shape[1]
    local, _, hidden = w_gate.shape
    tensor_size = lax.axis_size("tensor")
    expert_size = lax.axis_size("expert")
    dp_size = lax.axis_size("dp")
    token_count = seq_len * dp_size * expert_size
    rows = seq_len // tensor_size
    wide_width = width + LANES
    last = tensor_size - 1
    around = range(1, tensor_size)
    t_me, e_me, d_me = lax.axis_index("tensor"), lax.axis_index("expert"), lax.axis_index("dp")
    t_at = t_me.astype(jnp.int32).reshape(1)
    e_at = e_me.astype(jnp.int32).reshape(1)
    base = (e_me * local).astype(jnp.int32).reshape(1)
    d_at = jnp.stack([d_me, t_me]).astype(jnp.int32)
    cosine, sine = rope_tables(seq_len)
    gain_one, gain_two = gain_first[None], gain_second[None]
    down_flat = w_down.reshape(local * hidden, width)

    *cot_near, router = call(
        pieces_kernel,
        [shape((rows, wide_width), BF)] * tensor_size + [shape((LANES, width), BF)],
        (t_at, cotangent, routes.T, w_router.T),
        "pieces",
        "sbbb",
        scratch=[pltpu.VMEM((seq_len, LANES), F32)],
        limit=58,
    )
    cot_got = spread(cot_near[0], "expert")
    cot_got[0], tokens = tied(cot_got[0], tokens)

    heads, keys_wide = w_query.shape[1], w_key.shape[1]
    n_one, q, k, v, o, lse, xq, *rest = call(
        attend_kernel,
        [
            shape((seq_len, width), BF),
            shape((seq_len, heads), BF),
            shape((seq_len, keys_wide), BF),
            shape((seq_len, keys_wide), BF),
            shape((seq_len, heads), BF),
            shape((seq_len, LANES), F32),
            shape((rows, width), BF),
        ]
        + [shape((rows, width), F32)]
        + [shape((rows, width), BF)] * last,
        (t_at, tokens, gain_one, w_query, w_key, w_value, w_output, cosine, sine),
        "attend",
        "s" + "b" * 8,
        "bbbbbbv",
        scratch=[pltpu.VMEM((seq_len, width), F32)],
        limit=58,
        flops=2 * seq_len * width * 4 * heads,
    )
    parts = rest
    got = [swap(parts[r], "tensor", r) for r in around]
    h, n_two = call(
        norm_two_kernel,
        [shape((rows, width), F32), shape((rows, width), BF)],
        (xq, gain_two, parts[0], *got),
        "norm_two",
        "bbb",
        "vv",
        limit=58,
    )

    n_two, cot_got = tied(n_two, cot_got)
    cot_far = together(cot_got)
    wcat = gate_up_weights(w_gate, w_up)
    two_got = spread(n_two, "expert")
    two_got[0], cot_late = tied(two_got[0], cot_far)
    cot_far = [cot_far] + [swap(cot_far, "tensor", r) for r in range(1, last)]
    cot_far.append(swap(cot_late, "tensor", last))

    first = together([n_two, *two_got])
    twos = [first] + [swap(first, "tensor", r) for r in range(1, last)]
    _, late = tied(cot_far[:last], first)
    twos.append(swap(late, "tensor", last))

    run = functools.partial(
        run_experts, experts, base, router=router, wcat=wcat, down_flat=down_flat
    )
    counts = call(counts_kernel, [shape((1, LANES), F32)], (*cot_near, *cot_far), "counts")[0]
    counts = counts + swap(counts, "dp", 1)
    balance = experts * (counts / (token_count * TOP)) / token_count
    made = [run(twos[0], cot_near[0], cot_far[0], kind=F32)]
    got = []
    for r in around:
        made[-1], (two, cot) = tied(made[-1], (twos[r], cot_far[r]))
        if r == last:
            balance, two = tied(balance, two)
        made.append(run(two, cot_near[r], cot, kind=BF, apart=r == last))
        if r < last:
            got.append(swap(made[-1][3], "tensor", r))
    cots, dgus, hids, ds, moes = zip(*made)
    near_last, *far_last = ds[last]
    from_last = deal(far_last, "expert")
    grads = run_grads(twos, dgus, hids, cots, local, hidden)
    grads, (got, from_last) = tied(grads, (got, from_last))
    near, *across = split_sum([ds[0], *got], "dn_sum")
    through = added([near_last, *from_last], BF, "through")
    across[0], middle = tied(across[0], moes[1:last])
    across = deal(across, "expert")
    near_sums = [near, swap(through, "tensor", last), *across]
    moe_got = [swap(middle[r - 1], "tensor", r) for r in range(1, last)]
    moe_got, near_sums = tied(moe_got, near_sums)

    wide, dh, small = call(
        functools.partial(norm_back_kernel, experts, len(near_sums)),
        [shape((rows, wide_width), BF), shape((rows, width), F32), shape((8, width), F32)],
        (h, n_two, gain_two, router, balance, cot_near[0], *near_sums),
        "norm_back",
        "v",
        "vvv",
    )
    wides = [wide] + [swap(wide, "tensor", r) for r in around]
    _, late_grads = tied(wide, grads)
    grads_got = swap(late_grads, "dp", 1)
    grads_got, wides = tied(grads_got, wides)
    half = width // dp_size
    chunk = half // expert_size
    columns = heads + 2 * keys_wide
    all_columns = columns + heads + LANES
    own_block = pl.BlockSpec((1, rows, width), lambda i: (0, 0, 0))
    small, *back_parts, kept, sent = call(
        attend_back_kernel,
        [shape((8, width), F32), shape((rows, width), F32)]
        + [shape((rows, width), BF)] * last
        + [shape((half, all_columns), F32), shape((half, all_columns), BF)],
        (d_at, *wides, tokens, q, k, v, lse, w_query, w_key, w_value, w_output, cosine, sine, small)
        + (*twos, o, n_one),
        "attend_back",
        ["s"] + ["v"] * tensor_size + ["b"] * 12 + [own_block] * tensor_size + ["b"] * 2,
        "bvvvvbb",
        limit=58,
        scratch=[
            pltpu.VMEM((seq_len, heads), BF),
            pltpu.VMEM((seq_len, width), F32),
            pltpu.VMEM((seq_len, wide_width), BF),
            pltpu.VMEM((seq_len, columns), BF),
            pltpu.VMEM((seq_len, width), BF),
            pltpu.VMEM((width, all_columns), F32),
        ],
        flops=2 * seq_len * width * 4 * heads,
    )
    part_sums = [back_parts[0]] + [swap(back_parts[r], "tensor", r) for r in around]
    sent = swap(sent, "dp", 1)
    mine, *others, small = call(
        kept_and_dealt_kernel,
        [shape((chunk, all_columns), F32)]
        + [shape((chunk, all_columns), BF)] * (expert_size - 1)
        + [shape((8, width), F32)],
        (e_at, kept, sent, small, swap(small, "dp", 1)),
        "dense_dealt",
        "sbbbb",
        limit=58,
    )
    others = deal(others, "expert")
    expert_grads = both_copies(grads, grads_got)
    (expert_grads, others[0]), part_sums = tied((expert_grads, others[0]), part_sums)
    _, moe_last = tied(part_sums, moes[last])
    moe_got.append(swap(moe_last, "tensor", last))
    moe_near, *moe_across = split_sum([moes[0], *moe_got], "moe_sum")
    moe_sums = [moe_near, *deal(moe_across, "expert")]
    ig = call(
        input_grad_kernel, [shape((rows, width), BF)], (xq, gain_one, dh, *part_sums), "input_grad", "bbbb", limit=58
    )[0]
    igs = [ig] + [swap(ig, "tensor", r) for r in around]
    g_query, g_key, g_value, g_out, g_router, small = call(
        dense_sum_kernel,
        [
            shape((chunk, heads), F32),
            shape((chunk, keys_wide), F32),
            shape((chunk, keys_wide), F32),
            shape((heads, chunk), F32),
            shape((chunk, LANES), F32),
            shape((8, width), F32),
        ],
        (e_at, small, mine, *others),
        "dense_sum",
        "s",
        "bbbbbv",
        scratch=[pltpu.VMEM((expert_size, 8, width), F32)],
    )
    if chunk * HD != 8 * width:
        small = jnp.sum(lax.all_gather(small, "expert"), axis=0)
    igs, small = tied(igs, small)
    input_grad = call(
        natural_kernel, [shape((seq_len, width), F32)], (t_at, *igs), "input_grad_whole", "s", "b"
    )[0]
    out_piece = call(out_kernel, [shape((rows + 16, width), BF)], (h, small, *moe_sums), "out_piece")[0]
    outs = [out_piece] + [swap(out_piece, "tensor", r) for r in around]
    output, small = call(
        out_whole_kernel,
        [shape((seq_len, width), BF), shape((8, width), F32)],
        (t_at, *outs),
        "output",
        "s",
        "bv",
        scratch=[pltpu.VMEM((tensor_size, 8, width), F32)],
    )
    at = (d_me * expert_size + e_me) * chunk
    loss_value = (experts * balance * small[2:3, :LANES])[0, :experts]
    return (
        output,
        loss_value,
        input_grad,
        lax.dynamic_slice(small, (0, at), (1, chunk))[0],
        g_query,
        g_key,
        g_value,
        g_out,
        lax.dynamic_slice(small, (1, at), (1, chunk))[0],
        g_router[:, :experts],
        *expert_grads,
    )


def solution(mesh):
    rows = ("dp", "expert")
    placed = (
        P(rows, None),
        P(rows, None),
        P(),
        P(None, "tensor"),
        P(None, "tensor"),
        P(None, "tensor"),
        P("tensor", None),
        P(),
        P(),
        P("expert", None, "tensor"),
        P("expert", None, "tensor"),
        P("expert", "tensor", None),
        P(rows, None),
    )
    return jax.shard_map(
        on_device,
        mesh=mesh,
        in_specs=placed,
        out_specs=(
            P(rows, None),
            P(),
            P(rows, None),
            P(rows),
            P(rows, "tensor"),
            P(rows, "tensor"),
            P(rows, "tensor"),
            P("tensor", rows),
            P(rows),
            P(rows, None),
            P("expert", None, "tensor"),
            P("expert", None, "tensor"),
            P("expert", "tensor", None),
        ),
        check_vma=False,
    )
```

```python
import functools

import jax
import jax.numpy as jnp
import numpy as np
from jax import lax
from jax.experimental import pallas as pl
from jax.experimental.pallas import tpu as pltpu
from jax.sharding import PartitionSpec as P

HD = 64
TOP = 8
EPS = 1e-06
ROPE_BASE = 10000.0
MASKED = -1e30
BF = jnp.bfloat16
F32 = jnp.float32
FEW = 8
LANES = 128
MIB = 1 << 20


def dot(a, b, dims):
    return lax.dot_general(a, b, (dims, ((), ())), preferred_element_type=F32)


def nn(a, b):
    return dot(a, b, ((1,), (0,)))


def nt(a, b):
    return dot(a, b, ((1,), (1,)))


def tn(a, b):
    return dot(a, b, ((0,), (0,)))


def swap(x, axis, distance):
    size = lax.axis_size(axis)
    return lax.ppermute(x, axis, [(i, i ^ distance) for i in range(size)])


def backwards(make, size):
    return [make(r) for r in range(size - 1, 0, -1)][::-1]


def spread(x, axis):
    size = lax.axis_size(axis)
    if size <= FEW:
        return backwards(lambda r: swap(x, axis, r), size)
    whole = lax.all_gather(x, axis)
    order = jnp.arange(1, size) ^ lax.axis_index(axis)
    return list(jnp.take(whole, order, axis=0))


def deal(parts, axis):
    size = lax.axis_size(axis)
    if size <= FEW:
        return backwards(lambda r: swap(parts[r - 1], axis, r), size)
    order = jnp.arange(size) ^ lax.axis_index(axis)
    whole = jnp.take(jnp.stack([parts[0], *parts]), order, axis=0)
    back = lax.all_to_all(whole, axis, 0, 0, tiled=True)
    return list(jnp.take(back, order, axis=0)[1:])


def rope_tables(seq_len):
    half = HD // 2
    frequency = ROPE_BASE ** (-(np.arange(half, dtype=np.float32) * 2.0) / HD)
    angles = np.arange(seq_len, dtype=np.float32)[:, None] * frequency[None, :].astype(np.float32)
    cosine, sine = np.cos(angles), np.sin(angles)
    heads = LANES // HD
    return (
        np.tile(cosine, (1, 2 * heads)).astype(np.float32),
        np.tile(np.concatenate([-sine, sine], axis=1), (1, heads)).astype(np.float32),
    )


def lane_of(shape):
    return lax.broadcasted_iota(jnp.int32, shape, 1)


def halves_swapped(x):
    first = lane_of(x.shape) % HD < HD // 2
    half = HD // 2
    return jnp.where(first, pltpu.roll(x, LANES - half, 1), pltpu.roll(x, half, 1))


def low_high(x, head):
    other = pltpu.roll(x.astype(F32), HD, 1).astype(x.dtype)
    low = lane_of(x.shape) < HD
    zero = jnp.zeros_like(x)
    at_low, at_high = (x, other) if head == 0 else (other, x)
    return jnp.where(low, at_low, zero), jnp.where(low, zero, at_high)


def causal(scores):
    rows = lax.broadcasted_iota(jnp.int32, scores.shape, 0)
    return lane_of(scores.shape) <= rows


def shape(dims, kind):
    return jax.ShapeDtypeStruct(dims, kind)


def whole_block(dims):
    return pl.BlockSpec(dims, lambda i: (0,) * len(dims))


def call(kernel, outs, operands, name, places="", out_places="", scratch=(), limit=40, flops=0):
    kinds = {"s": pltpu.SMEM, "v": pltpu.VMEM}

    def spec(place, x):
        if not isinstance(place, str):
            return place
        if place == "b":
            return whole_block(x.shape)
        return pl.BlockSpec(memory_space=kinds[place])

    places = [*places] + ["v"] * (len(operands) - len(places))
    out_places = [*out_places] + ["v"] * (len(outs) - len(out_places))
    return pl.pallas_call(
        kernel,
        grid=(1,),
        out_shape=outs,
        in_specs=[spec(p, x) for p, x in zip(places, operands)],
        out_specs=[spec(p, x) for p, x in zip(out_places, outs)],
        scratch_shapes=list(scratch),
        compiler_params=pltpu.CompilerParams(vmem_limit_bytes=limit * MIB),
        cost_estimate=pl.CostEstimate(flops=int(100.0*(flops)), bytes_accessed=0, transcendentals=0),
        name=name,
    )(*operands)


def tied(first, then):
    return lax.optimization_barrier((first, then))


def pieces_kernel(me_ref, cot_ref, routes_ref, router_ref, *refs):
    cots, (router_out, held) = refs[:-2], refs[-2:]
    rows, width = cots[0].shape[0], cot_ref.shape[1]
    eye = lax.broadcasted_iota(jnp.int32, (TOP, LANES), 0) == lane_of((TOP, LANES))
    held[...] = tn(routes_ref[...].astype(F32).astype(BF), eye.astype(F32).astype(BF))
    for r, c in enumerate(cots):
        start = pl.multiple_of((me_ref[0] ^ r) * rows, rows)
        c[:, :width] = cot_ref[pl.ds(start, rows), :]
        c[:, width:] = held[pl.ds(start, rows), :].astype(BF)
    router_out[...] = jnp.zeros(router_out.shape, BF)
    router_out[: router_ref.shape[0], :] = router_ref[...]


def attend_kernel(
    me_ref, x_ref, gain_ref, wq_ref, wk_ref, wv_ref, wo_ref, cos_ref, sin_ref, *refs
):
    n_ref, q_ref, k_ref, v_ref, o_ref, lse_ref, xq_ref = refs[:7]
    parts, whole = refs[7:-1], refs[-1]
    rows, width = xq_ref.shape
    starts = [pl.multiple_of((me_ref[0] ^ r) * rows, rows) for r in range(4)]
    xq_ref[...] = x_ref[pl.ds(starts[0], rows), :]
    x = x_ref[...].astype(F32)
    inv = lax.rsqrt(jnp.mean(x * x, axis=-1, keepdims=True) + EPS)
    n = (x * inv * gain_ref[...]).astype(BF)
    n_ref[...] = n
    cosine, sine = cos_ref[...], sin_ref[...]
    q, k = nn(n, wq_ref[...]), nn(n, wk_ref[...])
    v_ref[...] = nn(n, wv_ref[...]).astype(BF)
    for at in range(0, q.shape[1], LANES):
        tile = q[:, at : at + LANES]
        q_ref[:, at : at + LANES] = (tile * cosine + halves_swapped(tile) * sine).astype(BF)
    for at in range(0, k.shape[1], LANES):
        tile = k[:, at : at + LANES]
        k_ref[:, at : at + LANES] = (tile * cosine + halves_swapped(tile) * sine).astype(BF)
    lse_all = jnp.zeros(lse_ref.shape, F32)
    for head in range(q.shape[1] // LANES):
        at = head // 2 * LANES
        keys = low_high(k_ref[:, at : at + LANES], head % 2)
        values = low_high(v_ref[:, at : at + LANES], head % 2)
        pair = q_ref[:, head * LANES : (head + 1) * LANES]
        mixed = 0.0
        for g in range(2):
            s = nt(pair, keys[g]) * HD ** (-0.5)
            s = jnp.where(causal(s), s, MASKED)
            peak = jnp.max(s, axis=-1, keepdims=True)
            e = jnp.exp(s - peak)
            total = jnp.sum(e, axis=-1, keepdims=True)
            mixed = mixed + nn((e / total).astype(BF), values[g])
            lse = peak + jnp.log(total)
            lse_all = jnp.where(lane_of(lse_all.shape) == 2 * head + g, lse, lse_all)
        o_ref[:, head * LANES : (head + 1) * LANES] = mixed.astype(BF)
    lse_ref[...] = lse_all
    whole[...] = nn(o_ref[...], wo_ref[...])
    for start, part in zip(starts, parts):
        part[...] = whole[pl.ds(start, rows), :].astype(part.dtype)


def norm_two_kernel(x_ref, gain_ref, own_ref, *refs):
    others, (h_ref, n_ref) = refs[:-2], refs[-2:]
    attn = own_ref[...]
    for other in others:
        attn = attn + other[...].astype(F32)
    h = x_ref[...].astype(F32) + attn
    inv = lax.rsqrt(jnp.mean(h * h, axis=-1, keepdims=True) + EPS)
    h_ref[...] = h
    n_ref[...] = (h * inv * gain_ref[...]).astype(BF)


def together_kernel(*refs):
    pieces, out = refs[:-1], refs[-1]
    at = 0
    for piece in pieces:
        if len(piece.shape) == 2:
            out[at] = piece[...]
            at += 1
        else:
            out[at : at + piece.shape[0]] = piece[...]
            at += piece.shape[0]


def together(pieces):
    count = sum(1 if x.ndim == 2 else x.shape[0] for x in pieces)
    return call(
        together_kernel, [shape((count, *pieces[0].shape[-2:]), pieces[0].dtype)], pieces, "together"
    )[0]


def router_of(rows, router_ref, routes, experts):
    z = nt(rows, router_ref[...])
    lane = lane_of(z.shape)
    z = jnp.where(lane < experts, z, MASKED)
    e = jnp.exp(z - jnp.max(z, axis=-1, keepdims=True))
    probs = e / jnp.sum(e, axis=-1, keepdims=True)
    chosen = chosen_of(lane, routes)
    zc = jnp.where(chosen, z, MASKED)
    ec = jnp.where(chosen, jnp.exp(zc - jnp.max(zc, axis=-1, keepdims=True)), 0.0)
    return probs, ec / jnp.sum(ec, axis=-1, keepdims=True)


def chosen_of(lane, routes):
    place, named = lane.astype(F32), routes.astype(F32)
    chosen = place == named[:, 0:1]
    for k in range(1, TOP):
        chosen = chosen | (place == named[:, k : k + 1])
    return chosen


def counts_kernel(*refs):
    pieces, out = refs[:-1], refs[-1]
    total = 0.0
    for piece in pieces:
        width = piece.shape[-1] - LANES
        blocks = [piece[:, width:]] if len(piece.shape) == 2 else [
            piece[i, :, width:] for i in range(piece.shape[0])
        ]
        for routes in blocks:
            named = chosen_of(lane_of(routes.shape), routes).astype(F32)
            total = total + jnp.sum(named, axis=0, keepdims=True)
    out[...] = total


def weights_kernel(wg_ref, wu_ref, out_ref):
    hidden = wg_ref.shape[2]
    out_ref[:, :hidden] = wg_ref[0]
    out_ref[:, hidden:] = wu_ref[0]


def gate_up_weights(w_gate, w_up):
    local, width, hidden = w_gate.shape
    block = pl.BlockSpec((1, width, hidden), lambda e: (e, 0, 0))
    return pl.pallas_call(
        weights_kernel,
        grid=(local,),
        in_specs=[block, block],
        out_specs=pl.BlockSpec((width, 2 * hidden), lambda e: (0, e)),
        out_shape=shape((width, 2 * hidden * local), BF),
        compiler_params=pltpu.CompilerParams(vmem_limit_bytes=30 * MIB),
        cost_estimate=pl.CostEstimate(flops=int(100.0*(0)), bytes_accessed=4 * w_gate.size * 2, transcendentals=0),
        name="gate_up_weights",
    )(w_gate, w_up)


def experts_kernel(experts, base_ref, x_ref, own_ref, far_ref, router_ref, wcat, wd_ref, *refs):
    cot_ref, dgu_ref, hg_ref, *ds, m_ref = refs
    hidden = LANES
    pair = 2 * hidden
    rows, width = cot_ref.shape
    x = x_ref[...].reshape(rows, width)
    if far_ref is None:
        routes = own_ref[:, width:]
        cot_ref[...] = own_ref[:, :width]
    else:
        pieces = [own_ref[...]] + [far_ref[i] for i in range(far_ref.shape[0])]
        routes = jnp.concatenate([piece[:, width:] for piece in pieces], axis=0)
        cot_ref[...] = jnp.concatenate([piece[:, :width] for piece in pieces], axis=0)
    _, gates = router_of(x, router_ref, routes, experts)
    lane = lane_of(gates.shape)
    dots = jnp.zeros(gates.shape, F32)
    for e in range(hg_ref.shape[1] // hidden):
        mine = lane == base_ref[0] + e
        g = jnp.sum(jnp.where(mine, gates, 0.0), axis=-1, keepdims=True)
        both = nn(x, wcat[:, e * pair : (e + 1) * pair])
        v = nt(cot_ref[...], wd_ref[e * hidden : (e + 1) * hidden, :])
        gate, up = both[:, :hidden], both[:, hidden:]
        sig = 1.0 / (1.0 + jnp.exp(-gate))
        act = gate * sig
        hid = act * up
        dots = jnp.where(mine, jnp.sum(hid * v, axis=-1, keepdims=True), dots)
        gv = g * v
        hg_ref[:, e * hidden : (e + 1) * hidden] = (g * hid).astype(BF)
        d_gate = gv * up * sig * (1.0 + gate * (1.0 - sig))
        dgu_ref[:, e * pair : e * pair + hidden] = d_gate.astype(BF)
        dgu_ref[:, e * pair + hidden : (e + 1) * pair] = (gv * act).astype(BF)

    def put(outs, columns, value):
        at = 0
        for out in outs:
            part = value.astype(out.dtype)
            if len(out.shape) == 2:
                out[:, columns] = part[at : at + out.shape[0]]
                at += out.shape[0]
            else:
                step = out.shape[1]
                for i in range(out.shape[0]):
                    out[i, :, columns] = part[i * step : (i + 1) * step]

    put(ds, slice(width, width + LANES), dots)
    step = 256
    for at in range(0, width, step):
        put(ds, slice(at, at + step), nt(dgu_ref[...], wcat[at : at + step, :]))
    put([m_ref], slice(0, width), nn(hg_ref[...], wd_ref[...]))


def run_experts(experts, base, x, own, far, router, wcat, down_flat, kind, apart=False):
    count, rows, width = x.shape
    inner = down_flat.shape[0]
    wide = width + LANES
    total = count * rows
    few = count <= FEW
    step = total if few else 256
    resident = pl.BlockSpec(memory_space=pltpu.VMEM)
    per = lambda w: resident if few else pl.BlockSpec((step, w), lambda i: (i, 0))
    kernel = functools.partial(experts_kernel, experts)
    if few:
        data, dims = [x, own, far], lambda w: (count, rows, w)
    else:
        joined = jnp.concatenate([own[None], far], axis=0)
        data, dims = [x.reshape(total, width), joined.reshape(total, wide)], lambda w: (total, w)
        whole_kernel = kernel
        kernel = lambda b, x, c, *refs: whole_kernel(b, x, c, None, *refs)
    if few and apart:
        d_shapes = [shape((rows, wide), BF if i else F32) for i in range(count)]
    else:
        d_shapes = [shape(dims(wide), kind)]
    cot, dgu, hid, *d, m = pl.pallas_call(
        kernel,
        grid=(total // step,),
        in_specs=[pl.BlockSpec(memory_space=pltpu.SMEM)]
        + [per(z.shape[-1]) for z in data]
        + [resident] * 3,
        out_specs=[per(width), per(2 * inner), per(inner)]
        + [per(wide)] * len(d_shapes)
        + [per(width)],
        out_shape=[
            shape((total, width), BF),
            shape((total, 2 * inner), BF),
            shape((total, inner), BF),
            *d_shapes,
            shape(dims(width), kind),
        ],
        compiler_params=pltpu.CompilerParams(vmem_limit_bytes=(14 if few else 30) * MIB),
        cost_estimate=pl.CostEstimate(flops=int(100.0*(total * width * inner // 8)), bytes_accessed=0, transcendentals=0),
        name="experts",
    )(base, *data, router, wcat, down_flat)
    if not few:
        d = list(d[0].reshape(count, rows, wide)) if apart else [d[0].reshape(count, rows, wide)]
    return cot, dgu, hid, d if apart else d[0], m.reshape(count, rows, width)


def split_sum_kernel(count, near, *refs):
    ins, outs = refs[:count], refs[count:]
    for s in range(ins[0].shape[0]):
        total = ins[0][s].astype(F32)
        for x in ins[1:]:
            total = total + x[s].astype(F32)
        outs[s][...] = total.astype(outs[s].dtype)


def split_sum(arrays, name):
    count, *dims = arrays[0].shape
    outs = [shape(dims, F32)] + [shape(dims, BF)] * (count - 1)
    return call(functools.partial(split_sum_kernel, len(arrays), True), outs, arrays, name)


def add_kernel(*refs):
    pieces, out = refs[:-1], refs[-1]
    total = pieces[0][...].astype(F32)
    for piece in pieces[1:]:
        total = total + piece[...].astype(F32)
    out[...] = total.astype(out.dtype)


def added(pieces, kind, name):
    return call(add_kernel, [shape(pieces[0].shape, kind)], pieces, name)[0]


def grads_kernel(*refs):
    ns, dgus, hs, cs = (refs[4 * i : 4 * i + 4] for i in range(4))
    out_ref = refs[16]
    hidden, width = hs[0].shape[1], ns[0].shape[1]
    both, down = 0.0, 0.0
    for n, dgu, h, c in zip(ns, dgus, hs, cs):
        both = both + tn(n[...], dgu[...])
        down = down + tn(h[...], c[...])
    out_ref[0, :width, :] = both[:, :hidden].astype(BF)
    out_ref[0, width : 2 * width, :] = both[:, hidden:].astype(BF)
    for at in range(0, width, hidden):
        out_ref[0, 2 * width + at : 2 * width + at + hidden, :] = down[:, at : at + hidden].astype(BF)


def run_grads(n, dgu, h, c, local, hidden):
    width = n[0].shape[-1]
    flat = lambda xs: [x.reshape(-1, x.shape[-1]) for x in xs]
    n, c = flat(n), flat(c)
    whole = lambda xs: [pl.BlockSpec(x.shape, lambda e: (0, 0)) for x in xs]
    cols = lambda xs, w: [pl.BlockSpec((x.shape[0], w), lambda e: (0, e)) for x in xs]
    few = n[0].shape[0] <= 512
    return pl.pallas_call(
        grads_kernel,
        grid=(local,),
        in_specs=whole(n) + cols(dgu, 2 * hidden) + cols(h, hidden) + whole(c),
        out_specs=pl.BlockSpec((1, 3 * width, hidden), lambda e: (e, 0, 0)),
        out_shape=shape((local, 3 * width, hidden), BF),
        compiler_params=pltpu.CompilerParams(vmem_limit_bytes=(20 if few else 58) * MIB),
        cost_estimate=pl.CostEstimate(flops=int(100.0*(24 * n[0].size * hidden * local)), bytes_accessed=0, transcendentals=0),
        name="expert_grads",
    )(*n, *dgu, *h, *c)


def both_copies_kernel(mine_ref, other_ref, out_ref):
    for e in range(mine_ref.shape[0]):
        total = mine_ref[e].astype(F32) + other_ref[e].astype(F32)
        hidden = total.shape[1]
        if out_ref.shape[2] == hidden:
            out_ref[e] = total
        else:
            for at in range(0, total.shape[0], hidden):
                out_ref[e, :, at : at + hidden] = total[at : at + hidden]


def both_copies(mine, other, which):
    local, rows, hidden = mine.shape
    width = rows // 3
    dims = (hidden, width) if which == 2 else (width, hidden)
    step = min(local, 2)
    block = pl.BlockSpec((step, width, hidden), lambda e: (e, which, 0))
    return pl.pallas_call(
        both_copies_kernel,
        grid=(local // step,),
        in_specs=[block, block],
        out_specs=pl.BlockSpec((step, *dims), lambda e: (e, 0, 0)),
        out_shape=shape((local, *dims), F32),
        compiler_params=pltpu.CompilerParams(vmem_limit_bytes=58 * MIB),
        cost_estimate=pl.CostEstimate(flops=int(100.0*(0)), bytes_accessed=8 * mine.size, transcendentals=0),
        name="both_copies",
    )(mine, other)


def norm_back_kernel(experts, count, h_ref, n_ref, gain_ref, router_ref, bal_ref, cot_ref, *refs):
    sums, (wide_ref, dh_ref, small_ref) = refs[:count], refs[count:]
    near = sums[0][...].astype(F32)
    for other in sums[1:]:
        near = near + other[...].astype(F32)
    rows, width = h_ref.shape
    dots = near[:, width:]
    probs, gates = router_of(n_ref[...], router_ref, cot_ref[:, width:], experts)
    bal = bal_ref[...]
    d_chosen = gates * (dots - jnp.sum(gates * dots, axis=-1, keepdims=True))
    dz = probs * (bal - jnp.sum(probs * bal, axis=-1, keepdims=True)) + d_chosen
    dz = dz.astype(BF)
    wide_ref[:, width:] = dz
    dn = near[:, :width] + nn(dz, router_ref[...])
    h = h_ref[...]
    inv = lax.rsqrt(jnp.mean(h * h, axis=-1, keepdims=True) + EPS)
    u = gain_ref[...] * dn
    dy = cot_ref[:, :width].astype(F32)
    dh = dy + inv * u - h * (inv * inv * inv * jnp.mean(u * h, axis=-1, keepdims=True))
    dh_ref[...] = dh
    wide_ref[:, :width] = dh.astype(BF)
    small_ref[...] = jnp.zeros(small_ref.shape, F32)
    small_ref[1:2, :] = jnp.sum(dn * h * inv, axis=0, keepdims=True)
    small_ref[2:3, : probs.shape[1]] = jnp.sum(probs, axis=0, keepdims=True)


def attend_back_kernel(
    me_ref, w0, w1, w2, w3, x_ref, q_ref, k_ref, v_ref, lse_ref, wq_ref, wk_ref, wv_ref, wo_ref, cos_ref, sin_ref,
    small_in, wide_ref, dq_ref, small_ref, p0, p1, p2, p3, do_ref, whole
):
    rows = w0.shape[0]
    width = x_ref.shape[1]
    for r, piece in enumerate((w0, w1, w2, w3)):
        start = pl.multiple_of((me_ref[0] ^ r) * rows, rows)
        wide_ref[pl.ds(start, rows), :] = piece[...]
    do_ref[...] = nt(wide_ref[:, :width], wo_ref[...]).astype(BF)
    cosine, sine = cos_ref[...], sin_ref[...]
    scale = HD ** (-0.5)
    heads, keys_wide = q_ref.shape[1], k_ref.shape[1]
    dk_tiles = [0.0] * (keys_wide // LANES)
    dv_tiles = [0.0] * (keys_wide // LANES)

    def back(tile):
        return (tile * cosine - halves_swapped(tile) * sine).astype(BF)

    for head in range(heads // LANES):
        at = head // 2 * LANES
        side = head % 2
        keys = low_high(k_ref[:, at : at + LANES], side)
        values = low_high(v_ref[:, at : at + LANES], side)
        pair = q_ref[:, head * LANES : (head + 1) * LANES]
        grad = do_ref[:, head * LANES : (head + 1) * LANES]
        dq = 0.0
        dk, dv = [], []
        for g in range(2):
            s = nt(pair, keys[g]) * scale
            lse = lse_ref[:, 2 * head + g : 2 * head + g + 1]
            p = jnp.where(causal(s), jnp.exp(s - lse), 0.0)
            dp = nt(grad, values[g])
            ds = (p * (dp - jnp.sum(p * dp, axis=-1, keepdims=True))).astype(BF)
            dq = dq + nn(ds, keys[g])
            dk.append(tn(ds, pair))
            dv.append(tn(p.astype(BF), grad))
        dq_ref[:, head * LANES : (head + 1) * LANES] = back(dq * scale)
        mine = lane_of(dk[0].shape) < HD
        if side == 0:
            dk_sum = jnp.where(mine, dk[0] + pltpu.roll(dk[1], HD, 1), 0.0)
            dv_sum = jnp.where(mine, dv[0] + pltpu.roll(dv[1], HD, 1), 0.0)
        else:
            dk_sum = jnp.where(mine, 0.0, pltpu.roll(dk[0], HD, 1) + dk[1])
            dv_sum = jnp.where(mine, 0.0, pltpu.roll(dv[0], HD, 1) + dv[1])
        dk_tiles[head // 2] = dk_tiles[head // 2] + dk_sum
        dv_tiles[head // 2] = dv_tiles[head // 2] + dv_sum
    for i, tile in enumerate(dk_tiles):
        at = heads + i * LANES
        dq_ref[:, at : at + LANES] = back(tile * scale)
    for i, tile in enumerate(dv_tiles):
        at = heads + keys_wide + i * LANES
        dq_ref[:, at : at + LANES] = tile.astype(BF)
    dn = nt(dq_ref[:, :heads], wq_ref[...])
    dn = dn + nt(dq_ref[:, heads : heads + keys_wide], wk_ref[...])
    whole[...] = dn + nt(dq_ref[:, heads + keys_wide :], wv_ref[...])
    x = x_ref[...].astype(F32)
    inv = lax.rsqrt(jnp.mean(x * x, axis=-1, keepdims=True) + EPS)
    small_ref[...] = small_in[...]
    small_ref[0:1, :] = jnp.sum(whole[...] * x * inv, axis=0, keepdims=True)
    for r, part in enumerate((p0, p1, p2, p3)):
        start = pl.multiple_of((me_ref[0] ^ r) * rows, rows)
        part[...] = whole[pl.ds(start, rows), :].astype(part.dtype)


def dense_kernel(me_ref, a0, a1, a2, a3, wide_ref, o_ref, n_ref, dq_ref, kept_ref, sent_ref, two_ref, whole):
    rows, width = a0.shape[1:]
    for r, piece in enumerate((a0, a1, a2, a3)):
        start = pl.multiple_of((me_ref[1] ^ r) * rows, rows)
        two_ref[pl.ds(start, rows), :] = piece[0]
    columns, heads = dq_ref.shape[1], o_ref.shape[1]
    whole[:, :columns] = tn(n_ref[...], dq_ref[...])
    whole[:, columns : columns + heads] = tn(wide_ref[:, :width], o_ref[...])
    whole[:, columns + heads :] = tn(two_ref[...], wide_ref[:, width:])
    half = kept_ref.shape[0]
    kept_ref[...] = whole[pl.ds(pl.multiple_of(me_ref[0] * half, half), half), :]
    sent_ref[...] = whole[pl.ds(pl.multiple_of((1 - me_ref[0]) * half, half), half), :].astype(BF)


def input_grad_kernel(x_ref, gain_ref, dh_ref, *refs):
    parts, ig_ref = refs[:-1], refs[-1]
    x = x_ref[...].astype(F32)
    inv = lax.rsqrt(jnp.mean(x * x, axis=-1, keepdims=True) + EPS)
    dn = parts[0][...].astype(F32)
    for part in parts[1:]:
        dn = dn + part[...].astype(F32)
    u = gain_ref[...] * dn
    ig = dh_ref[...] + inv * u - x * (inv * inv * inv * jnp.mean(u * x, axis=-1, keepdims=True))
    ig_ref[...] = ig.astype(BF)


def out_kernel(h_ref, small_ref, *refs):
    moes, out_ref = refs[:-1], refs[-1]
    rows = h_ref.shape[0]
    out = h_ref[...]
    for moe in moes:
        out = out + moe[...].astype(F32)
    out_ref[:rows, :] = out.astype(BF)
    small = small_ref[...]
    high = small.astype(BF).astype(F32)
    out_ref[rows:, :] = jnp.concatenate([high, small - high], axis=0).astype(BF)


def natural_kernel(me_ref, *refs):
    pieces, out = refs[:-1], refs[-1]
    rows = pieces[0].shape[0]
    for r, piece in enumerate(pieces):
        start = pl.multiple_of((me_ref[0] ^ r) * rows, rows)
        out[pl.ds(start, rows), :] = piece[...].astype(out.dtype)


def out_whole_kernel(me_ref, *refs):
    pieces, (out_ref, small_ref, held) = refs[:-3], refs[-3:]
    rows = pieces[0].shape[0] - 16
    for r, piece in enumerate(pieces):
        start = pl.multiple_of((me_ref[0] ^ r) * rows, rows)
        out_ref[pl.ds(start, rows), :] = piece[:rows, :]
        both = piece[rows:, :].astype(F32)
        held[me_ref[0] ^ r] = both[:8] + both[8:]
    total = held[0]
    for i in range(1, len(pieces)):
        total = total + held[i]
    small_ref[...] = total


def kept_and_dealt_kernel(me_ref, kept_ref, got_ref, small_ref, small_got_ref, *outs):
    small_out, outs = outs[-1], outs[:-1]
    small = small_ref[...] + small_got_ref[...]
    high = small[:4].astype(BF).astype(F32)
    both = jnp.concatenate([high, small[:4] - high], axis=0).astype(BF).astype(F32)
    small_out[...] = both
    rows, columns = outs[0].shape
    upper = lane_of((8, LANES)) >= HD
    parts = []
    for at in range(0, both.shape[1], LANES):
        tile = both[:, at : at + LANES]
        parts += [jnp.where(upper, pltpu.roll(tile, HD, 1), 0.0), jnp.where(upper, tile, 0.0)]
    if len(parts) * 8 == rows:
        extra = jnp.concatenate(parts, axis=0)
    else:
        extra = jnp.zeros((rows, LANES), F32)
    for r, out in enumerate(outs):
        start = pl.multiple_of((me_ref[0] ^ r) * rows, rows)
        at = pl.ds(start, rows)
        total = kept_ref[at, :] + got_ref[at, :].astype(F32)
        out[:, : columns - LANES] = total[:, : columns - LANES].astype(out.dtype)
        out[:, columns - LANES :] = (total[:, columns - LANES :] + extra).astype(out.dtype)


def dense_sum_kernel(me_ref, small_ref, mine_ref, *refs):
    others, outs, held = refs[:-7], refs[-7:-1], refs[-1]
    q_ref, k_ref, v_ref, o_ref, r_ref, small_out = outs
    total = mine_ref[...]
    for other in others:
        total = total + other[...].astype(F32)
    at = 0
    for out in (q_ref, k_ref, v_ref):
        out[...] = total[:, at : at + out.shape[1]]
        at += out.shape[1]
    o_ref[...] = total[:, at : at + o_ref.shape[0]].T
    at += o_ref.shape[0]
    r_ref[...] = total[:, at : at + r_ref.shape[1]]
    held[me_ref[0]] = small_ref[...]
    if total.shape[0] * HD != 8 * small_ref.shape[1]:
        others = []
    lower = lane_of((8, LANES)) < HD
    for i, other in enumerate(others):
        for j in range(small_ref.shape[1] // LANES):
            first = other[16 * j : 16 * j + 16, at : at + LANES].astype(F32)
            tile = jnp.where(lower, pltpu.roll(first[:8], HD, 1), first[8:])
            held[me_ref[0] ^ (i + 1), :, j * LANES : (j + 1) * LANES] = tile
    small = held[0] if others else small_ref[...]
    for i in range(1, len(others) + 1):
        small = small + held[i]
    small_out[...] = jnp.concatenate([small[:4] + small[4:], jnp.zeros_like(small[:4])], axis=0)


def on_device(
    tokens,
    routes,
    gain_first,
    w_query,
    w_key,
    w_value,
    w_output,
    gain_second,
    w_router,
    w_gate,
    w_up,
    w_down,
    cotangent,
):
    seq_len, width = tokens.shape
    experts = w_router.shape[1]
    local, _, hidden = w_gate.shape
    tensor_size = lax.axis_size("tensor")
    expert_size = lax.axis_size("expert")
    dp_size = lax.axis_size("dp")
    token_count = seq_len * dp_size * expert_size
    rows = seq_len // tensor_size
    wide_width = width + LANES
    last = tensor_size - 1
    around = range(1, tensor_size)
    t_me, e_me, d_me = lax.axis_index("tensor"), lax.axis_index("expert"), lax.axis_index("dp")
    t_at = t_me.astype(jnp.int32).reshape(1)
    e_at = e_me.astype(jnp.int32).reshape(1)
    base = (e_me * local).astype(jnp.int32).reshape(1)
    d_at = jnp.stack([d_me, t_me]).astype(jnp.int32)
    cosine, sine = rope_tables(seq_len)
    gain_one, gain_two = gain_first[None], gain_second[None]
    down_flat = w_down.reshape(local * hidden, width)

    *cot_near, router = call(
        pieces_kernel,
        [shape((rows, wide_width), BF)] * tensor_size + [shape((LANES, width), BF)],
        (t_at, cotangent, routes.T, w_router.T),
        "pieces",
        "sbbb",
        scratch=[pltpu.VMEM((seq_len, LANES), F32)],
        limit=58,
    )
    cot_got = spread(cot_near[0], "expert")
    cot_got[0], tokens = tied(cot_got[0], tokens)

    heads, keys_wide = w_query.shape[1], w_key.shape[1]
    n_one, q, k, v, o, lse, xq, *rest = call(
        attend_kernel,
        [
            shape((seq_len, width), BF),
            shape((seq_len, heads), BF),
            shape((seq_len, keys_wide), BF),
            shape((seq_len, keys_wide), BF),
            shape((seq_len, heads), BF),
            shape((seq_len, LANES), F32),
            shape((rows, width), BF),
        ]
        + [shape((rows, width), F32)]
        + [shape((rows, width), BF)] * last,
        (t_at, tokens, gain_one, w_query, w_key, w_value, w_output, cosine, sine),
        "attend",
        "s" + "b" * 8,
        "bbbbbbv",
        scratch=[pltpu.VMEM((seq_len, width), F32)],
        limit=58,
        flops=2 * seq_len * width * 4 * heads,
    )
    parts = rest
    got = backwards(lambda r: swap(parts[r], "tensor", r), tensor_size)
    h, n_two = call(
        norm_two_kernel,
        [shape((rows, width), F32), shape((rows, width), BF)],
        (xq, gain_two, parts[0], *got),
        "norm_two",
        "bbb",
        "vv",
        limit=58,
    )

    n_two, cot_got = tied(n_two, cot_got)
    cot_far = together(cot_got)
    wcat = gate_up_weights(w_gate, w_up)
    two_got = spread(n_two, "expert")
    two_got[0], cot_late = tied(two_got[0], cot_far)
    cot_far = [cot_far] + backwards(lambda r: swap(cot_far, "tensor", r), last)
    cot_far.append(swap(cot_late, "tensor", last))

    first = together([n_two, *two_got])
    twos = [first] + backwards(lambda r: swap(first, "tensor", r), last)
    _, late = tied(cot_far[:last], first)
    twos.append(swap(late, "tensor", last))

    run = functools.partial(
        run_experts, experts, base, router=router, wcat=wcat, down_flat=down_flat
    )
    counts = call(counts_kernel, [shape((1, LANES), F32)], (*cot_near, *cot_far), "counts")[0]
    counts = counts + swap(counts, "dp", 1)
    balance = experts * (counts / (token_count * TOP)) / token_count
    made = [run(twos[0], cot_near[0], cot_far[0], kind=F32)]
    got = []
    for r in around:
        made[-1], (two, cot) = tied(made[-1], (twos[r], cot_far[r]))
        if r == last:
            balance, two = tied(balance, two)
        made.append(run(two, cot_near[r], cot, kind=BF, apart=r == last))
        if r < last:
            got.append(swap(made[-1][3], "tensor", r))
    cots, dgus, hids, ds, moes = zip(*made)
    near_last, *far_last = ds[last]
    from_last = deal(far_last, "expert")
    grads = run_grads(twos, dgus, hids, cots, local, hidden)
    grads, (got, from_last) = tied(grads, (got, from_last))
    near, *across = split_sum([ds[0], *got], "dn_sum")
    across[0], middle = tied(across[0], moes[1:last])
    across = deal(across, "expert")
    across[0], near_last = tied(across[0], near_last)
    through = added([near_last, *from_last], BF, "through")
    near_sums = [near, swap(through, "tensor", last), *across]
    moe_got = [swap(middle[r - 1], "tensor", r) for r in range(1, last)]
    moe_got, near_sums = tied(moe_got, near_sums)

    wide, dh, small = call(
        functools.partial(norm_back_kernel, experts, len(near_sums)),
        [shape((rows, wide_width), BF), shape((rows, width), F32), shape((8, width), F32)],
        (h, n_two, gain_two, router, balance, cot_near[0], *near_sums),
        "norm_back",
        "v",
        "vvv",
    )
    wides = [wide] + backwards(lambda r: swap(wide, "tensor", r), tensor_size)
    _, late_grads = tied(wide, grads)
    grads_got = swap(late_grads, "dp", 1)
    grads_got, wides = tied(grads_got, wides)
    wides, moe_last = tied(wides, moes[last])
    moe_got.append(swap(moe_last, "tensor", last))

    wide_all, dqkv, small, *back_parts = call(
        attend_back_kernel,
        [
            shape((seq_len, wide_width), BF),
            shape((seq_len, heads + 2 * keys_wide), BF),
            shape((8, width), F32),
            shape((rows, width), F32),
        ]
        + [shape((rows, width), BF)] * last,
        (t_at, *wides, tokens, q, k, v, lse, w_query, w_key, w_value, w_output, cosine, sine, small),
        "attend_back",
        "s" + "v" * tensor_size + "b" * 11,
        "bb",
        limit=58,
        scratch=[
            pltpu.VMEM((seq_len, heads), BF),
            pltpu.VMEM((seq_len, width), F32),
        ],
        flops=2 * seq_len * width * 4 * heads,
    )
    part_sums = [back_parts[0]] + backwards(lambda r: swap(back_parts[r], "tensor", r), tensor_size)
    half = width // dp_size
    chunk = half // expert_size

    columns = heads + 2 * keys_wide
    all_columns = columns + heads + LANES
    own_block = pl.BlockSpec((1, rows, width), lambda i: (0, 0, 0))
    kept, sent = call(
        dense_kernel,
        [shape((half, all_columns), F32), shape((half, all_columns), BF)],
        (d_at, *twos, wide_all, o, n_one, dqkv),
        "dense",
        ["s"] + [own_block] * tensor_size + ["b"] * 4,
        "vv",
        limit=54,
        scratch=[
            pltpu.VMEM((seq_len, width), BF),
            pltpu.VMEM((width, all_columns), F32),
        ],
        flops=1,
    )
    mine, *others, small = call(
        kept_and_dealt_kernel,
        [shape((chunk, all_columns), F32)]
        + [shape((chunk, all_columns), BF)] * (expert_size - 1)
        + [shape((8, width), F32)],
        (e_at, kept, swap(sent, "dp", 1), small, swap(small, "dp", 1)),
        "dense_dealt",
        "s",
    )
    others = deal(others, "expert")
    grad_gate = both_copies(grads, grads_got, 0)
    (grad_gate, others[0]), part_sums = tied((grad_gate, others[0]), part_sums)
    moe_near, *moe_across = split_sum([moes[0], *moe_got], "moe_sum")
    moe_sums = [moe_near, *deal(moe_across, "expert")]
    ig = call(
        input_grad_kernel, [shape((rows, width), BF)], (xq, gain_one, dh, *part_sums), "input_grad", "bbbb", limit=58
    )[0]
    igs = [ig] + backwards(lambda r: swap(ig, "tensor", r), tensor_size)
    grad_up = both_copies(grads, grads_got, 1)
    grad_up, others = tied(grad_up, others)
    g_query, g_key, g_value, g_out, g_router, small = call(
        dense_sum_kernel,
        [
            shape((chunk, heads), F32),
            shape((chunk, keys_wide), F32),
            shape((chunk, keys_wide), F32),
            shape((heads, chunk), F32),
            shape((chunk, LANES), F32),
            shape((8, width), F32),
        ],
        (e_at, small, mine, *others),
        "dense_sum",
        "s",
        "bbbbbv",
        scratch=[pltpu.VMEM((expert_size, 8, width), F32)],
    )
    if chunk * HD != 8 * width:
        small = jnp.sum(lax.all_gather(small, "expert"), axis=0)
    igs, small = tied(igs, small)
    input_grad = call(
        natural_kernel, [shape((seq_len, width), F32)], (t_at, *igs), "input_grad_whole", "s", "b"
    )[0]
    out_piece = call(out_kernel, [shape((rows + 16, width), BF)], (h, small, *moe_sums), "out_piece")[0]
    outs = [out_piece] + backwards(lambda r: swap(out_piece, "tensor", r), tensor_size)
    grad_down = both_copies(grads, grads_got, 2)
    grad_down, outs = tied(grad_down, outs)
    output, small = call(
        out_whole_kernel,
        [shape((seq_len, width), BF), shape((8, width), F32)],
        (t_at, *outs),
        "output",
        "s",
        "bv",
        scratch=[pltpu.VMEM((tensor_size, 8, width), F32)],
    )
    at = (d_me * expert_size + e_me) * chunk
    loss_value = (experts * balance * small[2:3, :LANES])[0, :experts]
    return (
        output,
        loss_value,
        input_grad,
        lax.dynamic_slice(small, (0, at), (1, chunk))[0],
        g_query,
        g_key,
        g_value,
        g_out,
        lax.dynamic_slice(small, (1, at), (1, chunk))[0],
        g_router[:, :experts],
        grad_gate,
        grad_up,
        grad_down,
    )


def solution(mesh):
    rows = ("dp", "expert")
    placed = (
        P(rows, None),
        P(rows, None),
        P(),
        P(None, "tensor"),
        P(None, "tensor"),
        P(None, "tensor"),
        P("tensor", None),
        P(),
        P(),
        P("expert", None, "tensor"),
        P("expert", None, "tensor"),
        P("expert", "tensor", None),
        P(rows, None),
    )
    return jax.shard_map(
        on_device,
        mesh=mesh,
        in_specs=placed,
        out_specs=(
            P(rows, None),
            P(),
            P(rows, None),
            P(rows),
            P(rows, "tensor"),
            P(rows, "tensor"),
            P(rows, "tensor"),
            P("tensor", rows),
            P(rows),
            P(rows, None),
            P("expert", None, "tensor"),
            P("expert", None, "tensor"),
            P("expert", "tensor", None),
        ),
        check_vma=False,
    )
```

```python
import functools

import jax
import jax.numpy as jnp
import numpy as np
from jax import lax
from jax.experimental import pallas as pl
from jax.experimental.pallas import tpu as pltpu
from jax.sharding import PartitionSpec as P

HD = 64
TOP = 8
EPS = 1e-06
ROPE_BASE = 10000.0
MASKED = -1e30
BF = jnp.bfloat16
F32 = jnp.float32
FEW = 8
LANES = 128
MIB = 1 << 20


def dot(a, b, dims):
    return lax.dot_general(a, b, (dims, ((), ())), preferred_element_type=F32)


def nn(a, b):
    return dot(a, b, ((1,), (0,)))


def nt(a, b):
    return dot(a, b, ((1,), (1,)))


def tn(a, b):
    return dot(a, b, ((0,), (0,)))


def swap(x, axis, distance):
    size = lax.axis_size(axis)
    return lax.ppermute(x, axis, [(i, i ^ distance) for i in range(size)])


def backwards(make, size):
    return [make(r) for r in range(size - 1, 0, -1)][::-1]


def spread(x, axis):
    size = lax.axis_size(axis)
    if size <= FEW:
        return backwards(lambda r: swap(x, axis, r), size)
    whole = lax.all_gather(x, axis)
    order = jnp.arange(1, size) ^ lax.axis_index(axis)
    return list(jnp.take(whole, order, axis=0))


def deal(parts, axis):
    size = lax.axis_size(axis)
    if size <= FEW:
        return backwards(lambda r: swap(parts[r - 1], axis, r), size)
    order = jnp.arange(size) ^ lax.axis_index(axis)
    whole = jnp.take(jnp.stack([parts[0], *parts]), order, axis=0)
    back = lax.all_to_all(whole, axis, 0, 0, tiled=True)
    return list(jnp.take(back, order, axis=0)[1:])


def rope_tables(seq_len):
    half = HD // 2
    frequency = ROPE_BASE ** (-(np.arange(half, dtype=np.float32) * 2.0) / HD)
    angles = np.arange(seq_len, dtype=np.float32)[:, None] * frequency[None, :].astype(np.float32)
    cosine, sine = np.cos(angles), np.sin(angles)
    heads = LANES // HD
    return (
        np.tile(cosine, (1, 2 * heads)).astype(np.float32),
        np.tile(np.concatenate([-sine, sine], axis=1), (1, heads)).astype(np.float32),
    )


def lane_of(shape):
    return lax.broadcasted_iota(jnp.int32, shape, 1)


def halves_swapped(x):
    first = lane_of(x.shape) % HD < HD // 2
    half = HD // 2
    return jnp.where(first, pltpu.roll(x, LANES - half, 1), pltpu.roll(x, half, 1))


def low_high(x, head):
    other = pltpu.roll(x.astype(F32), HD, 1).astype(x.dtype)
    low = lane_of(x.shape) < HD
    zero = jnp.zeros_like(x)
    at_low, at_high = (x, other) if head == 0 else (other, x)
    return jnp.where(low, at_low, zero), jnp.where(low, zero, at_high)


def causal(scores):
    rows = lax.broadcasted_iota(jnp.int32, scores.shape, 0)
    return lane_of(scores.shape) <= rows


def shape(dims, kind):
    return jax.ShapeDtypeStruct(dims, kind)


def whole_block(dims):
    return pl.BlockSpec(dims, lambda i: (0,) * len(dims))


def call(kernel, outs, operands, name, places="", out_places="", scratch=(), limit=40, flops=0):
    kinds = {"s": pltpu.SMEM, "v": pltpu.VMEM}

    def spec(place, x):
        if not isinstance(place, str):
            return place
        if place == "b":
            return whole_block(x.shape)
        return pl.BlockSpec(memory_space=kinds[place])

    places = [*places] + ["v"] * (len(operands) - len(places))
    out_places = [*out_places] + ["v"] * (len(outs) - len(out_places))
    return pl.pallas_call(
        kernel,
        grid=(1,),
        out_shape=outs,
        in_specs=[spec(p, x) for p, x in zip(places, operands)],
        out_specs=[spec(p, x) for p, x in zip(out_places, outs)],
        scratch_shapes=list(scratch),
        compiler_params=pltpu.CompilerParams(vmem_limit_bytes=limit * MIB),
        cost_estimate=pl.CostEstimate(flops=int(100.0*(flops)), bytes_accessed=0, transcendentals=0),
        name=name,
    )(*operands)


def tied(first, then):
    return lax.optimization_barrier((first, then))


def pieces_kernel(me_ref, cot_ref, routes_ref, router_ref, *refs):
    cots, (router_out, held) = refs[:-2], refs[-2:]
    rows, width = cots[0].shape[0], cot_ref.shape[1]
    eye = lax.broadcasted_iota(jnp.int32, (TOP, LANES), 0) == lane_of((TOP, LANES))
    held[...] = tn(routes_ref[...].astype(F32).astype(BF), eye.astype(F32).astype(BF))
    for r, c in enumerate(cots):
        start = pl.multiple_of((me_ref[0] ^ r) * rows, rows)
        c[:, :width] = cot_ref[pl.ds(start, rows), :]
        c[:, width:] = held[pl.ds(start, rows), :].astype(BF)
    router_out[...] = jnp.zeros(router_out.shape, BF)
    router_out[: router_ref.shape[0], :] = router_ref[...]


def attend_kernel(
    me_ref, x_ref, gain_ref, wq_ref, wk_ref, wv_ref, wo_ref, cos_ref, sin_ref, *refs
):
    n_ref, q_ref, k_ref, v_ref, o_ref, lse_ref, xq_ref = refs[:7]
    parts, whole = refs[7:-1], refs[-1]
    rows, width = xq_ref.shape
    starts = [pl.multiple_of((me_ref[0] ^ r) * rows, rows) for r in range(4)]
    xq_ref[...] = x_ref[pl.ds(starts[0], rows), :]
    x = x_ref[...].astype(F32)
    inv = lax.rsqrt(jnp.mean(x * x, axis=-1, keepdims=True) + EPS)
    n = (x * inv * gain_ref[...]).astype(BF)
    n_ref[...] = n
    cosine, sine = cos_ref[...], sin_ref[...]
    q, k = nn(n, wq_ref[...]), nn(n, wk_ref[...])
    v_ref[...] = nn(n, wv_ref[...]).astype(BF)
    for at in range(0, q.shape[1], LANES):
        tile = q[:, at : at + LANES]
        q_ref[:, at : at + LANES] = (tile * cosine + halves_swapped(tile) * sine).astype(BF)
    for at in range(0, k.shape[1], LANES):
        tile = k[:, at : at + LANES]
        k_ref[:, at : at + LANES] = (tile * cosine + halves_swapped(tile) * sine).astype(BF)
    lse_all = jnp.zeros(lse_ref.shape, F32)
    for head in range(q.shape[1] // LANES):
        at = head // 2 * LANES
        keys = low_high(k_ref[:, at : at + LANES], head % 2)
        values = low_high(v_ref[:, at : at + LANES], head % 2)
        pair = q_ref[:, head * LANES : (head + 1) * LANES]
        mixed = 0.0
        for g in range(2):
            s = nt(pair, keys[g]) * HD ** (-0.5)
            s = jnp.where(causal(s), s, MASKED)
            peak = jnp.max(s, axis=-1, keepdims=True)
            e = jnp.exp(s - peak)
            total = jnp.sum(e, axis=-1, keepdims=True)
            mixed = mixed + nn((e / total).astype(BF), values[g])
            lse = peak + jnp.log(total)
            lse_all = jnp.where(lane_of(lse_all.shape) == 2 * head + g, lse, lse_all)
        o_ref[:, head * LANES : (head + 1) * LANES] = mixed.astype(BF)
    lse_ref[...] = lse_all
    whole[...] = nn(o_ref[...], wo_ref[...])
    for start, part in zip(starts, parts):
        part[...] = whole[pl.ds(start, rows), :].astype(part.dtype)


def norm_two_kernel(x_ref, gain_ref, own_ref, *refs):
    others, (h_ref, n_ref) = refs[:-2], refs[-2:]
    attn = own_ref[...]
    for other in others:
        attn = attn + other[...].astype(F32)
    h = x_ref[...].astype(F32) + attn
    inv = lax.rsqrt(jnp.mean(h * h, axis=-1, keepdims=True) + EPS)
    h_ref[...] = h
    n_ref[...] = (h * inv * gain_ref[...]).astype(BF)


def together_kernel(*refs):
    pieces, out = refs[:-1], refs[-1]
    at = 0
    for piece in pieces:
        if len(piece.shape) == 2:
            out[at] = piece[...]
            at += 1
        else:
            out[at : at + piece.shape[0]] = piece[...]
            at += piece.shape[0]


def together(pieces):
    count = sum(1 if x.ndim == 2 else x.shape[0] for x in pieces)
    return call(
        together_kernel, [shape((count, *pieces[0].shape[-2:]), pieces[0].dtype)], pieces, "together"
    )[0]


def router_of(rows, router_ref, routes, experts):
    z = nt(rows, router_ref[...])
    lane = lane_of(z.shape)
    z = jnp.where(lane < experts, z, MASKED)
    e = jnp.exp(z - jnp.max(z, axis=-1, keepdims=True))
    probs = e / jnp.sum(e, axis=-1, keepdims=True)
    chosen = chosen_of(lane, routes)
    zc = jnp.where(chosen, z, MASKED)
    ec = jnp.where(chosen, jnp.exp(zc - jnp.max(zc, axis=-1, keepdims=True)), 0.0)
    return probs, ec / jnp.sum(ec, axis=-1, keepdims=True)


def chosen_of(lane, routes):
    place, named = lane.astype(F32), routes.astype(F32)
    chosen = place == named[:, 0:1]
    for k in range(1, TOP):
        chosen = chosen | (place == named[:, k : k + 1])
    return chosen


def counts_kernel(*refs):
    pieces, out = refs[:-1], refs[-1]
    total = 0.0
    for piece in pieces:
        width = piece.shape[-1] - LANES
        blocks = [piece[:, width:]] if len(piece.shape) == 2 else [
            piece[i, :, width:] for i in range(piece.shape[0])
        ]
        for routes in blocks:
            named = chosen_of(lane_of(routes.shape), routes).astype(F32)
            total = total + jnp.sum(named, axis=0, keepdims=True)
    out[...] = total


def weights_kernel(wg_ref, wu_ref, out_ref):
    hidden = wg_ref.shape[2]
    out_ref[:, :hidden] = wg_ref[0]
    out_ref[:, hidden:] = wu_ref[0]


def gate_up_weights(w_gate, w_up):
    local, width, hidden = w_gate.shape
    block = pl.BlockSpec((1, width, hidden), lambda e: (e, 0, 0))
    return pl.pallas_call(
        weights_kernel,
        grid=(local,),
        in_specs=[block, block],
        out_specs=pl.BlockSpec((width, 2 * hidden), lambda e: (0, e)),
        out_shape=shape((width, 2 * hidden * local), BF),
        compiler_params=pltpu.CompilerParams(vmem_limit_bytes=30 * MIB),
        cost_estimate=pl.CostEstimate(flops=int(100.0*(0)), bytes_accessed=4 * w_gate.size * 2, transcendentals=0),
        name="gate_up_weights",
    )(w_gate, w_up)


def experts_kernel(experts, base_ref, x_ref, own_ref, far_ref, router_ref, wcat, wd_ref, *refs):
    cot_ref, dgu_ref, hg_ref, *ds, m_ref, v_ref = refs
    hidden = LANES
    pair = 2 * hidden
    rows, width = cot_ref.shape
    x = x_ref[...].reshape(rows, width)
    if far_ref is None:
        routes = own_ref[:, width:]
        cot_ref[...] = own_ref[:, :width]
    else:
        pieces = [own_ref[...]] + [far_ref[i] for i in range(far_ref.shape[0])]
        routes = jnp.concatenate([piece[:, width:] for piece in pieces], axis=0)
        cot_ref[...] = jnp.concatenate([piece[:, :width] for piece in pieces], axis=0)
    _, gates = router_of(x, router_ref, routes, experts)
    lane = lane_of(gates.shape)
    dots = jnp.zeros(gates.shape, F32)
    v_ref[...] = nt(cot_ref[...], wd_ref[...])
    for e in range(hg_ref.shape[1] // hidden):
        mine = lane == base_ref[0] + e
        g = jnp.sum(jnp.where(mine, gates, 0.0), axis=-1, keepdims=True)
        both = nn(x, wcat[:, e * pair : (e + 1) * pair])
        v = v_ref[:, e * hidden : (e + 1) * hidden]
        gate, up = both[:, :hidden], both[:, hidden:]
        sig = 1.0 / (1.0 + jnp.exp(-gate))
        act = gate * sig
        hid = act * up
        dots = jnp.where(mine, jnp.sum(hid * v, axis=-1, keepdims=True), dots)
        gv = g * v
        hg_ref[:, e * hidden : (e + 1) * hidden] = (g * hid).astype(BF)
        d_gate = gv * up * sig * (1.0 + gate * (1.0 - sig))
        dgu_ref[:, e * pair : e * pair + hidden] = d_gate.astype(BF)
        dgu_ref[:, e * pair + hidden : (e + 1) * pair] = (gv * act).astype(BF)

    def put(outs, columns, value):
        at = 0
        for out in outs:
            part = value.astype(out.dtype)
            if len(out.shape) == 2:
                out[:, columns] = part[at : at + out.shape[0]]
                at += out.shape[0]
            else:
                step = out.shape[1]
                for i in range(out.shape[0]):
                    out[i, :, columns] = part[i * step : (i + 1) * step]

    put(ds, slice(width, width + LANES), dots)
    step = 256
    for at in range(0, width, step):
        put(ds, slice(at, at + step), nt(dgu_ref[...], wcat[at : at + step, :]))
    put([m_ref], slice(0, width), nn(hg_ref[...], wd_ref[...]))


def run_experts(experts, base, x, own, far, router, wcat, down_flat, kind, apart=False):
    count, rows, width = x.shape
    inner = down_flat.shape[0]
    wide = width + LANES
    total = count * rows
    few = count <= FEW
    step = total if few else 256
    resident = pl.BlockSpec(memory_space=pltpu.VMEM)
    per = lambda w: resident if few else pl.BlockSpec((step, w), lambda i: (i, 0))
    kernel = functools.partial(experts_kernel, experts)
    if few:
        data, dims = [x, own, far], lambda w: (count, rows, w)
    else:
        joined = jnp.concatenate([own[None], far], axis=0)
        data, dims = [x.reshape(total, width), joined.reshape(total, wide)], lambda w: (total, w)
        whole_kernel = kernel
        kernel = lambda b, x, c, *refs: whole_kernel(b, x, c, None, *refs)
    if few and apart:
        d_shapes = [shape((rows, wide), BF if i else F32) for i in range(count)]
    else:
        d_shapes = [shape(dims(wide), kind)]
    cot, dgu, hid, *d, m = pl.pallas_call(
        kernel,
        grid=(total // step,),
        in_specs=[pl.BlockSpec(memory_space=pltpu.SMEM)]
        + [per(z.shape[-1]) for z in data]
        + [resident] * 3,
        out_specs=[per(width), per(2 * inner), per(inner)]
        + [per(wide)] * len(d_shapes)
        + [per(width)],
        out_shape=[
            shape((total, width), BF),
            shape((total, 2 * inner), BF),
            shape((total, inner), BF),
            *d_shapes,
            shape(dims(width), kind),
        ],
        scratch_shapes=[pltpu.VMEM((step, inner), F32)],
        compiler_params=pltpu.CompilerParams(vmem_limit_bytes=(14 if few else 30) * MIB),
        cost_estimate=pl.CostEstimate(flops=int(100.0*(total * width * inner // 8)), bytes_accessed=0, transcendentals=0),
        name="experts",
    )(base, *data, router, wcat, down_flat)
    if not few:
        d = list(d[0].reshape(count, rows, wide)) if apart else [d[0].reshape(count, rows, wide)]
    return cot, dgu, hid, d if apart else d[0], m.reshape(count, rows, width)


def split_sum_kernel(count, near, *refs):
    ins, outs = refs[:count], refs[count:]
    for s in range(ins[0].shape[0]):
        total = ins[0][s].astype(F32)
        for x in ins[1:]:
            total = total + x[s].astype(F32)
        outs[s][...] = total.astype(outs[s].dtype)


def split_sum(arrays, name):
    count, *dims = arrays[0].shape
    outs = [shape(dims, F32)] + [shape(dims, BF)] * (count - 1)
    return call(functools.partial(split_sum_kernel, len(arrays), True), outs, arrays, name)


def add_kernel(*refs):
    pieces, out = refs[:-1], refs[-1]
    total = pieces[0][...].astype(F32)
    for piece in pieces[1:]:
        total = total + piece[...].astype(F32)
    out[...] = total.astype(out.dtype)


def added(pieces, kind, name):
    return call(add_kernel, [shape(pieces[0].shape, kind)], pieces, name)[0]


def grads_kernel(*refs):
    ns, dgus, hs, cs = (refs[4 * i : 4 * i + 4] for i in range(4))
    out_ref = refs[16]
    hidden, width = hs[0].shape[1], ns[0].shape[1]
    both, down = 0.0, 0.0
    for n, dgu, h, c in zip(ns, dgus, hs, cs):
        both = both + tn(n[...], dgu[...])
        down = down + tn(h[...], c[...])
    out_ref[0, :width, :] = both[:, :hidden].astype(BF)
    out_ref[0, width : 2 * width, :] = both[:, hidden:].astype(BF)
    for at in range(0, width, hidden):
        out_ref[0, 2 * width + at : 2 * width + at + hidden, :] = down[:, at : at + hidden].astype(BF)


def run_grads(n, dgu, h, c, local, hidden):
    width = n[0].shape[-1]
    flat = lambda xs: [x.reshape(-1, x.shape[-1]) for x in xs]
    n, c = flat(n), flat(c)
    whole = lambda xs: [pl.BlockSpec(x.shape, lambda e: (0, 0)) for x in xs]
    cols = lambda xs, w: [pl.BlockSpec((x.shape[0], w), lambda e: (0, e)) for x in xs]
    few = n[0].shape[0] <= 512
    return pl.pallas_call(
        grads_kernel,
        grid=(local,),
        in_specs=whole(n) + cols(dgu, 2 * hidden) + cols(h, hidden) + whole(c),
        out_specs=pl.BlockSpec((1, 3 * width, hidden), lambda e: (e, 0, 0)),
        out_shape=shape((local, 3 * width, hidden), BF),
        compiler_params=pltpu.CompilerParams(vmem_limit_bytes=(20 if few else 58) * MIB),
        cost_estimate=pl.CostEstimate(flops=int(100.0*(24 * n[0].size * hidden * local)), bytes_accessed=0, transcendentals=0),
        name="expert_grads",
    )(*n, *dgu, *h, *c)


def both_copies_kernel(mine_ref, other_ref, out_ref):
    for e in range(mine_ref.shape[0]):
        total = mine_ref[e].astype(F32) + other_ref[e].astype(F32)
        hidden = total.shape[1]
        if out_ref.shape[2] == hidden:
            out_ref[e] = total
        else:
            for at in range(0, total.shape[0], hidden):
                out_ref[e, :, at : at + hidden] = total[at : at + hidden]


def both_copies(mine, other, which):
    local, rows, hidden = mine.shape
    width = rows // 3
    dims = (hidden, width) if which == 2 else (width, hidden)
    step = min(local, 2)
    block = pl.BlockSpec((step, width, hidden), lambda e: (e, which, 0))
    return pl.pallas_call(
        both_copies_kernel,
        grid=(local // step,),
        in_specs=[block, block],
        out_specs=pl.BlockSpec((step, *dims), lambda e: (e, 0, 0)),
        out_shape=shape((local, *dims), F32),
        compiler_params=pltpu.CompilerParams(vmem_limit_bytes=58 * MIB),
        cost_estimate=pl.CostEstimate(flops=int(100.0*(0)), bytes_accessed=8 * mine.size, transcendentals=0),
        name="both_copies",
    )(mine, other)


def norm_back_kernel(experts, count, h_ref, n_ref, gain_ref, router_ref, bal_ref, cot_ref, *refs):
    sums, (wide_ref, dh_ref, small_ref) = refs[:count], refs[count:]
    near = sums[0][...].astype(F32)
    for other in sums[1:]:
        near = near + other[...].astype(F32)
    rows, width = h_ref.shape
    dots = near[:, width:]
    probs, gates = router_of(n_ref[...], router_ref, cot_ref[:, width:], experts)
    bal = bal_ref[...]
    d_chosen = gates * (dots - jnp.sum(gates * dots, axis=-1, keepdims=True))
    dz = probs * (bal - jnp.sum(probs * bal, axis=-1, keepdims=True)) + d_chosen
    dz = dz.astype(BF)
    wide_ref[:, width:] = dz
    dn = near[:, :width] + nn(dz, router_ref[...])
    h = h_ref[...]
    inv = lax.rsqrt(jnp.mean(h * h, axis=-1, keepdims=True) + EPS)
    u = gain_ref[...] * dn
    dy = cot_ref[:, :width].astype(F32)
    dh = dy + inv * u - h * (inv * inv * inv * jnp.mean(u * h, axis=-1, keepdims=True))
    dh_ref[...] = dh
    wide_ref[:, :width] = dh.astype(BF)
    small_ref[...] = jnp.zeros(small_ref.shape, F32)
    small_ref[1:2, :] = jnp.sum(dn * h * inv, axis=0, keepdims=True)
    small_ref[2:3, : probs.shape[1]] = jnp.sum(probs, axis=0, keepdims=True)


def attend_back_kernel(
    me_ref, w0, w1, w2, w3, x_ref, q_ref, k_ref, v_ref, lse_ref, wq_ref, wk_ref, wv_ref, wo_ref, cos_ref, sin_ref,
    small_in, a0, a1, a2, a3, o_ref, n_ref, small_ref, p0, p1, p2, p3, kept_ref, sent_ref,
    do_ref, whole, wide_ref, dq_ref, two_ref, dense
):
    rows = w0.shape[0]
    width = x_ref.shape[1]
    for r, piece in enumerate((w0, w1, w2, w3)):
        start = pl.multiple_of((me_ref[1] ^ r) * rows, rows)
        wide_ref[pl.ds(start, rows), :] = piece[...]
    do_ref[...] = nt(wide_ref[:, :width], wo_ref[...]).astype(BF)
    cosine, sine = cos_ref[...], sin_ref[...]
    scale = HD ** (-0.5)
    heads, keys_wide = q_ref.shape[1], k_ref.shape[1]
    dk_tiles = [0.0] * (keys_wide // LANES)
    dv_tiles = [0.0] * (keys_wide // LANES)

    def back(tile):
        return (tile * cosine - halves_swapped(tile) * sine).astype(BF)

    for head in range(heads // LANES):
        at = head // 2 * LANES
        side = head % 2
        keys = low_high(k_ref[:, at : at + LANES], side)
        values = low_high(v_ref[:, at : at + LANES], side)
        pair = q_ref[:, head * LANES : (head + 1) * LANES]
        grad = do_ref[:, head * LANES : (head + 1) * LANES]
        dq = 0.0
        dk, dv = [], []
        for g in range(2):
            s = nt(pair, keys[g]) * scale
            lse = lse_ref[:, 2 * head + g : 2 * head + g + 1]
            p = jnp.where(causal(s), jnp.exp(s - lse), 0.0)
            dp = nt(grad, values[g])
            ds = (p * (dp - jnp.sum(p * dp, axis=-1, keepdims=True))).astype(BF)
            dq = dq + nn(ds, keys[g])
            dk.append(tn(ds, pair))
            dv.append(tn(p.astype(BF), grad))
        dq_ref[:, head * LANES : (head + 1) * LANES] = back(dq * scale)
        mine = lane_of(dk[0].shape) < HD
        if side == 0:
            dk_sum = jnp.where(mine, dk[0] + pltpu.roll(dk[1], HD, 1), 0.0)
            dv_sum = jnp.where(mine, dv[0] + pltpu.roll(dv[1], HD, 1), 0.0)
        else:
            dk_sum = jnp.where(mine, 0.0, pltpu.roll(dk[0], HD, 1) + dk[1])
            dv_sum = jnp.where(mine, 0.0, pltpu.roll(dv[0], HD, 1) + dv[1])
        dk_tiles[head // 2] = dk_tiles[head // 2] + dk_sum
        dv_tiles[head // 2] = dv_tiles[head // 2] + dv_sum
    for i, tile in enumerate(dk_tiles):
        at = heads + i * LANES
        dq_ref[:, at : at + LANES] = back(tile * scale)
    for i, tile in enumerate(dv_tiles):
        at = heads + keys_wide + i * LANES
        dq_ref[:, at : at + LANES] = tile.astype(BF)
    dn = nt(dq_ref[:, :heads], wq_ref[...])
    dn = dn + nt(dq_ref[:, heads : heads + keys_wide], wk_ref[...])
    whole[...] = dn + nt(dq_ref[:, heads + keys_wide :], wv_ref[...])
    x = x_ref[...].astype(F32)
    inv = lax.rsqrt(jnp.mean(x * x, axis=-1, keepdims=True) + EPS)
    small_ref[...] = small_in[...]
    small_ref[0:1, :] = jnp.sum(whole[...] * x * inv, axis=0, keepdims=True)
    for r, part in enumerate((p0, p1, p2, p3)):
        start = pl.multiple_of((me_ref[1] ^ r) * rows, rows)
        part[...] = whole[pl.ds(start, rows), :].astype(part.dtype)
    for r, piece in enumerate((a0, a1, a2, a3)):
        start = pl.multiple_of((me_ref[1] ^ r) * rows, rows)
        two_ref[pl.ds(start, rows), :] = piece[0]
    columns = dq_ref.shape[1]
    dense[:, :columns] = tn(n_ref[...], dq_ref[...])
    dense[:, columns : columns + heads] = tn(wide_ref[:, :width], o_ref[...])
    dense[:, columns + heads :] = tn(two_ref[...], wide_ref[:, width:])
    half = kept_ref.shape[0]
    kept_ref[...] = dense[pl.ds(pl.multiple_of(me_ref[0] * half, half), half), :]
    sent_ref[...] = dense[pl.ds(pl.multiple_of((1 - me_ref[0]) * half, half), half), :].astype(BF)


def input_grad_kernel(x_ref, gain_ref, dh_ref, *refs):
    parts, ig_ref = refs[:-1], refs[-1]
    x = x_ref[...].astype(F32)
    inv = lax.rsqrt(jnp.mean(x * x, axis=-1, keepdims=True) + EPS)
    dn = parts[0][...].astype(F32)
    for part in parts[1:]:
        dn = dn + part[...].astype(F32)
    u = gain_ref[...] * dn
    ig = dh_ref[...] + inv * u - x * (inv * inv * inv * jnp.mean(u * x, axis=-1, keepdims=True))
    ig_ref[...] = ig.astype(BF)


def out_kernel(h_ref, small_ref, *refs):
    moes, out_ref = refs[:-1], refs[-1]
    rows = h_ref.shape[0]
    out = h_ref[...]
    for moe in moes:
        out = out + moe[...].astype(F32)
    out_ref[:rows, :] = out.astype(BF)
    small = small_ref[...]
    high = small.astype(BF).astype(F32)
    out_ref[rows:, :] = jnp.concatenate([high, small - high], axis=0).astype(BF)


def natural_kernel(me_ref, *refs):
    pieces, out = refs[:-1], refs[-1]
    rows = pieces[0].shape[0]
    for r, piece in enumerate(pieces):
        start = pl.multiple_of((me_ref[0] ^ r) * rows, rows)
        out[pl.ds(start, rows), :] = piece[...].astype(out.dtype)


def out_whole_kernel(me_ref, *refs):
    pieces, (out_ref, small_ref, held) = refs[:-3], refs[-3:]
    rows = pieces[0].shape[0] - 16
    for r, piece in enumerate(pieces):
        start = pl.multiple_of((me_ref[0] ^ r) * rows, rows)
        out_ref[pl.ds(start, rows), :] = piece[:rows, :]
        both = piece[rows:, :].astype(F32)
        held[me_ref[0] ^ r] = both[:8] + both[8:]
    total = held[0]
    for i in range(1, len(pieces)):
        total = total + held[i]
    small_ref[...] = total


def kept_and_dealt_kernel(me_ref, kept_ref, got_ref, small_ref, small_got_ref, *outs):
    small_out, outs = outs[-1], outs[:-1]
    small = small_ref[...] + small_got_ref[...]
    high = small[:4].astype(BF).astype(F32)
    both = jnp.concatenate([high, small[:4] - high], axis=0).astype(BF).astype(F32)
    small_out[...] = both
    rows, columns = outs[0].shape
    upper = lane_of((8, LANES)) >= HD
    parts = []
    for at in range(0, both.shape[1], LANES):
        tile = both[:, at : at + LANES]
        parts += [jnp.where(upper, pltpu.roll(tile, HD, 1), 0.0), jnp.where(upper, tile, 0.0)]
    if len(parts) * 8 == rows:
        extra = jnp.concatenate(parts, axis=0)
    else:
        extra = jnp.zeros((rows, LANES), F32)
    for r, out in enumerate(outs):
        start = pl.multiple_of((me_ref[0] ^ r) * rows, rows)
        at = pl.ds(start, rows)
        total = kept_ref[at, :] + got_ref[at, :].astype(F32)
        out[:, : columns - LANES] = total[:, : columns - LANES].astype(out.dtype)
        out[:, columns - LANES :] = (total[:, columns - LANES :] + extra).astype(out.dtype)


def dense_sum_kernel(me_ref, small_ref, mine_ref, *refs):
    others, outs, held = refs[:-7], refs[-7:-1], refs[-1]
    q_ref, k_ref, v_ref, o_ref, r_ref, small_out = outs
    total = mine_ref[...]
    for other in others:
        total = total + other[...].astype(F32)
    at = 0
    for out in (q_ref, k_ref, v_ref):
        out[...] = total[:, at : at + out.shape[1]]
        at += out.shape[1]
    o_ref[...] = total[:, at : at + o_ref.shape[0]].T
    at += o_ref.shape[0]
    r_ref[...] = total[:, at : at + r_ref.shape[1]]
    held[me_ref[0]] = small_ref[...]
    if total.shape[0] * HD != 8 * small_ref.shape[1]:
        others = []
    lower = lane_of((8, LANES)) < HD
    for i, other in enumerate(others):
        for j in range(small_ref.shape[1] // LANES):
            first = other[16 * j : 16 * j + 16, at : at + LANES].astype(F32)
            tile = jnp.where(lower, pltpu.roll(first[:8], HD, 1), first[8:])
            held[me_ref[0] ^ (i + 1), :, j * LANES : (j + 1) * LANES] = tile
    small = held[0] if others else small_ref[...]
    for i in range(1, len(others) + 1):
        small = small + held[i]
    small_out[...] = jnp.concatenate([small[:4] + small[4:], jnp.zeros_like(small[:4])], axis=0)


def on_device(
    tokens,
    routes,
    gain_first,
    w_query,
    w_key,
    w_value,
    w_output,
    gain_second,
    w_router,
    w_gate,
    w_up,
    w_down,
    cotangent,
):
    seq_len, width = tokens.shape
    experts = w_router.shape[1]
    local, _, hidden = w_gate.shape
    tensor_size = lax.axis_size("tensor")
    expert_size = lax.axis_size("expert")
    dp_size = lax.axis_size("dp")
    token_count = seq_len * dp_size * expert_size
    rows = seq_len // tensor_size
    wide_width = width + LANES
    last = tensor_size - 1
    around = range(1, tensor_size)
    t_me, e_me, d_me = lax.axis_index("tensor"), lax.axis_index("expert"), lax.axis_index("dp")
    t_at = t_me.astype(jnp.int32).reshape(1)
    e_at = e_me.astype(jnp.int32).reshape(1)
    base = (e_me * local).astype(jnp.int32).reshape(1)
    d_at = jnp.stack([d_me, t_me]).astype(jnp.int32)
    cosine, sine = rope_tables(seq_len)
    gain_one, gain_two = gain_first[None], gain_second[None]
    down_flat = w_down.reshape(local * hidden, width)

    *cot_near, router = call(
        pieces_kernel,
        [shape((rows, wide_width), BF)] * tensor_size + [shape((LANES, width), BF)],
        (t_at, cotangent, routes.T, w_router.T),
        "pieces",
        "sbbb",
        scratch=[pltpu.VMEM((seq_len, LANES), F32)],
        limit=58,
    )
    cot_got = spread(cot_near[0], "expert")
    cot_got[0], tokens = tied(cot_got[0], tokens)

    heads, keys_wide = w_query.shape[1], w_key.shape[1]
    n_one, q, k, v, o, lse, xq, *rest = call(
        attend_kernel,
        [
            shape((seq_len, width), BF),
            shape((seq_len, heads), BF),
            shape((seq_len, keys_wide), BF),
            shape((seq_len, keys_wide), BF),
            shape((seq_len, heads), BF),
            shape((seq_len, LANES), F32),
            shape((rows, width), BF),
        ]
        + [shape((rows, width), F32)]
        + [shape((rows, width), BF)] * last,
        (t_at, tokens, gain_one, w_query, w_key, w_value, w_output, cosine, sine),
        "attend",
        "s" + "b" * 8,
        "bbbbbbv",
        scratch=[pltpu.VMEM((seq_len, width), F32)],
        limit=58,
        flops=2 * seq_len * width * 4 * heads,
    )
    parts = rest
    got = backwards(lambda r: swap(parts[r], "tensor", r), tensor_size)
    h, n_two = call(
        norm_two_kernel,
        [shape((rows, width), F32), shape((rows, width), BF)],
        (xq, gain_two, parts[0], *got),
        "norm_two",
        "bbb",
        "vv",
        limit=58,
    )

    n_two, cot_got = tied(n_two, cot_got)
    cot_far = together(cot_got)
    wcat = gate_up_weights(w_gate, w_up)
    two_got = spread(n_two, "expert")
    two_got[0], cot_late = tied(two_got[0], cot_far)
    cot_far = [cot_far] + backwards(lambda r: swap(cot_far, "tensor", r), last)
    cot_far.append(swap(cot_late, "tensor", last))

    first = together([n_two, *two_got])
    twos = [first] + backwards(lambda r: swap(first, "tensor", r), last)
    _, late = tied(cot_far[:last], first)
    twos.append(swap(late, "tensor", last))

    run = functools.partial(
        run_experts, experts, base, router=router, wcat=wcat, down_flat=down_flat
    )
    counts = call(counts_kernel, [shape((1, LANES), F32)], (*cot_near, *cot_far), "counts")[0]
    counts = counts + swap(counts, "dp", 1)
    balance = experts * (counts / (token_count * TOP)) / token_count
    made = [run(twos[0], cot_near[0], cot_far[0], kind=F32)]
    got = []
    for r in around:
        made[-1], (two, cot) = tied(made[-1], (twos[r], cot_far[r]))
        if r == last:
            balance, two = tied(balance, two)
        made.append(run(two, cot_near[r], cot, kind=BF, apart=r == last))
        if r < last:
            got.append(swap(made[-1][3], "tensor", r))
    cots, dgus, hids, ds, moes = zip(*made)
    near_last, *far_last = ds[last]
    from_last = deal(far_last, "expert")
    grads = run_grads(twos, dgus, hids, cots, local, hidden)
    grads, (got, from_last) = tied(grads, (got, from_last))
    near, *across = split_sum([ds[0], *got], "dn_sum")
    across[0], middle = tied(across[0], moes[1:last])
    across = deal(across, "expert")
    across[0], near_last = tied(across[0], near_last)
    through = added([near_last, *from_last], BF, "through")
    near_sums = [near, swap(through, "tensor", last), *across]
    moe_got = [swap(middle[r - 1], "tensor", r) for r in range(1, last)]
    moe_got, near_sums = tied(moe_got, near_sums)

    wide, dh, small = call(
        functools.partial(norm_back_kernel, experts, len(near_sums)),
        [shape((rows, wide_width), BF), shape((rows, width), F32), shape((8, width), F32)],
        (h, n_two, gain_two, router, balance, cot_near[0], *near_sums),
        "norm_back",
        "v",
        "vvv",
    )
    wides = [wide] + backwards(lambda r: swap(wide, "tensor", r), tensor_size)
    _, late_grads = tied(wide, grads)
    grads_got = swap(late_grads, "dp", 1)
    grads_got, wides = tied(grads_got, wides)
    wides, moe_last = tied(wides, moes[last])
    moe_got.append(swap(moe_last, "tensor", last))

    half = width // dp_size
    chunk = half // expert_size
    columns = heads + 2 * keys_wide
    all_columns = columns + heads + LANES
    own_block = pl.BlockSpec((1, rows, width), lambda i: (0, 0, 0))
    small, *back_parts, kept, sent = call(
        attend_back_kernel,
        [shape((8, width), F32), shape((rows, width), F32)]
        + [shape((rows, width), BF)] * last
        + [shape((half, all_columns), F32), shape((half, all_columns), BF)],
        (d_at, *wides, tokens, q, k, v, lse, w_query, w_key, w_value, w_output, cosine, sine, small)
        + (*twos, o, n_one),
        "attend_back",
        ["s"] + ["v"] * tensor_size + ["b"] * 12 + [own_block] * tensor_size + ["b"] * 2,
        "bvvvvbb",
        limit=58,
        scratch=[
            pltpu.VMEM((seq_len, heads), BF),
            pltpu.VMEM((seq_len, width), F32),
            pltpu.VMEM((seq_len, wide_width), BF),
            pltpu.VMEM((seq_len, columns), BF),
            pltpu.VMEM((seq_len, width), BF),
            pltpu.VMEM((width, all_columns), F32),
        ],
        flops=2 * seq_len * width * 4 * heads,
    )
    part_sums = [back_parts[0]] + backwards(lambda r: swap(back_parts[r], "tensor", r), tensor_size)
    mine, *others, small = call(
        kept_and_dealt_kernel,
        [shape((chunk, all_columns), F32)]
        + [shape((chunk, all_columns), BF)] * (expert_size - 1)
        + [shape((8, width), F32)],
        (e_at, kept, swap(sent, "dp", 1), small, swap(small, "dp", 1)),
        "dense_dealt",
        "s",
    )
    others = deal(others, "expert")
    grad_gate = both_copies(grads, grads_got, 0)
    (grad_gate, others[0]), part_sums = tied((grad_gate, others[0]), part_sums)
    moe_near, *moe_across = split_sum([moes[0], *moe_got], "moe_sum")
    moe_sums = [moe_near, *deal(moe_across, "expert")]
    ig = call(
        input_grad_kernel, [shape((rows, width), BF)], (xq, gain_one, dh, *part_sums), "input_grad", "bbbb", limit=58
    )[0]
    igs = [ig] + backwards(lambda r: swap(ig, "tensor", r), tensor_size)
    grad_up = both_copies(grads, grads_got, 1)
    grad_up, others = tied(grad_up, others)
    g_query, g_key, g_value, g_out, g_router, small = call(
        dense_sum_kernel,
        [
            shape((chunk, heads), F32),
            shape((chunk, keys_wide), F32),
            shape((chunk, keys_wide), F32),
            shape((heads, chunk), F32),
            shape((chunk, LANES), F32),
            shape((8, width), F32),
        ],
        (e_at, small, mine, *others),
        "dense_sum",
        "s",
        "bbbbbv",
        scratch=[pltpu.VMEM((expert_size, 8, width), F32)],
    )
    if chunk * HD != 8 * width:
        small = jnp.sum(lax.all_gather(small, "expert"), axis=0)
    igs, small = tied(igs, small)
    input_grad = call(
        natural_kernel, [shape((seq_len, width), F32)], (t_at, *igs), "input_grad_whole", "s", "b"
    )[0]
    out_piece = call(out_kernel, [shape((rows + 16, width), BF)], (h, small, *moe_sums), "out_piece")[0]
    outs = [out_piece] + backwards(lambda r: swap(out_piece, "tensor", r), tensor_size)
    grad_down = both_copies(grads, grads_got, 2)
    grad_down, outs = tied(grad_down, outs)
    output, small = call(
        out_whole_kernel,
        [shape((seq_len, width), BF), shape((8, width), F32)],
        (t_at, *outs),
        "output",
        "s",
        "bv",
        scratch=[pltpu.VMEM((tensor_size, 8, width), F32)],
    )
    at = (d_me * expert_size + e_me) * chunk
    loss_value = (experts * balance * small[2:3, :LANES])[0, :experts]
    return (
        output,
        loss_value,
        input_grad,
        lax.dynamic_slice(small, (0, at), (1, chunk))[0],
        g_query,
        g_key,
        g_value,
        g_out,
        lax.dynamic_slice(small, (1, at), (1, chunk))[0],
        g_router[:, :experts],
        grad_gate,
        grad_up,
        grad_down,
    )


def solution(mesh):
    rows = ("dp", "expert")
    placed = (
        P(rows, None),
        P(rows, None),
        P(),
        P(None, "tensor"),
        P(None, "tensor"),
        P(None, "tensor"),
        P("tensor", None),
        P(),
        P(),
        P("expert", None, "tensor"),
        P("expert", None, "tensor"),
        P("expert", "tensor", None),
        P(rows, None),
    )
    return jax.shard_map(
        on_device,
        mesh=mesh,
        in_specs=placed,
        out_specs=(
            P(rows, None),
            P(),
            P(rows, None),
            P(rows),
            P(rows, "tensor"),
            P(rows, "tensor"),
            P(rows, "tensor"),
            P("tensor", rows),
            P(rows),
            P(rows, None),
            P("expert", None, "tensor"),
            P("expert", None, "tensor"),
            P("expert", "tensor", None),
        ),
        check_vma=False,
    )
```

```python
import functools

import jax
import jax.numpy as jnp
import numpy as np
from jax import lax
from jax.experimental import pallas as pl
from jax.experimental.pallas import tpu as pltpu
from jax.sharding import PartitionSpec as P

HD = 64
TOP = 8
EPS = 1e-06
ROPE_BASE = 10000.0
MASKED = -1e30
BF = jnp.bfloat16
F32 = jnp.float32
FEW = 8
LANES = 128
MIB = 1 << 20


def dot(a, b, dims):
    return lax.dot_general(a, b, (dims, ((), ())), preferred_element_type=F32)


def nn(a, b):
    return dot(a, b, ((1,), (0,)))


def nt(a, b):
    return dot(a, b, ((1,), (1,)))


def tn(a, b):
    return dot(a, b, ((0,), (0,)))


def swap(x, axis, distance):
    size = lax.axis_size(axis)
    return lax.ppermute(x, axis, [(i, i ^ distance) for i in range(size)])


def backwards(make, size):
    return [make(r) for r in range(size - 1, 0, -1)][::-1]


def spread(x, axis):
    size = lax.axis_size(axis)
    if size <= FEW:
        return backwards(lambda r: swap(x, axis, r), size)
    whole = lax.all_gather(x, axis)
    order = jnp.arange(1, size) ^ lax.axis_index(axis)
    return list(jnp.take(whole, order, axis=0))


def deal(parts, axis):
    size = lax.axis_size(axis)
    if size <= FEW:
        return backwards(lambda r: swap(parts[r - 1], axis, r), size)
    order = jnp.arange(size) ^ lax.axis_index(axis)
    whole = jnp.take(jnp.stack([parts[0], *parts]), order, axis=0)
    back = lax.all_to_all(whole, axis, 0, 0, tiled=True)
    return list(jnp.take(back, order, axis=0)[1:])


def rope_tables(seq_len):
    half = HD // 2
    frequency = ROPE_BASE ** (-(np.arange(half, dtype=np.float32) * 2.0) / HD)
    angles = np.arange(seq_len, dtype=np.float32)[:, None] * frequency[None, :].astype(np.float32)
    cosine, sine = np.cos(angles), np.sin(angles)
    heads = LANES // HD
    return (
        np.tile(cosine, (1, 2 * heads)).astype(np.float32),
        np.tile(np.concatenate([-sine, sine], axis=1), (1, heads)).astype(np.float32),
    )


def lane_of(shape):
    return lax.broadcasted_iota(jnp.int32, shape, 1)


def halves_swapped(x):
    first = lane_of(x.shape) % HD < HD // 2
    half = HD // 2
    return jnp.where(first, pltpu.roll(x, LANES - half, 1), pltpu.roll(x, half, 1))


def low_high(x, head):
    other = pltpu.roll(x.astype(F32), HD, 1).astype(x.dtype)
    low = lane_of(x.shape) < HD
    zero = jnp.zeros_like(x)
    at_low, at_high = (x, other) if head == 0 else (other, x)
    return jnp.where(low, at_low, zero), jnp.where(low, zero, at_high)


def causal(scores):
    rows = lax.broadcasted_iota(jnp.int32, scores.shape, 0)
    return lane_of(scores.shape) <= rows


def shape(dims, kind):
    return jax.ShapeDtypeStruct(dims, kind)


def whole_block(dims):
    return pl.BlockSpec(dims, lambda i: (0,) * len(dims))


def call(kernel, outs, operands, name, places="", out_places="", scratch=(), limit=40, flops=0):
    kinds = {"s": pltpu.SMEM, "v": pltpu.VMEM}

    def spec(place, x):
        if not isinstance(place, str):
            return place
        if place == "b":
            return whole_block(x.shape)
        return pl.BlockSpec(memory_space=kinds[place])

    places = [*places] + ["v"] * (len(operands) - len(places))
    out_places = [*out_places] + ["v"] * (len(outs) - len(out_places))
    return pl.pallas_call(
        kernel,
        grid=(1,),
        out_shape=outs,
        in_specs=[spec(p, x) for p, x in zip(places, operands)],
        out_specs=[spec(p, x) for p, x in zip(out_places, outs)],
        scratch_shapes=list(scratch),
        compiler_params=pltpu.CompilerParams(vmem_limit_bytes=limit * MIB),
        cost_estimate=pl.CostEstimate(flops=int(100.0*(flops)), bytes_accessed=0, transcendentals=0),
        name=name,
    )(*operands)


def tied(first, then):
    return lax.optimization_barrier((first, then))


def pieces_kernel(me_ref, cot_ref, routes_ref, router_ref, *refs):
    cots, (router_out, held) = refs[:-2], refs[-2:]
    rows, width = cots[0].shape[0], cot_ref.shape[1]
    eye = lax.broadcasted_iota(jnp.int32, (TOP, LANES), 0) == lane_of((TOP, LANES))
    held[...] = tn(routes_ref[...].astype(F32).astype(BF), eye.astype(F32).astype(BF))
    for r, c in enumerate(cots):
        start = pl.multiple_of((me_ref[0] ^ r) * rows, rows)
        c[:, :width] = cot_ref[pl.ds(start, rows), :]
        c[:, width:] = held[pl.ds(start, rows), :].astype(BF)
    router_out[...] = jnp.zeros(router_out.shape, BF)
    router_out[: router_ref.shape[0], :] = router_ref[...]


def attend_kernel(
    me_ref, x_ref, gain_ref, wq_ref, wk_ref, wv_ref, wo_ref, cos_ref, sin_ref, *refs
):
    n_ref, q_ref, k_ref, v_ref, o_ref, lse_ref, xq_ref = refs[:7]
    parts, whole = refs[7:-1], refs[-1]
    rows, width = xq_ref.shape
    starts = [pl.multiple_of((me_ref[0] ^ r) * rows, rows) for r in range(4)]
    xq_ref[...] = x_ref[pl.ds(starts[0], rows), :]
    x = x_ref[...].astype(F32)
    inv = lax.rsqrt(jnp.mean(x * x, axis=-1, keepdims=True) + EPS)
    n = (x * inv * gain_ref[...]).astype(BF)
    n_ref[...] = n
    cosine, sine = cos_ref[...], sin_ref[...]
    q, k = nn(n, wq_ref[...]), nn(n, wk_ref[...])
    v_ref[...] = nn(n, wv_ref[...]).astype(BF)
    for at in range(0, q.shape[1], LANES):
        tile = q[:, at : at + LANES]
        q_ref[:, at : at + LANES] = (tile * cosine + halves_swapped(tile) * sine).astype(BF)
    for at in range(0, k.shape[1], LANES):
        tile = k[:, at : at + LANES]
        k_ref[:, at : at + LANES] = (tile * cosine + halves_swapped(tile) * sine).astype(BF)
    lse_all = jnp.zeros(lse_ref.shape, F32)
    for head in range(q.shape[1] // LANES):
        at = head // 2 * LANES
        keys = low_high(k_ref[:, at : at + LANES], head % 2)
        values = low_high(v_ref[:, at : at + LANES], head % 2)
        pair = q_ref[:, head * LANES : (head + 1) * LANES]
        mixed = 0.0
        for g in range(2):
            s = nt(pair, keys[g]) * HD ** (-0.5)
            s = jnp.where(causal(s), s, MASKED)
            peak = jnp.max(s, axis=-1, keepdims=True)
            e = jnp.exp(s - peak)
            total = jnp.sum(e, axis=-1, keepdims=True)
            mixed = mixed + nn((e / total).astype(BF), values[g])
            lse = peak + jnp.log(total)
            lse_all = jnp.where(lane_of(lse_all.shape) == 2 * head + g, lse, lse_all)
        o_ref[:, head * LANES : (head + 1) * LANES] = mixed.astype(BF)
    lse_ref[...] = lse_all
    whole[...] = nn(o_ref[...], wo_ref[...])
    for start, part in zip(starts, parts):
        part[...] = whole[pl.ds(start, rows), :].astype(part.dtype)


def norm_two_kernel(x_ref, gain_ref, own_ref, *refs):
    others, (h_ref, n_ref) = refs[:-2], refs[-2:]
    attn = own_ref[...]
    for other in others:
        attn = attn + other[...].astype(F32)
    h = x_ref[...].astype(F32) + attn
    inv = lax.rsqrt(jnp.mean(h * h, axis=-1, keepdims=True) + EPS)
    h_ref[...] = h
    n_ref[...] = (h * inv * gain_ref[...]).astype(BF)


def together_kernel(*refs):
    pieces, out = refs[:-1], refs[-1]
    at = 0
    for piece in pieces:
        if len(piece.shape) == 2:
            out[at] = piece[...]
            at += 1
        else:
            out[at : at + piece.shape[0]] = piece[...]
            at += piece.shape[0]


def together(pieces):
    count = sum(1 if x.ndim == 2 else x.shape[0] for x in pieces)
    return call(
        together_kernel, [shape((count, *pieces[0].shape[-2:]), pieces[0].dtype)], pieces, "together"
    )[0]


def router_of(rows, router_ref, routes, experts):
    z = nt(rows, router_ref[...])
    lane = lane_of(z.shape)
    z = jnp.where(lane < experts, z, MASKED)
    e = jnp.exp(z - jnp.max(z, axis=-1, keepdims=True))
    probs = e / jnp.sum(e, axis=-1, keepdims=True)
    chosen = chosen_of(lane, routes)
    zc = jnp.where(chosen, z, MASKED)
    ec = jnp.where(chosen, jnp.exp(zc - jnp.max(zc, axis=-1, keepdims=True)), 0.0)
    return probs, ec / jnp.sum(ec, axis=-1, keepdims=True)


def chosen_of(lane, routes):
    place, named = lane.astype(F32), routes.astype(F32)
    chosen = place == named[:, 0:1]
    for k in range(1, TOP):
        chosen = chosen | (place == named[:, k : k + 1])
    return chosen


def counts_kernel(*refs):
    pieces, out = refs[:-1], refs[-1]
    total = 0.0
    for piece in pieces:
        blocks = [piece] if len(piece.shape) == 2 else [piece.at[i] for i in range(piece.shape[0])]
        for block in blocks:
            routes = block[...]
            named = chosen_of(lane_of(routes.shape), routes).astype(F32)
            total = total + jnp.sum(named, axis=0, keepdims=True)
    out[...] = total


def last_lanes(x):
    at = x.shape[-1] // LANES - 1
    return pl.BlockSpec((*x.shape[:-1], LANES), lambda i: (0,) * (x.ndim - 1) + (at,))


def weights_kernel(wg_ref, wu_ref, out_ref):
    hidden = wg_ref.shape[2]
    out_ref[:, :hidden] = wg_ref[0]
    out_ref[:, hidden:] = wu_ref[0]


def gate_up_weights(w_gate, w_up):
    local, width, hidden = w_gate.shape
    block = pl.BlockSpec((1, width, hidden), lambda e: (e, 0, 0))
    return pl.pallas_call(
        weights_kernel,
        grid=(local,),
        in_specs=[block, block],
        out_specs=pl.BlockSpec((width, 2 * hidden), lambda e: (0, e)),
        out_shape=shape((width, 2 * hidden * local), BF),
        compiler_params=pltpu.CompilerParams(vmem_limit_bytes=30 * MIB),
        cost_estimate=pl.CostEstimate(flops=int(100.0*(0)), bytes_accessed=4 * w_gate.size * 2, transcendentals=0),
        name="gate_up_weights",
    )(w_gate, w_up)


def experts_kernel(experts, base_ref, x_ref, own_ref, far_ref, router_ref, wcat, wd_ref, *refs):
    cot_ref, dgu_ref, hg_ref, *ds, m_ref, v_ref = refs
    hidden = LANES
    pair = 2 * hidden
    rows, width = cot_ref.shape
    x = x_ref[...].reshape(rows, width)
    if far_ref is None:
        routes = own_ref[:, width:]
        cot_ref[...] = own_ref[:, :width]
    else:
        pieces = [own_ref[...]] + [far_ref[i] for i in range(far_ref.shape[0])]
        routes = jnp.concatenate([piece[:, width:] for piece in pieces], axis=0)
        cot_ref[...] = jnp.concatenate([piece[:, :width] for piece in pieces], axis=0)
    _, gates = router_of(x, router_ref, routes, experts)
    lane = lane_of(gates.shape)
    dots = jnp.zeros(gates.shape, F32)
    v_ref[...] = nt(cot_ref[...], wd_ref[...])
    for e in range(hg_ref.shape[1] // hidden):
        mine = lane == base_ref[0] + e
        g = jnp.sum(jnp.where(mine, gates, 0.0), axis=-1, keepdims=True)
        both = nn(x, wcat[:, e * pair : (e + 1) * pair])
        v = v_ref[:, e * hidden : (e + 1) * hidden]
        gate, up = both[:, :hidden], both[:, hidden:]
        sig = 1.0 / (1.0 + jnp.exp(-gate))
        act = gate * sig
        hid = act * up
        dots = jnp.where(mine, jnp.sum(hid * v, axis=-1, keepdims=True), dots)
        gv = g * v
        hg_ref[:, e * hidden : (e + 1) * hidden] = (g * hid).astype(BF)
        d_gate = gv * up * sig * (1.0 + gate * (1.0 - sig))
        dgu_ref[:, e * pair : e * pair + hidden] = d_gate.astype(BF)
        dgu_ref[:, e * pair + hidden : (e + 1) * pair] = (gv * act).astype(BF)

    def put(outs, columns, value):
        at = 0
        for out in outs:
            part = value.astype(out.dtype)
            if len(out.shape) == 2:
                out[:, columns] = part[at : at + out.shape[0]]
                at += out.shape[0]
            else:
                step = out.shape[1]
                for i in range(out.shape[0]):
                    out[i, :, columns] = part[i * step : (i + 1) * step]

    put(ds, slice(width, width + LANES), dots)
    step = 256
    for at in range(0, width, step):
        put(ds, slice(at, at + step), nt(dgu_ref[...], wcat[at : at + step, :]))
    put([m_ref], slice(0, width), nn(hg_ref[...], wd_ref[...]))


def run_experts(experts, base, x, own, far, router, wcat, down_flat, kind, apart=False):
    count, rows, width = x.shape
    inner = down_flat.shape[0]
    wide = width + LANES
    total = count * rows
    few = count <= FEW
    step = total if few else 256
    resident = pl.BlockSpec(memory_space=pltpu.VMEM)
    per = lambda w: resident if few else pl.BlockSpec((step, w), lambda i: (i, 0))
    kernel = functools.partial(experts_kernel, experts)
    if few:
        data, dims = [x, own, far], lambda w: (count, rows, w)
    else:
        joined = jnp.concatenate([own[None], far], axis=0)
        data, dims = [x.reshape(total, width), joined.reshape(total, wide)], lambda w: (total, w)
        whole_kernel = kernel
        kernel = lambda b, x, c, *refs: whole_kernel(b, x, c, None, *refs)
    if few and apart:
        d_shapes = [shape((rows, wide), BF if i else F32) for i in range(count)]
    else:
        d_shapes = [shape(dims(wide), kind)]
    cot, dgu, hid, *d, m = pl.pallas_call(
        kernel,
        grid=(total // step,),
        in_specs=[pl.BlockSpec(memory_space=pltpu.SMEM)]
        + [per(z.shape[-1]) for z in data]
        + [resident] * 3,
        out_specs=[per(width), per(2 * inner), per(inner)]
        + [per(wide)] * len(d_shapes)
        + [per(width)],
        out_shape=[
            shape((total, width), BF),
            shape((total, 2 * inner), BF),
            shape((total, inner), BF),
            *d_shapes,
            shape(dims(width), kind),
        ],
        scratch_shapes=[pltpu.VMEM((step, inner), F32)],
        compiler_params=pltpu.CompilerParams(vmem_limit_bytes=(14 if few else 30) * MIB),
        cost_estimate=pl.CostEstimate(flops=int(100.0*(total * width * inner // 8)), bytes_accessed=0, transcendentals=0),
        name="experts",
    )(base, *data, router, wcat, down_flat)
    if not few:
        d = list(d[0].reshape(count, rows, wide)) if apart else [d[0].reshape(count, rows, wide)]
    return cot, dgu, hid, d if apart else d[0], m.reshape(count, rows, width)


def split_sum_kernel(count, near, *refs):
    ins, outs = refs[:count], refs[count:]
    for s in range(ins[0].shape[0]):
        total = ins[0][s].astype(F32)
        for x in ins[1:]:
            total = total + x[s].astype(F32)
        outs[s][...] = total.astype(outs[s].dtype)


def split_sum(arrays, name):
    count, *dims = arrays[0].shape
    outs = [shape(dims, F32)] + [shape(dims, BF)] * (count - 1)
    return call(functools.partial(split_sum_kernel, len(arrays), True), outs, arrays, name)


def add_kernel(*refs):
    pieces, out = refs[:-1], refs[-1]
    total = pieces[0][...].astype(F32)
    for piece in pieces[1:]:
        total = total + piece[...].astype(F32)
    out[...] = total.astype(out.dtype)


def added(pieces, kind, name):
    return call(add_kernel, [shape(pieces[0].shape, kind)], pieces, name)[0]


def grads_kernel(*refs):
    ns, dgus, hs, cs = (refs[4 * i : 4 * i + 4] for i in range(4))
    out_ref = refs[16]
    hidden, width = hs[0].shape[1], ns[0].shape[1]
    both, down = 0.0, 0.0
    for n, dgu, h, c in zip(ns, dgus, hs, cs):
        both = both + tn(n[...], dgu[...])
        down = down + tn(h[...], c[...])
    out_ref[0, :width, :] = both[:, :hidden].astype(BF)
    out_ref[0, width : 2 * width, :] = both[:, hidden:].astype(BF)
    for at in range(0, width, hidden):
        out_ref[0, 2 * width + at : 2 * width + at + hidden, :] = down[:, at : at + hidden].astype(BF)


def run_grads(n, dgu, h, c, local, hidden):
    width = n[0].shape[-1]
    flat = lambda xs: [x.reshape(-1, x.shape[-1]) for x in xs]
    n, c = flat(n), flat(c)
    whole = lambda xs: [pl.BlockSpec(x.shape, lambda e: (0, 0)) for x in xs]
    cols = lambda xs, w: [pl.BlockSpec((x.shape[0], w), lambda e: (0, e)) for x in xs]
    few = n[0].shape[0] <= 512
    return pl.pallas_call(
        grads_kernel,
        grid=(local,),
        in_specs=whole(n) + cols(dgu, 2 * hidden) + cols(h, hidden) + whole(c),
        out_specs=pl.BlockSpec((1, 3 * width, hidden), lambda e: (e, 0, 0)),
        out_shape=shape((local, 3 * width, hidden), BF),
        compiler_params=pltpu.CompilerParams(vmem_limit_bytes=(20 if few else 58) * MIB),
        cost_estimate=pl.CostEstimate(flops=int(100.0*(24 * n[0].size * hidden * local)), bytes_accessed=0, transcendentals=0),
        name="expert_grads",
    )(*n, *dgu, *h, *c)


def both_copies_kernel(mine_ref, other_ref, out_ref):
    for e in range(mine_ref.shape[0]):
        total = mine_ref[e].astype(F32) + other_ref[e].astype(F32)
        hidden = total.shape[1]
        if out_ref.shape[2] == hidden:
            out_ref[e] = total
        else:
            for at in range(0, total.shape[0], hidden):
                out_ref[e, :, at : at + hidden] = total[at : at + hidden]


def both_copies(mine, other, which):
    local, rows, hidden = mine.shape
    width = rows // 3
    dims = (hidden, width) if which == 2 else (width, hidden)
    step = min(local, 2)
    block = pl.BlockSpec((step, width, hidden), lambda e: (e, which, 0))
    return pl.pallas_call(
        both_copies_kernel,
        grid=(local // step,),
        in_specs=[block, block],
        out_specs=pl.BlockSpec((step, *dims), lambda e: (e, 0, 0)),
        out_shape=shape((local, *dims), F32),
        compiler_params=pltpu.CompilerParams(vmem_limit_bytes=58 * MIB),
        cost_estimate=pl.CostEstimate(flops=int(100.0*(0)), bytes_accessed=8 * mine.size, transcendentals=0),
        name="both_copies",
    )(mine, other)


def norm_back_kernel(experts, count, h_ref, n_ref, gain_ref, router_ref, bal_ref, cot_ref, *refs):
    sums, (wide_ref, dh_ref, small_ref) = refs[:count], refs[count:]
    near = sums[0][...].astype(F32)
    for other in sums[1:]:
        near = near + other[...].astype(F32)
    rows, width = h_ref.shape
    dots = near[:, width:]
    probs, gates = router_of(n_ref[...], router_ref, cot_ref[:, width:], experts)
    bal = bal_ref[...]
    d_chosen = gates * (dots - jnp.sum(gates * dots, axis=-1, keepdims=True))
    dz = probs * (bal - jnp.sum(probs * bal, axis=-1, keepdims=True)) + d_chosen
    dz = dz.astype(BF)
    wide_ref[:, width:] = dz
    dn = near[:, :width] + nn(dz, router_ref[...])
    h = h_ref[...]
    inv = lax.rsqrt(jnp.mean(h * h, axis=-1, keepdims=True) + EPS)
    u = gain_ref[...] * dn
    dy = cot_ref[:, :width].astype(F32)
    dh = dy + inv * u - h * (inv * inv * inv * jnp.mean(u * h, axis=-1, keepdims=True))
    dh_ref[...] = dh
    wide_ref[:, :width] = dh.astype(BF)
    small_ref[...] = jnp.zeros(small_ref.shape, F32)
    small_ref[1:2, :] = jnp.sum(dn * h * inv, axis=0, keepdims=True)
    small_ref[2:3, : probs.shape[1]] = jnp.sum(probs, axis=0, keepdims=True)


def attend_back_kernel(
    me_ref, w0, w1, w2, w3, x_ref, q_ref, k_ref, v_ref, lse_ref, wq_ref, wk_ref, wv_ref, wo_ref, cos_ref, sin_ref,
    small_in, wide_ref, dq_ref, small_ref, p0, p1, p2, p3, do_ref, whole
):
    rows = w0.shape[0]
    width = x_ref.shape[1]
    for r, piece in enumerate((w0, w1, w2, w3)):
        start = pl.multiple_of((me_ref[0] ^ r) * rows, rows)
        wide_ref[pl.ds(start, rows), :] = piece[...]
    do_ref[...] = nt(wide_ref[:, :width], wo_ref[...]).astype(BF)
    cosine, sine = cos_ref[...], sin_ref[...]
    scale = HD ** (-0.5)
    heads, keys_wide = q_ref.shape[1], k_ref.shape[1]
    dk_tiles = [0.0] * (keys_wide // LANES)
    dv_tiles = [0.0] * (keys_wide // LANES)

    def back(tile):
        return (tile * cosine - halves_swapped(tile) * sine).astype(BF)

    for head in range(heads // LANES):
        at = head // 2 * LANES
        side = head % 2
        keys = low_high(k_ref[:, at : at + LANES], side)
        values = low_high(v_ref[:, at : at + LANES], side)
        pair = q_ref[:, head * LANES : (head + 1) * LANES]
        grad = do_ref[:, head * LANES : (head + 1) * LANES]
        dq = 0.0
        dk, dv = [], []
        for g in range(2):
            s = nt(pair, keys[g]) * scale
            lse = lse_ref[:, 2 * head + g : 2 * head + g + 1]
            p = jnp.where(causal(s), jnp.exp(s - lse), 0.0)
            dp = nt(grad, values[g])
            ds = (p * (dp - jnp.sum(p * dp, axis=-1, keepdims=True))).astype(BF)
            dq = dq + nn(ds, keys[g])
            dk.append(tn(ds, pair))
            dv.append(tn(p.astype(BF), grad))
        dq_ref[:, head * LANES : (head + 1) * LANES] = back(dq * scale)
        mine = lane_of(dk[0].shape) < HD
        if side == 0:
            dk_sum = jnp.where(mine, dk[0] + pltpu.roll(dk[1], HD, 1), 0.0)
            dv_sum = jnp.where(mine, dv[0] + pltpu.roll(dv[1], HD, 1), 0.0)
        else:
            dk_sum = jnp.where(mine, 0.0, pltpu.roll(dk[0], HD, 1) + dk[1])
            dv_sum = jnp.where(mine, 0.0, pltpu.roll(dv[0], HD, 1) + dv[1])
        dk_tiles[head // 2] = dk_tiles[head // 2] + dk_sum
        dv_tiles[head // 2] = dv_tiles[head // 2] + dv_sum
    for i, tile in enumerate(dk_tiles):
        at = heads + i * LANES
        dq_ref[:, at : at + LANES] = back(tile * scale)
    for i, tile in enumerate(dv_tiles):
        at = heads + keys_wide + i * LANES
        dq_ref[:, at : at + LANES] = tile.astype(BF)
    dn = nt(dq_ref[:, :heads], wq_ref[...])
    dn = dn + nt(dq_ref[:, heads : heads + keys_wide], wk_ref[...])
    whole[...] = dn + nt(dq_ref[:, heads + keys_wide :], wv_ref[...])
    x = x_ref[...].astype(F32)
    inv = lax.rsqrt(jnp.mean(x * x, axis=-1, keepdims=True) + EPS)
    small_ref[...] = small_in[...]
    small_ref[0:1, :] = jnp.sum(whole[...] * x * inv, axis=0, keepdims=True)
    for r, part in enumerate((p0, p1, p2, p3)):
        start = pl.multiple_of((me_ref[0] ^ r) * rows, rows)
        part[...] = whole[pl.ds(start, rows), :].astype(part.dtype)


def dense_kernel(me_ref, a0, a1, a2, a3, wide_ref, o_ref, n_ref, dq_ref, kept_ref, sent_ref, two_ref, whole):
    rows, width = a0.shape[1:]
    for r, piece in enumerate((a0, a1, a2, a3)):
        start = pl.multiple_of((me_ref[1] ^ r) * rows, rows)
        two_ref[pl.ds(start, rows), :] = piece[0]
    columns, heads = dq_ref.shape[1], o_ref.shape[1]
    whole[:, :columns] = tn(n_ref[...], dq_ref[...])
    whole[:, columns : columns + heads] = tn(wide_ref[:, :width], o_ref[...])
    whole[:, columns + heads :] = tn(two_ref[...], wide_ref[:, width:])
    half = kept_ref.shape[0]
    kept_ref[...] = whole[pl.ds(pl.multiple_of(me_ref[0] * half, half), half), :]
    sent_ref[...] = whole[pl.ds(pl.multiple_of((1 - me_ref[0]) * half, half), half), :].astype(BF)


def input_grad_kernel(x_ref, gain_ref, dh_ref, *refs):
    parts, ig_ref = refs[:-1], refs[-1]
    x = x_ref[...].astype(F32)
    inv = lax.rsqrt(jnp.mean(x * x, axis=-1, keepdims=True) + EPS)
    dn = parts[0][...].astype(F32)
    for part in parts[1:]:
        dn = dn + part[...].astype(F32)
    u = gain_ref[...] * dn
    ig = dh_ref[...] + inv * u - x * (inv * inv * inv * jnp.mean(u * x, axis=-1, keepdims=True))
    ig_ref[...] = ig.astype(BF)


def out_kernel(h_ref, small_ref, *refs):
    moes, out_ref = refs[:-1], refs[-1]
    rows = h_ref.shape[0]
    out = h_ref[...]
    for moe in moes:
        out = out + moe[...].astype(F32)
    out_ref[:rows, :] = out.astype(BF)
    small = small_ref[...]
    high = small.astype(BF).astype(F32)
    out_ref[rows:, :] = jnp.concatenate([high, small - high], axis=0).astype(BF)


def natural_kernel(me_ref, *refs):
    pieces, out = refs[:-1], refs[-1]
    rows = pieces[0].shape[0]
    for r, piece in enumerate(pieces):
        start = pl.multiple_of((me_ref[0] ^ r) * rows, rows)
        out[pl.ds(start, rows), :] = piece[...].astype(out.dtype)


def out_whole_kernel(me_ref, *refs):
    pieces, (out_ref, small_ref, held) = refs[:-3], refs[-3:]
    rows = pieces[0].shape[0] - 16
    for r, piece in enumerate(pieces):
        start = pl.multiple_of((me_ref[0] ^ r) * rows, rows)
        out_ref[pl.ds(start, rows), :] = piece[:rows, :]
        both = piece[rows:, :].astype(F32)
        held[me_ref[0] ^ r] = both[:8] + both[8:]
    total = held[0]
    for i in range(1, len(pieces)):
        total = total + held[i]
    small_ref[...] = total


def kept_and_dealt_kernel(me_ref, kept_ref, got_ref, small_ref, small_got_ref, *outs):
    small_out, outs = outs[-1], outs[:-1]
    small = small_ref[...] + small_got_ref[...]
    high = small[:4].astype(BF).astype(F32)
    both = jnp.concatenate([high, small[:4] - high], axis=0).astype(BF).astype(F32)
    small_out[...] = both
    rows, columns = outs[0].shape
    upper = lane_of((8, LANES)) >= HD
    parts = []
    for at in range(0, both.shape[1], LANES):
        tile = both[:, at : at + LANES]
        parts += [jnp.where(upper, pltpu.roll(tile, HD, 1), 0.0), jnp.where(upper, tile, 0.0)]
    if len(parts) * 8 == rows:
        extra = jnp.concatenate(parts, axis=0)
    else:
        extra = jnp.zeros((rows, LANES), F32)
    for r, out in enumerate(outs):
        start = pl.multiple_of((me_ref[0] ^ r) * rows, rows)
        at = pl.ds(start, rows)
        total = kept_ref[at, :] + got_ref[at, :].astype(F32)
        out[:, : columns - LANES] = total[:, : columns - LANES].astype(out.dtype)
        out[:, columns - LANES :] = (total[:, columns - LANES :] + extra).astype(out.dtype)


def dense_sum_kernel(me_ref, small_ref, mine_ref, *refs):
    others, outs, held = refs[:-7], refs[-7:-1], refs[-1]
    q_ref, k_ref, v_ref, o_ref, r_ref, small_out = outs
    total = mine_ref[...]
    for other in others:
        total = total + other[...].astype(F32)
    at = 0
    for out in (q_ref, k_ref, v_ref):
        out[...] = total[:, at : at + out.shape[1]]
        at += out.shape[1]
    o_ref[...] = total[:, at : at + o_ref.shape[0]].T
    at += o_ref.shape[0]
    r_ref[...] = total[:, at : at + r_ref.shape[1]]
    held[me_ref[0]] = small_ref[...]
    if total.shape[0] * HD != 8 * small_ref.shape[1]:
        others = []
    lower = lane_of((8, LANES)) < HD
    for i, other in enumerate(others):
        for j in range(small_ref.shape[1] // LANES):
            first = other[16 * j : 16 * j + 16, at : at + LANES].astype(F32)
            tile = jnp.where(lower, pltpu.roll(first[:8], HD, 1), first[8:])
            held[me_ref[0] ^ (i + 1), :, j * LANES : (j + 1) * LANES] = tile
    small = held[0] if others else small_ref[...]
    for i in range(1, len(others) + 1):
        small = small + held[i]
    small_out[...] = jnp.concatenate([small[:4] + small[4:], jnp.zeros_like(small[:4])], axis=0)


def on_device(
    tokens,
    routes,
    gain_first,
    w_query,
    w_key,
    w_value,
    w_output,
    gain_second,
    w_router,
    w_gate,
    w_up,
    w_down,
    cotangent,
):
    seq_len, width = tokens.shape
    experts = w_router.shape[1]
    local, _, hidden = w_gate.shape
    tensor_size = lax.axis_size("tensor")
    expert_size = lax.axis_size("expert")
    dp_size = lax.axis_size("dp")
    token_count = seq_len * dp_size * expert_size
    rows = seq_len // tensor_size
    wide_width = width + LANES
    last = tensor_size - 1
    around = range(1, tensor_size)
    t_me, e_me, d_me = lax.axis_index("tensor"), lax.axis_index("expert"), lax.axis_index("dp")
    t_at = t_me.astype(jnp.int32).reshape(1)
    e_at = e_me.astype(jnp.int32).reshape(1)
    base = (e_me * local).astype(jnp.int32).reshape(1)
    d_at = jnp.stack([d_me, t_me]).astype(jnp.int32)
    cosine, sine = rope_tables(seq_len)
    gain_one, gain_two = gain_first[None], gain_second[None]
    down_flat = w_down.reshape(local * hidden, width)

    *cot_near, router = call(
        pieces_kernel,
        [shape((rows, wide_width), BF)] * tensor_size + [shape((LANES, width), BF)],
        (t_at, cotangent, routes.T, w_router.T),
        "pieces",
        "sbbb",
        scratch=[pltpu.VMEM((seq_len, LANES), F32)],
        limit=58,
    )
    cot_got = spread(cot_near[0], "expert")
    cot_got[0], tokens = tied(cot_got[0], tokens)

    heads, keys_wide = w_query.shape[1], w_key.shape[1]
    n_one, q, k, v, o, lse, xq, *rest = call(
        attend_kernel,
        [
            shape((seq_len, width), BF),
            shape((seq_len, heads), BF),
            shape((seq_len, keys_wide), BF),
            shape((seq_len, keys_wide), BF),
            shape((seq_len, heads), BF),
            shape((seq_len, LANES), F32),
            shape((rows, width), BF),
        ]
        + [shape((rows, width), F32)]
        + [shape((rows, width), BF)] * last,
        (t_at, tokens, gain_one, w_query, w_key, w_value, w_output, cosine, sine),
        "attend",
        "s" + "b" * 8,
        "bbbbbbv",
        scratch=[pltpu.VMEM((seq_len, width), F32)],
        limit=58,
        flops=2 * seq_len * width * 4 * heads,
    )
    parts = rest
    got = backwards(lambda r: swap(parts[r], "tensor", r), tensor_size)
    h, n_two = call(
        norm_two_kernel,
        [shape((rows, width), F32), shape((rows, width), BF)],
        (xq, gain_two, parts[0], *got),
        "norm_two",
        "bbb",
        "vv",
        limit=58,
    )

    n_two, cot_got = tied(n_two, cot_got)
    cot_far = together(cot_got)
    wcat = gate_up_weights(w_gate, w_up)
    two_got = spread(n_two, "expert")
    two_got[0], cot_late = tied(two_got[0], cot_far)
    cot_far = [cot_far] + backwards(lambda r: swap(cot_far, "tensor", r), last)
    cot_far.append(swap(cot_late, "tensor", last))

    first = together([n_two, *two_got])
    twos = [first] + backwards(lambda r: swap(first, "tensor", r), last)
    _, late = tied(cot_far[:last], first)
    twos.append(swap(late, "tensor", last))

    run = functools.partial(
        run_experts, experts, base, router=router, wcat=wcat, down_flat=down_flat
    )
    named = (*cot_near, *cot_far)
    counts = call(
        counts_kernel, [shape((1, LANES), F32)], named, "counts", [last_lanes(x) for x in named]
    )[0]
    counts = counts + swap(counts, "dp", 1)
    balance = experts * (counts / (token_count * TOP)) / token_count
    made = [run(twos[0], cot_near[0], cot_far[0], kind=F32)]
    got = []
    for r in around:
        made[-1], (two, cot) = tied(made[-1], (twos[r], cot_far[r]))
        if r == last:
            balance, two = tied(balance, two)
        made.append(run(two, cot_near[r], cot, kind=BF, apart=r == last))
        if r < last:
            got.append(swap(made[-1][3], "tensor", r))
    cots, dgus, hids, ds, moes = zip(*made)
    near_last, *far_last = ds[last]
    from_last = deal(far_last, "expert")
    grads = run_grads(twos, dgus, hids, cots, local, hidden)
    grads, (got, from_last) = tied(grads, (got, from_last))
    near, *across = split_sum([ds[0], *got], "dn_sum")
    across[0], middle = tied(across[0], moes[1:last])
    across = deal(across, "expert")
    across[0], near_last = tied(across[0], near_last)
    through = added([near_last, *from_last], BF, "through")
    near_sums = [near, swap(through, "tensor", last), *across]
    moe_got = [swap(middle[r - 1], "tensor", r) for r in range(1, last)]
    moe_got, near_sums = tied(moe_got, near_sums)

    wide, dh, small = call(
        functools.partial(norm_back_kernel, experts, len(near_sums)),
        [shape((rows, wide_width), BF), shape((rows, width), F32), shape((8, width), F32)],
        (h, n_two, gain_two, router, balance, cot_near[0], *near_sums),
        "norm_back",
        "v",
        "vvv",
    )
    wides = [wide] + backwards(lambda r: swap(wide, "tensor", r), tensor_size)
    _, late_grads = tied(wide, grads)
    grads_got = swap(late_grads, "dp", 1)
    grads_got, wides = tied(grads_got, wides)
    wides, moe_last = tied(wides, moes[last])
    moe_got.append(swap(moe_last, "tensor", last))

    wide_all, dqkv, small, *back_parts = call(
        attend_back_kernel,
        [
            shape((seq_len, wide_width), BF),
            shape((seq_len, heads + 2 * keys_wide), BF),
            shape((8, width), F32),
            shape((rows, width), F32),
        ]
        + [shape((rows, width), BF)] * last,
        (t_at, *wides, tokens, q, k, v, lse, w_query, w_key, w_value, w_output, cosine, sine, small),
        "attend_back",
        "s" + "v" * tensor_size + "b" * 11,
        "bb",
        limit=58,
        scratch=[
            pltpu.VMEM((seq_len, heads), BF),
            pltpu.VMEM((seq_len, width), F32),
        ],
        flops=2 * seq_len * width * 4 * heads,
    )
    part_sums = [back_parts[0]] + backwards(lambda r: swap(back_parts[r], "tensor", r), tensor_size)
    half = width // dp_size
    chunk = half // expert_size

    columns = heads + 2 * keys_wide
    all_columns = columns + heads + LANES
    own_block = pl.BlockSpec((1, rows, width), lambda i: (0, 0, 0))
    kept, sent = call(
        dense_kernel,
        [shape((half, all_columns), F32), shape((half, all_columns), BF)],
        (d_at, *twos, wide_all, o, n_one, dqkv),
        "dense",
        ["s"] + [own_block] * tensor_size + ["b"] * 4,
        "vv",
        limit=54,
        scratch=[
            pltpu.VMEM((seq_len, width), BF),
            pltpu.VMEM((width, all_columns), F32),
        ],
        flops=1,
    )
    mine, *others, small = call(
        kept_and_dealt_kernel,
        [shape((chunk, all_columns), F32)]
        + [shape((chunk, all_columns), BF)] * (expert_size - 1)
        + [shape((8, width), F32)],
        (e_at, kept, swap(sent, "dp", 1), small, swap(small, "dp", 1)),
        "dense_dealt",
        "s",
    )
    others = deal(others, "expert")
    grad_gate = both_copies(grads, grads_got, 0)
    (grad_gate, others[0]), part_sums = tied((grad_gate, others[0]), part_sums)
    moe_near, *moe_across = split_sum([moes[0], *moe_got], "moe_sum")
    moe_sums = [moe_near, *deal(moe_across, "expert")]
    ig = call(
        input_grad_kernel, [shape((rows, width), BF)], (xq, gain_one, dh, *part_sums), "input_grad", "bbbb", limit=58
    )[0]
    igs = [ig] + backwards(lambda r: swap(ig, "tensor", r), tensor_size)
    grad_up = both_copies(grads, grads_got, 1)
    grad_up, others = tied(grad_up, others)
    g_query, g_key, g_value, g_out, g_router, small = call(
        dense_sum_kernel,
        [
            shape((chunk, heads), F32),
            shape((chunk, keys_wide), F32),
            shape((chunk, keys_wide), F32),
            shape((heads, chunk), F32),
            shape((chunk, LANES), F32),
            shape((8, width), F32),
        ],
        (e_at, small, mine, *others),
        "dense_sum",
        "s",
        "bbbbbv",
        scratch=[pltpu.VMEM((expert_size, 8, width), F32)],
    )
    if chunk * HD != 8 * width:
        small = jnp.sum(lax.all_gather(small, "expert"), axis=0)
    igs, small = tied(igs, small)
    input_grad = call(
        natural_kernel, [shape((seq_len, width), F32)], (t_at, *igs), "input_grad_whole", "s", "b"
    )[0]
    out_piece = call(out_kernel, [shape((rows + 16, width), BF)], (h, small, *moe_sums), "out_piece")[0]
    outs = [out_piece] + backwards(lambda r: swap(out_piece, "tensor", r), tensor_size)
    grad_down = both_copies(grads, grads_got, 2)
    grad_down, outs = tied(grad_down, outs)
    output, small = call(
        out_whole_kernel,
        [shape((seq_len, width), BF), shape((8, width), F32)],
        (t_at, *outs),
        "output",
        "s",
        "bv",
        scratch=[pltpu.VMEM((tensor_size, 8, width), F32)],
    )
    at = (d_me * expert_size + e_me) * chunk
    loss_value = (experts * balance * small[2:3, :LANES])[0, :experts]
    return (
        output,
        loss_value,
        input_grad,
        lax.dynamic_slice(small, (0, at), (1, chunk))[0],
        g_query,
        g_key,
        g_value,
        g_out,
        lax.dynamic_slice(small, (1, at), (1, chunk))[0],
        g_router[:, :experts],
        grad_gate,
        grad_up,
        grad_down,
    )


def solution(mesh):
    rows = ("dp", "expert")
    placed = (
        P(rows, None),
        P(rows, None),
        P(),
        P(None, "tensor"),
        P(None, "tensor"),
        P(None, "tensor"),
        P("tensor", None),
        P(),
        P(),
        P("expert", None, "tensor"),
        P("expert", None, "tensor"),
        P("expert", "tensor", None),
        P(rows, None),
    )
    return jax.shard_map(
        on_device,
        mesh=mesh,
        in_specs=placed,
        out_specs=(
            P(rows, None),
            P(),
            P(rows, None),
            P(rows),
            P(rows, "tensor"),
            P(rows, "tensor"),
            P(rows, "tensor"),
            P("tensor", rows),
            P(rows),
            P(rows, None),
            P("expert", None, "tensor"),
            P("expert", None, "tensor"),
            P("expert", "tensor", None),
        ),
        check_vma=False,
    )
```

```python
import functools

import jax
import jax.numpy as jnp
import numpy as np
from jax import lax
from jax.experimental import pallas as pl
from jax.experimental.pallas import tpu as pltpu
from jax.sharding import PartitionSpec as P

HD = 64
TOP = 8
EPS = 1e-06
ROPE_BASE = 10000.0
MASKED = -1e30
BF = jnp.bfloat16
F32 = jnp.float32
FEW = 8
LANES = 128
MIB = 1 << 20


def dot(a, b, dims):
    return lax.dot_general(a, b, (dims, ((), ())), preferred_element_type=F32)


def nn(a, b):
    return dot(a, b, ((1,), (0,)))


def nt(a, b):
    return dot(a, b, ((1,), (1,)))


def tn(a, b):
    return dot(a, b, ((0,), (0,)))


def swap(x, axis, distance):
    size = lax.axis_size(axis)
    return lax.ppermute(x, axis, [(i, i ^ distance) for i in range(size)])


def backwards(make, size):
    return [make(r) for r in range(size - 1, 0, -1)][::-1]


def spread(x, axis):
    size = lax.axis_size(axis)
    if size <= FEW:
        return backwards(lambda r: swap(x, axis, r), size)
    whole = lax.all_gather(x, axis)
    order = jnp.arange(1, size) ^ lax.axis_index(axis)
    return list(jnp.take(whole, order, axis=0))


def deal(parts, axis):
    size = lax.axis_size(axis)
    if size <= FEW:
        return backwards(lambda r: swap(parts[r - 1], axis, r), size)
    order = jnp.arange(size) ^ lax.axis_index(axis)
    whole = jnp.take(jnp.stack([parts[0], *parts]), order, axis=0)
    back = lax.all_to_all(whole, axis, 0, 0, tiled=True)
    return list(jnp.take(back, order, axis=0)[1:])


def rope_tables(seq_len):
    half = HD // 2
    frequency = ROPE_BASE ** (-(np.arange(half, dtype=np.float32) * 2.0) / HD)
    angles = np.arange(seq_len, dtype=np.float32)[:, None] * frequency[None, :].astype(np.float32)
    cosine, sine = np.cos(angles), np.sin(angles)
    heads = LANES // HD
    return (
        np.tile(cosine, (1, 2 * heads)).astype(np.float32),
        np.tile(np.concatenate([-sine, sine], axis=1), (1, heads)).astype(np.float32),
    )


def lane_of(shape):
    return lax.broadcasted_iota(jnp.int32, shape, 1)


def halves_swapped(x):
    first = lane_of(x.shape) % HD < HD // 2
    half = HD // 2
    return jnp.where(first, pltpu.roll(x, LANES - half, 1), pltpu.roll(x, half, 1))


def low_high(x, head):
    other = pltpu.roll(x.astype(F32), HD, 1).astype(x.dtype)
    low = lane_of(x.shape) < HD
    zero = jnp.zeros_like(x)
    at_low, at_high = (x, other) if head == 0 else (other, x)
    return jnp.where(low, at_low, zero), jnp.where(low, zero, at_high)


def causal(scores):
    rows = lax.broadcasted_iota(jnp.int32, scores.shape, 0)
    return lane_of(scores.shape) <= rows


def shape(dims, kind):
    return jax.ShapeDtypeStruct(dims, kind)


def whole_block(dims):
    return pl.BlockSpec(dims, lambda i: (0,) * len(dims))


def call(kernel, outs, operands, name, places="", out_places="", scratch=(), limit=40, flops=0):
    kinds = {"s": pltpu.SMEM, "v": pltpu.VMEM}

    def spec(place, x):
        if not isinstance(place, str):
            return place
        if place == "b":
            return whole_block(x.shape)
        return pl.BlockSpec(memory_space=kinds[place])

    places = [*places] + ["v"] * (len(operands) - len(places))
    out_places = [*out_places] + ["v"] * (len(outs) - len(out_places))
    return pl.pallas_call(
        kernel,
        grid=(1,),
        out_shape=outs,
        in_specs=[spec(p, x) for p, x in zip(places, operands)],
        out_specs=[spec(p, x) for p, x in zip(out_places, outs)],
        scratch_shapes=list(scratch),
        compiler_params=pltpu.CompilerParams(vmem_limit_bytes=limit * MIB),
        cost_estimate=pl.CostEstimate(flops=int(100.0*(flops)), bytes_accessed=0, transcendentals=0),
        name=name,
    )(*operands)


def tied(first, then):
    return lax.optimization_barrier((first, then))


def pieces_kernel(me_ref, cot_ref, routes_ref, router_ref, *refs):
    cots, (router_out, held) = refs[:-2], refs[-2:]
    rows, width = cots[0].shape[0], cot_ref.shape[1]
    eye = lax.broadcasted_iota(jnp.int32, (TOP, LANES), 0) == lane_of((TOP, LANES))
    held[...] = tn(routes_ref[...].astype(F32).astype(BF), eye.astype(F32).astype(BF))
    for r, c in enumerate(cots):
        start = pl.multiple_of((me_ref[0] ^ r) * rows, rows)
        c[:, :width] = cot_ref[pl.ds(start, rows), :]
        c[:, width:] = held[pl.ds(start, rows), :].astype(BF)
    router_out[...] = jnp.zeros(router_out.shape, BF)
    router_out[: router_ref.shape[0], :] = router_ref[...]


def attend_kernel(
    me_ref, x_ref, gain_ref, wq_ref, wk_ref, wv_ref, wo_ref, cos_ref, sin_ref, *refs
):
    n_ref, q_ref, k_ref, v_ref, o_ref, lse_ref, xq_ref = refs[:7]
    parts, whole = refs[7:-1], refs[-1]
    rows, width = xq_ref.shape
    starts = [pl.multiple_of((me_ref[0] ^ r) * rows, rows) for r in range(4)]
    xq_ref[...] = x_ref[pl.ds(starts[0], rows), :]
    x = x_ref[...].astype(F32)
    inv = lax.rsqrt(jnp.mean(x * x, axis=-1, keepdims=True) + EPS)
    n = (x * inv * gain_ref[...]).astype(BF)
    n_ref[...] = n
    cosine, sine = cos_ref[...], sin_ref[...]
    q, k = nn(n, wq_ref[...]), nn(n, wk_ref[...])
    v_ref[...] = nn(n, wv_ref[...]).astype(BF)
    for at in range(0, q.shape[1], LANES):
        tile = q[:, at : at + LANES]
        q_ref[:, at : at + LANES] = (tile * cosine + halves_swapped(tile) * sine).astype(BF)
    for at in range(0, k.shape[1], LANES):
        tile = k[:, at : at + LANES]
        k_ref[:, at : at + LANES] = (tile * cosine + halves_swapped(tile) * sine).astype(BF)
    lse_all = jnp.zeros(lse_ref.shape, F32)
    for head in range(q.shape[1] // LANES):
        at = head // 2 * LANES
        keys = low_high(k_ref[:, at : at + LANES], head % 2)
        values = low_high(v_ref[:, at : at + LANES], head % 2)
        pair = q_ref[:, head * LANES : (head + 1) * LANES]
        mixed = 0.0
        for g in range(2):
            s = nt(pair, keys[g]) * HD ** (-0.5)
            s = jnp.where(causal(s), s, MASKED)
            peak = jnp.max(s, axis=-1, keepdims=True)
            e = jnp.exp(s - peak)
            total = jnp.sum(e, axis=-1, keepdims=True)
            mixed = mixed + nn((e / total).astype(BF), values[g])
            lse = peak + jnp.log(total)
            lse_all = jnp.where(lane_of(lse_all.shape) == 2 * head + g, lse, lse_all)
        o_ref[:, head * LANES : (head + 1) * LANES] = mixed.astype(BF)
    lse_ref[...] = lse_all
    whole[...] = nn(o_ref[...], wo_ref[...])
    for start, part in zip(starts, parts):
        part[...] = whole[pl.ds(start, rows), :].astype(part.dtype)


def norm_two_kernel(x_ref, gain_ref, own_ref, *refs):
    others, (h_ref, n_ref) = refs[:-2], refs[-2:]
    attn = own_ref[...]
    for other in others:
        attn = attn + other[...].astype(F32)
    h = x_ref[...].astype(F32) + attn
    inv = lax.rsqrt(jnp.mean(h * h, axis=-1, keepdims=True) + EPS)
    h_ref[...] = h
    n_ref[...] = (h * inv * gain_ref[...]).astype(BF)


def together_kernel(*refs):
    pieces, out = refs[:-1], refs[-1]
    at = 0
    for piece in pieces:
        if len(piece.shape) == 2:
            out[at] = piece[...]
            at += 1
        else:
            out[at : at + piece.shape[0]] = piece[...]
            at += piece.shape[0]


def together(pieces):
    count = sum(1 if x.ndim == 2 else x.shape[0] for x in pieces)
    return call(
        together_kernel, [shape((count, *pieces[0].shape[-2:]), pieces[0].dtype)], pieces, "together"
    )[0]


def router_of(rows, router_ref, routes, experts):
    z = nt(rows, router_ref[...])
    lane = lane_of(z.shape)
    z = jnp.where(lane < experts, z, MASKED)
    e = jnp.exp(z - jnp.max(z, axis=-1, keepdims=True))
    probs = e / jnp.sum(e, axis=-1, keepdims=True)
    chosen = chosen_of(lane, routes)
    zc = jnp.where(chosen, z, MASKED)
    ec = jnp.where(chosen, jnp.exp(zc - jnp.max(zc, axis=-1, keepdims=True)), 0.0)
    return probs, ec / jnp.sum(ec, axis=-1, keepdims=True)


def chosen_of(lane, routes):
    place, named = lane.astype(F32), routes.astype(F32)
    chosen = place == named[:, 0:1]
    for k in range(1, TOP):
        chosen = chosen | (place == named[:, k : k + 1])
    return chosen


def counts_kernel(*refs):
    pieces, out = refs[:-1], refs[-1]
    total = 0.0
    for piece in pieces:
        width = piece.shape[-1] - LANES
        blocks = [piece[:, width:]] if len(piece.shape) == 2 else [
            piece[i, :, width:] for i in range(piece.shape[0])
        ]
        for routes in blocks:
            named = chosen_of(lane_of(routes.shape), routes).astype(F32)
            total = total + jnp.sum(named, axis=0, keepdims=True)
    out[...] = total


def weights_kernel(wg_ref, wu_ref, out_ref):
    hidden = wg_ref.shape[2]
    out_ref[:, :hidden] = wg_ref[0]
    out_ref[:, hidden:] = wu_ref[0]


def gate_up_weights(w_gate, w_up):
    local, width, hidden = w_gate.shape
    block = pl.BlockSpec((1, width, hidden), lambda e: (e, 0, 0))
    return pl.pallas_call(
        weights_kernel,
        grid=(local,),
        in_specs=[block, block],
        out_specs=pl.BlockSpec((width, 2 * hidden), lambda e: (0, e)),
        out_shape=shape((width, 2 * hidden * local), BF),
        compiler_params=pltpu.CompilerParams(vmem_limit_bytes=30 * MIB),
        cost_estimate=pl.CostEstimate(flops=int(100.0*(0)), bytes_accessed=4 * w_gate.size * 2, transcendentals=0),
        name="gate_up_weights",
    )(w_gate, w_up)


def experts_kernel(experts, base_ref, x_ref, own_ref, far_ref, router_ref, wcat, wd_ref, *refs):
    cot_ref, dgu_ref, hg_ref, *ds, m_ref = refs
    hidden = LANES
    pair = 2 * hidden
    rows, width = cot_ref.shape
    x = x_ref[...].reshape(rows, width)
    if far_ref is None:
        routes = own_ref[:, width:]
        cot_ref[...] = own_ref[:, :width]
    else:
        pieces = [own_ref[...]] + [far_ref[i] for i in range(far_ref.shape[0])]
        routes = jnp.concatenate([piece[:, width:] for piece in pieces], axis=0)
        cot_ref[...] = jnp.concatenate([piece[:, :width] for piece in pieces], axis=0)
    _, gates = router_of(x, router_ref, routes, experts)
    lane = lane_of(gates.shape)
    dots = jnp.zeros(gates.shape, F32)
    for e in range(hg_ref.shape[1] // hidden):
        mine = lane == base_ref[0] + e
        g = jnp.sum(jnp.where(mine, gates, 0.0), axis=-1, keepdims=True)
        both = nn(x, wcat[:, e * pair : (e + 1) * pair])
        v = nt(cot_ref[...], wd_ref[e * hidden : (e + 1) * hidden, :])
        gate, up = both[:, :hidden], both[:, hidden:]
        sig = 1.0 / (1.0 + jnp.exp(-gate))
        act = gate * sig
        hid = act * up
        dots = jnp.where(mine, jnp.sum(hid * v, axis=-1, keepdims=True), dots)
        gv = g * v
        hg_ref[:, e * hidden : (e + 1) * hidden] = (g * hid).astype(BF)
        d_gate = gv * up * sig * (1.0 + gate * (1.0 - sig))
        dgu_ref[:, e * pair : e * pair + hidden] = d_gate.astype(BF)
        dgu_ref[:, e * pair + hidden : (e + 1) * pair] = (gv * act).astype(BF)

    def put(outs, columns, value):
        at = 0
        for out in outs:
            part = value.astype(out.dtype)
            if len(out.shape) == 2:
                out[:, columns] = part[at : at + out.shape[0]]
                at += out.shape[0]
            else:
                step = out.shape[1]
                for i in range(out.shape[0]):
                    out[i, :, columns] = part[i * step : (i + 1) * step]

    put(ds, slice(width, width + LANES), dots)
    step = 256
    for at in range(0, width, step):
        put(ds, slice(at, at + step), nt(dgu_ref[...], wcat[at : at + step, :]))
    put([m_ref], slice(0, width), nn(hg_ref[...], wd_ref[...]))


def run_experts(experts, base, x, own, far, router, wcat, down_flat, kind, apart=False):
    count, rows, width = x.shape
    inner = down_flat.shape[0]
    wide = width + LANES
    total = count * rows
    few = count <= FEW
    step = total if few else 256
    resident = pl.BlockSpec(memory_space=pltpu.VMEM)
    per = lambda w: resident if few else pl.BlockSpec((step, w), lambda i: (i, 0))
    kernel = functools.partial(experts_kernel, experts)
    if few:
        data, dims = [x, own, far], lambda w: (count, rows, w)
    else:
        joined = jnp.concatenate([own[None], far], axis=0)
        data, dims = [x.reshape(total, width), joined.reshape(total, wide)], lambda w: (total, w)
        whole_kernel = kernel
        kernel = lambda b, x, c, *refs: whole_kernel(b, x, c, None, *refs)
    if few and apart:
        d_shapes = [shape((rows, wide), BF if i else F32) for i in range(count)]
    else:
        d_shapes = [shape(dims(wide), kind)]
    cot, dgu, hid, *d, m = pl.pallas_call(
        kernel,
        grid=(total // step,),
        in_specs=[pl.BlockSpec(memory_space=pltpu.SMEM)]
        + [per(z.shape[-1]) for z in data]
        + [resident] * 3,
        out_specs=[per(width), per(2 * inner), per(inner)]
        + [per(wide)] * len(d_shapes)
        + [per(width)],
        out_shape=[
            shape((total, width), BF),
            shape((total, 2 * inner), BF),
            shape((total, inner), BF),
            *d_shapes,
            shape(dims(width), kind),
        ],
        compiler_params=pltpu.CompilerParams(vmem_limit_bytes=(14 if few else 30) * MIB),
        cost_estimate=pl.CostEstimate(flops=int(100.0*(total * width * inner // 8)), bytes_accessed=0, transcendentals=0),
        name="experts",
    )(base, *data, router, wcat, down_flat)
    if not few:
        d = list(d[0].reshape(count, rows, wide)) if apart else [d[0].reshape(count, rows, wide)]
    return cot, dgu, hid, d if apart else d[0], m.reshape(count, rows, width)


def split_sum_kernel(count, near, *refs):
    ins, outs = refs[:count], refs[count:]
    for s in range(ins[0].shape[0]):
        total = ins[0][s].astype(F32)
        for x in ins[1:]:
            total = total + x[s].astype(F32)
        outs[s][...] = total.astype(outs[s].dtype)


def split_sum(arrays, name):
    count, *dims = arrays[0].shape
    outs = [shape(dims, F32)] + [shape(dims, BF)] * (count - 1)
    return call(functools.partial(split_sum_kernel, len(arrays), True), outs, arrays, name)


def add_kernel(*refs):
    pieces, out = refs[:-1], refs[-1]
    total = pieces[0][...].astype(F32)
    for piece in pieces[1:]:
        total = total + piece[...].astype(F32)
    out[...] = total.astype(out.dtype)


def added(pieces, kind, name):
    return call(add_kernel, [shape(pieces[0].shape, kind)], pieces, name)[0]


def grads_kernel(*refs):
    ns, dgus, hs, cs = (refs[4 * i : 4 * i + 4] for i in range(4))
    out_ref = refs[16]
    hidden, width = hs[0].shape[1], ns[0].shape[1]
    both, down = 0.0, 0.0
    for n, dgu, h, c in zip(ns, dgus, hs, cs):
        both = both + tn(n[...], dgu[...])
        down = down + tn(h[...], c[...])
    out_ref[0, :width, :] = both[:, :hidden].astype(BF)
    out_ref[0, width : 2 * width, :] = both[:, hidden:].astype(BF)
    for at in range(0, width, hidden):
        out_ref[0, 2 * width + at : 2 * width + at + hidden, :] = down[:, at : at + hidden].astype(BF)


def run_grads(n, dgu, h, c, local, hidden):
    width = n[0].shape[-1]
    flat = lambda xs: [x.reshape(-1, x.shape[-1]) for x in xs]
    n, c = flat(n), flat(c)
    whole = lambda xs: [pl.BlockSpec(x.shape, lambda e: (0, 0)) for x in xs]
    cols = lambda xs, w: [pl.BlockSpec((x.shape[0], w), lambda e: (0, e)) for x in xs]
    few = n[0].shape[0] <= 512
    return pl.pallas_call(
        grads_kernel,
        grid=(local,),
        in_specs=whole(n) + cols(dgu, 2 * hidden) + cols(h, hidden) + whole(c),
        out_specs=pl.BlockSpec((1, 3 * width, hidden), lambda e: (e, 0, 0)),
        out_shape=shape((local, 3 * width, hidden), BF),
        compiler_params=pltpu.CompilerParams(vmem_limit_bytes=(20 if few else 58) * MIB),
        cost_estimate=pl.CostEstimate(flops=int(100.0*(24 * n[0].size * hidden * local)), bytes_accessed=0, transcendentals=0),
        name="expert_grads",
    )(*n, *dgu, *h, *c)


def both_copies_kernel(mine_ref, other_ref, out_ref):
    for e in range(mine_ref.shape[0]):
        total = mine_ref[e].astype(F32) + other_ref[e].astype(F32)
        hidden = total.shape[1]
        if out_ref.shape[2] == hidden:
            out_ref[e] = total
        else:
            for at in range(0, total.shape[0], hidden):
                out_ref[e, :, at : at + hidden] = total[at : at + hidden]


def both_copies(mine, other, which):
    local, rows, hidden = mine.shape
    width = rows // 3
    dims = (hidden, width) if which == 2 else (width, hidden)
    step = min(local, 2)
    block = pl.BlockSpec((step, width, hidden), lambda e: (e, which, 0))
    return pl.pallas_call(
        both_copies_kernel,
        grid=(local // step,),
        in_specs=[block, block],
        out_specs=pl.BlockSpec((step, *dims), lambda e: (e, 0, 0)),
        out_shape=shape((local, *dims), F32),
        compiler_params=pltpu.CompilerParams(vmem_limit_bytes=58 * MIB),
        cost_estimate=pl.CostEstimate(flops=int(100.0*(0)), bytes_accessed=8 * mine.size, transcendentals=0),
        name="both_copies",
    )(mine, other)


def norm_back_kernel(experts, count, h_ref, n_ref, gain_ref, router_ref, bal_ref, cot_ref, *refs):
    sums, (wide_ref, dh_ref, small_ref) = refs[:count], refs[count:]
    near = sums[0][...].astype(F32)
    for other in sums[1:]:
        near = near + other[...].astype(F32)
    rows, width = h_ref.shape
    dots = near[:, width:]
    probs, gates = router_of(n_ref[...], router_ref, cot_ref[:, width:], experts)
    bal = bal_ref[...]
    d_chosen = gates * (dots - jnp.sum(gates * dots, axis=-1, keepdims=True))
    dz = probs * (bal - jnp.sum(probs * bal, axis=-1, keepdims=True)) + d_chosen
    dz = dz.astype(BF)
    wide_ref[:, width:] = dz
    dn = near[:, :width] + nn(dz, router_ref[...])
    h = h_ref[...]
    inv = lax.rsqrt(jnp.mean(h * h, axis=-1, keepdims=True) + EPS)
    u = gain_ref[...] * dn
    dy = cot_ref[:, :width].astype(F32)
    dh = dy + inv * u - h * (inv * inv * inv * jnp.mean(u * h, axis=-1, keepdims=True))
    dh_ref[...] = dh
    wide_ref[:, :width] = dh.astype(BF)
    small_ref[...] = jnp.zeros(small_ref.shape, F32)
    small_ref[1:2, :] = jnp.sum(dn * h * inv, axis=0, keepdims=True)
    small_ref[2:3, : probs.shape[1]] = jnp.sum(probs, axis=0, keepdims=True)


def attend_back_kernel(
    me_ref, w0, w1, w2, w3, x_ref, q_ref, k_ref, v_ref, lse_ref, wq_ref, wk_ref, wv_ref, wo_ref, cos_ref, sin_ref,
    small_in, wide_ref, dq_ref, small_ref, p0, p1, p2, p3, do_ref, whole
):
    rows = w0.shape[0]
    width = x_ref.shape[1]
    for r, piece in enumerate((w0, w1, w2, w3)):
        start = pl.multiple_of((me_ref[0] ^ r) * rows, rows)
        wide_ref[pl.ds(start, rows), :] = piece[...]
    do_ref[...] = nt(wide_ref[:, :width], wo_ref[...]).astype(BF)
    cosine, sine = cos_ref[...], sin_ref[...]
    scale = HD ** (-0.5)
    heads, keys_wide = q_ref.shape[1], k_ref.shape[1]
    dk_tiles = [0.0] * (keys_wide // LANES)
    dv_tiles = [0.0] * (keys_wide // LANES)

    def back(tile):
        return (tile * cosine - halves_swapped(tile) * sine).astype(BF)

    for head in range(heads // LANES):
        at = head // 2 * LANES
        side = head % 2
        keys = low_high(k_ref[:, at : at + LANES], side)
        values = low_high(v_ref[:, at : at + LANES], side)
        pair = q_ref[:, head * LANES : (head + 1) * LANES]
        grad = do_ref[:, head * LANES : (head + 1) * LANES]
        dq = 0.0
        dk, dv = [], []
        for g in range(2):
            s = nt(pair, keys[g]) * scale
            lse = lse_ref[:, 2 * head + g : 2 * head + g + 1]
            p = jnp.where(causal(s), jnp.exp(s - lse), 0.0)
            dp = nt(grad, values[g])
            ds = (p * (dp - jnp.sum(p * dp, axis=-1, keepdims=True))).astype(BF)
            dq = dq + nn(ds, keys[g])
            dk.append(tn(ds, pair))
            dv.append(tn(p.astype(BF), grad))
        dq_ref[:, head * LANES : (head + 1) * LANES] = back(dq * scale)
        mine = lane_of(dk[0].shape) < HD
        if side == 0:
            dk_sum = jnp.where(mine, dk[0] + pltpu.roll(dk[1], HD, 1), 0.0)
            dv_sum = jnp.where(mine, dv[0] + pltpu.roll(dv[1], HD, 1), 0.0)
        else:
            dk_sum = jnp.where(mine, 0.0, pltpu.roll(dk[0], HD, 1) + dk[1])
            dv_sum = jnp.where(mine, 0.0, pltpu.roll(dv[0], HD, 1) + dv[1])
        dk_tiles[head // 2] = dk_tiles[head // 2] + dk_sum
        dv_tiles[head // 2] = dv_tiles[head // 2] + dv_sum
    for i, tile in enumerate(dk_tiles):
        at = heads + i * LANES
        dq_ref[:, at : at + LANES] = back(tile * scale)
    for i, tile in enumerate(dv_tiles):
        at = heads + keys_wide + i * LANES
        dq_ref[:, at : at + LANES] = tile.astype(BF)
    dn = nt(dq_ref[:, :heads], wq_ref[...])
    dn = dn + nt(dq_ref[:, heads : heads + keys_wide], wk_ref[...])
    whole[...] = dn + nt(dq_ref[:, heads + keys_wide :], wv_ref[...])
    x = x_ref[...].astype(F32)
    inv = lax.rsqrt(jnp.mean(x * x, axis=-1, keepdims=True) + EPS)
    small_ref[...] = small_in[...]
    small_ref[0:1, :] = jnp.sum(whole[...] * x * inv, axis=0, keepdims=True)
    for r, part in enumerate((p0, p1, p2, p3)):
        start = pl.multiple_of((me_ref[0] ^ r) * rows, rows)
        part[...] = whole[pl.ds(start, rows), :].astype(part.dtype)


def dense_kernel(me_ref, a0, a1, a2, a3, wide_ref, o_ref, n_ref, dq_ref, kept_ref, sent_ref, two_ref, whole):
    rows, width = a0.shape[1:]
    for r, piece in enumerate((a0, a1, a2, a3)):
        start = pl.multiple_of((me_ref[1] ^ r) * rows, rows)
        two_ref[pl.ds(start, rows), :] = piece[0]
    columns, heads = dq_ref.shape[1], o_ref.shape[1]
    whole[:, :columns] = tn(n_ref[...], dq_ref[...])
    whole[:, columns : columns + heads] = tn(wide_ref[:, :width], o_ref[...])
    whole[:, columns + heads :] = tn(two_ref[...], wide_ref[:, width:])
    half = kept_ref.shape[0]
    kept_ref[...] = whole[pl.ds(pl.multiple_of(me_ref[0] * half, half), half), :]
    sent_ref[...] = whole[pl.ds(pl.multiple_of((1 - me_ref[0]) * half, half), half), :].astype(BF)


def input_grad_kernel(x_ref, gain_ref, dh_ref, *refs):
    parts, ig_ref = refs[:-1], refs[-1]
    x = x_ref[...].astype(F32)
    inv = lax.rsqrt(jnp.mean(x * x, axis=-1, keepdims=True) + EPS)
    dn = parts[0][...].astype(F32)
    for part in parts[1:]:
        dn = dn + part[...].astype(F32)
    u = gain_ref[...] * dn
    ig = dh_ref[...] + inv * u - x * (inv * inv * inv * jnp.mean(u * x, axis=-1, keepdims=True))
    ig_ref[...] = ig.astype(BF)


def out_kernel(h_ref, small_ref, *refs):
    moes, out_ref = refs[:-1], refs[-1]
    rows = h_ref.shape[0]
    out = h_ref[...]
    for moe in moes:
        out = out + moe[...].astype(F32)
    out_ref[:rows, :] = out.astype(BF)
    small = small_ref[...]
    high = small.astype(BF).astype(F32)
    out_ref[rows:, :] = jnp.concatenate([high, small - high], axis=0).astype(BF)


def natural_kernel(me_ref, *refs):
    pieces, out = refs[:-1], refs[-1]
    rows = pieces[0].shape[0]
    for r, piece in enumerate(pieces):
        start = pl.multiple_of((me_ref[0] ^ r) * rows, rows)
        out[pl.ds(start, rows), :] = piece[...].astype(out.dtype)


def out_whole_kernel(me_ref, *refs):
    pieces, (out_ref, small_ref, held) = refs[:-3], refs[-3:]
    rows = pieces[0].shape[0] - 16
    for r, piece in enumerate(pieces):
        start = pl.multiple_of((me_ref[0] ^ r) * rows, rows)
        out_ref[pl.ds(start, rows), :] = piece[:rows, :]
        both = piece[rows:, :].astype(F32)
        held[me_ref[0] ^ r] = both[:8] + both[8:]
    total = held[0]
    for i in range(1, len(pieces)):
        total = total + held[i]
    small_ref[...] = total


def kept_and_dealt_kernel(me_ref, kept_ref, got_ref, small_ref, small_got_ref, *outs):
    small_out, outs = outs[-1], outs[:-1]
    small = small_ref[...] + small_got_ref[...]
    high = small[:4].astype(BF).astype(F32)
    both = jnp.concatenate([high, small[:4] - high], axis=0).astype(BF).astype(F32)
    small_out[...] = both
    rows, columns = outs[0].shape
    upper = lane_of((8, LANES)) >= HD
    parts = []
    for at in range(0, both.shape[1], LANES):
        tile = both[:, at : at + LANES]
        parts += [jnp.where(upper, pltpu.roll(tile, HD, 1), 0.0), jnp.where(upper, tile, 0.0)]
    if len(parts) * 8 == rows:
        extra = jnp.concatenate(parts, axis=0)
    else:
        extra = jnp.zeros((rows, LANES), F32)
    for r, out in enumerate(outs):
        start = pl.multiple_of((me_ref[0] ^ r) * rows, rows)
        at = pl.ds(start, rows)
        total = kept_ref[at, :] + got_ref[at, :].astype(F32)
        out[:, : columns - LANES] = total[:, : columns - LANES].astype(out.dtype)
        out[:, columns - LANES :] = (total[:, columns - LANES :] + extra).astype(out.dtype)


def dense_sum_kernel(me_ref, small_ref, mine_ref, *refs):
    others, outs, held = refs[:-7], refs[-7:-1], refs[-1]
    q_ref, k_ref, v_ref, o_ref, r_ref, small_out = outs
    total = mine_ref[...]
    for other in others:
        total = total + other[...].astype(F32)
    at = 0
    for out in (q_ref, k_ref, v_ref):
        out[...] = total[:, at : at + out.shape[1]]
        at += out.shape[1]
    o_ref[...] = total[:, at : at + o_ref.shape[0]].T
    at += o_ref.shape[0]
    r_ref[...] = total[:, at : at + r_ref.shape[1]]
    held[me_ref[0]] = small_ref[...]
    if total.shape[0] * HD != 8 * small_ref.shape[1]:
        others = []
    lower = lane_of((8, LANES)) < HD
    for i, other in enumerate(others):
        for j in range(small_ref.shape[1] // LANES):
            first = other[16 * j : 16 * j + 16, at : at + LANES].astype(F32)
            tile = jnp.where(lower, pltpu.roll(first[:8], HD, 1), first[8:])
            held[me_ref[0] ^ (i + 1), :, j * LANES : (j + 1) * LANES] = tile
    small = held[0] if others else small_ref[...]
    for i in range(1, len(others) + 1):
        small = small + held[i]
    small_out[...] = jnp.concatenate([small[:4] + small[4:], jnp.zeros_like(small[:4])], axis=0)


def on_device(
    tokens,
    routes,
    gain_first,
    w_query,
    w_key,
    w_value,
    w_output,
    gain_second,
    w_router,
    w_gate,
    w_up,
    w_down,
    cotangent,
):
    seq_len, width = tokens.shape
    experts = w_router.shape[1]
    local, _, hidden = w_gate.shape
    tensor_size = lax.axis_size("tensor")
    expert_size = lax.axis_size("expert")
    dp_size = lax.axis_size("dp")
    token_count = seq_len * dp_size * expert_size
    rows = seq_len // tensor_size
    wide_width = width + LANES
    last = tensor_size - 1
    around = range(1, tensor_size)
    t_me, e_me, d_me = lax.axis_index("tensor"), lax.axis_index("expert"), lax.axis_index("dp")
    t_at = t_me.astype(jnp.int32).reshape(1)
    e_at = e_me.astype(jnp.int32).reshape(1)
    base = (e_me * local).astype(jnp.int32).reshape(1)
    d_at = jnp.stack([d_me, t_me]).astype(jnp.int32)
    cosine, sine = rope_tables(seq_len)
    gain_one, gain_two = gain_first[None], gain_second[None]
    down_flat = w_down.reshape(local * hidden, width)

    *cot_near, router = call(
        pieces_kernel,
        [shape((rows, wide_width), BF)] * tensor_size + [shape((LANES, width), BF)],
        (t_at, cotangent, routes.T, w_router.T),
        "pieces",
        "sbbb",
        scratch=[pltpu.VMEM((seq_len, LANES), F32)],
        limit=58,
    )
    cot_got = spread(cot_near[0], "expert")
    cot_got[0], tokens = tied(cot_got[0], tokens)

    heads, keys_wide = w_query.shape[1], w_key.shape[1]
    n_one, q, k, v, o, lse, xq, *rest = call(
        attend_kernel,
        [
            shape((seq_len, width), BF),
            shape((seq_len, heads), BF),
            shape((seq_len, keys_wide), BF),
            shape((seq_len, keys_wide), BF),
            shape((seq_len, heads), BF),
            shape((seq_len, LANES), F32),
            shape((rows, width), BF),
        ]
        + [shape((rows, width), F32)]
        + [shape((rows, width), BF)] * last,
        (t_at, tokens, gain_one, w_query, w_key, w_value, w_output, cosine, sine),
        "attend",
        "s" + "b" * 8,
        "bbbbbbv",
        scratch=[pltpu.VMEM((seq_len, width), F32)],
        limit=58,
        flops=2 * seq_len * width * 4 * heads,
    )
    parts = rest
    got = backwards(lambda r: swap(parts[r], "tensor", r), tensor_size)
    h, n_two = call(
        norm_two_kernel,
        [shape((rows, width), F32), shape((rows, width), BF)],
        (xq, gain_two, parts[0], *got),
        "norm_two",
        "bbb",
        "vv",
        limit=58,
    )

    n_two, cot_got = tied(n_two, cot_got)
    cot_far = together(cot_got)
    wcat = gate_up_weights(w_gate, w_up)
    two_got = spread(n_two, "expert")
    two_got[0], cot_late = tied(two_got[0], cot_far)
    cot_far = [cot_far] + backwards(lambda r: swap(cot_far, "tensor", r), last)
    cot_far.append(swap(cot_late, "tensor", last))

    first = together([n_two, *two_got])
    twos = [first] + backwards(lambda r: swap(first, "tensor", r), last)
    _, late = tied(cot_far[:last], first)
    twos.append(swap(late, "tensor", last))

    run = functools.partial(
        run_experts, experts, base, router=router, wcat=wcat, down_flat=down_flat
    )
    counts = call(counts_kernel, [shape((1, LANES), F32)], (*cot_near, *cot_far), "counts")[0]
    counts = counts + swap(counts, "dp", 1)
    balance = experts * (counts / (token_count * TOP)) / token_count
    made = [run(twos[0], cot_near[0], cot_far[0], kind=F32)]
    got = []
    for r in around:
        made[-1], (two, cot) = tied(made[-1], (twos[r], cot_far[r]))
        if r == last:
            balance, two = tied(balance, two)
        made.append(run(two, cot_near[r], cot, kind=BF, apart=r == last))
        if r < last:
            got.append(swap(made[-1][3], "tensor", r))
    cots, dgus, hids, ds, moes = zip(*made)
    near_last, *far_last = ds[last]
    from_last = deal(far_last, "expert")
    grads = run_grads(twos, dgus, hids, cots, local, hidden)
    grads, (got, from_last) = tied(grads, (got, from_last))
    near, *across = split_sum([ds[0], *got], "dn_sum")
    across[0], middle = tied(across[0], moes[1:last])
    across = deal(across, "expert")
    across[0], near_last = tied(across[0], near_last)
    through = added([near_last, *from_last], BF, "through")
    near_sums = [near, swap(through, "tensor", last), *across]
    moe_got = [swap(middle[r - 1], "tensor", r) for r in range(1, last)]
    moe_got, near_sums = tied(moe_got, near_sums)

    wide, dh, small = call(
        functools.partial(norm_back_kernel, experts, len(near_sums)),
        [shape((rows, wide_width), BF), shape((rows, width), F32), shape((8, width), F32)],
        (h, n_two, gain_two, router, balance, cot_near[0], *near_sums),
        "norm_back",
        "v",
        "vvv",
    )
    wides = [wide] + backwards(lambda r: swap(wide, "tensor", r), tensor_size)
    _, late_grads = tied(wide, grads)
    grads_got = swap(late_grads, "dp", 1)
    grads_got, wides = tied(grads_got, wides)
    wides, moe_last = tied(wides, moes[last])
    moe_got.append(swap(moe_last, "tensor", last))

    wide_all, dqkv, small, *back_parts = call(
        attend_back_kernel,
        [
            shape((seq_len, wide_width), BF),
            shape((seq_len, heads + 2 * keys_wide), BF),
            shape((8, width), F32),
            shape((rows, width), F32),
        ]
        + [shape((rows, width), BF)] * last,
        (t_at, *wides, tokens, q, k, v, lse, w_query, w_key, w_value, w_output, cosine, sine, small),
        "attend_back",
        "s" + "v" * tensor_size + "b" * 11,
        "bb",
        limit=58,
        scratch=[
            pltpu.VMEM((seq_len, heads), BF),
            pltpu.VMEM((seq_len, width), F32),
        ],
        flops=2 * seq_len * width * 4 * heads,
    )
    part_sums = [back_parts[0]] + backwards(lambda r: swap(back_parts[r], "tensor", r), tensor_size)
    half = width // dp_size
    chunk = half // expert_size

    columns = heads + 2 * keys_wide
    all_columns = columns + heads + LANES
    own_block = pl.BlockSpec((1, rows, width), lambda i: (0, 0, 0))
    kept, sent = call(
        dense_kernel,
        [shape((half, all_columns), F32), shape((half, all_columns), BF)],
        (d_at, *twos, wide_all, o, n_one, dqkv),
        "dense",
        ["s"] + [own_block] * tensor_size + ["b"] * 4,
        "vv",
        limit=54,
        scratch=[
            pltpu.VMEM((seq_len, width), BF),
            pltpu.VMEM((width, all_columns), F32),
        ],
        flops=1,
    )
    mine, *others, small = call(
        kept_and_dealt_kernel,
        [shape((chunk, all_columns), F32)]
        + [shape((chunk, all_columns), BF)] * (expert_size - 1)
        + [shape((8, width), F32)],
        (e_at, kept, swap(sent, "dp", 1), small, swap(small, "dp", 1)),
        "dense_dealt",
        "s",
    )
    others = deal(others, "expert")
    grad_gate = both_copies(grads, grads_got, 0)
    (grad_gate, others[0]), part_sums = tied((grad_gate, others[0]), part_sums)
    moe_near, *moe_across = split_sum([moes[0], *moe_got], "moe_sum")
    moe_across, part_sums = tied(moe_across, part_sums)
    moe_sums = [moe_near, *deal(moe_across, "expert")]
    ig = call(
        input_grad_kernel, [shape((rows, width), BF)], (xq, gain_one, dh, *part_sums), "input_grad", "bbbb", limit=58
    )[0]
    igs = [ig] + backwards(lambda r: swap(ig, "tensor", r), tensor_size)
    grad_up = both_copies(grads, grads_got, 1)
    grad_up, others = tied(grad_up, others)
    g_query, g_key, g_value, g_out, g_router, small = call(
        dense_sum_kernel,
        [
            shape((chunk, heads), F32),
            shape((chunk, keys_wide), F32),
            shape((chunk, keys_wide), F32),
            shape((heads, chunk), F32),
            shape((chunk, LANES), F32),
            shape((8, width), F32),
        ],
        (e_at, small, mine, *others),
        "dense_sum",
        "s",
        "bbbbbv",
        scratch=[pltpu.VMEM((expert_size, 8, width), F32)],
    )
    if chunk * HD != 8 * width:
        small = jnp.sum(lax.all_gather(small, "expert"), axis=0)
    igs, small = tied(igs, small)
    input_grad = call(
        natural_kernel, [shape((seq_len, width), F32)], (t_at, *igs), "input_grad_whole", "s", "b"
    )[0]
    out_piece = call(out_kernel, [shape((rows + 16, width), BF)], (h, small, *moe_sums), "out_piece")[0]
    outs = [out_piece] + backwards(lambda r: swap(out_piece, "tensor", r), tensor_size)
    grad_down = both_copies(grads, grads_got, 2)
    grad_down, outs = tied(grad_down, outs)
    output, small = call(
        out_whole_kernel,
        [shape((seq_len, width), BF), shape((8, width), F32)],
        (t_at, *outs),
        "output",
        "s",
        "bv",
        scratch=[pltpu.VMEM((tensor_size, 8, width), F32)],
    )
    at = (d_me * expert_size + e_me) * chunk
    loss_value = (experts * balance * small[2:3, :LANES])[0, :experts]
    return (
        output,
        loss_value,
        input_grad,
        lax.dynamic_slice(small, (0, at), (1, chunk))[0],
        g_query,
        g_key,
        g_value,
        g_out,
        lax.dynamic_slice(small, (1, at), (1, chunk))[0],
        g_router[:, :experts],
        grad_gate,
        grad_up,
        grad_down,
    )


def solution(mesh):
    rows = ("dp", "expert")
    placed = (
        P(rows, None),
        P(rows, None),
        P(),
        P(None, "tensor"),
        P(None, "tensor"),
        P(None, "tensor"),
        P("tensor", None),
        P(),
        P(),
        P("expert", None, "tensor"),
        P("expert", None, "tensor"),
        P("expert", "tensor", None),
        P(rows, None),
    )
    return jax.shard_map(
        on_device,
        mesh=mesh,
        in_specs=placed,
        out_specs=(
            P(rows, None),
            P(),
            P(rows, None),
            P(rows),
            P(rows, "tensor"),
            P(rows, "tensor"),
            P(rows, "tensor"),
            P("tensor", rows),
            P(rows),
            P(rows, None),
            P("expert", None, "tensor"),
            P("expert", None, "tensor"),
            P("expert", "tensor", None),
        ),
        check_vma=False,
    )
```
